32 devices in a mesh: gx: 4 (over y, x), gy: 4 (over z), gz: 2 (over core).
Axes of the slice: x: 2, y: 2, z: 4, core: 2. Of those that a mesh axis runs over, the one named last changes fastest.
Arguments:
- phase: int32 [32, 256, 256], P('gx', 'gy', 'gz'), may hold values 0 or 1
- density: float32 [32, 256, 256], P('gx', 'gy', 'gz'), may hold values from 0.5 to 2
- rhs: float32 [1, 32, 256, 256], P(None, 'gx', 'gy', 'gz'), may hold values from -6 to 6
Outputs:
- scaled_solution: float32 [1, 32, 256, 256], P(None, 'gx', 'gy', 'gz')
- residual: float32 [1, 32, 256, 256], P(None, 'gx', 'gy', 'gz')
The draws below stay inside these ranges and needn't reach their ends.
All inputs are finite; a program needn't handle non-finite values. No bound on the sum of `phase` on one device may be relied on, other than what follows from the above.
Results may differ from the reference program's by a relative error of at most 0.0003.
Values sent between devices are 32-bit elements; how exact they have to be, the bound alone decides.
No kernel may reach another device: no remote copies, remote signals or barrier semaphores. Data moves between devices by JAX's collectives and lax.ppermute only.
A program may use at most 128 MiB of HBM per device.

```python
import math
import jax
import jax.numpy as jnp
from jax import lax

NRHS = 1
LEVELS = 4
SWEEPS = 2
COARSE_SWEEPS = 4
NX = 32
NY = 256
NZ = 256


def draw_rhs(key, part):
    shape = (NRHS, NX, NY, NZ)
    values = jnp.clip(jax.random.normal(key, shape, jnp.float32), -6.0, 6.0)
    return values.astype(jnp.float32)


def plant(result, key, smallest, largest):
    longest = result.shape.index(max(result.shape))
    spots = []
    for shift in (0, 1):
        where = [jax.random.randint(jax.random.fold_in(key, axis), (), 0, length) for axis, length in enumerate(result.shape)]
        where[longest] = (where[longest] + shift) % result.shape[longest]
        spots.append(tuple(where))
    return result.at[spots[0]].set(smallest).at[spots[1]].set(largest)


def steps_of(key, dims, shards, least, top_value):
    level, own = 1.0, jax.random.fold_in(key, 6)
    for axis_at, blocks in shards:
        steps = jnp.exp(jax.random.uniform(jax.random.fold_in(own, axis_at), (blocks,), jnp.float32, least / len(shards), top_value / len(shards)))
        level = level * jnp.repeat(steps, dims[axis_at] // blocks).reshape([-1 if axis == axis_at else 1 for axis in range(len(dims))])
    return level


def setup_inputs(seed: int = 0) -> dict:
    streams_of = jax.random.split(jax.random.key(seed), 4)
    phase = plant((jax.random.randint(streams_of[0], (NX, NY, NZ), 0, 3) < 1).astype(jnp.int32), jax.random.fold_in(streams_of[0], 1), 0, 1)
    density = jnp.clip(jnp.exp(math.log(2.0) - 1.3862944 * jax.random.uniform(streams_of[1], (NX, NY, NZ), jnp.float32) ** steps_of(streams_of[1], (NX, NY, NZ), ((0, 4), (1, 4), (2, 2)), -0.2, 0.2)), 0.5, 2.0)
    rhs = draw_rhs(jax.random.fold_in(streams_of[3], 71), 0)
    return {"phase": phase, "density": density, "rhs": rhs}


damping = 2.0 / 3.0


def face_pair(rho, up_nb, down_nb, top, bottom):
    face_up = 2.0 / (rho + up_nb)
    face_down = 2.0 / (rho + down_nb)
    return face_up, face_down, jnp.where(top, 0.0, face_up), jnp.where(bottom, 0.0, face_down)


def make_coef(rho):
    nx, ny, nz = rho.shape
    ext = jnp.pad(rho, 1, mode="edge")
    row_x = lax.broadcasted_iota(jnp.int32, (nx, 1, 1), 0)
    row_y = lax.broadcasted_iota(jnp.int32, (1, ny, 1), 1)
    row_z = lax.broadcasted_iota(jnp.int32, (1, 1, nz), 2)
    fxu, fxd, kxu, kxd = face_pair(rho, ext[2:, 1:-1, 1:-1], ext[:-2, 1:-1, 1:-1], row_x == nx - 1, row_x == 0)
    fyu, fyd, kyu, kyd = face_pair(rho, ext[1:-1, 2:, 1:-1], ext[1:-1, :-2, 1:-1], row_y == ny - 1, row_y == 0)
    fzu, fzd, kzu, kzd = face_pair(rho, ext[1:-1, 1:-1, 2:], ext[1:-1, 1:-1, :-2], row_z == nz - 1, row_z == 0)
    diag = fxu + fxd + fyu + fyd + fzu + fzd
    return jnp.stack([diag, kxu, kxd, kyu, kyd, kzu, kzd])


def blocks(a):
    s = a.shape
    lead = s[:-3]
    return a.reshape(lead + (s[-3] // 2, 2, s[-2] // 2, 2, s[-1] // 2, 2)).sum(axis=(-5, -3, -1))


def prolong(e):
    s = e.shape
    lead = s[:-3]
    wide = e.reshape(lead + (s[-3], 1, s[-2], 1, s[-1], 1))
    wide = jnp.broadcast_to(wide, lead + (s[-3], 2, s[-2], 2, s[-1], 2))
    return wide.reshape(lead + (2 * s[-3], 2 * s[-2], 2 * s[-1]))


def face_x(a, offset):
    b = a[offset::2]
    n0, n1, n2 = b.shape
    return b.reshape(n0, n1 // 2, 2, n2 // 2, 2).sum(axis=(2, 4))


def face_y(a, offset):
    b = a[:, offset::2]
    n0, n1, n2 = b.shape
    return b.reshape(n0 // 2, 2, n1, n2 // 2, 2).sum(axis=(1, 4))


def face_z(a, offset):
    b = a[:, :, offset::2]
    n0, n1, n2 = b.shape
    return b.reshape(n0 // 2, 2, n1 // 2, 2, n2).sum(axis=(1, 3))


def coarsen(coef):
    inner = face_x(coef[1], 0) + face_y(coef[3], 0) + face_z(coef[5], 0)
    diag = blocks(coef[0]) - 2.0 * inner
    return jnp.stack([diag, face_x(coef[1], 1), face_x(coef[2], 0), face_y(coef[3], 1), face_y(coef[4], 0), face_z(coef[5], 1), face_z(coef[6], 0)])


def stencil(padded, field, coef):
    beside = coef[1] * padded[:, 2:, 1:-1, 1:-1] + coef[2] * padded[:, :-2, 1:-1, 1:-1]
    beside = beside + coef[3] * padded[:, 1:-1, 2:, 1:-1] + coef[4] * padded[:, 1:-1, :-2, 1:-1]
    beside = beside + coef[5] * padded[:, 1:-1, 1:-1, 2:] + coef[6] * padded[:, 1:-1, 1:-1, :-2]
    return coef[0] * field - beside


def apply_op(field, coef):
    return stencil(jnp.pad(field, ((0, 0), (1, 1), (1, 1), (1, 1))), field, coef)


def sweep(field, source, coef):
    return field + (damping * (source - apply_op(field, coef))) / coef[0]


def vcycle(level, source, coefs):
    coef = coefs[level]
    field = jnp.zeros_like(source)
    if level == LEVELS - 1:
        for step in range(COARSE_SWEEPS):
            field = sweep(field, source, coef)
        return field
    for step in range(SWEEPS):
        field = sweep(field, source, coef)
    remain = source - apply_op(field, coef)
    correction = vcycle(level + 1, blocks(remain), coefs)
    field = field + prolong(correction)
    for step in range(SWEEPS):
        field = sweep(field, source, coef)
    return field


def reference(phase, density, rhs):
    rho = jnp.where(phase == 1, 1000.0, 1.0).astype(jnp.float32) * density
    coefs = [make_coef(rho)]
    for level in range(LEVELS - 1):
        coefs.append(coarsen(coefs[-1]))
    solution = vcycle(0, rhs, coefs)
    scaled_solution = coefs[0][0] * solution
    residual = rhs - apply_op(solution, coefs[0])
    return scaled_solution, residual
```

```python
import functools

import jax
import jax.numpy as jnp
from jax import lax
from jax.experimental import pallas as pl
from jax.experimental.pallas import tpu as pltpu
from jax.sharding import PartitionSpec as P


DAMPING = 2.0 / 3.0
LANES = 128
WIDE = 256
F32 = jnp.float32
VMEM_LIMIT = 52 * 1024 * 1024


class Plan:
    def __init__(self, sizes, shape):
        self.gx, self.gy, self.gz = sizes
        self.px, self.ny, self.nz = shape
        self.nx = self.px * self.gx
        self.by = self.ny // self.gx
        self.blocks = self.gx * self.gy
        self.rows = 3 * self.by
        order = [0, 1, 3, 2] if self.gx == 4 else list(range(self.gx))
        self.place = [order.index(i) for i in range(self.gx)]
        self.order = order

    def device(self, block):
        j, q = divmod(block, self.gx)
        i = self.order[q if j % 2 == 0 else self.gx - 1 - q]
        return i * self.gy + j

    def part(self, i, odd):
        q = self.place[i]
        return q + odd * (self.gx - 1 - 2 * q)

    def block_here(self):
        i, j = lax.axis_index("gx"), lax.axis_index("gy")
        q = sum(jnp.where(i == k, self.place[k], 0) for k in range(self.gx))
        odd = lax.rem(j, 2)
        return j * self.gx + q + odd * (self.gx - 1 - 2 * q)


def y_up(a):
    return pltpu.roll(a, a.shape[0] - 1, 0)


def y_down(a):
    return pltpu.roll(a, 1, 0)


def z_up(a, g):
    return pltpu.roll(a, a.shape[1] - g, 1)


def z_down(a, g):
    return pltpu.roll(a, g, 1)


def each(count, step, body):
    if count <= step:
        for i in range(count):
            body(i)
        return

    def go(c, _):
        for k in range(step):
            body(c * step + k)
        return 0

    lax.fori_loop(0, count // step, go, 0)


class Wide:
    def __init__(self, ref):
        self.ref = ref
        self.shape = (ref.shape[0], ref.shape[2], WIDE)

    def __getitem__(self, key):
        p, rows = key if isinstance(key, tuple) else (key, slice(None))
        return jnp.concatenate([self.ref[p, 0, rows, :], self.ref[p, 1, rows, :]], axis=1)

    def __setitem__(self, key, value):
        p, rows = key if isinstance(key, tuple) else (key, slice(None))
        self.ref[p, 0, rows, :] = value[:, :LANES]
        self.ref[p, 1, rows, :] = value[:, LANES:]


class Level:
    def __init__(self, n, g, kx, ky, kz, d, w, f):
        self.n, self.g = n, g
        self.kx, self.ky, self.kz, self.d, self.w, self.f = kx, ky, kz, d, w, f
        self.step = 2

    def beside(self, u, p):
        here = u[p]
        s = self.kx[p + 1] * u[jnp.minimum(p + 1, self.n - 1)]
        s = s + self.kx[p] * u[jnp.maximum(p - 1, 0)]
        ky = self.ky[p]
        s = s + (ky * y_up(here) + y_down(ky * here))
        kz = self.kz[p]
        return s + (kz * z_up(here, self.g) + z_down(kz * here, self.g))

    def first(self, u):
        def body(p):
            w = DAMPING / self.d[p]
            self.w[p] = w
            u[p] = w * self.f[p]

        each(self.n, self.step, body)

    def sweep(self, u, v):
        def body(p):
            v[p] = (1.0 / 3.0) * u[p] + self.w[p] * (self.f[p] + self.beside(u, p))

        each(self.n, self.step, body)

    def residual_pairs(self, u, r):
        def one(p):
            return self.f[p] + self.beside(u, p) - self.d[p] * u[p]

        def body(x):
            r[x] = one(2 * x) + one(2 * x + 1)

        each(self.n // 2, 1, body)

    def coarsen(self, r, base, count, keep):
        g = self.g
        even = pl.ds(base, count, stride=2)
        odd = pl.ds(base + 1, count, stride=2)
        lane = lax.broadcasted_iota(jnp.int32, (count, WIDE), 1)
        low = (lane & g) == 0

        def z_pair(a):
            return a + jnp.where(low, z_up(a, g), z_down(a, g))

        def both(ref, p, rows):
            return ref[p, rows] + ref[p + 1, rows]

        def body(x):
            p = 2 * x
            kx = self.kx[p + 2, even] + self.kx[p + 2, odd]
            inner = self.kx[p + 1, even] + self.kx[p + 1, odd]
            kz = both(self.kz, p, even) + both(self.kz, p, odd)
            inner = inner + both(self.ky, p, even) + jnp.where(low, kz, 0.0)
            d = both(self.d, p, even) + both(self.d, p, odd) - 2.0 * inner
            keep(
                x,
                z_pair(r[x, even] + r[x, odd]),
                z_pair(kx),
                z_pair(both(self.ky, p, odd)),
                jnp.where(low, z_up(kz, g), kz),
                z_pair(d),
            )

        each(self.n // 2, 1, body)

    def correct(self, u, e, rows, t):
        count = u.shape[1] // 2

        def body(x):
            part = e[x, rows]
            t[x, pl.ds(0, count, stride=2)] = part
            t[x, pl.ds(1, count, stride=2)] = part
            wide = t[x]
            u[2 * x] = u[2 * x] + wide
            u[2 * x + 1] = u[2 * x + 1] + wide

        each(self.n // 2, 1, body)


def store_level(level):
    def keep(x, f, kx, ky, kz, d):
        level.f[x] = f
        level.kx[x + 1] = kx
        level.ky[x] = ky
        level.kz[x] = kz
        level.d[x] = d

    level.kx[0] = jnp.zeros(level.kx.shape[1:], F32)
    return keep


def prepare_kernel(plan, phase, density, rhs, out):
    odd = lax.rem(lax.axis_index("gy"), 2)
    for i in range(plan.gx):
        start = pl.multiple_of(plan.part(i, odd) * plan.by, plan.by)
        rows = pl.ds(start, plan.by)
        heavy = jnp.where(phase[:, rows, :] == 1, 1000.0, 1.0).astype(F32)
        out[i, 0] = heavy * density[:, rows, :]
        out[i, 1] = rhs[0, :, rows, :]


def split_dot(a, b):
    high = a.astype(jnp.bfloat16)
    rest = a - high.astype(F32)
    mid = rest.astype(jnp.bfloat16)
    low = (rest - mid.astype(F32)).astype(jnp.bfloat16)
    dot = functools.partial(jnp.dot, preferred_element_type=F32)
    return dot(high, b) + dot(mid, b) + dot(low, b)


def down_kernel(plan, c, lo, hi, zc, zlo, zhi, *refs):
    gathered, pack = refs[0], refs[-1]
    outs, scratch = [Wide(r) for r in refs[1:13]], [Wide(r) for r in refs[13:-1]]
    f_w, u_w, kx_w, ky_w, kz_w, d_w, f1, u1, kx1, ky1, kz1, d1 = outs
    rho_s, f0, kx0, ky0, kz0, d0, w0, ua, ub, r0, w1, uc, r1 = scratch
    nx, by, rows, px = plan.nx, plan.by, plan.rows, plan.px
    shape = (rows, WIDE)
    window = slice(by // 2, rows - by // 2)

    y = (plan.block_here() - 1) * by + lax.broadcasted_iota(jnp.int32, shape, 0)
    lane = lax.broadcasted_iota(jnp.int32, shape, 1)
    z = lax.axis_index("gz") * LANES + jnp.where(lane < LANES + LANES // 2, lane, lane - WIDE)
    y_count, z_count = plan.by * plan.blocks, plan.nz * plan.gz
    inside = (y >= 0) & (y < y_count) & (z >= 0) & (z < z_count)
    y_top, y_bottom = y == y_count - 1, y == 0
    z_top, z_bottom = z == z_count - 1, z == 0
    y_open = (y >= 0) & (y < y_count - 1)
    z_open = (z >= 0) & (z < z_count - 1)

    def load(p, field):
        s, k = lax.div(p, px), lax.rem(p, px)
        parts = [
            jnp.concatenate([a[s, field, k], b[s, field, k]], axis=1)
            for a, b in ((lo, zlo), (c, zc), (hi, zhi))
        ]
        return jnp.concatenate(parts, axis=0)

    def take(p):
        rho_s[p] = jnp.where(inside, load(p, 0), 1.0)
        f = load(p, 1)
        f0[p] = f
        f_w[p] = f[window]

    each(nx, 2, take)

    first = rho_s[0]
    kx0[0] = 2.0 / (first + first)

    def faces(p):
        rho = rho_s[p]
        alone = 1.0 / rho
        x_up = 2.0 / (rho + rho_s[jnp.minimum(p + 1, nx - 1)])
        x_down = kx0[p]
        kx0[p + 1] = x_up
        up = 2.0 / (rho + jnp.where(y_top, rho, y_up(rho)))
        down = jnp.where(y_bottom, alone, y_down(up))
        right = 2.0 / (rho + jnp.where(z_top, rho, z_up(rho, 1)))
        left = jnp.where(z_bottom, alone, z_down(right, 1))
        ky = jnp.where(y_open, up, 0.0)
        kz = jnp.where(z_open, right, 0.0)
        d = x_up + x_down + up + down + right + left
        w = DAMPING / d
        ky0[p], kz0[p], d0[p], w0[p] = ky, kz, d, w
        ua[p] = w * f0[p]
        kx_w[p] = x_down[window]
        ky_w[p], kz_w[p], d_w[p] = ky[window], kz[window], d[window]

    each(nx, 2, faces)
    nothing = jnp.zeros(shape, F32)
    kx0[0] = nothing
    kx0[nx] = nothing
    kx_w[0] = nothing[window]
    kx_w[nx] = nothing[window]

    fine = Level(nx, 1, kx0, ky0, kz0, d0, w0, f0)
    fine.sweep(ua, ub)
    fine.residual_pairs(ub, r0)

    def show(p):
        u_w[p] = ub[p, window]

    each(nx, 4, show)

    middle = Level(nx // 2, 2, kx1, ky1, kz1, d1, w1, f1)
    fine.coarsen(r0, 0, rows // 2, store_level(middle))
    middle.first(uc)
    middle.sweep(uc, u1)
    middle.residual_pairs(u1, r1)

    half = nx // 8
    four = by // 4

    def keep(x, *fields):
        for t, a in enumerate(fields):
            at = (t * half + x % half) * four
            pack[x // half, pl.ds(at, four), :] = a

    own = Level(nx // 2, 2, kx1, ky1, kz1, d1, w1, f1)
    own_coarsen(own, r1, by // 2, four, keep)

    lane = lax.broadcasted_iota(jnp.int32, (WIDE, LANES), 0)
    cell = lax.broadcasted_iota(jnp.int32, (WIDE, LANES), 1)
    total = jnp.zeros(gathered.shape, F32)
    for h in range(2):
        pick = jnp.where(lane == 4 * (cell - h * (WIDE // 4)), 1.0, 0.0).astype(jnp.bfloat16)
        total = total + split_dot(pack[h], pick)
    gathered[...] = total


def own_coarsen(level, r, base, count, keep):
    n = level.n
    g = level.g
    even = pl.ds(base, count, stride=2)
    odd = pl.ds(base + 1, count, stride=2)
    lane = lax.broadcasted_iota(jnp.int32, (count, WIDE), 1)
    low = (lane & g) == 0

    def z_pair(a):
        return a + jnp.where(low, z_up(a, g), z_down(a, g))

    def both(ref, p, rows):
        return ref[p, rows] + ref[p + 1, rows]

    for x in range(n // 2):
        p = 2 * x
        kx = level.kx[p + 2, even] + level.kx[p + 2, odd]
        inner = level.kx[p + 1, even] + level.kx[p + 1, odd]
        kz = both(level.kz, p, even) + both(level.kz, p, odd)
        inner = inner + both(level.ky, p, even) + jnp.where(low, kz, 0.0)
        d = both(level.d, p, even) + both(level.d, p, odd) - 2.0 * inner
        keep(
            x,
            z_pair(r[x, even] + r[x, odd]),
            z_pair(kx),
            z_pair(both(level.ky, p, odd)),
            jnp.where(low, z_up(kz, g), kz),
            z_pair(d),
        )


def up_kernel(plan, g, f0, u0, kx0, ky0, kz0, d0, f1, u1, kx1, ky1, kz1, d1, out, *scratch):
    nx, by, px = plan.nx, plan.by, plan.px
    stage, scratch = scratch[0], [Wide(r) for r in scratch[1:]]
    f0, u0, kx0, ky0, kz0, d0 = [Wide(r) for r in (f0, u0, kx0, ky0, kz0, d0)]
    f1, u1, kx1, ky1, kz1, d1 = [Wide(r) for r in (f1, u1, kx1, ky1, kz1, d1)]
    f2, kx2, ky2, kz2, d2, w2, ua2, ub2, r2 = scratch[:9]
    f3, kx3, ky3, kz3, d3, w3, ua3, ub3 = scratch[9:17]
    pad2, t2, t1, t0, w1, ua1, ub1, w0, ua0, ub0 = scratch[17:]
    half, four = nx // 8, by // 4

    for block in range(plan.blocks):
        i, j = divmod(block, plan.gy)
        at = (j * plan.gx + plan.part(i, j % 2)) * four
        for k in range(5 * half):
            stage[k, pl.ds(at, four), :] = g[block, pl.ds(k * four, four), :]

    cell = lax.broadcasted_iota(jnp.int32, (LANES, 2 * WIDE), 0)
    lane = lax.broadcasted_iota(jnp.int32, (LANES, 2 * WIDE), 1)
    spread = jnp.where(cell == lax.div(lane, 4), 1.0, 0.0).astype(jnp.bfloat16)
    for t, ref in enumerate((f2, kx2, ky2, kz2, d2)):
        for k in range(half):
            both = split_dot(stage[t * half + k], spread)
            shift = 1 if t == 1 else 0
            ref[k + shift] = both[:, :WIDE]
            ref[k + half + shift] = both[:, WIDE:]
    kx2[0] = jnp.zeros(kx2.shape[1:], F32)

    two = Level(nx // 4, 4, kx2, ky2, kz2, d2, w2, f2)
    three = Level(nx // 8, 8, kx3, ky3, kz3, d3, w3, f3)
    two.first(ua2)
    two.sweep(ua2, ub2)
    two.residual_pairs(ub2, r2)
    two.coarsen(r2, 0, f2.shape[1] // 2, store_level(three))
    three.first(ua3)
    three.sweep(ua3, ub3)
    three.sweep(ub3, ua3)
    three.sweep(ua3, ub3)
    two.correct(ub2, ub3, slice(None), t2)
    two.sweep(ub2, ua2)
    two.sweep(ua2, ub2)

    height = f2.shape[1]
    empty = jnp.zeros((8, WIDE), F32)
    for x in range(nx // 4):
        pad2[x, pl.ds(0, 8)] = empty
        pad2[x, pl.ds(8, height)] = ub2[x]
        pad2[x, pl.ds(8 + height, 8)] = empty
    one = Level(nx // 2, 2, kx1, ky1, kz1, d1, w1, f1)
    for p in range(nx // 2):
        w1[p] = DAMPING / d1[p]
        ua1[p] = u1[p]
    rows = pl.ds(8 + (plan.block_here() - 1) * four, 3 * four)
    one.correct(ua1, pad2, rows, t1)
    one.sweep(ua1, ub1)
    one.sweep(ub1, ua1)

    zero = Level(nx, 1, kx0, ky0, kz0, d0, w0, f0)

    def begin(p):
        w0[p] = DAMPING / d0[p]
        ua0[p] = u0[p]

    each(nx, 2, begin)
    zero.correct(ua0, ua1, slice(by // 4, by // 4 + by), t0)
    zero.sweep(ua0, ub0)
    zero.sweep(ub0, ua0)
    own = slice(by // 2, by // 2 + by)

    def finish(p):
        s, k = lax.div(p, px), lax.rem(p, px)
        u = ua0[p]
        scaled = d0[p] * u
        r = f0[p] + zero.beside(ua0, p) - scaled
        out[s, 0, k] = scaled[own, :LANES]
        out[s, 1, k] = r[own, :LANES]

    each(nx, 2, finish)


def place_kernel(plan, parts, scaled, residual):
    odd = lax.rem(lax.axis_index("gy"), 2)
    for i in range(plan.gx):
        start = pl.multiple_of(plan.part(i, odd) * plan.by, plan.by)
        rows = pl.ds(start, plan.by)
        scaled[0, :, rows, :] = parts[i, 0]
        residual[0, :, rows, :] = parts[i, 1]


def in_tiles(shapes):
    return [(s[0], 2, s[1], LANES) if s[-1] == WIDE else s for s in shapes]


def call(kernel, out_shape, scratch=()):
    return pl.pallas_call(
        kernel,
        out_shape=out_shape,
        scratch_shapes=[pltpu.VMEM(s, F32) for s in scratch],
        compiler_params=pltpu.CompilerParams(vmem_limit_bytes=VMEM_LIMIT),
    )


def f32(*shape):
    return jax.ShapeDtypeStruct(shape, F32)


def beside_in_z(plan, a):
    count = plan.gz
    if count == 2:
        return lax.ppermute(a, "gz", [(0, 1), (1, 0)])
    cut = LANES // 2
    right = lax.ppermute(a[..., :cut], "gz", [(i + 1, i) for i in range(count - 1)])
    left = lax.ppermute(a[..., cut:], "gz", [(i, i + 1) for i in range(count - 1)])
    return jnp.concatenate([right, left], axis=-1)


def on_device(plan, phase, density, rhs):
    nx, by, rows, px = plan.nx, plan.by, plan.rows, plan.px
    parts = call(
        functools.partial(prepare_kernel, plan), f32(plan.gx, 2, px, by, LANES)
    )(phase, density, rhs)
    c = lax.all_to_all(parts, "gx", 0, 0, tiled=True)
    up = [(plan.device(b), plan.device(b + 1)) for b in range(plan.blocks - 1)]
    lo = lax.ppermute(c, ("gx", "gy"), up)
    hi = lax.ppermute(c, ("gx", "gy"), [(b, a) for a, b in up])
    zc = beside_in_z(plan, c)
    zlo = beside_in_z(plan, lo)
    zhi = beside_in_z(plan, hi)

    mid, win = rows // 2, rows - by
    four = by // 4
    packed = 5 * (nx // 8) * four
    level1 = [f32(nx // 2 + (k == 2), 2, mid, LANES) for k in range(6)]
    level0 = [f32(nx + (k == 2), 2, win, LANES) for k in range(6)]
    full = (nx, rows, WIDE)
    scratch = [full, full, (nx + 1, rows, WIDE), full, full, full, full, full, full]
    scratch += [(nx // 2, rows, WIDE), (nx // 2, mid, WIDE), (nx // 2, mid, WIDE)]
    scratch += [(nx // 4, mid, WIDE)]
    scratch = in_tiles(scratch) + [(2, packed, WIDE)]
    down = call(
        functools.partial(down_kernel, plan), [f32(packed, LANES)] + level0 + level1, scratch
    )(c, lo, hi, zc, zlo, zhi)

    gathered = lax.all_gather(down[0], ("gx", "gy"))

    height = four * plan.blocks
    l2 = (nx // 4, height, WIDE)
    l3 = (nx // 8, height // 2, WIDE)
    l1 = (nx // 2, mid, WIDE)
    l0 = (nx, win, WIDE)
    scratch = [(5 * (nx // 8), height, LANES), l2, (nx // 4 + 1, height, WIDE), l2, l2, l2, l2, l2, l2]
    scratch += [(nx // 8, height, WIDE)]
    scratch += [l3, (nx // 8 + 1, height // 2, WIDE), l3, l3, l3, l3, l3, l3]
    scratch += [(nx // 4, height + 16, WIDE), (nx // 8, height, WIDE), (nx // 4, mid, WIDE), (nx // 2, win, WIDE)]
    scratch += [l1, l1, l1, l0, l0, l0]
    scratch = in_tiles(scratch)
    result = call(
        functools.partial(up_kernel, plan), f32(plan.gx, 2, px, by, LANES), scratch
    )(gathered, *down[1:])

    result = lax.all_to_all(result, "gx", 0, 0, tiled=True)
    return call(
        functools.partial(place_kernel, plan), [f32(1, px, plan.ny, LANES)] * 2
    )(result)


def solution(mesh):
    sizes = [mesh.shape[a] for a in ("gx", "gy", "gz")]

    def local(phase, density, rhs):
        return tuple(on_device(Plan(sizes, phase.shape), phase, density, rhs))

    in_specs = (P("gx", "gy", "gz"), P("gx", "gy", "gz"), P(None, "gx", "gy", "gz"))
    out_specs = (P(None, "gx", "gy", "gz"), P(None, "gx", "gy", "gz"))
    return jax.shard_map(local, mesh=mesh, in_specs=in_specs, out_specs=out_specs, check_vma=False)
```

```python
import functools

import jax
import jax.numpy as jnp
from jax import lax
from jax.experimental import pallas as pl
from jax.experimental.pallas import tpu as pltpu
from jax.sharding import PartitionSpec as P


DAMPING = 2.0 / 3.0
LANES = 128
WIDE = 256
F32 = jnp.float32
VMEM_LIMIT = 24 * 1024 * 1024


class Plan:
    def __init__(self, sizes, shape):
        self.gx, self.gy, self.gz = sizes
        self.px, self.ny, self.nz = shape
        self.nx = self.px * self.gx
        self.by = self.ny // self.gx
        self.blocks = self.gx * self.gy
        self.rows = 3 * self.by
        order = [0, 1, 3, 2] if self.gx == 4 else list(range(self.gx))
        self.place = [order.index(i) for i in range(self.gx)]
        self.order = order

    def device(self, block):
        j, q = divmod(block, self.gx)
        i = self.order[q if j % 2 == 0 else self.gx - 1 - q]
        return i * self.gy + j

    def part(self, i, odd):
        q = self.place[i]
        return q + odd * (self.gx - 1 - 2 * q)

    def block_here(self):
        i, j = lax.axis_index("gx"), lax.axis_index("gy")
        q = sum(jnp.where(i == k, self.place[k], 0) for k in range(self.gx))
        odd = lax.rem(j, 2)
        return j * self.gx + q + odd * (self.gx - 1 - 2 * q)


def y_up(a):
    return pltpu.roll(a, a.shape[0] - 1, 0)


def y_down(a):
    return pltpu.roll(a, 1, 0)


def z_up(a, g):
    return pltpu.roll(a, a.shape[1] - g, 1)


def z_down(a, g):
    return pltpu.roll(a, g, 1)


def each(count, step, body):
    if count <= step:
        for i in range(count):
            body(i)
        return

    def go(c, _):
        for k in range(step):
            body(c * step + k)
        return 0

    lax.fori_loop(0, count // step, go, 0)


class Wide:
    def __init__(self, ref):
        self.ref = ref
        self.shape = (ref.shape[0], ref.shape[2], WIDE)

    def __getitem__(self, key):
        p, rows = key if isinstance(key, tuple) else (key, slice(None))
        return jnp.concatenate([self.ref[p, 0, rows, :], self.ref[p, 1, rows, :]], axis=1)

    def __setitem__(self, key, value):
        p, rows = key if isinstance(key, tuple) else (key, slice(None))
        self.ref[p, 0, rows, :] = value[:, :LANES]
        self.ref[p, 1, rows, :] = value[:, LANES:]


class Level:
    def __init__(self, n, g, kx, ky, kz, d, w, f):
        self.n, self.g = n, g
        self.kx, self.ky, self.kz, self.d, self.w, self.f = kx, ky, kz, d, w, f
        self.step = 2

    def beside(self, u, p):
        here = u[p]
        s = self.kx[p + 1] * u[jnp.minimum(p + 1, self.n - 1)]
        s = s + self.kx[p] * u[jnp.maximum(p - 1, 0)]
        ky = self.ky[p]
        s = s + (ky * y_up(here) + y_down(ky * here))
        kz = self.kz[p]
        return s + (kz * z_up(here, self.g) + z_down(kz * here, self.g))

    def first(self, u):
        def body(p):
            w = DAMPING / self.d[p]
            self.w[p] = w
            u[p] = w * self.f[p]

        each(self.n, self.step, body)

    def sweep(self, u, v):
        def body(p):
            v[p] = (1.0 / 3.0) * u[p] + self.w[p] * (self.f[p] + self.beside(u, p))

        each(self.n, self.step, body)

    def residual_pairs(self, u, r):
        def one(p):
            return self.f[p] + self.beside(u, p) - self.d[p] * u[p]

        def body(x):
            r[x] = one(2 * x) + one(2 * x + 1)

        each(self.n // 2, 1, body)

    def coarsen(self, r, base, count, keep):
        g = self.g
        even = pl.ds(base, count, stride=2)
        odd = pl.ds(base + 1, count, stride=2)
        lane = lax.broadcasted_iota(jnp.int32, (count, WIDE), 1)
        low = (lane & g) == 0

        def z_pair(a):
            return a + jnp.where(low, z_up(a, g), z_down(a, g))

        def both(ref, p, rows):
            return ref[p, rows] + ref[p + 1, rows]

        def body(x):
            p = 2 * x
            kx = self.kx[p + 2, even] + self.kx[p + 2, odd]
            inner = self.kx[p + 1, even] + self.kx[p + 1, odd]
            kz = both(self.kz, p, even) + both(self.kz, p, odd)
            inner = inner + both(self.ky, p, even) + jnp.where(low, kz, 0.0)
            d = both(self.d, p, even) + both(self.d, p, odd) - 2.0 * inner
            keep(
                x,
                z_pair(r[x, even] + r[x, odd]),
                z_pair(kx),
                z_pair(both(self.ky, p, odd)),
                jnp.where(low, z_up(kz, g), kz),
                z_pair(d),
            )

        each(self.n // 2, 1, body)

    def correct(self, u, e, rows, t):
        count = u.shape[1] // 2

        def body(x):
            part = e[x, rows]
            t[x, pl.ds(0, count, stride=2)] = part
            t[x, pl.ds(1, count, stride=2)] = part
            wide = t[x]
            u[2 * x] = u[2 * x] + wide
            u[2 * x + 1] = u[2 * x + 1] + wide

        each(self.n // 2, 1, body)


def store_level(level):
    def keep(x, f, kx, ky, kz, d):
        level.f[x] = f
        level.kx[x + 1] = kx
        level.ky[x] = ky
        level.kz[x] = kz
        level.d[x] = d

    level.kx[0] = jnp.zeros(level.kx.shape[1:], F32)
    return keep


def prepare_kernel(plan, phase, density, rhs, out):
    odd = lax.rem(lax.axis_index("gy"), 2)
    for i in range(plan.gx):
        start = pl.multiple_of(plan.part(i, odd) * plan.by, plan.by)
        rows = pl.ds(start, plan.by)
        heavy = jnp.where(phase[:, rows, :] == 1, 1000.0, 1.0).astype(F32)
        out[i, 0] = heavy * density[:, rows, :]
        out[i, 1] = rhs[0, :, rows, :]


def split_dot(a, b):
    high = a.astype(jnp.bfloat16)
    rest = a - high.astype(F32)
    mid = rest.astype(jnp.bfloat16)
    low = (rest - mid.astype(F32)).astype(jnp.bfloat16)
    dot = functools.partial(jnp.dot, preferred_element_type=F32)
    return dot(high, b) + dot(mid, b) + dot(low, b)


def down_kernel(plan, c, lo, hi, zc, zlo, zhi, *refs):
    gathered, pack = refs[0], refs[-1]
    outs, scratch = [Wide(r) for r in refs[1:13]], [Wide(r) for r in refs[13:-1]]
    f_w, u_w, kx_w, ky_w, kz_w, d_w, f1, u1, kx1, ky1, kz1, d1 = outs
    rho_s, f0, kx0, ky0, kz0, d0, w0, ua, ub, r0, w1, uc, r1 = scratch
    nx, by, rows, px = plan.nx, plan.by, plan.rows, plan.px
    shape = (rows, WIDE)
    window = slice(by // 2, rows - by // 2)

    y = (plan.block_here() - 1) * by + lax.broadcasted_iota(jnp.int32, shape, 0)
    lane = lax.broadcasted_iota(jnp.int32, shape, 1)
    z = lax.axis_index("gz") * LANES + jnp.where(lane < LANES + LANES // 2, lane, lane - WIDE)
    y_count, z_count = plan.by * plan.blocks, plan.nz * plan.gz
    inside = (y >= 0) & (y < y_count) & (z >= 0) & (z < z_count)
    y_top, y_bottom = y == y_count - 1, y == 0
    z_top, z_bottom = z == z_count - 1, z == 0
    y_open = (y >= 0) & (y < y_count - 1)
    z_open = (z >= 0) & (z < z_count - 1)

    def load(p, field):
        s, k = lax.div(p, px), lax.rem(p, px)
        parts = [
            jnp.concatenate([a[s, field, k], b[s, field, k]], axis=1)
            for a, b in ((lo, zlo), (c, zc), (hi, zhi))
        ]
        return jnp.concatenate(parts, axis=0)

    def take(p):
        rho_s[p] = jnp.where(inside, load(p, 0), 1.0)
        f = load(p, 1)
        f0[p] = f
        f_w[p] = f[window]

    each(nx, 2, take)

    first = rho_s[0]
    kx0[0] = 2.0 / (first + first)

    def faces(p):
        rho = rho_s[p]
        alone = 1.0 / rho
        x_up = 2.0 / (rho + rho_s[jnp.minimum(p + 1, nx - 1)])
        x_down = kx0[p]
        kx0[p + 1] = x_up
        up = 2.0 / (rho + jnp.where(y_top, rho, y_up(rho)))
        down = jnp.where(y_bottom, alone, y_down(up))
        right = 2.0 / (rho + jnp.where(z_top, rho, z_up(rho, 1)))
        left = jnp.where(z_bottom, alone, z_down(right, 1))
        ky = jnp.where(y_open, up, 0.0)
        kz = jnp.where(z_open, right, 0.0)
        d = x_up + x_down + up + down + right + left
        w = DAMPING / d
        ky0[p], kz0[p], d0[p], w0[p] = ky, kz, d, w
        ua[p] = w * f0[p]
        kx_w[p] = x_down[window]
        ky_w[p], kz_w[p], d_w[p] = ky[window], kz[window], d[window]

    each(nx, 2, faces)
    nothing = jnp.zeros(shape, F32)
    kx0[0] = nothing
    kx0[nx] = nothing
    kx_w[0] = nothing[window]
    kx_w[nx] = nothing[window]

    fine = Level(nx, 1, kx0, ky0, kz0, d0, w0, f0)
    fine.sweep(ua, ub)
    fine.residual_pairs(ub, r0)

    def show(p):
        u_w[p] = ub[p, window]

    each(nx, 4, show)

    middle = Level(nx // 2, 2, kx1, ky1, kz1, d1, w1, f1)
    fine.coarsen(r0, 0, rows // 2, store_level(middle))
    middle.first(uc)
    middle.sweep(uc, u1)
    middle.residual_pairs(u1, r1)

    half = nx // 8
    four = by // 4

    def keep(x, *fields):
        for t, a in enumerate(fields):
            at = (t * half + x % half) * four
            pack[x // half, pl.ds(at, four), :] = a

    own = Level(nx // 2, 2, kx1, ky1, kz1, d1, w1, f1)
    own_coarsen(own, r1, by // 2, four, keep)

    lane = lax.broadcasted_iota(jnp.int32, (WIDE, LANES), 0)
    cell = lax.broadcasted_iota(jnp.int32, (WIDE, LANES), 1)
    total = jnp.zeros(gathered.shape[1:], F32)
    for h in range(2):
        pick = jnp.where(lane == 4 * (cell - h * (WIDE // 4)), 1.0, 0.0).astype(jnp.bfloat16)
        total = total + split_dot(pack[h], pick)
    for k in range(gathered.shape[0]):
        gathered[k] = total


def own_coarsen(level, r, base, count, keep):
    n = level.n
    g = level.g
    even = pl.ds(base, count, stride=2)
    odd = pl.ds(base + 1, count, stride=2)
    lane = lax.broadcasted_iota(jnp.int32, (count, WIDE), 1)
    low = (lane & g) == 0

    def z_pair(a):
        return a + jnp.where(low, z_up(a, g), z_down(a, g))

    def both(ref, p, rows):
        return ref[p, rows] + ref[p + 1, rows]

    for x in range(n // 2):
        p = 2 * x
        kx = level.kx[p + 2, even] + level.kx[p + 2, odd]
        inner = level.kx[p + 1, even] + level.kx[p + 1, odd]
        kz = both(level.kz, p, even) + both(level.kz, p, odd)
        inner = inner + both(level.ky, p, even) + jnp.where(low, kz, 0.0)
        d = both(level.d, p, even) + both(level.d, p, odd) - 2.0 * inner
        keep(
            x,
            z_pair(r[x, even] + r[x, odd]),
            z_pair(kx),
            z_pair(both(level.ky, p, odd)),
            jnp.where(low, z_up(kz, g), kz),
            z_pair(d),
        )


def up_kernel(plan, g, f0, u0, kx0, ky0, kz0, d0, f1, u1, kx1, ky1, kz1, d1, out, *scratch):
    nx, by, px = plan.nx, plan.by, plan.px
    stage, scratch = scratch[0], [Wide(r) for r in scratch[1:]]
    f0, u0, kx0, ky0, kz0, d0 = [Wide(r) for r in (f0, u0, kx0, ky0, kz0, d0)]
    f1, u1, kx1, ky1, kz1, d1 = [Wide(r) for r in (f1, u1, kx1, ky1, kz1, d1)]
    f2, kx2, ky2, kz2, d2, w2, ua2, ub2, r2 = scratch[:9]
    f3, kx3, ky3, kz3, d3, w3, ua3, ub3 = scratch[9:17]
    pad2, t2, t1, t0, w1, ua1, ub1, w0, ua0, ub0 = scratch[17:]
    half, four = nx // 8, by // 4

    for block in range(plan.blocks):
        i, j = divmod(block, plan.gy)
        at = (j * plan.gx + plan.part(i, j % 2)) * four
        for k in range(5 * half):
            stage[k, pl.ds(at, four), :] = g[block, pl.ds(k * four, four), :]

    cell = lax.broadcasted_iota(jnp.int32, (LANES, 2 * WIDE), 0)
    lane = lax.broadcasted_iota(jnp.int32, (LANES, 2 * WIDE), 1)
    spread = jnp.where(cell == lax.div(lane, 4), 1.0, 0.0).astype(jnp.bfloat16)
    for t, ref in enumerate((f2, kx2, ky2, kz2, d2)):
        for k in range(half):
            both = split_dot(stage[t * half + k], spread)
            shift = 1 if t == 1 else 0
            ref[k + shift] = both[:, :WIDE]
            ref[k + half + shift] = both[:, WIDE:]
    kx2[0] = jnp.zeros(kx2.shape[1:], F32)

    two = Level(nx // 4, 4, kx2, ky2, kz2, d2, w2, f2)
    three = Level(nx // 8, 8, kx3, ky3, kz3, d3, w3, f3)
    two.first(ua2)
    two.sweep(ua2, ub2)
    two.residual_pairs(ub2, r2)
    two.coarsen(r2, 0, f2.shape[1] // 2, store_level(three))
    three.first(ua3)
    three.sweep(ua3, ub3)
    three.sweep(ub3, ua3)
    three.sweep(ua3, ub3)
    two.correct(ub2, ub3, slice(None), t2)
    two.sweep(ub2, ua2)
    two.sweep(ua2, ub2)

    height = f2.shape[1]
    empty = jnp.zeros((8, WIDE), F32)
    for x in range(nx // 4):
        pad2[x, pl.ds(0, 8)] = empty
        pad2[x, pl.ds(8, height)] = ub2[x]
        pad2[x, pl.ds(8 + height, 8)] = empty
    one = Level(nx // 2, 2, kx1, ky1, kz1, d1, w1, f1)
    for p in range(nx // 2):
        w1[p] = DAMPING / d1[p]
        ua1[p] = u1[p]
    rows = pl.ds(8 + (plan.block_here() - 1) * four, 3 * four)
    one.correct(ua1, pad2, rows, t1)
    one.sweep(ua1, ub1)
    one.sweep(ub1, ua1)

    zero = Level(nx, 1, kx0, ky0, kz0, d0, w0, f0)

    def begin(p):
        w0[p] = DAMPING / d0[p]
        ua0[p] = u0[p]

    each(nx, 2, begin)
    zero.correct(ua0, ua1, slice(by // 4, by // 4 + by), t0)
    zero.sweep(ua0, ub0)
    zero.sweep(ub0, ua0)
    own = slice(by // 2, by // 2 + by)

    def finish(p):
        s, k = lax.div(p, px), lax.rem(p, px)
        u = ua0[p]
        scaled = d0[p] * u
        r = f0[p] + zero.beside(ua0, p) - scaled
        out[s, 0, k] = scaled[own, :LANES]
        out[s, 1, k] = r[own, :LANES]

    each(nx, 2, finish)


def place_kernel(plan, parts, scaled, residual):
    odd = lax.rem(lax.axis_index("gy"), 2)
    for i in range(plan.gx):
        start = pl.multiple_of(plan.part(i, odd) * plan.by, plan.by)
        rows = pl.ds(start, plan.by)
        scaled[0, :, rows, :] = parts[i, 0]
        residual[0, :, rows, :] = parts[i, 1]


def in_tiles(shapes):
    return [(s[0], 2, s[1], LANES) if s[-1] == WIDE else s for s in shapes]


def call(kernel, out_shape, scratch=(), last=False):
    if not last:
        out_shape = [pltpu.VMEM(s.shape, s.dtype) for s in out_shape]
    run = pl.pallas_call(
        kernel,
        out_shape=out_shape,
        scratch_shapes=[pltpu.VMEM(s, F32) for s in scratch],
        compiler_params=pltpu.CompilerParams(vmem_limit_bytes=VMEM_LIMIT),
    )

    def go(*args):
        return run(*[pltpu.with_memory_space_constraint(a, pltpu.VMEM) for a in args])

    return go


def f32(*shape):
    return jax.ShapeDtypeStruct(shape, F32)


def beside_in_z(plan, a):
    count = plan.gz
    if count == 2:
        return lax.ppermute(a, "gz", [(0, 1), (1, 0)])
    cut = LANES // 2
    right = lax.ppermute(a[..., :cut], "gz", [(i + 1, i) for i in range(count - 1)])
    left = lax.ppermute(a[..., cut:], "gz", [(i, i + 1) for i in range(count - 1)])
    return jnp.concatenate([right, left], axis=-1)


def on_device(plan, phase, density, rhs):
    nx, by, rows, px = plan.nx, plan.by, plan.rows, plan.px
    parts = call(
        functools.partial(prepare_kernel, plan), [f32(plan.gx, 2, px, by, LANES)]
    )(phase, density, rhs)[0]
    c = lax.all_to_all(parts, "gx", 0, 0, tiled=True)
    up = [(plan.device(b), plan.device(b + 1)) for b in range(plan.blocks - 1)]
    lo = lax.ppermute(c, ("gx", "gy"), up)
    hi = lax.ppermute(c, ("gx", "gy"), [(b, a) for a, b in up])
    zc = beside_in_z(plan, c)
    zlo = beside_in_z(plan, lo)
    zhi = beside_in_z(plan, hi)

    mid, win = rows // 2, rows - by
    four = by // 4
    packed = 5 * (nx // 8) * four
    level1 = [f32(nx // 2 + (k == 2), 2, mid, LANES) for k in range(6)]
    level0 = [f32(nx + (k == 2), 2, win, LANES) for k in range(6)]
    full = (nx, rows, WIDE)
    scratch = [full, full, (nx + 1, rows, WIDE), full, full, full, full, full, full]
    scratch += [(nx // 2, rows, WIDE), (nx // 2, mid, WIDE), (nx // 2, mid, WIDE)]
    scratch += [(nx // 4, mid, WIDE)]
    scratch = in_tiles(scratch) + [(2, packed, WIDE)]
    down = call(
        functools.partial(down_kernel, plan), [f32(plan.blocks, packed, LANES)] + level0 + level1, scratch
    )(c, lo, hi, zc, zlo, zhi)

    gathered = lax.all_to_all(down[0], ("gx", "gy"), 0, 0, tiled=True)

    height = four * plan.blocks
    l2 = (nx // 4, height, WIDE)
    l3 = (nx // 8, height // 2, WIDE)
    l1 = (nx // 2, mid, WIDE)
    l0 = (nx, win, WIDE)
    scratch = [(5 * (nx // 8), height, LANES), l2, (nx // 4 + 1, height, WIDE), l2, l2, l2, l2, l2, l2]
    scratch += [(nx // 8, height, WIDE)]
    scratch += [l3, (nx // 8 + 1, height // 2, WIDE), l3, l3, l3, l3, l3, l3]
    scratch += [(nx // 4, height + 16, WIDE), (nx // 8, height, WIDE), (nx // 4, mid, WIDE), (nx // 2, win, WIDE)]
    scratch += [l1, l1, l1, l0, l0, l0]
    scratch = in_tiles(scratch)
    result = call(
        functools.partial(up_kernel, plan), [f32(plan.gx, 2, px, by, LANES)], scratch
    )(gathered, *down[1:])[0]

    result = lax.all_to_all(result, "gx", 0, 0, tiled=True)
    return call(
        functools.partial(place_kernel, plan), [f32(1, px, plan.ny, LANES)] * 2, last=True
    )(result)


def solution(mesh):
    sizes = [mesh.shape[a] for a in ("gx", "gy", "gz")]

    def local(phase, density, rhs):
        return tuple(on_device(Plan(sizes, phase.shape), phase, density, rhs))

    in_specs = (P("gx", "gy", "gz"), P("gx", "gy", "gz"), P(None, "gx", "gy", "gz"))
    out_specs = (P(None, "gx", "gy", "gz"), P(None, "gx", "gy", "gz"))
    return jax.shard_map(local, mesh=mesh, in_specs=in_specs, out_specs=out_specs, check_vma=False)
```

```python
import functools

import jax
import jax.numpy as jnp
from jax import lax
from jax.experimental import pallas as pl
from jax.experimental.pallas import tpu as pltpu
from jax.sharding import PartitionSpec as P


DAMPING = 2.0 / 3.0
LANES = 128
WIDE = 256
HALO = 7
FAR = 3
F32 = jnp.float32
VMEM_LIMIT = 24 * 1024 * 1024


class Plan:
    def __init__(self, sizes, shape):
        self.gx, self.gy, self.gz = sizes
        self.px, self.ny, self.nz = shape
        self.nx = self.px * self.gx
        self.by = self.ny // self.gx
        self.blocks = self.gx * self.gy
        self.rows = self.by + 2 * HALO
        self.paired = self.gz == 2
        order = [0, 1, 3, 2] if self.gx == 4 else list(range(self.gx))
        self.place = [order.index(i) for i in range(self.gx)]
        self.order = order

    def device(self, block):
        j, q = divmod(block, self.gx)
        i = self.order[q if j % 2 == 0 else self.gx - 1 - q]
        return i * self.gy + j

    def part(self, i, odd):
        q = self.place[i]
        return q + odd * (self.gx - 1 - 2 * q)

    def block_here(self):
        i, j = lax.axis_index("gx"), lax.axis_index("gy")
        q = sum(jnp.where(i == k, self.place[k], 0) for k in range(self.gx))
        odd = lax.rem(j, 2)
        return j * self.gx + q + odd * (self.gx - 1 - 2 * q)


def x_up(a, s=1):
    return pltpu.roll(a, a.shape[0] - s, 0)


def x_down(a, s=1):
    return pltpu.roll(a, s, 0)


def z_up(a, g):
    return pltpu.roll(a, a.shape[1] - g, 1)


def z_down(a, g):
    return pltpu.roll(a, g, 1)


def inverse(a):
    r = pl.reciprocal(a, approx=True)
    return r * (2.0 - a * r)


def each(first, last, step, body):
    count = last + 1 - first
    if count <= 2 * step:
        for i in range(first, last + 1):
            body(i)
        return

    def go(c, _):
        for k in range(step):
            body(first + c * step + k)
        return 0

    lax.fori_loop(0, count // step, go, 0)
    for i in range(first + count // step * step, last + 1):
        body(i)


class Wide:
    def __init__(self, ref):
        self.ref = ref

    def __getitem__(self, key):
        r, xs = key if isinstance(key, tuple) else (key, slice(None))
        return jnp.concatenate([self.ref[r, 0, xs, :], self.ref[r, 1, xs, :]], axis=1)

    def __setitem__(self, key, value):
        r, xs = key if isinstance(key, tuple) else (key, slice(None))
        self.ref[r, 0, xs, :] = value[:, :LANES]
        self.ref[r, 1, xs, :] = value[:, LANES:]


class Level:
    def __init__(self, s, g, kx, ky, kz, d, w, f, step=2):
        self.s, self.g, self.step = s, g, step
        self.kx, self.ky, self.kz, self.d, self.w, self.f = kx, ky, kz, d, w, f

    def beside(self, u, r):
        here = u[r]
        kx, kz = self.kx[r], self.kz[r]
        a = kx * x_up(here, self.s) + x_down(kx * here, self.s)
        b = kz * z_up(here, self.g) + z_down(kz * here, self.g)
        return a + b + (self.ky[r + 1] * u[r + 1] + self.ky[r] * u[r - 1])

    def weigh(self, first, last):
        def body(r):
            self.w[r] = DAMPING * inverse(self.d[r])

        each(first, last, self.step, body)

    def first(self, u, first, last):
        def body(r):
            u[r] = self.w[r] * self.f[r]

        each(first, last, self.step, body)

    def sweep(self, u, v, first, last):
        def body(r):
            v[r] = (1.0 / 3.0) * u[r] + self.w[r] * (self.f[r] + self.beside(u, r))

        each(first, last, self.step, body)

    def residual(self, u, r):
        return self.f[r] + self.beside(u, r) - self.d[r] * u[r]

    def residual_pairs(self, u, out, first, count):
        def body(j):
            out[j] = self.residual(u, first + 2 * j) + self.residual(u, first + 2 * j + 1)

        each(0, count - 1, max(1, self.step // 2), body)


def z_pairs(low, g):
    return lambda a: a + jnp.where(low, z_up(a, g), z_down(a, g))


def coarse_coefficients(level, r, x_count):
    even, odd = pl.ds(0, x_count, stride=2), pl.ds(1, x_count, stride=2)
    g = level.g
    low = (lax.broadcasted_iota(jnp.int32, (x_count, WIDE), 1) & g) == 0
    z_pair = z_pairs(low, g)

    def all_x(ref, row):
        return ref[row, even] + ref[row, odd]

    kx = level.kx[r, odd] + level.kx[r + 1, odd]
    inner = level.kx[r, even] + level.kx[r + 1, even] + all_x(level.ky, r + 1)
    kz = all_x(level.kz, r) + all_x(level.kz, r + 1)
    d = all_x(level.d, r) + all_x(level.d, r + 1)
    d = d - 2.0 * (inner + jnp.where(low, kz, 0.0))
    return z_pair(kx), coarse_sum(level.ky, r + 2, x_count, g), jnp.where(low, z_up(kz, g), kz), z_pair(d)


def coarse_sum(ref, r, x_count, g):
    even, odd = pl.ds(0, x_count, stride=2), pl.ds(1, x_count, stride=2)
    low = (lax.broadcasted_iota(jnp.int32, (x_count, WIDE), 1) & g) == 0
    return z_pairs(low, g)(ref[r, even] + ref[r, odd])


def correct(u, v, e, t, x_count, first, last, to):
    def body(j):
        part = e[j]
        t[j, pl.ds(0, x_count, stride=2)] = part
        t[j, pl.ds(1, x_count, stride=2)] = part
        wide = t[j]
        r = to + 2 * (j - first)
        v[r] = u[r] + wide
        v[r + 1] = u[r + 1] + wide

    each(first, last, 2, body)


def split_dot(a, b):
    high = a.astype(jnp.bfloat16)
    rest = a - high.astype(F32)
    mid = rest.astype(jnp.bfloat16)
    low = (rest - mid.astype(F32)).astype(jnp.bfloat16)
    dot = functools.partial(jnp.dot, preferred_element_type=F32)
    return dot(high, b) + dot(mid, b) + dot(low, b)


def prepare_kernel(plan, phase_in, density_in, rhs_in, out, phase, density, rhs, sems):
    pairs = ((phase_in, phase), (density_in, density), (rhs_in, rhs))
    copies = [pltpu.make_async_copy(a, b, sems.at[k]) for k, (a, b) in enumerate(pairs)]
    for copy in copies:
        copy.start()
    for copy in copies:
        copy.wait()
    odd = lax.rem(lax.axis_index("gy"), 2)
    by, px = plan.by, plan.px
    for i in range(plan.gx):
        start = pl.multiple_of(plan.part(i, odd) * by, by)
        rows = pl.ds(start, by)
        for p in range(px):
            half = jnp.where(phase[p, rows, :] == 1, 500.0, 0.5).astype(F32)
            at = i * by * 2 * px + p
            out[pl.ds(at, by, stride=2 * px), :] = half * density[p, rows, :]
            out[pl.ds(at + px, by, stride=2 * px), :] = rhs[0, p, rows, :]


def down_kernel(plan, c, lo, hi, zc, zh, *refs):
    near_count = 1 if plan.paired else 2
    pack, nears, refs = refs[0], refs[1 : 1 + near_count], refs[1 + near_count :]
    kx0, ky0, kz0, d0, w0, f0, ub, kx1, ky1, kz1, w1, f1, u1 = [Wide(r) for r in refs[:13]]
    h0, ua, r0, uc, r1, d1 = [Wide(r) for r in refs[13:19]]
    stage = refs[19]
    nx, by, rows, gx = plan.nx, plan.by, plan.rows, plan.gx
    shape = (nx, WIDE)
    base = plan.block_here() * by - HALO
    y_count, z_count = plan.by * plan.blocks, plan.nz * plan.gz

    x = lax.broadcasted_iota(jnp.int32, shape, 0)
    lane = lax.broadcasted_iota(jnp.int32, shape, 1)
    core = lax.axis_index("gz")
    if plan.paired:
        z = lax.rem(core * LANES + lane, WIDE)
    else:
        z = core * LANES + jnp.where(lane < LANES + LANES // 2, lane, lane - WIDE)
    x_top, x_bottom = x == nx - 1, x == 0
    z_top, z_bottom = z == z_count - 1, z == 0
    z_shut = (z < 0) | (z >= z_count - 1)
    z_out = (z < 0) | (z >= z_count)

    def take(a, b, shift, r, to):
        def field(t):
            left = jnp.concatenate([a[s, r, t] for s in range(gx)], axis=0)
            right = jnp.concatenate([b[shift + s, r, t] for s in range(gx)], axis=0)
            return jnp.concatenate([left, right], axis=1)

        y = base + to
        h = jnp.where((y >= 0) & (y < y_count), field(0), 0.5)
        h0[to] = h if plan.paired else jnp.where(z_out, 0.5, h)
        f0[to] = field(1)

    each(0, HALO - 1, 2, lambda r: take(lo, zh, 0, r, r))
    each(0, by - 1, 2, lambda r: take(c, zc, 0, r, r + HALO))
    each(0, HALO - 1, 2, lambda r: take(hi, zh, gx, r, r + HALO + by))

    def is_open(r):
        y = base + r
        return (y >= 0) & (y < y_count - 1)

    def face_above(r, h):
        return inverse(h + jnp.where(base + r == y_count - 1, h, h0[r + 1]))

    below = face_above(0, h0[0])
    ky0[1] = jnp.where(is_open(0), below, 0.0)

    def faces(r, below):
        h = h0[r]
        alone = 0.5 * inverse(h)
        xu = inverse(h + jnp.where(x_top, h, x_up(h)))
        xd = jnp.where(x_bottom, alone, x_down(xu))
        yu = face_above(r, h)
        yd = jnp.where(base + r == 0, alone, below)
        zu = inverse(h + jnp.where(z_top, h, z_up(h, 1)))
        zd = jnp.where(z_bottom, alone, z_down(zu, 1))
        d = xu + xd + yu + yd + zu + zd
        w = DAMPING * inverse(d)
        kx0[r] = jnp.where(x_top, 0.0, xu)
        ky0[r + 1] = jnp.where(is_open(r), yu, 0.0)
        kz0[r] = jnp.where(z_shut, 0.0, zu)
        d0[r], w0[r] = d, w
        ua[r] = w * f0[r]
        return yu

    def two_faces(k, below):
        return faces(2 * k + 2, faces(2 * k + 1, below))

    lax.fori_loop(0, (rows - 2) // 2, two_faces, below)

    fine = Level(1, 1, kx0, ky0, kz0, d0, w0, f0)
    fine.sweep(ua, ub, 2, rows - 3)
    fine.residual_pairs(ub, r0, 3, by // 2 + 4)

    own = by // 2
    half_x = nx // 2
    middle = Level(1, 2, kx1, ky1, kz1, d1, w1, f1)
    ky1[1] = coarse_sum(ky0, 1, half_x, 1)

    def coarsen(j):
        kx1[j], ky1[j + 1], kz1[j], d1[j] = coarse_coefficients(fine, 2 * j - 1, half_x)

    each(1, own + 6, 1, coarsen)

    def restrict(j):
        f1[j] = coarse_sum(r0, j - 2, half_x, 1)

    each(2, own + 5, 2, restrict)
    middle.weigh(1, own + 6)
    middle.first(uc, 2, own + 5)
    middle.sweep(uc, u1, 3, own + 4)
    middle.residual_pairs(u1, r1, 4, own // 2)

    quarter_x = nx // 4
    own2 = own // 2
    part = own2 // 2
    for j in range(own2):
        fields = (coarse_sum(r1, j, quarter_x, 2),) + coarse_coefficients(middle, 4 + 2 * j, quarter_x)
        for t, a in enumerate(fields):
            stage[j // part, pl.ds((t * part + j % part) * quarter_x, quarter_x), :] = a
    lane = lax.broadcasted_iota(jnp.int32, (WIDE, LANES), 0)
    cell = lax.broadcasted_iota(jnp.int32, (WIDE, LANES), 1)
    total = jnp.zeros(pack.shape, F32)
    for k in range(2):
        pick = jnp.where(lane == 4 * (cell - k * (WIDE // 4)), 1.0, 0.0).astype(jnp.bfloat16)
        total = total + split_dot(stage[k], pick)
    pack[...] = total

    size = pack.shape[0]

    def near(out, first):
        out[pl.ds(0, size), :] = total
        for k, (ref, r) in enumerate(((u1, first), (u1, first + 1), (u1, first + 2), (f1, first + 1))):
            for s in range(2):
                out[pl.ds(size + (2 * k + s) * half_x, half_x), :] = ref.ref[r, s]

    top = own
    if plan.paired:
        near(nears[0], top - (top - 5) * core)
    else:
        near(nears[0], top)
        near(nears[1], 5)


def up_kernel(plan, pack, below, above, *refs):
    refs, out, scratch = refs[:13], refs[13], refs[14:]
    kx0, ky0, kz0, d0, w0, f0, u0, kx1, ky1, kz1, w1, f1_in, u1_in = [Wide(r) for r in refs]
    stage = scratch[0]
    wide = [Wide(r) for r in scratch[1:]]
    f2, kx2, ky2, kz2, d2, w2, ua2, ub2, r2 = wide[:9]
    f3, kx3, ky3, kz3, d3, w3, ua3, ub3 = wide[9:17]
    t1, t0, f1, ua1, ub1, ua0, ub0 = wide[17:]
    nx, by = plan.nx, plan.by
    own, own2 = by // 2, by // 4
    part = own2 // 2
    half_x, quarter_x = nx // 2, nx // 4
    size = pack.shape[0]
    side = size + 8 * half_x
    core = lax.axis_index("gz")
    block = plan.block_here()
    zero = jnp.int32(0)

    for r in range(2, own + 6):
        f1[r] = f1_in[r]
    for r in range(3, own + 5):
        ua1[r] = u1_in[r]

    def spread_out(lower, upper, turn_lower, turn_upper):
        for k in range(FAR):
            at = 0 if k == 0 else side + (k - 1) * size
            stage[FAR - 1 - k] = lower[pl.ds(at, size), :]
            stage[FAR + 1 + k] = upper[pl.ds(at, size), :]
        for k, (ref, r_low, r_up) in enumerate(
            ((ua1, 0, own + 5), (ua1, 1, own + 6), (ua1, 2, own + 7), (f1, 1, own + 6))
        ):
            for s in range(2):
                rows = pl.ds(size + (2 * k + s) * half_x, half_x)
                ref.ref[r_low, s ^ turn_lower] = lower[rows, :]
                ref.ref[r_up, s ^ turn_upper] = upper[rows, :]

    stage[FAR] = pack[...]
    if plan.paired:
        turn_lower, turn_upper = core, 1 - core

        @pl.when(core == 0)
        def _():
            spread_out(below, above, 0, 1)

        @pl.when(core != 0)
        def _():
            spread_out(above, below, 1, 0)
    else:
        turn_lower, turn_upper = zero, zero
        spread_out(below, above, 0, 0)

    cell = lax.broadcasted_iota(jnp.int32, (LANES, 2 * WIDE), 0)
    lane = lax.broadcasted_iota(jnp.int32, (LANES, 2 * WIDE), 1)
    spread = jnp.where(cell == lax.div(lane, 4), 1.0, 0.0).astype(jnp.bfloat16)

    def expand(k):
        there = block + k - FAR
        exists = (there >= 0) & (there < plan.blocks)
        turn = jnp.where(k < FAR, turn_lower, jnp.where(k > FAR, turn_upper, 0))
        rows = split_dot(stage[k], spread)
        for t, ref in enumerate((f2, kx2, ky2, kz2, d2)):
            for j in range(own2):
                at = (t * part + j % part) * quarter_x
                a = rows[at : at + quarter_x, (j // part) * WIDE : (j // part + 1) * WIDE]
                if t == 4:
                    a = jnp.where(exists, a, 1.0)
                r = k * own2 + j + (1 if t == 2 else 0)
                ref.ref[r, turn] = a[:, :LANES]
                ref.ref[r, 1 - turn] = a[:, LANES:]

    each(0, 2 * FAR, 1, expand)

    rows2 = (2 * FAR + 1) * own2
    two = Level(1, 4, kx2, ky2, kz2, d2, w2, f2, 4)
    two.weigh(0, rows2 - 1)
    two.first(ua2, 0, rows2 - 1)
    two.sweep(ua2, ub2, 1, rows2 - 2)
    two.residual_pairs(ub2, r2, 2, rows2 // 2 - 2)

    x = lax.broadcasted_iota(jnp.int32, (quarter_x, WIDE), 0)
    even_x = (x & 1) == 0
    low = (lax.broadcasted_iota(jnp.int32, (quarter_x, WIDE), 1) & 4) == 0
    z_pair = z_pairs(low, 4)

    def x_pair(a):
        return a + jnp.where(even_x, x_up(a), x_down(a))

    last3 = rows2 // 2 - 2

    def coarsen(j):
        r = 2 * j
        kx = kx2[r] + kx2[r + 1]
        kz = kz2[r] + kz2[r + 1]
        inner = ky2[r + 1] + jnp.where(even_x, kx, 0.0) + jnp.where(low, kz, 0.0)
        f3[j] = z_pair(x_pair(r2[j - 1]))
        kx3[j] = z_pair(jnp.where(even_x, x_up(kx), kx))
        ky3[j + 1] = z_pair(x_pair(ky2[r + 2]))
        kz = x_pair(kz)
        kz3[j] = jnp.where(low, z_up(kz, 4), kz)
        d3[j] = z_pair(x_pair(d2[r] + d2[r + 1] - 2.0 * inner))

    each(1, last3, 2, coarsen)
    three = Level(2, 8, kx3, ky3, kz3, d3, w3, f3, 4)
    three.weigh(1, last3)
    three.first(ua3, 1, last3)
    three.sweep(ua3, ub3, 2, last3 - 1)
    three.sweep(ub3, ua3, 3, last3 - 2)
    three.sweep(ua3, ub3, 4, last3 - 3)

    first2 = FAR * own2
    for j in range(4, last3 - 2):
        e = ub3[j]
        ua2[2 * j] = ub2[2 * j] + e
        ua2[2 * j + 1] = ub2[2 * j + 1] + e
    two.sweep(ua2, ub2, first2 - 3, first2 + own2 + 2)
    two.sweep(ub2, ua2, first2 - 2, first2 + own2 + 1)

    one = Level(1, 2, kx1, ky1, kz1, None, w1, f1)
    correct(ua1, ub1, ua2, t1, quarter_x, first2 - 2, first2 + own2 + 1, 0)
    one.sweep(ub1, ua1, 1, own + 6)
    one.sweep(ua1, ub1, 2, own + 5)

    finest = Level(1, 1, kx0, ky0, kz0, d0, w0, f0)
    correct(u0, ua0, ub1, t0, half_x, 2, own + 5, 3)
    finest.sweep(ua0, ub0, HALO - 2, HALO + by + 1)
    finest.sweep(ub0, ua0, HALO - 1, HALO + by)

    def finish(r):
        scaled = d0[r] * ua0[r]
        rest = f0[r] + finest.beside(ua0, r) - scaled
        for s in range(plan.gx):
            part = slice(s * plan.px, (s + 1) * plan.px)
            out[s, r - HALO, 0] = scaled[part, :LANES]
            out[s, r - HALO, 1] = rest[part, :LANES]

    each(HALO, HALO + by - 1, 2, finish)


def place_kernel(plan, parts, scaled, residual):
    odd = lax.rem(lax.axis_index("gy"), 2)
    by, px = plan.by, plan.px
    for i in range(plan.gx):
        start = pl.multiple_of(plan.part(i, odd) * by, by)
        for p in range(px):
            at = i * by * 2 * px + p
            scaled[0, p, pl.ds(start, by), :] = parts[pl.ds(at, by, stride=2 * px), :]
            residual[0, p, pl.ds(start, by), :] = parts[pl.ds(at + px, by, stride=2 * px), :]


def in_vmem(*shape):
    return pltpu.VMEM(shape, F32)


def call(kernel, out_shape, scratch=(), **more):
    return pl.pallas_call(
        kernel,
        out_shape=out_shape,
        scratch_shapes=list(scratch),
        compiler_params=pltpu.CompilerParams(vmem_limit_bytes=VMEM_LIMIT),
        **more,
    )


def pinned(*arrays):
    return [pltpu.with_memory_space_constraint(a, pltpu.VMEM) for a in arrays]


def beside_in_z(plan, a):
    count = plan.gz
    if plan.paired:
        return lax.ppermute(a, "gz", [(0, 1), (1, 0)])
    cut = LANES // 2
    right = lax.ppermute(a[..., :cut], "gz", [(i + 1, i) for i in range(count - 1)])
    left = lax.ppermute(a[..., cut:], "gz", [(i, i + 1) for i in range(count - 1)])
    return jnp.concatenate([right, left], axis=-1)


def shift(plan, a, k):
    pairs = [(plan.device(b), plan.device(b + k)) for b in range(plan.blocks) if 0 <= b + k < plan.blocks]
    return lax.ppermute(a, ("gx", "gy"), pairs)


def shift_apart(plan, a, k):
    pairs = []
    for b in range(plan.blocks):
        for core, to in ((0, b + k), (1, b - k)):
            if 0 <= to < plan.blocks:
                pairs.append((2 * plan.device(b) + core, 2 * plan.device(to) + core))
    return lax.ppermute(a, ("gx", "gy", "gz"), pairs)


def on_device(plan, phase, density, rhs):
    nx, by, rows, px, gx = plan.nx, plan.by, plan.rows, plan.px, plan.gx
    flat = gx * by * 2 * px
    block = (px, plan.ny, LANES)
    anywhere = pl.BlockSpec(memory_space=pl.ANY)
    (parts,) = call(
        functools.partial(prepare_kernel, plan),
        [in_vmem(flat, LANES)],
        [pltpu.VMEM(block, jnp.int32), in_vmem(*block), in_vmem(1, *block), pltpu.SemaphoreType.DMA((3,))],
        in_specs=[anywhere] * 3,
    )(phase, density, rhs)
    parts = parts.reshape(gx, by, 2, px, LANES)
    c = lax.all_to_all(parts, "gx", 0, 0, tiled=True)
    lo = shift(plan, c[:, by - HALO :], 1)
    hi = shift(plan, c[:, :HALO], -1)
    zc = beside_in_z(plan, c)
    zh = beside_in_z(plan, jnp.concatenate([lo, hi], axis=0))

    own, own2 = by // 2, by // 4
    size = 5 * (own2 // 2) * (nx // 4)
    side = size + 8 * (nx // 2)

    def level0(n):
        return in_vmem(n, 2, nx, LANES)

    def level1(n):
        return in_vmem(n, 2, nx // 2, LANES)

    outs = [in_vmem(size, LANES)] + [in_vmem(side, LANES)] * (1 if plan.paired else 2)
    fields = [level0(rows)] * 7 + [level1(own + 8)] * 6
    scratch = [level0(rows)] * 2 + [level0(own + 4), level1(own + 8), level1(own2), level1(own + 8)]
    scratch += [in_vmem(2, size, WIDE)]
    down = call(functools.partial(down_kernel, plan), outs + fields, scratch)(*pinned(c, lo, hi, zc, zh))
    pack, nears, fields = down[0], down[1 : len(outs)], down[len(outs) :]

    if plan.paired:
        mine = [shift_apart(plan, a, k + 1) for k, a in enumerate([nears[0]] + [pack] * (FAR - 1))]
        below = jnp.concatenate(mine, axis=0)
        above = lax.ppermute(below, "gz", [(0, 1), (1, 0)])
    else:
        below = jnp.concatenate(
            [shift(plan, a, k + 1) for k, a in enumerate([nears[0]] + [pack] * (FAR - 1))], axis=0
        )
        above = jnp.concatenate(
            [shift(plan, a, -k - 1) for k, a in enumerate([nears[1]] + [pack] * (FAR - 1))], axis=0
        )

    rows2 = (2 * FAR + 1) * own2
    scratch = [in_vmem(2 * FAR + 1, size, LANES)]
    scratch += [in_vmem(rows2 + 1, 2, nx // 4, LANES)] * 9 + [in_vmem(rows2 // 2 + 1, 2, nx // 4, LANES)] * 8
    scratch += [level1(rows2), level0(own + 8)] + [level1(own + 8)] * 3 + [level0(rows)] * 2
    (result,) = call(
        functools.partial(up_kernel, plan), [in_vmem(gx, by, 2, px, LANES)], scratch
    )(*pinned(pack, below, above, *fields))

    result = lax.all_to_all(result, "gx", 0, 0, tiled=True)
    return call(
        functools.partial(place_kernel, plan),
        [jax.ShapeDtypeStruct((1, px, plan.ny, LANES), F32)] * 2,
    )(*pinned(result.reshape(flat, LANES)))


def solution(mesh):
    sizes = [mesh.shape[a] for a in ("gx", "gy", "gz")]

    def local(phase, density, rhs):
        return tuple(on_device(Plan(sizes, phase.shape), phase, density, rhs))

    in_specs = (P("gx", "gy", "gz"), P("gx", "gy", "gz"), P(None, "gx", "gy", "gz"))
    out_specs = (P(None, "gx", "gy", "gz"), P(None, "gx", "gy", "gz"))
    return jax.shard_map(local, mesh=mesh, in_specs=in_specs, out_specs=out_specs, check_vma=False)
```

```python
import functools

import jax
import jax.numpy as jnp
from jax import lax
from jax.experimental import pallas as pl
from jax.experimental.pallas import tpu as pltpu
from jax.sharding import PartitionSpec as P


DAMPING = 2.0 / 3.0
LANES = 128
WIDE = 256
HALO = 7
FAR = 3
F32 = jnp.float32
VMEM_LIMIT = 24 * 1024 * 1024


class Plan:
    def __init__(self, sizes, shape):
        self.gx, self.gy, self.gz = sizes
        self.px, self.ny, self.nz = shape
        self.nx = self.px * self.gx
        self.by = self.ny // self.gx
        self.blocks = self.gx * self.gy
        self.rows = self.by + 2 * HALO
        self.paired = self.gz == 2
        order = [0, 1, 3, 2] if self.gx == 4 else list(range(self.gx))
        self.place = [order.index(i) for i in range(self.gx)]
        self.order = order

    def device(self, block):
        j, q = divmod(block, self.gx)
        i = self.order[q if j % 2 == 0 else self.gx - 1 - q]
        return i * self.gy + j

    def part(self, i, odd):
        q = self.place[i]
        return q + odd * (self.gx - 1 - 2 * q)

    def block_here(self):
        i, j = lax.axis_index("gx"), lax.axis_index("gy")
        q = sum(jnp.where(i == k, self.place[k], 0) for k in range(self.gx))
        odd = lax.rem(j, 2)
        return j * self.gx + q + odd * (self.gx - 1 - 2 * q)


def x_up(a, s=1):
    return pltpu.roll(a, a.shape[0] - s, 0)


def x_down(a, s=1):
    return pltpu.roll(a, s, 0)


def z_up(a, g):
    return pltpu.roll(a, a.shape[1] - g, 1)


def z_down(a, g):
    return pltpu.roll(a, g, 1)


def inverse(a):
    r = pl.reciprocal(a, approx=True)
    return r * (2.0 - a * r)


def each(first, last, step, body):
    count = last + 1 - first
    if count <= 2 * step:
        for i in range(first, last + 1):
            body(i)
        return

    def go(c, _):
        for k in range(step):
            body(first + c * step + k)
        return 0

    lax.fori_loop(0, count // step, go, 0)
    for i in range(first + count // step * step, last + 1):
        body(i)


class Wide:
    def __init__(self, ref):
        self.ref = ref

    def __getitem__(self, key):
        r, xs = key if isinstance(key, tuple) else (key, slice(None))
        return jnp.concatenate([self.ref[r, 0, xs, :], self.ref[r, 1, xs, :]], axis=1)

    def __setitem__(self, key, value):
        r, xs = key if isinstance(key, tuple) else (key, slice(None))
        self.ref[r, 0, xs, :] = value[:, :LANES]
        self.ref[r, 1, xs, :] = value[:, LANES:]


class Level:
    def __init__(self, s, g, kx, ky, kz, d, w, f, step=2):
        self.s, self.g, self.step = s, g, step
        self.kx, self.ky, self.kz, self.d, self.w, self.f = kx, ky, kz, d, w, f

    def beside(self, u, r):
        here = u[r]
        kx, kz = self.kx[r], self.kz[r]
        a = kx * x_up(here, self.s) + x_down(kx * here, self.s)
        b = kz * z_up(here, self.g) + z_down(kz * here, self.g)
        return a + b + (self.ky[r + 1] * u[r + 1] + self.ky[r] * u[r - 1])

    def weigh(self, first, last):
        def body(r):
            self.w[r] = DAMPING * inverse(self.d[r])

        each(first, last, self.step, body)

    def first(self, u, first, last):
        def body(r):
            u[r] = self.w[r] * self.f[r]

        each(first, last, self.step, body)

    def sweep(self, u, v, first, last):
        def body(r):
            v[r] = (1.0 / 3.0) * u[r] + self.w[r] * (self.f[r] + self.beside(u, r))

        each(first, last, self.step, body)

    def residual(self, u, r):
        return self.f[r] + self.beside(u, r) - self.d[r] * u[r]

    def residual_pairs(self, u, out, first, count):
        def body(j):
            out[j] = self.residual(u, first + 2 * j) + self.residual(u, first + 2 * j + 1)

        each(0, count - 1, max(1, self.step // 2), body)


def z_pairs(low, g):
    return lambda a: a + jnp.where(low, z_up(a, g), z_down(a, g))


def coarse_coefficients(level, r, x_count):
    even, odd = pl.ds(0, x_count, stride=2), pl.ds(1, x_count, stride=2)
    g = level.g
    low = (lax.broadcasted_iota(jnp.int32, (x_count, WIDE), 1) & g) == 0
    z_pair = z_pairs(low, g)

    def all_x(ref, row):
        return ref[row, even] + ref[row, odd]

    kx = level.kx[r, odd] + level.kx[r + 1, odd]
    inner = level.kx[r, even] + level.kx[r + 1, even] + all_x(level.ky, r + 1)
    kz = all_x(level.kz, r) + all_x(level.kz, r + 1)
    d = all_x(level.d, r) + all_x(level.d, r + 1)
    d = d - 2.0 * (inner + jnp.where(low, kz, 0.0))
    return z_pair(kx), coarse_sum(level.ky, r + 2, x_count, g), jnp.where(low, z_up(kz, g), kz), z_pair(d)


def coarse_sum(ref, r, x_count, g):
    even, odd = pl.ds(0, x_count, stride=2), pl.ds(1, x_count, stride=2)
    low = (lax.broadcasted_iota(jnp.int32, (x_count, WIDE), 1) & g) == 0
    return z_pairs(low, g)(ref[r, even] + ref[r, odd])


def correct(u, v, e, t, x_count, first, last, to):
    def body(j):
        part = e[j]
        t[j, pl.ds(0, x_count, stride=2)] = part
        t[j, pl.ds(1, x_count, stride=2)] = part
        wide = t[j]
        r = to + 2 * (j - first)
        v[r] = u[r] + wide
        v[r + 1] = u[r + 1] + wide

    each(first, last, 2, body)


def pick_lanes(a, lanes):
    return jnp.take_along_axis(a, lanes, axis=1, mode="promise_in_bounds")


def prepare_kernel(plan, phase_in, density_in, rhs_in, out, phase, density, rhs, sems):
    pairs = ((phase_in, phase), (density_in, density), (rhs_in, rhs))
    copies = [pltpu.make_async_copy(a, b, sems.at[k]) for k, (a, b) in enumerate(pairs)]
    for copy in copies:
        copy.start()
    for copy in copies:
        copy.wait()
    odd = lax.rem(lax.axis_index("gy"), 2)
    by, px = plan.by, plan.px
    for i in range(plan.gx):
        start = pl.multiple_of(plan.part(i, odd) * by, by)
        rows = pl.ds(start, by)
        for p in range(px):
            half = jnp.where(phase[p, rows, :] == 1, 500.0, 0.5).astype(F32)
            at = i * by * 2 * px + p
            out[pl.ds(at, by, stride=2 * px), :] = half * density[p, rows, :]
            out[pl.ds(at + px, by, stride=2 * px), :] = rhs[0, p, rows, :]


def down_kernel(plan, c, lo, hi, zc, zh, *refs):
    near_count = 1 if plan.paired else 2
    pack, nears, refs = refs[0], refs[1 : 1 + near_count], refs[1 + near_count :]
    kx0, ky0, kz0, d0, w0, f0, ub, kx1, ky1, kz1, w1, f1, u1 = [Wide(r) for r in refs[:13]]
    h0, ua, r0, uc, r1, d1 = [Wide(r) for r in refs[13:19]]
    stage = refs[19]
    nx, by, rows, gx = plan.nx, plan.by, plan.rows, plan.gx
    shape = (nx, WIDE)
    base = plan.block_here() * by - HALO
    y_count, z_count = plan.by * plan.blocks, plan.nz * plan.gz

    x = lax.broadcasted_iota(jnp.int32, shape, 0)
    lane = lax.broadcasted_iota(jnp.int32, shape, 1)
    core = lax.axis_index("gz")
    if plan.paired:
        z = lax.rem(core * LANES + lane, WIDE)
    else:
        z = core * LANES + jnp.where(lane < LANES + LANES // 2, lane, lane - WIDE)
    x_top, x_bottom = x == nx - 1, x == 0
    z_top, z_bottom = z == z_count - 1, z == 0
    z_shut = (z < 0) | (z >= z_count - 1)
    z_out = (z < 0) | (z >= z_count)

    def take(a, b, shift, r, to):
        def field(t):
            left = jnp.concatenate([a[s, r, t] for s in range(gx)], axis=0)
            right = jnp.concatenate([b[shift + s, r, t] for s in range(gx)], axis=0)
            return jnp.concatenate([left, right], axis=1)

        y = base + to
        h = jnp.where((y >= 0) & (y < y_count), field(0), 0.5)
        h0[to] = h if plan.paired else jnp.where(z_out, 0.5, h)
        f0[to] = field(1)

    each(0, HALO - 1, 2, lambda r: take(lo, zh, 0, r, r))
    each(0, by - 1, 2, lambda r: take(c, zc, 0, r, r + HALO))
    each(0, HALO - 1, 2, lambda r: take(hi, zh, gx, r, r + HALO + by))

    def is_open(r):
        y = base + r
        return (y >= 0) & (y < y_count - 1)

    def face_above(r, h):
        return inverse(h + jnp.where(base + r == y_count - 1, h, h0[r + 1]))

    below = face_above(0, h0[0])
    ky0[1] = jnp.where(is_open(0), below, 0.0)

    def faces(r, below):
        h = h0[r]
        alone = 0.5 * inverse(h)
        xu = inverse(h + jnp.where(x_top, h, x_up(h)))
        xd = jnp.where(x_bottom, alone, x_down(xu))
        yu = face_above(r, h)
        yd = jnp.where(base + r == 0, alone, below)
        zu = inverse(h + jnp.where(z_top, h, z_up(h, 1)))
        zd = jnp.where(z_bottom, alone, z_down(zu, 1))
        d = xu + xd + yu + yd + zu + zd
        w = DAMPING * inverse(d)
        kx0[r] = jnp.where(x_top, 0.0, xu)
        ky0[r + 1] = jnp.where(is_open(r), yu, 0.0)
        kz0[r] = jnp.where(z_shut, 0.0, zu)
        d0[r], w0[r] = d, w
        ua[r] = w * f0[r]
        return yu

    def two_faces(k, below):
        return faces(2 * k + 2, faces(2 * k + 1, below))

    lax.fori_loop(0, (rows - 2) // 2, two_faces, below)

    fine = Level(1, 1, kx0, ky0, kz0, d0, w0, f0)
    fine.sweep(ua, ub, 2, rows - 3)
    fine.residual_pairs(ub, r0, 3, by // 2 + 4)

    own = by // 2
    half_x = nx // 2
    middle = Level(1, 2, kx1, ky1, kz1, d1, w1, f1)
    ky1[1] = coarse_sum(ky0, 1, half_x, 1)

    def coarsen(j):
        kx1[j], ky1[j + 1], kz1[j], d1[j] = coarse_coefficients(fine, 2 * j - 1, half_x)

    each(1, own + 6, 1, coarsen)

    def restrict(j):
        f1[j] = coarse_sum(r0, j - 2, half_x, 1)

    each(2, own + 5, 2, restrict)
    middle.weigh(1, own + 6)
    middle.first(uc, 2, own + 5)
    middle.sweep(uc, u1, 3, own + 4)
    middle.residual_pairs(u1, r1, 4, own // 2)

    quarter_x = nx // 4
    own2 = own // 2
    part = own2 // 2
    for j in range(own2):
        fields = (coarse_sum(r1, j, quarter_x, 2),) + coarse_coefficients(middle, 4 + 2 * j, quarter_x)
        for t, a in enumerate(fields):
            stage[j // part, pl.ds((t * part + j % part) * quarter_x, quarter_x), :] = a
    cell = lax.broadcasted_iota(jnp.int32, pack.shape, 1)
    lanes = lax.rem(4 * cell, LANES)
    quarter = lax.div(4 * cell, LANES)
    total = pick_lanes(stage[0, :, :LANES], lanes)
    for k in range(1, 4):
        half = slice((k % 2) * LANES, (k % 2 + 1) * LANES)
        total = jnp.where(quarter == k, pick_lanes(stage[k // 2, :, half], lanes), total)
    pack[...] = total

    size = pack.shape[0]

    def near(out, first):
        out[pl.ds(0, size), :] = total
        for k, (ref, r) in enumerate(((u1, first), (u1, first + 1), (u1, first + 2), (f1, first + 1))):
            for s in range(2):
                out[pl.ds(size + (2 * k + s) * half_x, half_x), :] = ref.ref[r, s]

    top = own
    if plan.paired:
        near(nears[0], top - (top - 5) * core)
    else:
        near(nears[0], top)
        near(nears[1], 5)


def up_kernel(plan, pack, below, above, *refs):
    refs, out, scratch = refs[:13], refs[13], refs[14:]
    kx0, ky0, kz0, d0, w0, f0, u0, kx1, ky1, kz1, w1, f1_in, u1_in = [Wide(r) for r in refs]
    stage = scratch[0]
    wide = [Wide(r) for r in scratch[1:]]
    f2, kx2, ky2, kz2, d2, w2, ua2, ub2, r2 = wide[:9]
    f3, kx3, ky3, kz3, d3, w3, ua3, ub3 = wide[9:17]
    t1, t0, f1, ua1, ub1, ua0, ub0 = wide[17:]
    nx, by = plan.nx, plan.by
    own, own2 = by // 2, by // 4
    part = own2 // 2
    half_x, quarter_x = nx // 2, nx // 4
    size = pack.shape[0]
    side = size + 8 * half_x
    core = lax.axis_index("gz")
    block = plan.block_here()
    zero = jnp.int32(0)

    for r in range(2, own + 6):
        f1[r] = f1_in[r]
    for r in range(3, own + 5):
        ua1[r] = u1_in[r]

    def spread_out(lower, upper, turn_lower, turn_upper):
        for k in range(FAR):
            at = 0 if k == 0 else side + (k - 1) * size
            stage[FAR - 1 - k] = lower[pl.ds(at, size), :]
            stage[FAR + 1 + k] = upper[pl.ds(at, size), :]
        for k, (ref, r_low, r_up) in enumerate(
            ((ua1, 0, own + 5), (ua1, 1, own + 6), (ua1, 2, own + 7), (f1, 1, own + 6))
        ):
            for s in range(2):
                rows = pl.ds(size + (2 * k + s) * half_x, half_x)
                ref.ref[r_low, s ^ turn_lower] = lower[rows, :]
                ref.ref[r_up, s ^ turn_upper] = upper[rows, :]

    stage[FAR] = pack[...]
    if plan.paired:
        turn_lower, turn_upper = core, 1 - core

        @pl.when(core == 0)
        def _():
            spread_out(below, above, 0, 1)

        @pl.when(core != 0)
        def _():
            spread_out(above, below, 1, 0)
    else:
        turn_lower, turn_upper = zero, zero
        spread_out(below, above, 0, 0)

    lane = lax.broadcasted_iota(jnp.int32, (size, LANES), 1)
    lanes = [lax.div(lane, 4) + k * (LANES // 4) for k in range(4)]

    def expand(k):
        there = block + k - FAR
        exists = (there >= 0) & (there < plan.blocks)
        turn = jnp.where(k < FAR, turn_lower, jnp.where(k > FAR, turn_upper, 0))
        rows = stage[k]
        for quarter in range(4):
            part_of, half = divmod(quarter, 2)
            a = pick_lanes(rows, lanes[quarter])
            for t, ref in enumerate((f2, kx2, ky2, kz2, d2)):
                for j in range(part):
                    at = (t * part + j) * quarter_x
                    b = a[at : at + quarter_x]
                    if t == 4:
                        b = jnp.where(exists, b, 1.0)
                    r = k * own2 + part_of * part + j + (1 if t == 2 else 0)
                    ref.ref[r, turn if half == 0 else 1 - turn] = b

    each(0, 2 * FAR, 1, expand)

    rows2 = (2 * FAR + 1) * own2
    two = Level(1, 4, kx2, ky2, kz2, d2, w2, f2, 4)
    two.weigh(0, rows2 - 1)
    two.first(ua2, 0, rows2 - 1)
    two.sweep(ua2, ub2, 1, rows2 - 2)
    two.residual_pairs(ub2, r2, 2, rows2 // 2 - 2)

    x = lax.broadcasted_iota(jnp.int32, (quarter_x, WIDE), 0)
    even_x = (x & 1) == 0
    low = (lax.broadcasted_iota(jnp.int32, (quarter_x, WIDE), 1) & 4) == 0
    z_pair = z_pairs(low, 4)

    def x_pair(a):
        return a + jnp.where(even_x, x_up(a), x_down(a))

    last3 = rows2 // 2 - 2

    def coarsen(j):
        r = 2 * j
        kx = kx2[r] + kx2[r + 1]
        kz = kz2[r] + kz2[r + 1]
        inner = ky2[r + 1] + jnp.where(even_x, kx, 0.0) + jnp.where(low, kz, 0.0)
        f3[j] = z_pair(x_pair(r2[j - 1]))
        kx3[j] = z_pair(jnp.where(even_x, x_up(kx), kx))
        ky3[j + 1] = z_pair(x_pair(ky2[r + 2]))
        kz = x_pair(kz)
        kz3[j] = jnp.where(low, z_up(kz, 4), kz)
        d3[j] = z_pair(x_pair(d2[r] + d2[r + 1] - 2.0 * inner))

    each(1, last3, 2, coarsen)
    three = Level(2, 8, kx3, ky3, kz3, d3, w3, f3, 4)
    three.weigh(1, last3)
    three.first(ua3, 1, last3)
    three.sweep(ua3, ub3, 2, last3 - 1)
    three.sweep(ub3, ua3, 3, last3 - 2)
    three.sweep(ua3, ub3, 4, last3 - 3)

    first2 = FAR * own2
    for j in range(4, last3 - 2):
        e = ub3[j]
        ua2[2 * j] = ub2[2 * j] + e
        ua2[2 * j + 1] = ub2[2 * j + 1] + e
    two.sweep(ua2, ub2, first2 - 3, first2 + own2 + 2)
    two.sweep(ub2, ua2, first2 - 2, first2 + own2 + 1)

    one = Level(1, 2, kx1, ky1, kz1, None, w1, f1)
    correct(ua1, ub1, ua2, t1, quarter_x, first2 - 2, first2 + own2 + 1, 0)
    one.sweep(ub1, ua1, 1, own + 6)
    one.sweep(ua1, ub1, 2, own + 5)

    finest = Level(1, 1, kx0, ky0, kz0, d0, w0, f0)
    correct(u0, ua0, ub1, t0, half_x, 2, own + 5, 3)
    finest.sweep(ua0, ub0, HALO - 2, HALO + by + 1)
    finest.sweep(ub0, ua0, HALO - 1, HALO + by)

    def finish(r):
        scaled = d0[r] * ua0[r]
        rest = f0[r] + finest.beside(ua0, r) - scaled
        for s in range(plan.gx):
            part = slice(s * plan.px, (s + 1) * plan.px)
            out[s, r - HALO, 0] = scaled[part, :LANES]
            out[s, r - HALO, 1] = rest[part, :LANES]

    each(HALO, HALO + by - 1, 2, finish)


def place_kernel(plan, parts, scaled, residual):
    odd = lax.rem(lax.axis_index("gy"), 2)
    by, px = plan.by, plan.px
    for i in range(plan.gx):
        start = pl.multiple_of(plan.part(i, odd) * by, by)
        for p in range(px):
            at = i * by * 2 * px + p
            scaled[0, p, pl.ds(start, by), :] = parts[pl.ds(at, by, stride=2 * px), :]
            residual[0, p, pl.ds(start, by), :] = parts[pl.ds(at + px, by, stride=2 * px), :]


def in_vmem(*shape):
    return pltpu.VMEM(shape, F32)


def call(kernel, out_shape, scratch=(), **more):
    return pl.pallas_call(
        kernel,
        out_shape=out_shape,
        scratch_shapes=list(scratch),
        compiler_params=pltpu.CompilerParams(vmem_limit_bytes=VMEM_LIMIT),
        **more,
    )


def pinned(*arrays, where=pltpu.VMEM):
    return [pltpu.with_memory_space_constraint(a, where) for a in arrays]


def beside_in_z(plan, a):
    count = plan.gz
    if plan.paired:
        return lax.ppermute(a, "gz", [(0, 1), (1, 0)])
    cut = LANES // 2
    right = lax.ppermute(a[..., :cut], "gz", [(i + 1, i) for i in range(count - 1)])
    left = lax.ppermute(a[..., cut:], "gz", [(i, i + 1) for i in range(count - 1)])
    return jnp.concatenate([right, left], axis=-1)


def shift(plan, a, k):
    pairs = [(plan.device(b), plan.device(b + k)) for b in range(plan.blocks) if 0 <= b + k < plan.blocks]
    return lax.ppermute(a, ("gx", "gy"), pairs)


def shift_apart(plan, a, k):
    pairs = []
    for b in range(plan.blocks):
        for core, to in ((0, b + k), (1, b - k)):
            if 0 <= to < plan.blocks:
                pairs.append((2 * plan.device(b) + core, 2 * plan.device(to) + core))
    return lax.ppermute(a, ("gx", "gy", "gz"), pairs)


def on_device(plan, phase, density, rhs):
    nx, by, rows, px, gx = plan.nx, plan.by, plan.rows, plan.px, plan.gx
    flat = gx * by * 2 * px
    block = (px, plan.ny, LANES)
    outside = pl.BlockSpec(memory_space=pltpu.HBM)
    (parts,) = call(
        functools.partial(prepare_kernel, plan),
        [in_vmem(flat, LANES)],
        [pltpu.VMEM(block, jnp.int32), in_vmem(*block), in_vmem(1, *block), pltpu.SemaphoreType.DMA((3,))],
        in_specs=[outside] * 3,
    )(*pinned(phase, density, rhs, where=pltpu.HBM))
    parts = parts.reshape(gx, by, 2, px, LANES)
    c = lax.all_to_all(parts, "gx", 0, 0, tiled=True)
    lo = shift(plan, c[:, by - HALO :], 1)
    hi = shift(plan, c[:, :HALO], -1)
    zc = beside_in_z(plan, c)
    zh = beside_in_z(plan, jnp.concatenate([lo, hi], axis=0))

    own, own2 = by // 2, by // 4
    size = 5 * (own2 // 2) * (nx // 4)
    side = size + 8 * (nx // 2)

    def level0(n):
        return in_vmem(n, 2, nx, LANES)

    def level1(n):
        return in_vmem(n, 2, nx // 2, LANES)

    outs = [in_vmem(size, LANES)] + [in_vmem(side, LANES)] * (1 if plan.paired else 2)
    fields = [level0(rows)] * 7 + [level1(own + 8)] * 6
    scratch = [level0(rows)] * 2 + [level0(own + 4), level1(own + 8), level1(own2), level1(own + 8)]
    scratch += [in_vmem(2, size, WIDE)]
    down = call(functools.partial(down_kernel, plan), outs + fields, scratch)(*pinned(c, lo, hi, zc, zh))
    pack, nears, fields = down[0], down[1 : len(outs)], down[len(outs) :]

    if plan.paired:
        first = shift_apart(plan, nears[0], 1)
        both = jnp.concatenate([pack, first[:size]], axis=0)
        below = jnp.concatenate([first, shift_apart(plan, both, 2)], axis=0)
        above = lax.ppermute(below, "gz", [(0, 1), (1, 0)])
    else:
        sides = []
        for way, near in ((1, nears[0]), (-1, nears[1])):
            first = shift(plan, near, way)
            both = jnp.concatenate([pack, first[:size]], axis=0)
            sides.append(jnp.concatenate([first, shift(plan, both, 2 * way)], axis=0))
        below, above = sides

    rows2 = (2 * FAR + 1) * own2
    scratch = [in_vmem(2 * FAR + 1, size, LANES)]
    scratch += [in_vmem(rows2 + 1, 2, nx // 4, LANES)] * 9 + [in_vmem(rows2 // 2 + 1, 2, nx // 4, LANES)] * 8
    scratch += [level1(rows2), level0(own + 8)] + [level1(own + 8)] * 3 + [level0(rows)] * 2
    (result,) = call(
        functools.partial(up_kernel, plan), [in_vmem(gx, by, 2, px, LANES)], scratch
    )(*pinned(pack, below, above, *fields))

    result = lax.all_to_all(result, "gx", 0, 0, tiled=True)
    return call(
        functools.partial(place_kernel, plan),
        [jax.ShapeDtypeStruct((1, px, plan.ny, LANES), F32)] * 2,
    )(*pinned(result.reshape(flat, LANES)))


def solution(mesh):
    sizes = [mesh.shape[a] for a in ("gx", "gy", "gz")]

    def local(phase, density, rhs):
        return tuple(on_device(Plan(sizes, phase.shape), phase, density, rhs))

    in_specs = (P("gx", "gy", "gz"), P("gx", "gy", "gz"), P(None, "gx", "gy", "gz"))
    out_specs = (P(None, "gx", "gy", "gz"), P(None, "gx", "gy", "gz"))
    return jax.shard_map(local, mesh=mesh, in_specs=in_specs, out_specs=out_specs, check_vma=False)
```

```python
import functools

import jax
import jax.numpy as jnp
from jax import lax
from jax.experimental import pallas as pl
from jax.experimental.pallas import tpu as pltpu
from jax.sharding import PartitionSpec as P


DAMPING = 2.0 / 3.0
LANES = 128
WIDE = 256
HALO = 7
FAR = 3
F32 = jnp.float32
VMEM_LIMIT = 24 * 1024 * 1024


class Plan:
    def __init__(self, sizes, shape):
        self.gx, self.gy, self.gz = sizes
        self.px, self.ny, self.nz = shape
        self.nx = self.px * self.gx
        self.by = self.ny // self.gx
        self.blocks = self.gx * self.gy
        self.rows = self.by + 2 * HALO
        self.paired = self.gz == 2
        order = [0, 1, 3, 2] if self.gx == 4 else list(range(self.gx))
        self.place = [order.index(i) for i in range(self.gx)]
        self.order = order

    def device(self, block):
        j, q = divmod(block, self.gx)
        i = self.order[q if j % 2 == 0 else self.gx - 1 - q]
        return i * self.gy + j

    def part(self, i, odd):
        q = self.place[i]
        return q + odd * (self.gx - 1 - 2 * q)

    def block_here(self):
        i, j = lax.axis_index("gx"), lax.axis_index("gy")
        q = sum(jnp.where(i == k, self.place[k], 0) for k in range(self.gx))
        odd = lax.rem(j, 2)
        return j * self.gx + q + odd * (self.gx - 1 - 2 * q)


def x_up(a, s=1):
    return pltpu.roll(a, a.shape[0] - s, 0)


def x_down(a, s=1):
    return pltpu.roll(a, s, 0)


def z_up(a, g):
    return pltpu.roll(a, a.shape[1] - g, 1)


def z_down(a, g):
    return pltpu.roll(a, g, 1)


def inverse(a):
    r = pl.reciprocal(a, approx=True)
    return r * (2.0 - a * r)


def each(first, last, step, body):
    count = last + 1 - first
    if count <= 2 * step:
        for i in range(first, last + 1):
            body(i)
        return

    def go(c, _):
        for k in range(step):
            body(first + c * step + k)
        return 0

    lax.fori_loop(0, count // step, go, 0)
    for i in range(first + count // step * step, last + 1):
        body(i)


def wave(*stages):
    start = min(first + delay for _, first, _, delay in stages)
    end = max(last + delay for _, _, last, delay in stages)
    full = max(first + delay for _, first, _, delay in stages)
    full_end = min(last + delay for _, _, last, delay in stages)

    def step(t):
        for body, first, last, delay in stages:
            if first <= t - delay <= last:
                body(t - delay)

    def all_of_them(t, _):
        for body, _, _, delay in stages:
            body(t - delay)
        return 0

    if full_end - full < 3:
        full = full_end = end + 1
    for t in range(start, min(full, end + 1)):
        step(t)
    if full <= end:
        lax.fori_loop(full, full_end + 1, all_of_them, 0)
        for t in range(full_end + 1, end + 1):
            step(t)


class Wide:
    def __init__(self, ref):
        self.ref = ref

    def __getitem__(self, key):
        r, xs = key if isinstance(key, tuple) else (key, slice(None))
        return jnp.concatenate([self.ref[r, 0, xs, :], self.ref[r, 1, xs, :]], axis=1)

    def __setitem__(self, key, value):
        r, xs = key if isinstance(key, tuple) else (key, slice(None))
        self.ref[r, 0, xs, :] = value[:, :LANES]
        self.ref[r, 1, xs, :] = value[:, LANES:]


class Level:
    def __init__(self, s, g, kx, ky, kz, d, w, f, step=2):
        self.s, self.g, self.step = s, g, step
        self.kx, self.ky, self.kz, self.d, self.w, self.f = kx, ky, kz, d, w, f

    def beside(self, u, r):
        here = u[r]
        kx, kz = self.kx[r], self.kz[r]
        a = kx * x_up(here, self.s) + x_down(kx * here, self.s)
        b = kz * z_up(here, self.g) + z_down(kz * here, self.g)
        return a + b + (self.ky[r + 1] * u[r + 1] + self.ky[r] * u[r - 1])

    def weigh(self, first, last):
        def body(r):
            self.w[r] = DAMPING * inverse(self.d[r])

        each(first, last, self.step, body)

    def first(self, u, first, last):
        def body(r):
            u[r] = self.w[r] * self.f[r]

        each(first, last, self.step, body)

    def swept(self, u, r):
        return (1.0 / 3.0) * u[r] + self.w[r] * (self.f[r] + self.beside(u, r))

    def sweep(self, u, v, first, last):
        def body(r):
            v[r] = self.swept(u, r)

        each(first, last, self.step, body)

    def residual(self, u, r):
        return self.f[r] + self.beside(u, r) - self.d[r] * u[r]

    def residual_pairs(self, u, out, first, count):
        def body(j):
            out[j] = self.residual(u, first + 2 * j) + self.residual(u, first + 2 * j + 1)

        each(0, count - 1, self.step // 2, body)


def z_pairs(low, g):
    return lambda a: a + jnp.where(low, z_up(a, g), z_down(a, g))


def coarse_coefficients(level, r, x_count):
    even, odd = pl.ds(0, x_count, stride=2), pl.ds(1, x_count, stride=2)
    g = level.g
    low = (lax.broadcasted_iota(jnp.int32, (x_count, WIDE), 1) & g) == 0
    z_pair = z_pairs(low, g)

    def all_x(ref, row):
        return ref[row, even] + ref[row, odd]

    kx = level.kx[r, odd] + level.kx[r + 1, odd]
    inner = level.kx[r, even] + level.kx[r + 1, even] + all_x(level.ky, r + 1)
    kz = all_x(level.kz, r) + all_x(level.kz, r + 1)
    d = all_x(level.d, r) + all_x(level.d, r + 1)
    d = d - 2.0 * (inner + jnp.where(low, kz, 0.0))
    return z_pair(kx), coarse_sum(level.ky, r + 2, x_count, g), jnp.where(low, z_up(kz, g), kz), z_pair(d)


def coarse_sum(ref, r, x_count, g):
    even, odd = pl.ds(0, x_count, stride=2), pl.ds(1, x_count, stride=2)
    low = (lax.broadcasted_iota(jnp.int32, (x_count, WIDE), 1) & g) == 0
    return z_pairs(low, g)(ref[r, even] + ref[r, odd])


def correct(u, v, e, t, x_count, first, last, to):
    def body(j):
        part = e[j]
        t[j, pl.ds(0, x_count, stride=2)] = part
        t[j, pl.ds(1, x_count, stride=2)] = part
        wide = t[j]
        r = to + 2 * (j - first)
        v[r] = u[r] + wide
        v[r + 1] = u[r + 1] + wide

    each(first, last, 2, body)


def pick_lanes(a, lanes):
    return jnp.take_along_axis(a, lanes, axis=1, mode="promise_in_bounds")


def prepare_kernel(plan, phase_in, density_in, rhs_in, out, phase, density, rhs, sems):
    pairs = ((phase_in, phase), (density_in, density), (rhs_in, rhs))
    copies = [pltpu.make_async_copy(a, b, sems.at[k]) for k, (a, b) in enumerate(pairs)]
    for copy in copies:
        copy.start()
    for copy in copies:
        copy.wait()
    odd = lax.rem(lax.axis_index("gy"), 2)
    by, px = plan.by, plan.px
    for i in range(plan.gx):
        start = pl.multiple_of(plan.part(i, odd) * by, by)
        rows = pl.ds(start, by)
        for p in range(px):
            half = jnp.where(phase[p, rows, :] == 1, 500.0, 0.5).astype(F32)
            at = i * by * 2 * px + p
            out[pl.ds(at, by, stride=2 * px), :] = half * density[p, rows, :]
            out[pl.ds(at + px, by, stride=2 * px), :] = rhs[0, p, rows, :]


def down_kernel(plan, c, lo, hi, zc, zh, *refs):
    near_count = 1 if plan.paired else 2
    pack, nears, refs = refs[0], refs[1 : 1 + near_count], refs[1 + near_count :]
    kx0, ky0, kz0, d0, w0, f0, ub, kx1, ky1, kz1, w1, f1, u1 = [Wide(r) for r in refs[:13]]
    h0, ua, face, r0, uc, r1, d1 = [Wide(r) for r in refs[13:20]]
    stage = refs[20]
    nx, by, rows, gx = plan.nx, plan.by, plan.rows, plan.gx
    shape = (nx, WIDE)
    base = plan.block_here() * by - HALO
    y_count, z_count = plan.by * plan.blocks, plan.nz * plan.gz

    x = lax.broadcasted_iota(jnp.int32, shape, 0)
    lane = lax.broadcasted_iota(jnp.int32, shape, 1)
    core = lax.axis_index("gz")
    if plan.paired:
        z = lax.rem(core * LANES + lane, WIDE)
    else:
        z = core * LANES + jnp.where(lane < LANES + LANES // 2, lane, lane - WIDE)
    x_top, x_bottom = x == nx - 1, x == 0
    z_top, z_bottom = z == z_count - 1, z == 0
    z_shut = (z < 0) | (z >= z_count - 1)
    z_out = (z < 0) | (z >= z_count)

    def take(a, b, shift, r, to):
        def field(t):
            left = jnp.concatenate([a[s, r, t] for s in range(gx)], axis=0)
            right = jnp.concatenate([b[shift + s, r, t] for s in range(gx)], axis=0)
            return jnp.concatenate([left, right], axis=1)

        y = base + to
        h = jnp.where((y >= 0) & (y < y_count), field(0), 0.5)
        h0[to] = h if plan.paired else jnp.where(z_out, 0.5, h)
        f0[to] = field(1)

    each(0, HALO - 1, 4, lambda r: take(lo, zh, 0, r, r))
    each(0, by - 1, 4, lambda r: take(c, zc, 0, r, r + HALO))
    each(0, HALO - 1, 4, lambda r: take(hi, zh, gx, r, r + HALO + by))

    block = plan.block_here()

    @pl.when(block == 0)
    def _():
        h0[HALO - 1] = h0[HALO]

    @pl.when(block == plan.blocks - 1)
    def _():
        h0[HALO + by] = h0[HALO + by - 1]

    def is_open(r):
        y = base + r
        return (y >= 0) & (y < y_count - 1)

    first_face = inverse(h0[0] + h0[1])
    face[1] = first_face
    ky0[1] = jnp.where(is_open(0), first_face, 0.0)

    def faces(j):
        yd = face[2 * j - 1]
        for r in (2 * j - 1, 2 * j):
            h = h0[r]
            alone = 0.5 * inverse(h)
            xu = inverse(h + jnp.where(x_top, h, x_up(h)))
            xd = jnp.where(x_bottom, alone, x_down(xu))
            yu = inverse(h + h0[r + 1])
            zu = inverse(h + jnp.where(z_top, h, z_up(h, 1)))
            zd = jnp.where(z_bottom, alone, z_down(zu, 1))
            d = xu + xd + yu + yd + zu + zd
            w = DAMPING * inverse(d)
            kx0[r] = jnp.where(x_top, 0.0, xu)
            ky0[r + 1] = jnp.where(is_open(r), yu, 0.0)
            kz0[r] = jnp.where(z_shut, 0.0, zu)
            d0[r], w0[r] = d, w
            ua[r] = w * f0[r]
            yd = yu
        face[2 * j + 1] = yd

    fine = Level(1, 1, kx0, ky0, kz0, d0, w0, f0)

    own = by // 2
    half_x = nx // 2
    middle = Level(1, 2, kx1, ky1, kz1, d1, w1, f1, 8)
    def coarsen(j):
        kx1[j], ky1[j + 1], kz1[j], d1[j] = coarse_coefficients(fine, 2 * j - 1, half_x)

    def restrict(j):
        f1[j] = coarse_sum(r0, j, half_x, 1)

    def sweep(j):
        ub[2 * j] = fine.swept(ua, 2 * j)
        ub[2 * j + 1] = fine.swept(ua, 2 * j + 1)

    def residual(j):
        r0[j] = fine.residual(ub, 2 * j - 1) + fine.residual(ub, 2 * j)

    wave(
        (restrict, 2, own + 5, 4),
        (residual, 2, own + 5, 3),
        (sweep, 1, own + 5, 2),
        (coarsen, 1, own + 6, 1),
        (faces, 1, own + 6, 0),
    )
    ky1[1] = coarse_sum(ky0, 1, half_x, 1)
    middle.weigh(1, own + 6)
    middle.first(uc, 2, own + 5)
    middle.sweep(uc, u1, 3, own + 4)
    middle.residual_pairs(u1, r1, 4, own // 2)

    quarter_x = nx // 4
    own2 = own // 2
    part = own2 // 2
    for j in range(own2):
        fields = (coarse_sum(r1, j, quarter_x, 2),) + coarse_coefficients(middle, 4 + 2 * j, quarter_x)
        for t, a in enumerate(fields):
            stage[j // part, pl.ds((t * part + j % part) * quarter_x, quarter_x), :] = a
    cell = lax.broadcasted_iota(jnp.int32, pack.shape, 1)
    lanes = lax.rem(4 * cell, LANES)
    quarter = lax.div(4 * cell, LANES)
    total = pick_lanes(stage[0, :, :LANES], lanes)
    for k in range(1, 4):
        half = slice((k % 2) * LANES, (k % 2 + 1) * LANES)
        total = jnp.where(quarter == k, pick_lanes(stage[k // 2, :, half], lanes), total)
    pack[...] = total

    size = pack.shape[0]

    def near(out, first):
        out[pl.ds(0, size), :] = total
        for k, (ref, r) in enumerate(((u1, first), (u1, first + 1), (u1, first + 2), (f1, first + 1))):
            for s in range(2):
                out[pl.ds(size + (2 * k + s) * half_x, half_x), :] = ref.ref[r, s]

    top = own
    if plan.paired:
        near(nears[0], top - (top - 5) * core)
    else:
        near(nears[0], top)
        near(nears[1], 5)


def up_kernel(plan, pack, below, above, *refs):
    refs, out, scratch = refs[:13], refs[13], refs[14:]
    kx0, ky0, kz0, d0, w0, f0, u0, kx1, ky1, kz1, w1, f1_in, u1_in = [Wide(r) for r in refs]
    stage = scratch[0]
    wide = [Wide(r) for r in scratch[1:]]
    f2, kx2, ky2, kz2, d2, w2, ua2, ub2, r2 = wide[:9]
    f3, kx3, ky3, kz3, d3, w3, ua3, ub3 = wide[9:17]
    t1, t0, f1, ua1, ub1, ua0, ub0, uc0 = wide[17:]
    nx, by = plan.nx, plan.by
    own, own2 = by // 2, by // 4
    part = own2 // 2
    half_x, quarter_x = nx // 2, nx // 4
    size = pack.shape[0]
    side = size + 8 * half_x
    core = lax.axis_index("gz")
    block = plan.block_here()
    zero = jnp.int32(0)

    for r in range(2, own + 6):
        f1[r] = f1_in[r]
    for r in range(3, own + 5):
        ua1[r] = u1_in[r]

    def spread_out(lower, upper, turn_lower, turn_upper):
        for k in range(FAR):
            at = 0 if k == 0 else side + (k - 1) * size
            stage[FAR - 1 - k] = lower[pl.ds(at, size), :]
            stage[FAR + 1 + k] = upper[pl.ds(at, size), :]
        for k, (ref, r_low, r_up) in enumerate(
            ((ua1, 0, own + 5), (ua1, 1, own + 6), (ua1, 2, own + 7), (f1, 1, own + 6))
        ):
            for s in range(2):
                rows = pl.ds(size + (2 * k + s) * half_x, half_x)
                ref.ref[r_low, s ^ turn_lower] = lower[rows, :]
                ref.ref[r_up, s ^ turn_upper] = upper[rows, :]

    stage[FAR] = pack[...]
    if plan.paired:
        turn_lower, turn_upper = core, 1 - core

        @pl.when(core == 0)
        def _():
            spread_out(below, above, 0, 1)

        @pl.when(core != 0)
        def _():
            spread_out(above, below, 1, 0)
    else:
        turn_lower, turn_upper = zero, zero
        spread_out(below, above, 0, 0)

    lane = lax.broadcasted_iota(jnp.int32, (size, LANES), 1)
    lanes = [lax.div(lane, 4) + k * (LANES // 4) for k in range(4)]

    def expand(k):
        there = block + k - FAR
        exists = (there >= 0) & (there < plan.blocks)
        turn = jnp.where(k < FAR, turn_lower, jnp.where(k > FAR, turn_upper, 0))
        rows = stage[k]
        for quarter in range(4):
            part_of, half = divmod(quarter, 2)
            a = pick_lanes(rows, lanes[quarter])
            for t, ref in enumerate((f2, kx2, ky2, kz2, d2)):
                for j in range(part):
                    at = (t * part + j) * quarter_x
                    b = a[at : at + quarter_x]
                    if t == 4:
                        b = jnp.where(exists, b, 1.0)
                    r = k * own2 + part_of * part + j + (1 if t == 2 else 0)
                    ref.ref[r, turn if half == 0 else 1 - turn] = b

    each(0, 2 * FAR, 4, expand)

    rows2 = (2 * FAR + 1) * own2
    two = Level(1, 4, kx2, ky2, kz2, d2, w2, f2, 14)
    two.weigh(0, rows2 - 1)
    two.first(ua2, 0, rows2 - 1)
    two.sweep(ua2, ub2, 1, rows2 - 2)
    two.residual_pairs(ub2, r2, 2, rows2 // 2 - 2)

    x = lax.broadcasted_iota(jnp.int32, (quarter_x, WIDE), 0)
    even_x = (x & 1) == 0
    low = (lax.broadcasted_iota(jnp.int32, (quarter_x, WIDE), 1) & 4) == 0
    z_pair = z_pairs(low, 4)

    def x_pair(a):
        return a + jnp.where(even_x, x_up(a), x_down(a))

    last3 = rows2 // 2 - 2

    def coarsen(j):
        r = 2 * j
        kx = kx2[r] + kx2[r + 1]
        kz = kz2[r] + kz2[r + 1]
        inner = ky2[r + 1] + jnp.where(even_x, kx, 0.0) + jnp.where(low, kz, 0.0)
        f3[j] = z_pair(x_pair(r2[j - 1]))
        kx3[j] = z_pair(jnp.where(even_x, x_up(kx), kx))
        ky3[j + 1] = z_pair(x_pair(ky2[r + 2]))
        kz = x_pair(kz)
        kz3[j] = jnp.where(low, z_up(kz, 4), kz)
        d3[j] = z_pair(x_pair(d2[r] + d2[r + 1] - 2.0 * inner))

    each(1, last3, 6, coarsen)
    three = Level(2, 8, kx3, ky3, kz3, d3, w3, f3, 16)
    three.weigh(1, last3)
    three.first(ua3, 1, last3)
    three.sweep(ua3, ub3, 2, last3 - 1)
    three.sweep(ub3, ua3, 3, last3 - 2)
    three.sweep(ua3, ub3, 4, last3 - 3)

    first2 = FAR * own2
    for j in range(4, last3 - 2):
        e = ub3[j]
        ua2[2 * j] = ub2[2 * j] + e
        ua2[2 * j + 1] = ub2[2 * j + 1] + e
    two.sweep(ua2, ub2, first2 - 3, first2 + own2 + 2)
    two.sweep(ub2, ua2, first2 - 2, first2 + own2 + 1)

    one = Level(1, 2, kx1, ky1, kz1, None, w1, f1, 8)
    correct(ua1, ub1, ua2, t1, quarter_x, first2 - 2, first2 + own2 + 1, 0)
    one.sweep(ub1, ua1, 1, own + 6)
    one.sweep(ua1, ub1, 2, own + 5)

    finest = Level(1, 1, kx0, ky0, kz0, d0, w0, f0)

    def corrected(j):
        part = ub1[j]
        t0[j, pl.ds(0, half_x, stride=2)] = part
        t0[j, pl.ds(1, half_x, stride=2)] = part
        both = t0[j]
        ua0[2 * j - 1] = u0[2 * j - 1] + both
        ua0[2 * j] = u0[2 * j] + both

    def sweep(j):
        ub0[2 * j - 1] = finest.swept(ua0, 2 * j - 1)
        ub0[2 * j] = finest.swept(ua0, 2 * j)

    def sweep_again(j):
        uc0[2 * j] = finest.swept(ub0, 2 * j)
        uc0[2 * j + 1] = finest.swept(ub0, 2 * j + 1)

    def finish(j):
        for r in (2 * j - 1, 2 * j):
            scaled = d0[r] * uc0[r]
            rest = f0[r] + finest.beside(uc0, r) - scaled
            for s in range(plan.gx):
                part = slice(s * plan.px, (s + 1) * plan.px)
                out[s, r - HALO, 0] = scaled[part, :LANES]
                out[s, r - HALO, 1] = rest[part, :LANES]

    wave(
        (finish, 4, own + 3, 5),
        (sweep_again, 3, own + 3, 4),
        (sweep, 3, own + 4, 2),
        (corrected, 2, own + 5, 0),
    )


def place_kernel(plan, parts, scaled, residual):
    odd = lax.rem(lax.axis_index("gy"), 2)
    by, px = plan.by, plan.px
    for i in range(plan.gx):
        start = pl.multiple_of(plan.part(i, odd) * by, by)
        for p in range(px):
            at = i * by * 2 * px + p
            scaled[0, p, pl.ds(start, by), :] = parts[pl.ds(at, by, stride=2 * px), :]
            residual[0, p, pl.ds(start, by), :] = parts[pl.ds(at + px, by, stride=2 * px), :]


def in_vmem(*shape):
    return pltpu.VMEM(shape, F32)


def call(kernel, out_shape, scratch=(), **more):
    return pl.pallas_call(
        kernel,
        out_shape=out_shape,
        scratch_shapes=list(scratch),
        compiler_params=pltpu.CompilerParams(vmem_limit_bytes=VMEM_LIMIT),
        **more,
    )


def pinned(*arrays, where=pltpu.VMEM):
    return [pltpu.with_memory_space_constraint(a, where) for a in arrays]


def beside_in_z(plan, a):
    count = plan.gz
    if plan.paired:
        return lax.ppermute(a, "gz", [(0, 1), (1, 0)])
    cut = LANES // 2
    right = lax.ppermute(a[..., :cut], "gz", [(i + 1, i) for i in range(count - 1)])
    left = lax.ppermute(a[..., cut:], "gz", [(i, i + 1) for i in range(count - 1)])
    return jnp.concatenate([right, left], axis=-1)


def shift(plan, a, k):
    pairs = [(plan.device(b), plan.device(b + k)) for b in range(plan.blocks) if 0 <= b + k < plan.blocks]
    return lax.ppermute(a, ("gx", "gy"), pairs)


def shift_apart(plan, a, k):
    pairs = []
    for b in range(plan.blocks):
        for core, to in ((0, b + k), (1, b - k)):
            if 0 <= to < plan.blocks:
                pairs.append((2 * plan.device(b) + core, 2 * plan.device(to) + core))
    return lax.ppermute(a, ("gx", "gy", "gz"), pairs)


def on_device(plan, phase, density, rhs):
    nx, by, rows, px, gx = plan.nx, plan.by, plan.rows, plan.px, plan.gx
    flat = gx * by * 2 * px
    block = (px, plan.ny, LANES)
    outside = pl.BlockSpec(memory_space=pltpu.HBM)
    (parts,) = call(
        functools.partial(prepare_kernel, plan),
        [in_vmem(flat, LANES)],
        [pltpu.VMEM(block, jnp.int32), in_vmem(*block), in_vmem(1, *block), pltpu.SemaphoreType.DMA((3,))],
        in_specs=[outside] * 3,
    )(*pinned(phase, density, rhs, where=pltpu.HBM))
    parts = parts.reshape(gx, by, 2, px, LANES)
    c = lax.all_to_all(parts, "gx", 0, 0, tiled=True)
    lo = shift(plan, c[:, by - HALO :], 1)
    hi = shift(plan, c[:, :HALO], -1)
    zc = beside_in_z(plan, c)
    zh = beside_in_z(plan, jnp.concatenate([lo, hi], axis=0))

    own, own2 = by // 2, by // 4
    size = 5 * (own2 // 2) * (nx // 4)
    side = size + 8 * (nx // 2)

    def level0(n):
        return in_vmem(n, 2, nx, LANES)

    def level1(n):
        return in_vmem(n, 2, nx // 2, LANES)

    outs = [in_vmem(size, LANES)] + [in_vmem(side, LANES)] * (1 if plan.paired else 2)
    fields = [level0(rows)] * 7 + [level1(own + 8)] * 6
    scratch = [level0(rows)] * 3 + [level0(own + 8), level1(own + 8), level1(own2), level1(own + 8)]
    scratch += [in_vmem(2, size, WIDE)]
    down = call(functools.partial(down_kernel, plan), outs + fields, scratch)(*pinned(c, lo, hi, zc, zh))
    pack, nears, fields = down[0], down[1 : len(outs)], down[len(outs) :]

    if plan.paired:
        first = shift_apart(plan, nears[0], 1)
        both = jnp.concatenate([pack, first[:size]], axis=0)
        below = jnp.concatenate([first, shift_apart(plan, both, 2)], axis=0)
        above = lax.ppermute(below, "gz", [(0, 1), (1, 0)])
    else:
        sides = []
        for way, near in ((1, nears[0]), (-1, nears[1])):
            first = shift(plan, near, way)
            both = jnp.concatenate([pack, first[:size]], axis=0)
            sides.append(jnp.concatenate([first, shift(plan, both, 2 * way)], axis=0))
        below, above = sides

    rows2 = (2 * FAR + 1) * own2
    scratch = [in_vmem(2 * FAR + 1, size, LANES)]
    scratch += [in_vmem(rows2 + 1, 2, nx // 4, LANES)] * 9 + [in_vmem(rows2 // 2 + 1, 2, nx // 4, LANES)] * 8
    scratch += [level1(rows2), level0(own + 8)] + [level1(own + 8)] * 3 + [level0(rows)] * 3
    (result,) = call(
        functools.partial(up_kernel, plan), [in_vmem(gx, by, 2, px, LANES)], scratch
    )(*pinned(pack, below, above, *fields))

    result = lax.all_to_all(result, "gx", 0, 0, tiled=True)
    return call(
        functools.partial(place_kernel, plan),
        [jax.ShapeDtypeStruct((1, px, plan.ny, LANES), F32)] * 2,
    )(*pinned(result.reshape(flat, LANES)))


def solution(mesh):
    sizes = [mesh.shape[a] for a in ("gx", "gy", "gz")]

    def local(phase, density, rhs):
        return tuple(on_device(Plan(sizes, phase.shape), phase, density, rhs))

    in_specs = (P("gx", "gy", "gz"), P("gx", "gy", "gz"), P(None, "gx", "gy", "gz"))
    out_specs = (P(None, "gx", "gy", "gz"), P(None, "gx", "gy", "gz"))
    return jax.shard_map(local, mesh=mesh, in_specs=in_specs, out_specs=out_specs, check_vma=False)
```

```python
import functools

import jax
import jax.numpy as jnp
from jax import lax
from jax.experimental import pallas as pl
from jax.experimental.pallas import tpu as pltpu
from jax.sharding import PartitionSpec as P


DAMPING = 2.0 / 3.0
LANES = 128
WIDE = 256
HALO = 7
FAR = 3
F32 = jnp.float32
VMEM_LIMIT = 24 * 1024 * 1024


class Plan:
    def __init__(self, sizes, shape):
        self.gx, self.gy, self.gz = sizes
        self.px, self.ny, self.nz = shape
        self.nx = self.px * self.gx
        self.by = self.ny // self.gx
        self.blocks = self.gx * self.gy
        self.rows = self.by + 2 * HALO
        self.paired = self.gz == 2
        order = [0, 1, 3, 2] if self.gx == 4 else list(range(self.gx))
        self.place = [order.index(i) for i in range(self.gx)]
        self.order = order

    def device(self, block):
        j, q = divmod(block, self.gx)
        i = self.order[q if j % 2 == 0 else self.gx - 1 - q]
        return i * self.gy + j

    def part(self, i, odd):
        q = self.place[i]
        return q + odd * (self.gx - 1 - 2 * q)

    def block_here(self):
        i, j = lax.axis_index("gx"), lax.axis_index("gy")
        q = sum(jnp.where(i == k, self.place[k], 0) for k in range(self.gx))
        odd = lax.rem(j, 2)
        return j * self.gx + q + odd * (self.gx - 1 - 2 * q)


def x_up(a, s=1):
    return pltpu.roll(a, a.shape[0] - s, 0)


def x_down(a, s=1):
    return pltpu.roll(a, s, 0)


def z_up(a, g):
    return pltpu.roll(a, a.shape[1] - g, 1)


def z_down(a, g):
    return pltpu.roll(a, g, 1)


def inverse(a):
    r = pl.reciprocal(a, approx=True)
    return r * (2.0 - a * r)


def each(first, last, step, body):
    count = last + 1 - first
    if count <= 2 * step:
        for i in range(first, last + 1):
            body(i)
        return

    def go(c, _):
        for k in range(step):
            body(first + c * step + k)
        return 0

    lax.fori_loop(0, count // step, go, 0)
    for i in range(first + count // step * step, last + 1):
        body(i)


def wave(*stages):
    start = min(first + delay for _, first, _, delay in stages)
    end = max(last + delay for _, _, last, delay in stages)
    full = max(first + delay for _, first, _, delay in stages)
    full_end = min(last + delay for _, _, last, delay in stages)

    def step(t):
        for body, first, last, delay in stages:
            if first <= t - delay <= last:
                body(t - delay)

    def all_of_them(t, _):
        for body, _, _, delay in stages:
            body(t - delay)
        return 0

    if full_end - full < 3:
        full = full_end = end + 1
    for t in range(start, min(full, end + 1)):
        step(t)
    if full <= end:
        lax.fori_loop(full, full_end + 1, all_of_them, 0)
        for t in range(full_end + 1, end + 1):
            step(t)


class Wide:
    def __init__(self, ref):
        self.ref = ref

    def __getitem__(self, key):
        r, xs = key if isinstance(key, tuple) else (key, slice(None))
        return jnp.concatenate([self.ref[r, 0, xs, :], self.ref[r, 1, xs, :]], axis=1)

    def __setitem__(self, key, value):
        r, xs = key if isinstance(key, tuple) else (key, slice(None))
        self.ref[r, 0, xs, :] = value[:, :LANES]
        self.ref[r, 1, xs, :] = value[:, LANES:]


class Level:
    def __init__(self, s, g, kx, ky, kz, d, w, f, step=2):
        self.s, self.g, self.step = s, g, step
        self.kx, self.ky, self.kz, self.d, self.w, self.f = kx, ky, kz, d, w, f

    def beside(self, u, r):
        here = u[r]
        kx, kz = self.kx[r], self.kz[r]
        a = kx * x_up(here, self.s) + x_down(kx * here, self.s)
        b = kz * z_up(here, self.g) + z_down(kz * here, self.g)
        return a + b + (self.ky[r + 1] * u[r + 1] + self.ky[r] * u[r - 1])

    def weigh(self, first, last):
        def body(r):
            self.w[r] = DAMPING * inverse(self.d[r])

        each(first, last, self.step, body)

    def first(self, u, first, last):
        def body(r):
            u[r] = self.w[r] * self.f[r]

        each(first, last, self.step, body)

    def swept(self, u, r):
        return (1.0 / 3.0) * u[r] + self.w[r] * (self.f[r] + self.beside(u, r))

    def sweep(self, u, v, first, last):
        def body(r):
            v[r] = self.swept(u, r)

        each(first, last, self.step, body)

    def residual(self, u, r):
        return self.f[r] + self.beside(u, r) - self.d[r] * u[r]

    def residual_pairs(self, u, out, first, count):
        def body(j):
            out[j] = self.residual(u, first + 2 * j) + self.residual(u, first + 2 * j + 1)

        each(0, count - 1, self.step // 2, body)


def z_pairs(low, g):
    return lambda a: a + jnp.where(low, z_up(a, g), z_down(a, g))


def coarse_coefficients(level, r, x_count):
    even, odd = pl.ds(0, x_count, stride=2), pl.ds(1, x_count, stride=2)
    g = level.g
    low = (lax.broadcasted_iota(jnp.int32, (x_count, WIDE), 1) & g) == 0
    z_pair = z_pairs(low, g)

    def all_x(ref, row):
        return ref[row, even] + ref[row, odd]

    kx = level.kx[r, odd] + level.kx[r + 1, odd]
    inner = level.kx[r, even] + level.kx[r + 1, even] + all_x(level.ky, r + 1)
    kz = all_x(level.kz, r) + all_x(level.kz, r + 1)
    d = all_x(level.d, r) + all_x(level.d, r + 1)
    d = d - 2.0 * (inner + jnp.where(low, kz, 0.0))
    return z_pair(kx), coarse_sum(level.ky, r + 2, x_count, g), jnp.where(low, z_up(kz, g), kz), z_pair(d)


def coarse_sum(ref, r, x_count, g):
    even, odd = pl.ds(0, x_count, stride=2), pl.ds(1, x_count, stride=2)
    low = (lax.broadcasted_iota(jnp.int32, (x_count, WIDE), 1) & g) == 0
    return z_pairs(low, g)(ref[r, even] + ref[r, odd])


def correct(u, v, e, t, x_count, first, last, to):
    def body(j):
        part = e[j]
        t[j, pl.ds(0, x_count, stride=2)] = part
        t[j, pl.ds(1, x_count, stride=2)] = part
        wide = t[j]
        r = to + 2 * (j - first)
        v[r] = u[r] + wide
        v[r + 1] = u[r + 1] + wide

    each(first, last, 2, body)


def pick_lanes(a, lanes):
    return jnp.take_along_axis(a, lanes, axis=1, mode="promise_in_bounds")


def prepare_kernel(plan, phase_in, density_in, rhs_in, out, phase, density, rhs, sems):
    pairs = ((phase_in, phase), (density_in, density), (rhs_in, rhs))
    copies = [pltpu.make_async_copy(a, b, sems.at[k]) for k, (a, b) in enumerate(pairs)]
    for copy in copies:
        copy.start()
    for copy in copies:
        copy.wait()
    odd = lax.rem(lax.axis_index("gy"), 2)
    by, px = plan.by, plan.px
    for i in range(plan.gx):
        start = pl.multiple_of(plan.part(i, odd) * by, by)
        rows = pl.ds(start, by)
        for p in range(px):
            half = jnp.where(phase[p, rows, :] == 1, 500.0, 0.5).astype(F32)
            at = i * by * 2 * px + p
            out[pl.ds(at, by, stride=2 * px), :] = half * density[p, rows, :]
            out[pl.ds(at + px, by, stride=2 * px), :] = rhs[0, p, rows, :]


def down_kernel(plan, c, zc, mine, theirs, *refs):
    near_count = 1 if plan.paired else 2
    pack, nears, refs = refs[0], refs[1 : 1 + near_count], refs[1 + near_count :]
    kx0, ky0, kz0, d0, w0, f0, ub, kx1, ky1, kz1, w1, f1, u1 = [Wide(r) for r in refs[:13]]
    h0, ua, face, r0, uc, r1, d1 = [Wide(r) for r in refs[13:20]]
    stage = refs[20]
    nx, by, rows, gx = plan.nx, plan.by, plan.rows, plan.gx
    shape = (nx, WIDE)
    base = plan.block_here() * by - HALO
    y_count, z_count = plan.by * plan.blocks, plan.nz * plan.gz

    x = lax.broadcasted_iota(jnp.int32, shape, 0)
    lane = lax.broadcasted_iota(jnp.int32, shape, 1)
    core = lax.axis_index("gz")
    if plan.paired:
        z = lax.rem(core * LANES + lane, WIDE)
    else:
        z = core * LANES + jnp.where(lane < LANES + LANES // 2, lane, lane - WIDE)
    x_top, x_bottom = x == nx - 1, x == 0
    z_top, z_bottom = z == z_count - 1, z == 0
    z_shut = (z < 0) | (z >= z_count - 1)
    z_out = (z < 0) | (z >= z_count)

    def take(a, b, a_at, b_at, r, to):
        def field(t):
            left = jnp.concatenate([a[a_at + s, r, t] for s in range(gx)], axis=0)
            right = jnp.concatenate([b[b_at + s, r, t] for s in range(gx)], axis=0)
            return jnp.concatenate([left, right], axis=1)

        y = base + to
        h = jnp.where((y >= 0) & (y < y_count), field(0), 0.5)
        h0[to] = h if plan.paired else jnp.where(z_out, 0.5, h)
        f0[to] = field(1)

    each(0, by - 1, 4, lambda r: take(c, zc, 0, 0, r, r + HALO))

    def take_halo(lower, upper):
        each(0, HALO - 1, 4, lambda r: take(*lower, r, r))
        each(0, HALO - 1, 4, lambda r: take(*upper, r, r + HALO + by))

    here, there = (mine, mine, 0, gx), (theirs, theirs, gx, 0)
    if plan.paired:
        pl.when(core == 0)(lambda: take_halo(here, there))
        pl.when(core != 0)(lambda: take_halo(there, here))
    else:
        take_halo(here, there)

    block = plan.block_here()

    @pl.when(block == 0)
    def _():
        h0[HALO - 1] = h0[HALO]

    @pl.when(block == plan.blocks - 1)
    def _():
        h0[HALO + by] = h0[HALO + by - 1]

    def is_open(r):
        y = base + r
        return (y >= 0) & (y < y_count - 1)

    first_face = inverse(h0[0] + h0[1])
    face[1] = first_face
    ky0[1] = jnp.where(is_open(0), first_face, 0.0)

    def faces(j):
        yd = face[2 * j - 1]
        for r in (2 * j - 1, 2 * j):
            h = h0[r]
            alone = 0.5 * inverse(h)
            xu = inverse(h + jnp.where(x_top, h, x_up(h)))
            xd = jnp.where(x_bottom, alone, x_down(xu))
            yu = inverse(h + h0[r + 1])
            zu = inverse(h + jnp.where(z_top, h, z_up(h, 1)))
            zd = jnp.where(z_bottom, alone, z_down(zu, 1))
            d = xu + xd + yu + yd + zu + zd
            w = DAMPING * inverse(d)
            kx0[r] = jnp.where(x_top, 0.0, xu)
            ky0[r + 1] = jnp.where(is_open(r), yu, 0.0)
            kz0[r] = jnp.where(z_shut, 0.0, zu)
            d0[r], w0[r] = d, w
            ua[r] = w * f0[r]
            yd = yu
        face[2 * j + 1] = yd

    fine = Level(1, 1, kx0, ky0, kz0, d0, w0, f0)

    own = by // 2
    half_x = nx // 2
    middle = Level(1, 2, kx1, ky1, kz1, d1, w1, f1, 8)
    def coarsen(j):
        kx1[j], ky1[j + 1], kz1[j], d1[j] = coarse_coefficients(fine, 2 * j - 1, half_x)

    def restrict(j):
        f1[j] = coarse_sum(r0, j, half_x, 1)

    def sweep(j):
        ub[2 * j] = fine.swept(ua, 2 * j)
        ub[2 * j + 1] = fine.swept(ua, 2 * j + 1)

    def residual(j):
        r0[j] = fine.residual(ub, 2 * j - 1) + fine.residual(ub, 2 * j)

    wave(
        (restrict, 2, own + 5, 4),
        (residual, 2, own + 5, 3),
        (sweep, 1, own + 5, 2),
        (coarsen, 1, own + 6, 1),
        (faces, 1, own + 6, 0),
    )
    ky1[1] = coarse_sum(ky0, 1, half_x, 1)
    middle.weigh(1, own + 6)
    middle.first(uc, 2, own + 5)
    middle.sweep(uc, u1, 3, own + 4)
    middle.residual_pairs(u1, r1, 4, own // 2)

    quarter_x = nx // 4
    own2 = own // 2
    part = own2 // 2
    for j in range(own2):
        fields = (coarse_sum(r1, j, quarter_x, 2),) + coarse_coefficients(middle, 4 + 2 * j, quarter_x)
        for t, a in enumerate(fields):
            stage[j // part, pl.ds((t * part + j % part) * quarter_x, quarter_x), :] = a
    cell = lax.broadcasted_iota(jnp.int32, pack.shape, 1)
    lanes = lax.rem(4 * cell, LANES)
    quarter = lax.div(4 * cell, LANES)
    total = pick_lanes(stage[0, :, :LANES], lanes)
    for k in range(1, 4):
        half = slice((k % 2) * LANES, (k % 2 + 1) * LANES)
        total = jnp.where(quarter == k, pick_lanes(stage[k // 2, :, half], lanes), total)
    pack[...] = total

    size = pack.shape[0]

    def near(out, first):
        out[pl.ds(0, size), :] = total
        for k, (ref, r) in enumerate(((u1, first), (u1, first + 1), (u1, first + 2), (f1, first + 1))):
            for s in range(2):
                out[pl.ds(size + (2 * k + s) * half_x, half_x), :] = ref.ref[r, s]

    top = own
    if plan.paired:
        near(nears[0], top - (top - 5) * core)
    else:
        near(nears[0], top)
        near(nears[1], 5)


def up_kernel(plan, pack, below, above, *refs):
    refs, out, scratch = refs[:13], refs[13], refs[14:]
    kx0, ky0, kz0, d0, w0, f0, u0, kx1, ky1, kz1, w1, f1_in, u1_in = [Wide(r) for r in refs]
    stage = scratch[0]
    wide = [Wide(r) for r in scratch[1:]]
    f2, kx2, ky2, kz2, d2, w2, ua2, ub2, r2 = wide[:9]
    f3, kx3, ky3, kz3, d3, w3, ua3, ub3 = wide[9:17]
    t1, t0, f1, ua1, ub1, ua0, ub0, uc0 = wide[17:]
    nx, by = plan.nx, plan.by
    own, own2 = by // 2, by // 4
    part = own2 // 2
    half_x, quarter_x = nx // 2, nx // 4
    size = pack.shape[0]
    side = size + 8 * half_x
    core = lax.axis_index("gz")
    block = plan.block_here()
    zero = jnp.int32(0)

    for r in range(2, own + 6):
        f1[r] = f1_in[r]
    for r in range(3, own + 5):
        ua1[r] = u1_in[r]

    def spread_out(lower, upper, turn_lower, turn_upper):
        for k in range(FAR):
            at = 0 if k == 0 else side + (k - 1) * size
            stage[FAR - 1 - k] = lower[pl.ds(at, size), :]
            stage[FAR + 1 + k] = upper[pl.ds(at, size), :]
        for k, (ref, r_low, r_up) in enumerate(
            ((ua1, 0, own + 5), (ua1, 1, own + 6), (ua1, 2, own + 7), (f1, 1, own + 6))
        ):
            for s in range(2):
                rows = pl.ds(size + (2 * k + s) * half_x, half_x)
                ref.ref[r_low, s ^ turn_lower] = lower[rows, :]
                ref.ref[r_up, s ^ turn_upper] = upper[rows, :]

    stage[FAR] = pack[...]
    if plan.paired:
        turn_lower, turn_upper = core, 1 - core

        @pl.when(core == 0)
        def _():
            spread_out(below, above, 0, 1)

        @pl.when(core != 0)
        def _():
            spread_out(above, below, 1, 0)
    else:
        turn_lower, turn_upper = zero, zero
        spread_out(below, above, 0, 0)

    lane = lax.broadcasted_iota(jnp.int32, (size, LANES), 1)
    lanes = [lax.div(lane, 4) + k * (LANES // 4) for k in range(4)]

    def expand(k):
        there = block + k - FAR
        exists = (there >= 0) & (there < plan.blocks)
        turn = jnp.where(k < FAR, turn_lower, jnp.where(k > FAR, turn_upper, 0))
        rows = stage[k]
        for quarter in range(4):
            part_of, half = divmod(quarter, 2)
            a = pick_lanes(rows, lanes[quarter])
            for t, ref in enumerate((f2, kx2, ky2, kz2, d2)):
                for j in range(part):
                    at = (t * part + j) * quarter_x
                    b = a[at : at + quarter_x]
                    if t == 4:
                        b = jnp.where(exists, b, 1.0)
                    r = k * own2 + part_of * part + j + (1 if t == 2 else 0)
                    ref.ref[r, turn if half == 0 else 1 - turn] = b

    each(0, 2 * FAR, 4, expand)

    rows2 = (2 * FAR + 1) * own2
    two = Level(1, 4, kx2, ky2, kz2, d2, w2, f2, 14)
    two.weigh(0, rows2 - 1)
    two.first(ua2, 0, rows2 - 1)
    two.sweep(ua2, ub2, 1, rows2 - 2)
    two.residual_pairs(ub2, r2, 2, rows2 // 2 - 2)

    x = lax.broadcasted_iota(jnp.int32, (quarter_x, WIDE), 0)
    even_x = (x & 1) == 0
    low = (lax.broadcasted_iota(jnp.int32, (quarter_x, WIDE), 1) & 4) == 0
    z_pair = z_pairs(low, 4)

    def x_pair(a):
        return a + jnp.where(even_x, x_up(a), x_down(a))

    last3 = rows2 // 2 - 2

    def coarsen(j):
        r = 2 * j
        kx = kx2[r] + kx2[r + 1]
        kz = kz2[r] + kz2[r + 1]
        inner = ky2[r + 1] + jnp.where(even_x, kx, 0.0) + jnp.where(low, kz, 0.0)
        f3[j] = z_pair(x_pair(r2[j - 1]))
        kx3[j] = z_pair(jnp.where(even_x, x_up(kx), kx))
        ky3[j + 1] = z_pair(x_pair(ky2[r + 2]))
        kz = x_pair(kz)
        kz3[j] = jnp.where(low, z_up(kz, 4), kz)
        d3[j] = z_pair(x_pair(d2[r] + d2[r + 1] - 2.0 * inner))

    each(1, last3, 6, coarsen)
    three = Level(2, 8, kx3, ky3, kz3, d3, w3, f3, 16)
    three.weigh(1, last3)
    three.first(ua3, 1, last3)
    three.sweep(ua3, ub3, 2, last3 - 1)
    three.sweep(ub3, ua3, 3, last3 - 2)
    three.sweep(ua3, ub3, 4, last3 - 3)

    first2 = FAR * own2
    for j in range(4, last3 - 2):
        e = ub3[j]
        ua2[2 * j] = ub2[2 * j] + e
        ua2[2 * j + 1] = ub2[2 * j + 1] + e
    two.sweep(ua2, ub2, first2 - 3, first2 + own2 + 2)
    two.sweep(ub2, ua2, first2 - 2, first2 + own2 + 1)

    one = Level(1, 2, kx1, ky1, kz1, None, w1, f1, 8)
    correct(ua1, ub1, ua2, t1, quarter_x, first2 - 2, first2 + own2 + 1, 0)
    one.sweep(ub1, ua1, 1, own + 6)
    one.sweep(ua1, ub1, 2, own + 5)

    finest = Level(1, 1, kx0, ky0, kz0, d0, w0, f0)

    def corrected(j):
        part = ub1[j]
        t0[j, pl.ds(0, half_x, stride=2)] = part
        t0[j, pl.ds(1, half_x, stride=2)] = part
        both = t0[j]
        ua0[2 * j - 1] = u0[2 * j - 1] + both
        ua0[2 * j] = u0[2 * j] + both

    def sweep(j):
        ub0[2 * j - 1] = finest.swept(ua0, 2 * j - 1)
        ub0[2 * j] = finest.swept(ua0, 2 * j)

    def sweep_again(j):
        uc0[2 * j] = finest.swept(ub0, 2 * j)
        uc0[2 * j + 1] = finest.swept(ub0, 2 * j + 1)

    def finish(j):
        for r in (2 * j - 1, 2 * j):
            scaled = d0[r] * uc0[r]
            rest = f0[r] + finest.beside(uc0, r) - scaled
            for s in range(plan.gx):
                part = slice(s * plan.px, (s + 1) * plan.px)
                out[s, r - HALO, 0] = scaled[part, :LANES]
                out[s, r - HALO, 1] = rest[part, :LANES]

    wave(
        (finish, 4, own + 3, 5),
        (sweep_again, 3, own + 3, 4),
        (sweep, 3, own + 4, 2),
        (corrected, 2, own + 5, 0),
    )


def place_kernel(plan, parts, scaled, residual):
    odd = lax.rem(lax.axis_index("gy"), 2)
    by, px = plan.by, plan.px
    for i in range(plan.gx):
        start = pl.multiple_of(plan.part(i, odd) * by, by)
        for p in range(px):
            at = i * by * 2 * px + p
            scaled[0, p, pl.ds(start, by), :] = parts[pl.ds(at, by, stride=2 * px), :]
            residual[0, p, pl.ds(start, by), :] = parts[pl.ds(at + px, by, stride=2 * px), :]


def in_vmem(*shape):
    return pltpu.VMEM(shape, F32)


def call(kernel, out_shape, scratch=(), **more):
    return pl.pallas_call(
        kernel,
        out_shape=out_shape,
        scratch_shapes=list(scratch),
        compiler_params=pltpu.CompilerParams(vmem_limit_bytes=VMEM_LIMIT),
        **more,
    )


def pinned(*arrays, where=pltpu.VMEM):
    return [pltpu.with_memory_space_constraint(a, where) for a in arrays]


def beside_in_z(plan, a):
    count = plan.gz
    if plan.paired:
        return lax.ppermute(a, "gz", [(0, 1), (1, 0)])
    cut = LANES // 2
    right = lax.ppermute(a[..., :cut], "gz", [(i + 1, i) for i in range(count - 1)])
    left = lax.ppermute(a[..., cut:], "gz", [(i, i + 1) for i in range(count - 1)])
    return jnp.concatenate([right, left], axis=-1)


def shift(plan, a, k):
    pairs = [(plan.device(b), plan.device(b + k)) for b in range(plan.blocks) if 0 <= b + k < plan.blocks]
    return lax.ppermute(a, ("gx", "gy"), pairs)


def shift_apart(plan, a, k, cross=0):
    pairs = []
    for b in range(plan.blocks):
        for core, to in ((0, b + k), (1, b - k)):
            if 0 <= to < plan.blocks:
                pairs.append((2 * plan.device(b) + (core ^ cross), 2 * plan.device(to) + core))
    return lax.ppermute(a, ("gx", "gy", "gz"), pairs)


def swap(a):
    return lax.ppermute(a, "gz", [(0, 1), (1, 0)])


def halos(plan, c):
    last, first = c[:, plan.by - HALO :], c[:, :HALO]
    if plan.paired:
        low = lax.axis_index("gz") == 0
        own = shift_apart(plan, jnp.where(low, last, first), 1)
        other = shift_apart(plan, jnp.where(low, first, last), 1, cross=1)
        mine = jnp.concatenate([own, other], axis=0)
        return mine, swap(mine)
    lo, hi = shift(plan, last, 1), shift(plan, first, -1)
    mine = jnp.concatenate([lo, beside_in_z(plan, lo)], axis=0)
    return mine, jnp.concatenate([beside_in_z(plan, hi), hi], axis=0)


def far_blocks(plan, pack, nears):
    def side(move, near):
        parts = [move(pack, k) for k in range(FAR, 1, -1)] + [move(near, 1)]
        return jnp.concatenate(parts[::-1], axis=0)

    if plan.paired:
        mine = side(functools.partial(shift_apart, plan), nears[0])
        return mine, swap(mine)
    return side(functools.partial(shift, plan), nears[0]), side(lambda a, k: shift(plan, a, -k), nears[1])


def on_device(plan, phase, density, rhs):
    nx, by, rows, px, gx = plan.nx, plan.by, plan.rows, plan.px, plan.gx
    flat = gx * by * 2 * px
    block = (px, plan.ny, LANES)
    outside = pl.BlockSpec(memory_space=pltpu.HBM)
    (parts,) = call(
        functools.partial(prepare_kernel, plan),
        [in_vmem(flat, LANES)],
        [pltpu.VMEM(block, jnp.int32), in_vmem(*block), in_vmem(1, *block), pltpu.SemaphoreType.DMA((3,))],
        in_specs=[outside] * 3,
    )(*pinned(phase, density, rhs, where=pltpu.HBM))
    parts = parts.reshape(gx, by, 2, px, LANES)
    c = lax.all_to_all(parts, "gx", 0, 0, tiled=True)
    zc = beside_in_z(plan, c)
    mine, theirs = halos(plan, c)

    own, own2 = by // 2, by // 4
    size = 5 * (own2 // 2) * (nx // 4)
    side = size + 8 * (nx // 2)

    def level0(n):
        return in_vmem(n, 2, nx, LANES)

    def level1(n):
        return in_vmem(n, 2, nx // 2, LANES)

    outs = [in_vmem(size, LANES)] + [in_vmem(side, LANES)] * (1 if plan.paired else 2)
    fields = [level0(rows)] * 7 + [level1(own + 8)] * 6
    scratch = [level0(rows)] * 3 + [level0(own + 8), level1(own + 8), level1(own2), level1(own + 8)]
    scratch += [in_vmem(2, size, WIDE)]
    down = call(functools.partial(down_kernel, plan), outs + fields, scratch)(*pinned(c, zc, mine, theirs))
    pack, nears, fields = down[0], down[1 : len(outs)], down[len(outs) :]

    below, above = far_blocks(plan, pack, nears)
    rows2 = (2 * FAR + 1) * own2
    scratch = [in_vmem(2 * FAR + 1, size, LANES)]
    scratch += [in_vmem(rows2 + 1, 2, nx // 4, LANES)] * 9 + [in_vmem(rows2 // 2 + 1, 2, nx // 4, LANES)] * 8
    scratch += [level1(rows2), level0(own + 8)] + [level1(own + 8)] * 3 + [level0(rows)] * 3
    (result,) = call(
        functools.partial(up_kernel, plan), [in_vmem(gx, by, 2, px, LANES)], scratch
    )(*pinned(pack, below, above, *fields))

    result = lax.all_to_all(result, "gx", 0, 0, tiled=True)
    return call(
        functools.partial(place_kernel, plan),
        [jax.ShapeDtypeStruct((1, px, plan.ny, LANES), F32)] * 2,
    )(*pinned(result.reshape(flat, LANES)))


def solution(mesh):
    sizes = [mesh.shape[a] for a in ("gx", "gy", "gz")]

    def local(phase, density, rhs):
        return tuple(on_device(Plan(sizes, phase.shape), phase, density, rhs))

    in_specs = (P("gx", "gy", "gz"), P("gx", "gy", "gz"), P(None, "gx", "gy", "gz"))
    out_specs = (P(None, "gx", "gy", "gz"), P(None, "gx", "gy", "gz"))
    return jax.shard_map(local, mesh=mesh, in_specs=in_specs, out_specs=out_specs, check_vma=False)
```

```python
import functools

import jax
import jax.numpy as jnp
from jax import lax
from jax.experimental import pallas as pl
from jax.experimental.pallas import tpu as pltpu
from jax.sharding import PartitionSpec as P


DAMPING = 2.0 / 3.0
LANES = 128
WIDE = 256
HALO = 7
FAR = 3
F32 = jnp.float32
VMEM_LIMIT = 24 * 1024 * 1024


class Plan:
    def __init__(self, sizes, shape):
        self.gx, self.gy, self.gz = sizes
        self.px, self.ny, self.nz = shape
        self.nx = self.px * self.gx
        self.by = self.ny // self.gx
        self.blocks = self.gx * self.gy
        self.rows = self.by + 2 * HALO
        self.paired = self.gz == 2
        order = [0, 1, 3, 2] if self.gx == 4 else list(range(self.gx))
        self.place = [order.index(i) for i in range(self.gx)]
        self.order = order

    def device(self, block):
        j, q = divmod(block, self.gx)
        i = self.order[q if j % 2 == 0 else self.gx - 1 - q]
        return i * self.gy + j

    def part(self, i, odd):
        q = self.place[i]
        return q + odd * (self.gx - 1 - 2 * q)

    def block_here(self):
        i, j = lax.axis_index("gx"), lax.axis_index("gy")
        q = sum(jnp.where(i == k, self.place[k], 0) for k in range(self.gx))
        odd = lax.rem(j, 2)
        return j * self.gx + q + odd * (self.gx - 1 - 2 * q)


def x_up(a, s=1):
    return pltpu.roll(a, a.shape[0] - s, 0)


def x_down(a, s=1):
    return pltpu.roll(a, s, 0)


def z_up(a, g):
    return pltpu.roll(a, a.shape[1] - g, 1)


def z_down(a, g):
    return pltpu.roll(a, g, 1)


def inverse(a):
    r = pl.reciprocal(a, approx=True)
    return r * (2.0 - a * r)


def each(first, last, step, body):
    count = last + 1 - first
    if count <= 2 * step:
        for i in range(first, last + 1):
            body(i)
        return

    def go(c, _):
        for k in range(step):
            body(first + c * step + k)
        return 0

    lax.fori_loop(0, count // step, go, 0)
    for i in range(first + count // step * step, last + 1):
        body(i)


def wave(*stages):
    start = min(first + delay for _, first, _, delay in stages)
    end = max(last + delay for _, _, last, delay in stages)
    full = max(first + delay for _, first, _, delay in stages)
    full_end = min(last + delay for _, _, last, delay in stages)

    def step(t):
        for body, first, last, delay in stages:
            if first <= t - delay <= last:
                body(t - delay)

    def all_of_them(t, _):
        for body, _, _, delay in stages:
            body(t - delay)
        return 0

    if full_end - full < 3:
        full = full_end = end + 1
    for t in range(start, min(full, end + 1)):
        step(t)
    if full <= end:
        lax.fori_loop(full, full_end + 1, all_of_them, 0)
        for t in range(full_end + 1, end + 1):
            step(t)


class Wide:
    def __init__(self, ref):
        self.ref = ref

    def __getitem__(self, key):
        r, xs = key if isinstance(key, tuple) else (key, slice(None))
        return jnp.concatenate([self.ref[r, 0, xs, :], self.ref[r, 1, xs, :]], axis=1)

    def __setitem__(self, key, value):
        r, xs = key if isinstance(key, tuple) else (key, slice(None))
        self.ref[r, 0, xs, :] = value[:, :LANES]
        self.ref[r, 1, xs, :] = value[:, LANES:]


class Level:
    def __init__(self, s, g, kx, ky, kz, d, w, f, step=2):
        self.s, self.g, self.step = s, g, step
        self.kx, self.ky, self.kz, self.d, self.w, self.f = kx, ky, kz, d, w, f

    def beside(self, u, r):
        here = u[r]
        kx, kz = self.kx[r], self.kz[r]
        a = kx * x_up(here, self.s) + x_down(kx * here, self.s)
        b = kz * z_up(here, self.g) + z_down(kz * here, self.g)
        return a + b + (self.ky[r + 1] * u[r + 1] + self.ky[r] * u[r - 1])

    def weigh(self, first, last):
        def body(r):
            self.w[r] = DAMPING * inverse(self.d[r])

        each(first, last, self.step, body)

    def first(self, u, first, last):
        def body(r):
            u[r] = self.w[r] * self.f[r]

        each(first, last, self.step, body)

    def swept(self, u, r):
        return (1.0 / 3.0) * u[r] + self.w[r] * (self.f[r] + self.beside(u, r))

    def sweep(self, u, v, first, last):
        def body(r):
            v[r] = self.swept(u, r)

        each(first, last, self.step, body)

    def residual(self, u, r):
        return self.f[r] + self.beside(u, r) - self.d[r] * u[r]

    def residual_pairs(self, u, out, first, count):
        def body(j):
            out[j] = self.residual(u, first + 2 * j) + self.residual(u, first + 2 * j + 1)

        each(0, count - 1, self.step // 2, body)


def z_pairs(low, g):
    return lambda a: a + jnp.where(low, z_up(a, g), z_down(a, g))


def coarse_coefficients(level, r, x_count):
    even, odd = pl.ds(0, x_count, stride=2), pl.ds(1, x_count, stride=2)
    g = level.g
    low = (lax.broadcasted_iota(jnp.int32, (x_count, WIDE), 1) & g) == 0
    z_pair = z_pairs(low, g)

    def all_x(ref, row):
        return ref[row, even] + ref[row, odd]

    kx = level.kx[r, odd] + level.kx[r + 1, odd]
    inner = level.kx[r, even] + level.kx[r + 1, even] + all_x(level.ky, r + 1)
    kz = all_x(level.kz, r) + all_x(level.kz, r + 1)
    d = all_x(level.d, r) + all_x(level.d, r + 1)
    d = d - 2.0 * (inner + jnp.where(low, kz, 0.0))
    return z_pair(kx), coarse_sum(level.ky, r + 2, x_count, g), jnp.where(low, z_up(kz, g), kz), z_pair(d)


def coarse_sum(ref, r, x_count, g):
    even, odd = pl.ds(0, x_count, stride=2), pl.ds(1, x_count, stride=2)
    low = (lax.broadcasted_iota(jnp.int32, (x_count, WIDE), 1) & g) == 0
    return z_pairs(low, g)(ref[r, even] + ref[r, odd])


def correct(u, v, e, t, x_count, first, last, to):
    def body(j):
        part = e[j]
        t[j, pl.ds(0, x_count, stride=2)] = part
        t[j, pl.ds(1, x_count, stride=2)] = part
        wide = t[j]
        r = to + 2 * (j - first)
        v[r] = u[r] + wide
        v[r + 1] = u[r + 1] + wide

    each(first, last, 2, body)


def pick_lanes(a, lanes):
    return jnp.take_along_axis(a, lanes, axis=1, mode="promise_in_bounds")


def prepare_kernel(plan, phase_in, density_in, rhs_in, out, phase, density, rhs, sems):
    pairs = ((phase_in, phase), (density_in, density), (rhs_in, rhs))
    copies = [pltpu.make_async_copy(a, b, sems.at[k]) for k, (a, b) in enumerate(pairs)]
    for copy in copies:
        copy.start()
    for copy in copies:
        copy.wait()
    odd = lax.rem(lax.axis_index("gy"), 2)
    by, px = plan.by, plan.px
    for i in range(plan.gx):
        start = pl.multiple_of(plan.part(i, odd) * by, by)
        rows = pl.ds(start, by)
        for p in range(px):
            half = jnp.where(phase[p, rows, :] == 1, 500.0, 0.5).astype(F32)
            at = i * by * 2 * px + p
            out[pl.ds(at, by, stride=2 * px), :] = half * density[p, rows, :]
            out[pl.ds(at + px, by, stride=2 * px), :] = rhs[0, p, rows, :]


def down_kernel(plan, c, lo, hi, zc, zh, *refs):
    near_count = 1 if plan.paired else 2
    pack, nears, refs = refs[0], refs[1 : 1 + near_count], refs[1 + near_count :]
    kx0, ky0, kz0, d0, w0, f0, ub, kx1, ky1, kz1, w1, f1, u1 = [Wide(r) for r in refs[:13]]
    h0, ua, face, r0, uc, r1, d1 = [Wide(r) for r in refs[13:20]]
    stage = refs[20]
    nx, by, rows, gx = plan.nx, plan.by, plan.rows, plan.gx
    shape = (nx, WIDE)
    base = plan.block_here() * by - HALO
    y_count, z_count = plan.by * plan.blocks, plan.nz * plan.gz

    x = lax.broadcasted_iota(jnp.int32, shape, 0)
    lane = lax.broadcasted_iota(jnp.int32, shape, 1)
    core = lax.axis_index("gz")
    if plan.paired:
        z = lax.rem(core * LANES + lane, WIDE)
    else:
        z = core * LANES + jnp.where(lane < LANES + LANES // 2, lane, lane - WIDE)
    x_top, x_bottom = x == nx - 1, x == 0
    z_top, z_bottom = z == z_count - 1, z == 0
    z_shut = (z < 0) | (z >= z_count - 1)
    z_out = (z < 0) | (z >= z_count)

    def take(a, b, shift, r, to):
        def field(t):
            left = jnp.concatenate([a[s, r, t] for s in range(gx)], axis=0)
            right = jnp.concatenate([b[shift + s, r, t] for s in range(gx)], axis=0)
            return jnp.concatenate([left, right], axis=1)

        y = base + to
        h = jnp.where((y >= 0) & (y < y_count), field(0), 0.5)
        h0[to] = h if plan.paired else jnp.where(z_out, 0.5, h)
        f0[to] = field(1)

    each(0, HALO - 1, 4, lambda r: take(lo, zh, 0, r, r))
    each(0, by - 1, 4, lambda r: take(c, zc, 0, r, r + HALO))
    each(0, HALO - 1, 4, lambda r: take(hi, zh, gx, r, r + HALO + by))

    block = plan.block_here()

    @pl.when(block == 0)
    def _():
        h0[HALO - 1] = h0[HALO]

    @pl.when(block == plan.blocks - 1)
    def _():
        h0[HALO + by] = h0[HALO + by - 1]

    def is_open(r):
        y = base + r
        return (y >= 0) & (y < y_count - 1)

    first_face = inverse(h0[0] + h0[1])
    face[1] = first_face
    ky0[1] = jnp.where(is_open(0), first_face, 0.0)

    def faces(j):
        yd = face[2 * j - 1]
        for r in (2 * j - 1, 2 * j):
            h = h0[r]
            alone = 0.5 * inverse(h)
            xu = inverse(h + jnp.where(x_top, h, x_up(h)))
            xd = jnp.where(x_bottom, alone, x_down(xu))
            yu = inverse(h + h0[r + 1])
            zu = inverse(h + jnp.where(z_top, h, z_up(h, 1)))
            zd = jnp.where(z_bottom, alone, z_down(zu, 1))
            d = xu + xd + yu + yd + zu + zd
            w = DAMPING * inverse(d)
            kx0[r] = jnp.where(x_top, 0.0, xu)
            ky0[r + 1] = jnp.where(is_open(r), yu, 0.0)
            kz0[r] = jnp.where(z_shut, 0.0, zu)
            d0[r], w0[r] = d, w
            ua[r] = w * f0[r]
            yd = yu
        face[2 * j + 1] = yd

    fine = Level(1, 1, kx0, ky0, kz0, d0, w0, f0)

    own = by // 2
    half_x = nx // 2
    middle = Level(1, 2, kx1, ky1, kz1, d1, w1, f1, 8)
    def coarsen(j):
        kx1[j], ky1[j + 1], kz1[j], d1[j] = coarse_coefficients(fine, 2 * j - 1, half_x)

    def restrict(j):
        f1[j] = coarse_sum(r0, j, half_x, 1)

    def sweep(j):
        ub[2 * j] = fine.swept(ua, 2 * j)
        ub[2 * j + 1] = fine.swept(ua, 2 * j + 1)

    def residual(j):
        r0[j] = fine.residual(ub, 2 * j - 1) + fine.residual(ub, 2 * j)

    wave(
        (restrict, 2, own + 5, 4),
        (residual, 2, own + 5, 3),
        (sweep, 1, own + 5, 2),
        (coarsen, 1, own + 6, 1),
        (faces, 1, own + 6, 0),
    )
    ky1[1] = coarse_sum(ky0, 1, half_x, 1)
    middle.weigh(1, own + 6)
    middle.first(uc, 2, own + 5)
    middle.sweep(uc, u1, 3, own + 4)
    middle.residual_pairs(u1, r1, 4, own // 2)

    quarter_x = nx // 4
    own2 = own // 2
    part = own2 // 2
    for j in range(own2):
        fields = (coarse_sum(r1, j, quarter_x, 2),) + coarse_coefficients(middle, 4 + 2 * j, quarter_x)
        for t, a in enumerate(fields):
            stage[j // part, pl.ds((t * part + j % part) * quarter_x, quarter_x), :] = a
    cell = lax.broadcasted_iota(jnp.int32, pack.shape, 1)
    lanes = lax.rem(4 * cell, LANES)
    quarter = lax.div(4 * cell, LANES)
    total = pick_lanes(stage[0, :, :LANES], lanes)
    for k in range(1, 4):
        half = slice((k % 2) * LANES, (k % 2 + 1) * LANES)
        total = jnp.where(quarter == k, pick_lanes(stage[k // 2, :, half], lanes), total)
    pack[...] = total

    size = pack.shape[0]

    def near(out, first):
        out[pl.ds(0, size), :] = total
        for k, (ref, r) in enumerate(((u1, first), (u1, first + 1), (u1, first + 2), (f1, first + 1))):
            for s in range(2):
                out[pl.ds(size + (2 * k + s) * half_x, half_x), :] = ref.ref[r, s]

    top = own
    if plan.paired:
        near(nears[0], top - (top - 5) * core)
    else:
        near(nears[0], top)
        near(nears[1], 5)


def up_kernel(plan, pack, below, above, *refs):
    refs, out, scratch = refs[:13], refs[13], refs[14:]
    kx0, ky0, kz0, d0, w0, f0, u0, kx1, ky1, kz1, w1, f1_in, u1_in = [Wide(r) for r in refs]
    stage = scratch[0]
    wide = [Wide(r) for r in scratch[1:]]
    f2, kx2, ky2, kz2, d2, w2, ua2, ub2, r2 = wide[:9]
    f3, kx3, ky3, kz3, d3, w3, ua3, ub3 = wide[9:17]
    t1, t0, f1, ua1, ub1, ua0, ub0, uc0 = wide[17:]
    nx, by = plan.nx, plan.by
    own, own2 = by // 2, by // 4
    part = own2 // 2
    half_x, quarter_x = nx // 2, nx // 4
    size = pack.shape[0]
    side = size + 8 * half_x
    core = lax.axis_index("gz")
    block = plan.block_here()
    zero = jnp.int32(0)

    for r in range(2, own + 6):
        f1[r] = f1_in[r]
    for r in range(3, own + 5):
        ua1[r] = u1_in[r]

    def spread_out(lower, upper, turn_lower, turn_upper):
        for k in range(FAR):
            at = 0 if k == 0 else side + (k - 1) * size
            stage[FAR - 1 - k] = lower[pl.ds(at, size), :]
            stage[FAR + 1 + k] = upper[pl.ds(at, size), :]
        for k, (ref, r_low, r_up) in enumerate(
            ((ua1, 0, own + 5), (ua1, 1, own + 6), (ua1, 2, own + 7), (f1, 1, own + 6))
        ):
            for s in range(2):
                rows = pl.ds(size + (2 * k + s) * half_x, half_x)
                ref.ref[r_low, s ^ turn_lower] = lower[rows, :]
                ref.ref[r_up, s ^ turn_upper] = upper[rows, :]

    stage[FAR] = pack[...]
    if plan.paired:
        turn_lower, turn_upper = core, 1 - core

        @pl.when(core == 0)
        def _():
            spread_out(below, above, 0, 1)

        @pl.when(core != 0)
        def _():
            spread_out(above, below, 1, 0)
    else:
        turn_lower, turn_upper = zero, zero
        spread_out(below, above, 0, 0)

    lane = lax.broadcasted_iota(jnp.int32, (size, LANES), 1)
    lanes = [lax.div(lane, 4) + k * (LANES // 4) for k in range(4)]

    def expand(k):
        there = block + k - FAR
        exists = (there >= 0) & (there < plan.blocks)
        turn = jnp.where(k < FAR, turn_lower, jnp.where(k > FAR, turn_upper, 0))
        rows = stage[k]
        for quarter in range(4):
            part_of, half = divmod(quarter, 2)
            a = pick_lanes(rows, lanes[quarter])
            for t, ref in enumerate((f2, kx2, ky2, kz2, d2)):
                for j in range(part):
                    at = (t * part + j) * quarter_x
                    b = a[at : at + quarter_x]
                    if t == 4:
                        b = jnp.where(exists, b, 1.0)
                    r = k * own2 + part_of * part + j + (1 if t == 2 else 0)
                    ref.ref[r, turn if half == 0 else 1 - turn] = b

    each(0, 2 * FAR, 4, expand)

    rows2 = (2 * FAR + 1) * own2
    two = Level(1, 4, kx2, ky2, kz2, d2, w2, f2, 14)
    two.weigh(0, rows2 - 1)
    two.first(ua2, 0, rows2 - 1)
    two.sweep(ua2, ub2, 1, rows2 - 2)
    two.residual_pairs(ub2, r2, 2, rows2 // 2 - 2)

    x = lax.broadcasted_iota(jnp.int32, (quarter_x, WIDE), 0)
    even_x = (x & 1) == 0
    low = (lax.broadcasted_iota(jnp.int32, (quarter_x, WIDE), 1) & 4) == 0
    z_pair = z_pairs(low, 4)

    def x_pair(a):
        return a + jnp.where(even_x, x_up(a), x_down(a))

    last3 = rows2 // 2 - 2

    def coarsen(j):
        r = 2 * j
        kx = kx2[r] + kx2[r + 1]
        kz = kz2[r] + kz2[r + 1]
        inner = ky2[r + 1] + jnp.where(even_x, kx, 0.0) + jnp.where(low, kz, 0.0)
        f3[j] = z_pair(x_pair(r2[j - 1]))
        kx3[j] = z_pair(jnp.where(even_x, x_up(kx), kx))
        ky3[j + 1] = z_pair(x_pair(ky2[r + 2]))
        kz = x_pair(kz)
        kz3[j] = jnp.where(low, z_up(kz, 4), kz)
        d3[j] = z_pair(x_pair(d2[r] + d2[r + 1] - 2.0 * inner))

    each(1, last3, 6, coarsen)
    three = Level(2, 8, kx3, ky3, kz3, d3, w3, f3, 16)
    three.weigh(1, last3)
    three.first(ua3, 1, last3)
    three.sweep(ua3, ub3, 2, last3 - 1)
    three.sweep(ub3, ua3, 3, last3 - 2)
    three.sweep(ua3, ub3, 4, last3 - 3)

    first2 = FAR * own2
    for j in range(4, last3 - 2):
        e = ub3[j]
        ua2[2 * j] = ub2[2 * j] + e
        ua2[2 * j + 1] = ub2[2 * j + 1] + e
    two.sweep(ua2, ub2, first2 - 3, first2 + own2 + 2)
    two.sweep(ub2, ua2, first2 - 2, first2 + own2 + 1)

    one = Level(1, 2, kx1, ky1, kz1, None, w1, f1, 8)
    correct(ua1, ub1, ua2, t1, quarter_x, first2 - 2, first2 + own2 + 1, 0)
    one.sweep(ub1, ua1, 1, own + 6)
    one.sweep(ua1, ub1, 2, own + 5)

    finest = Level(1, 1, kx0, ky0, kz0, d0, w0, f0)

    def corrected(j):
        part = ub1[j]
        t0[j, pl.ds(0, half_x, stride=2)] = part
        t0[j, pl.ds(1, half_x, stride=2)] = part
        both = t0[j]
        ua0[2 * j - 1] = u0[2 * j - 1] + both
        ua0[2 * j] = u0[2 * j] + both

    def sweep(j):
        ub0[2 * j - 1] = finest.swept(ua0, 2 * j - 1)
        ub0[2 * j] = finest.swept(ua0, 2 * j)

    def sweep_again(j):
        uc0[2 * j] = finest.swept(ub0, 2 * j)
        uc0[2 * j + 1] = finest.swept(ub0, 2 * j + 1)

    def finish(j):
        for r in (2 * j - 1, 2 * j):
            scaled = d0[r] * uc0[r]
            rest = f0[r] + finest.beside(uc0, r) - scaled
            for s in range(plan.gx):
                part = slice(s * plan.px, (s + 1) * plan.px)
                out[s, r - HALO, 0] = scaled[part, :LANES]
                out[s, r - HALO, 1] = rest[part, :LANES]

    wave(
        (finish, 4, own + 3, 5),
        (sweep_again, 3, own + 3, 4),
        (sweep, 3, own + 4, 2),
        (corrected, 2, own + 5, 0),
    )


def place_kernel(plan, mine, first, second, third, scaled, residual):
    odd = lax.rem(lax.axis_index("gy"), 2)
    here = lax.axis_index("gx")
    by, px = plan.by, plan.px
    size = by * 2 * px

    def put(parts, base, i):
        q = sum(jnp.where(i == k, plan.place[k], 0) for k in range(plan.gx))
        start = pl.multiple_of((q + odd * (plan.gx - 1 - 2 * q)) * by, by)
        for p in range(px):
            at = base + p
            scaled[0, p, pl.ds(start, by), :] = parts[pl.ds(at, by, stride=2 * px), :]
            residual[0, p, pl.ds(start, by), :] = parts[pl.ds(at + px, by, stride=2 * px), :]

    put(mine, here * size, here)
    for k, parts in ((1, first), (2, second), (3, third)):
        put(parts, 0, here ^ k)


def in_vmem(*shape):
    return pltpu.VMEM(shape, F32)


def call(kernel, out_shape, scratch=(), **more):
    return pl.pallas_call(
        kernel,
        out_shape=out_shape,
        scratch_shapes=list(scratch),
        compiler_params=pltpu.CompilerParams(vmem_limit_bytes=VMEM_LIMIT),
        **more,
    )


def pinned(*arrays, where=pltpu.VMEM):
    return [pltpu.with_memory_space_constraint(a, where) for a in arrays]


def beside_in_z(plan, a):
    count = plan.gz
    if plan.paired:
        return lax.ppermute(a, "gz", [(0, 1), (1, 0)])
    cut = LANES // 2
    right = lax.ppermute(a[..., :cut], "gz", [(i + 1, i) for i in range(count - 1)])
    left = lax.ppermute(a[..., cut:], "gz", [(i, i + 1) for i in range(count - 1)])
    return jnp.concatenate([right, left], axis=-1)


def shift(plan, a, k):
    pairs = [(plan.device(b), plan.device(b + k)) for b in range(plan.blocks) if 0 <= b + k < plan.blocks]
    return lax.ppermute(a, ("gx", "gy"), pairs)


def shift_apart(plan, a, k):
    pairs = []
    for b in range(plan.blocks):
        for core, to in ((0, b + k), (1, b - k)):
            if 0 <= to < plan.blocks:
                pairs.append((2 * plan.device(b) + core, 2 * plan.device(to) + core))
    return lax.ppermute(a, ("gx", "gy", "gz"), pairs)


def on_device(plan, phase, density, rhs):
    nx, by, rows, px, gx = plan.nx, plan.by, plan.rows, plan.px, plan.gx
    flat = gx * by * 2 * px
    block = (px, plan.ny, LANES)
    outside = pl.BlockSpec(memory_space=pltpu.HBM)
    (parts,) = call(
        functools.partial(prepare_kernel, plan),
        [in_vmem(flat, LANES)],
        [pltpu.VMEM(block, jnp.int32), in_vmem(*block), in_vmem(1, *block), pltpu.SemaphoreType.DMA((3,))],
        in_specs=[outside] * 3,
    )(*pinned(phase, density, rhs, where=pltpu.HBM))
    parts = parts.reshape(gx, by, 2, px, LANES)
    c = lax.all_to_all(parts, "gx", 0, 0, tiled=True)
    lo = shift(plan, c[:, by - HALO :], 1)
    hi = shift(plan, c[:, :HALO], -1)
    zc = beside_in_z(plan, c)
    zh = beside_in_z(plan, jnp.concatenate([lo, hi], axis=0))

    own, own2 = by // 2, by // 4
    size = 5 * (own2 // 2) * (nx // 4)
    side = size + 8 * (nx // 2)

    def level0(n):
        return in_vmem(n, 2, nx, LANES)

    def level1(n):
        return in_vmem(n, 2, nx // 2, LANES)

    outs = [in_vmem(size, LANES)] + [in_vmem(side, LANES)] * (1 if plan.paired else 2)
    fields = [level0(rows)] * 7 + [level1(own + 8)] * 6
    scratch = [level0(rows)] * 3 + [level0(own + 8), level1(own + 8), level1(own2), level1(own + 8)]
    scratch += [in_vmem(2, size, WIDE)]
    down = call(functools.partial(down_kernel, plan), outs + fields, scratch)(*pinned(c, lo, hi, zc, zh))
    pack, nears, fields = down[0], down[1 : len(outs)], down[len(outs) :]

    if plan.paired:
        first = shift_apart(plan, nears[0], 1)
        both = jnp.concatenate([pack, first[:size]], axis=0)
        below = jnp.concatenate([first, shift_apart(plan, both, 2)], axis=0)
        above = lax.ppermute(below, "gz", [(0, 1), (1, 0)])
    else:
        sides = []
        for way, near in ((1, nears[0]), (-1, nears[1])):
            first = shift(plan, near, way)
            both = jnp.concatenate([pack, first[:size]], axis=0)
            sides.append(jnp.concatenate([first, shift(plan, both, 2 * way)], axis=0))
        below, above = sides

    rows2 = (2 * FAR + 1) * own2
    scratch = [in_vmem(2 * FAR + 1, size, LANES)]
    scratch += [in_vmem(rows2 + 1, 2, nx // 4, LANES)] * 9 + [in_vmem(rows2 // 2 + 1, 2, nx // 4, LANES)] * 8
    scratch += [level1(rows2), level0(own + 8)] + [level1(own + 8)] * 3 + [level0(rows)] * 3
    (result,) = call(
        functools.partial(up_kernel, plan), [in_vmem(gx, by, 2, px, LANES)], scratch
    )(*pinned(pack, below, above, *fields))

    here = lax.axis_index("gx")
    arrived = {}
    for k in (3, 1, 2):
        part = lax.dynamic_index_in_dim(result, here ^ k, 0, keepdims=False)
        arrived[k] = lax.ppermute(part, "gx", [(i, i ^ k) for i in range(gx)]).reshape(flat // gx, LANES)
    return call(
        functools.partial(place_kernel, plan),
        [jax.ShapeDtypeStruct((1, px, plan.ny, LANES), F32)] * 2,
    )(*pinned(result.reshape(flat, LANES), arrived[1], arrived[2], arrived[3]))


def solution(mesh):
    sizes = [mesh.shape[a] for a in ("gx", "gy", "gz")]

    def local(phase, density, rhs):
        return tuple(on_device(Plan(sizes, phase.shape), phase, density, rhs))

    in_specs = (P("gx", "gy", "gz"), P("gx", "gy", "gz"), P(None, "gx", "gy", "gz"))
    out_specs = (P(None, "gx", "gy", "gz"), P(None, "gx", "gy", "gz"))
    return jax.shard_map(local, mesh=mesh, in_specs=in_specs, out_specs=out_specs, check_vma=False)
```

```python
import functools

import jax
import jax.numpy as jnp
from jax import lax
from jax.experimental import pallas as pl
from jax.experimental.pallas import tpu as pltpu
from jax.sharding import PartitionSpec as P


DAMPING = 2.0 / 3.0
LANES = 128
WIDE = 256
HALO = 7
FAR = 3
F32 = jnp.float32
VMEM_LIMIT = 24 * 1024 * 1024


class Plan:
    def __init__(self, sizes, shape):
        self.gx, self.gy, self.gz = sizes
        self.px, self.ny, self.nz = shape
        self.nx = self.px * self.gx
        self.by = self.ny // self.gx
        self.blocks = self.gx * self.gy
        self.rows = self.by + 2 * HALO
        self.paired = self.gz == 2
        order = [0, 1, 3, 2] if self.gx == 4 else list(range(self.gx))
        self.place = [order.index(i) for i in range(self.gx)]
        self.order = order

    def device(self, block):
        j, q = divmod(block, self.gx)
        i = self.order[q if j % 2 == 0 else self.gx - 1 - q]
        return i * self.gy + j

    def look_up(self, table, i):
        return sum(jnp.where(i == k, v, 0) for k, v in enumerate(table))

    def start_of(self, i):
        q = self.look_up(self.place, i)
        q = jnp.where(lax.rem(lax.axis_index("gy"), 2) == 0, q, self.gx - 1 - q)
        return pl.multiple_of(q * self.by, self.by)

    def block_here(self):
        q = self.look_up(self.place, lax.axis_index("gx"))
        j = lax.axis_index("gy")
        return j * self.gx + jnp.where(lax.rem(j, 2) == 0, q, self.gx - 1 - q)

    def gx_of(self, block):
        block = jnp.clip(block, 0, self.blocks - 1)
        j, q = lax.div(block, self.gx), lax.rem(block, self.gx)
        return self.look_up(self.order, jnp.where(lax.rem(j, 2) == 0, q, self.gx - 1 - q))

    def is_up(self, block, k, one):
        return lax.rem(lax.div(block, k), 2) == one


def x_up(a, s=1):
    return pltpu.roll(a, a.shape[0] - s, 0)


def x_down(a, s=1):
    return pltpu.roll(a, s, 0)


def z_up(a, g):
    return pltpu.roll(a, a.shape[1] - g, 1)


def z_down(a, g):
    return pltpu.roll(a, g, 1)


def inverse(a):
    r = pl.reciprocal(a, approx=True)
    return r * (2.0 - a * r)


def each(first, last, step, body):
    count = last + 1 - first
    if count <= 2 * step:
        for i in range(first, last + 1):
            body(i)
        return

    def go(c, _):
        for k in range(step):
            body(first + c * step + k)
        return 0

    lax.fori_loop(0, count // step, go, 0)
    for i in range(first + count // step * step, last + 1):
        body(i)


def wave(*stages):
    start = min(first + delay for _, first, _, delay in stages)
    end = max(last + delay for _, _, last, delay in stages)
    full = max(first + delay for _, first, _, delay in stages)
    full_end = min(last + delay for _, _, last, delay in stages)

    def step(t):
        for body, first, last, delay in stages:
            if first <= t - delay <= last:
                body(t - delay)

    def all_of_them(t, _):
        for body, _, _, delay in stages:
            body(t - delay)
        return 0

    if full_end - full < 3:
        full = full_end = end + 1
    for t in range(start, min(full, end + 1)):
        step(t)
    if full <= end:
        lax.fori_loop(full, full_end + 1, all_of_them, 0)
        for t in range(full_end + 1, end + 1):
            step(t)


class Wide:
    def __init__(self, ref):
        self.ref = ref

    def __getitem__(self, key):
        r, xs = key if isinstance(key, tuple) else (key, slice(None))
        return jnp.concatenate([self.ref[r, 0, xs, :], self.ref[r, 1, xs, :]], axis=1)

    def __setitem__(self, key, value):
        r, xs = key if isinstance(key, tuple) else (key, slice(None))
        self.ref[r, 0, xs, :] = value[:, :LANES]
        self.ref[r, 1, xs, :] = value[:, LANES:]


class Level:
    def __init__(self, s, g, kx, ky, kz, d, w, f, step=2):
        self.s, self.g, self.step = s, g, step
        self.kx, self.ky, self.kz, self.d, self.w, self.f = kx, ky, kz, d, w, f

    def beside(self, u, r):
        here = u[r]
        kx, kz = self.kx[r], self.kz[r]
        a = kx * x_up(here, self.s) + x_down(kx * here, self.s)
        b = kz * z_up(here, self.g) + z_down(kz * here, self.g)
        return a + b + (self.ky[r + 1] * u[r + 1] + self.ky[r] * u[r - 1])

    def weigh(self, first, last):
        def body(r):
            self.w[r] = DAMPING * inverse(self.d[r])

        each(first, last, self.step, body)

    def first(self, u, first, last):
        def body(r):
            u[r] = self.w[r] * self.f[r]

        each(first, last, self.step, body)

    def swept(self, u, r):
        return (1.0 / 3.0) * u[r] + self.w[r] * (self.f[r] + self.beside(u, r))

    def sweep(self, u, v, first, last):
        def body(r):
            v[r] = self.swept(u, r)

        each(first, last, self.step, body)

    def residual(self, u, r):
        return self.f[r] + self.beside(u, r) - self.d[r] * u[r]

    def residual_pairs(self, u, out, first, count):
        def body(j):
            out[j] = self.residual(u, first + 2 * j) + self.residual(u, first + 2 * j + 1)

        each(0, count - 1, self.step // 2, body)


def z_pairs(low, g):
    return lambda a: a + jnp.where(low, z_up(a, g), z_down(a, g))


def coarse_coefficients(level, r, x_count):
    even, odd = pl.ds(0, x_count, stride=2), pl.ds(1, x_count, stride=2)
    g = level.g
    low = (lax.broadcasted_iota(jnp.int32, (x_count, WIDE), 1) & g) == 0
    z_pair = z_pairs(low, g)

    def all_x(ref, row):
        return ref[row, even] + ref[row, odd]

    kx = level.kx[r, odd] + level.kx[r + 1, odd]
    inner = level.kx[r, even] + level.kx[r + 1, even] + all_x(level.ky, r + 1)
    kz = all_x(level.kz, r) + all_x(level.kz, r + 1)
    d = all_x(level.d, r) + all_x(level.d, r + 1)
    d = d - 2.0 * (inner + jnp.where(low, kz, 0.0))
    return z_pair(kx), coarse_sum(level.ky, r + 2, x_count, g), jnp.where(low, z_up(kz, g), kz), z_pair(d)


def coarse_sum(ref, r, x_count, g):
    even, odd = pl.ds(0, x_count, stride=2), pl.ds(1, x_count, stride=2)
    low = (lax.broadcasted_iota(jnp.int32, (x_count, WIDE), 1) & g) == 0
    return z_pairs(low, g)(ref[r, even] + ref[r, odd])


def correct(u, v, e, t, x_count, first, last, to):
    def body(j):
        part = e[j]
        t[j, pl.ds(0, x_count, stride=2)] = part
        t[j, pl.ds(1, x_count, stride=2)] = part
        wide = t[j]
        r = to + 2 * (j - first)
        v[r] = u[r] + wide
        v[r + 1] = u[r + 1] + wide

    each(first, last, 2, body)


def pick_lanes(a, lanes):
    return jnp.take_along_axis(a, lanes, axis=1, mode="promise_in_bounds")


def prepare_kernel(plan, phase_in, density_in, rhs_in, *refs):
    outs, (phase, density, rhs, sems) = refs[: plan.gx], refs[plan.gx :]
    pairs = ((phase_in, phase), (density_in, density), (rhs_in, rhs))
    copies = [pltpu.make_async_copy(a, b, sems.at[k]) for k, (a, b) in enumerate(pairs)]
    for copy in copies:
        copy.start()
    for copy in copies:
        copy.wait()
    here = lax.axis_index("gx")
    by, px = plan.by, plan.px
    for k, out in enumerate(outs):
        rows = pl.ds(plan.start_of(here ^ k), by)
        for p in range(px):
            half = jnp.where(phase[p, rows, :] == 1, 500.0, 0.5).astype(F32)
            out[pl.ds(p, by, stride=2 * px), :] = half * density[p, rows, :]
            out[pl.ds(px + p, by, stride=2 * px), :] = rhs[0, p, rows, :]


def gather_kernel(plan, *refs):
    parts, (c, *sets) = refs[: plan.gx], refs[plan.gx :]
    block = plan.block_here()
    for k, part in enumerate(parts):
        c[k] = part[...]
        for one, out in enumerate(sets):
            first = jnp.where(plan.is_up(block, 1, one), plan.by - HALO, 0)
            out[k] = part[pl.ds(first, HALO)]


def down_kernel(plan, c, zc, sides, zsides, *refs):
    near_count = 1 if plan.paired else 2
    pack, nears, refs = refs[0], refs[1 : 1 + near_count], refs[1 + near_count :]
    kx0, ky0, kz0, d0, w0, f0, ub, kx1, ky1, kz1, w1, f1, u1 = [Wide(r) for r in refs[:13]]
    h0, ua, face, r0, uc, r1, d1 = [Wide(r) for r in refs[13:20]]
    stage = refs[20]
    nx, by, rows, gx, px = plan.nx, plan.by, plan.rows, plan.gx, plan.px
    shape = (nx, WIDE)
    block, here = plan.block_here(), lax.axis_index("gx")
    base = block * by - HALO
    y_count, z_count = plan.by * plan.blocks, plan.nz * plan.gz

    x = lax.broadcasted_iota(jnp.int32, shape, 0)
    lane = lax.broadcasted_iota(jnp.int32, shape, 1)
    core = lax.axis_index("gz")
    if plan.paired:
        z = lax.rem(core * LANES + lane, WIDE)
    else:
        z = core * LANES + jnp.where(lane < LANES + LANES // 2, lane, lane - WIDE)
    x_top, x_bottom = x == nx - 1, x == 0
    z_top, z_bottom = z == z_count - 1, z == 0
    z_shut = (z < 0) | (z >= z_count - 1)
    z_out = (z < 0) | (z >= z_count)

    def take(a, b, at, other, r, to):
        y = base + to
        inside = (y >= 0) & (y < y_count)
        for k in range(gx):
            xs = pl.ds(pl.multiple_of((other ^ k) * px, px), px)
            for s, ref in enumerate((a, b)):
                h = jnp.where(inside, ref[at + k, r, 0], 0.5)
                if not plan.paired:
                    h = jnp.where(z_out[:px, s * LANES : (s + 1) * LANES], 0.5, h)
                h0.ref[to, s, xs, :] = h
                f0.ref[to, s, xs, :] = ref[at + k, r, 1]

    each(0, by - 1, 4, lambda r: take(c, zc, 0, here, r, r + HALO))
    up_first = plan.is_up(block, 1, 0)
    below, above = jnp.where(up_first, gx, 0), jnp.where(up_first, 0, gx)
    gx_below, gx_above = plan.gx_of(block - 1), plan.gx_of(block + 1)
    each(0, HALO - 1, 4, lambda r: take(sides, zsides, below, gx_below, r, r))
    each(0, HALO - 1, 4, lambda r: take(sides, zsides, above, gx_above, r, r + HALO + by))

    @pl.when(block == 0)
    def _():
        h0[HALO - 1] = h0[HALO]

    @pl.when(block == plan.blocks - 1)
    def _():
        h0[HALO + by] = h0[HALO + by - 1]

    def is_open(r):
        y = base + r
        return (y >= 0) & (y < y_count - 1)

    first_face = inverse(h0[0] + h0[1])
    face[1] = first_face
    ky0[1] = jnp.where(is_open(0), first_face, 0.0)

    def faces(j):
        yd = face[2 * j - 1]
        for r in (2 * j - 1, 2 * j):
            h = h0[r]
            alone = 0.5 * inverse(h)
            xu = inverse(h + jnp.where(x_top, h, x_up(h)))
            xd = jnp.where(x_bottom, alone, x_down(xu))
            yu = inverse(h + h0[r + 1])
            zu = inverse(h + jnp.where(z_top, h, z_up(h, 1)))
            zd = jnp.where(z_bottom, alone, z_down(zu, 1))
            d = xu + xd + yu + yd + zu + zd
            w = DAMPING * inverse(d)
            kx0[r] = jnp.where(x_top, 0.0, xu)
            ky0[r + 1] = jnp.where(is_open(r), yu, 0.0)
            kz0[r] = jnp.where(z_shut, 0.0, zu)
            d0[r], w0[r] = d, w
            ua[r] = w * f0[r]
            yd = yu
        face[2 * j + 1] = yd

    fine = Level(1, 1, kx0, ky0, kz0, d0, w0, f0)

    own = by // 2
    half_x = nx // 2
    middle = Level(1, 2, kx1, ky1, kz1, d1, w1, f1, 8)
    def coarsen(j):
        kx1[j], ky1[j + 1], kz1[j], d1[j] = coarse_coefficients(fine, 2 * j - 1, half_x)

    def restrict(j):
        f1[j] = coarse_sum(r0, j, half_x, 1)

    def sweep(j):
        ub[2 * j] = fine.swept(ua, 2 * j)
        ub[2 * j + 1] = fine.swept(ua, 2 * j + 1)

    def residual(j):
        r0[j] = fine.residual(ub, 2 * j - 1) + fine.residual(ub, 2 * j)

    wave(
        (restrict, 2, own + 5, 4),
        (residual, 2, own + 5, 3),
        (sweep, 1, own + 5, 2),
        (coarsen, 1, own + 6, 1),
        (faces, 1, own + 6, 0),
    )
    ky1[1] = coarse_sum(ky0, 1, half_x, 1)
    middle.weigh(1, own + 6)
    middle.first(uc, 2, own + 5)
    middle.sweep(uc, u1, 3, own + 4)
    middle.residual_pairs(u1, r1, 4, own // 2)

    quarter_x = nx // 4
    own2 = own // 2
    part = own2 // 2
    for j in range(own2):
        fields = (coarse_sum(r1, j, quarter_x, 2),) + coarse_coefficients(middle, 4 + 2 * j, quarter_x)
        for t, a in enumerate(fields):
            stage[j // part, pl.ds((t * part + j % part) * quarter_x, quarter_x), :] = a
    cell = lax.broadcasted_iota(jnp.int32, pack.shape, 1)
    lanes = lax.rem(4 * cell, LANES)
    quarter = lax.div(4 * cell, LANES)
    total = pick_lanes(stage[0, :, :LANES], lanes)
    for k in range(1, 4):
        half = slice((k % 2) * LANES, (k % 2 + 1) * LANES)
        total = jnp.where(quarter == k, pick_lanes(stage[k // 2, :, half], lanes), total)
    pack[...] = total

    size = pack.shape[0]

    def near(out, first):
        out[pl.ds(0, size), :] = total
        for k, (ref, r) in enumerate(((u1, first), (u1, first + 1), (u1, first + 2), (f1, first + 1))):
            for s in range(2):
                out[pl.ds(size + (2 * k + s) * half_x, half_x), :] = ref.ref[r, s]

    for one, out in enumerate(nears):
        near(out, jnp.where(plan.is_up(block, 1, core if plan.paired else one), own, 5))


def up_kernel(plan, pack, mine, theirs, *refs):
    refs, out, scratch = refs[:13], refs[13], refs[14:]
    kx0, ky0, kz0, d0, w0, f0, u0, kx1, ky1, kz1, w1, f1_in, u1_in = [Wide(r) for r in refs]
    stage = scratch[0]
    wide = [Wide(r) for r in scratch[1:]]
    f2, kx2, ky2, kz2, d2, w2, ua2, ub2, r2 = wide[:9]
    f3, kx3, ky3, kz3, d3, w3, ua3, ub3 = wide[9:17]
    t1, t0, f1, ua1, ub1, ua0, ub0, uc0 = wide[17:]
    nx, by = plan.nx, plan.by
    own, own2 = by // 2, by // 4
    part = own2 // 2
    half_x, quarter_x = nx // 2, nx // 4
    size = pack.shape[0]
    side = size + 8 * half_x
    core = lax.axis_index("gz")
    block = plan.block_here()
    here = lax.axis_index("gx")
    turn = 1 if plan.paired else 0

    for r in range(2, own + 6):
        f1[r] = f1_in[r]
    for r in range(3, own + 5):
        ua1[r] = u1_in[r]

    ups = {k: plan.is_up(block, k, core if plan.paired else 0) for k in range(1, FAR + 1)}
    stage[FAR] = pack[...]
    for k, up in ups.items():
        at = 0 if k == 1 else side + (k - 2) * size
        stage[jnp.where(up, FAR + k, FAR - k)] = mine[pl.ds(at, size), :]
        stage[jnp.where(up, FAR - k, FAR + k)] = theirs[pl.ds(at, size), :]
    for ref, up, half_turn in ((mine, ups[1], 0), (theirs, jnp.logical_not(ups[1]), turn)):
        row = jnp.where(up, own + 5, 0)
        for k, (to, r) in enumerate(((ua1, row), (ua1, row + 1), (ua1, row + 2), (f1, row + 1))):
            for s in range(2):
                to.ref[r, s ^ half_turn] = ref[pl.ds(size + (2 * k + s) * half_x, half_x), :]

    lane = lax.broadcasted_iota(jnp.int32, (size, LANES), 1)
    lanes = [lax.div(lane, 4) + k * (LANES // 4) for k in range(4)]

    def expand(k):
        there = block + k - FAR
        exists = (there >= 0) & (there < plan.blocks)
        swapped = 0
        if plan.paired and k != FAR:
            swapped = jnp.where(ups[abs(k - FAR)] == (k > FAR), 0, 1)
        rows = stage[k]
        for quarter in range(4):
            part_of, half = divmod(quarter, 2)
            a = pick_lanes(rows, lanes[quarter])
            for t, ref in enumerate((f2, kx2, ky2, kz2, d2)):
                for j in range(part):
                    at = (t * part + j) * quarter_x
                    b = a[at : at + quarter_x]
                    if t == 4:
                        b = jnp.where(exists, b, 1.0)
                    r = k * own2 + part_of * part + j + (1 if t == 2 else 0)
                    ref.ref[r, swapped if half == 0 else 1 - swapped] = b

    for k in range(2 * FAR + 1):
        expand(k)

    rows2 = (2 * FAR + 1) * own2
    two = Level(1, 4, kx2, ky2, kz2, d2, w2, f2, 14)
    two.weigh(0, rows2 - 1)
    two.first(ua2, 0, rows2 - 1)
    two.sweep(ua2, ub2, 1, rows2 - 2)
    two.residual_pairs(ub2, r2, 2, rows2 // 2 - 2)

    x = lax.broadcasted_iota(jnp.int32, (quarter_x, WIDE), 0)
    even_x = (x & 1) == 0
    low = (lax.broadcasted_iota(jnp.int32, (quarter_x, WIDE), 1) & 4) == 0
    z_pair = z_pairs(low, 4)

    def x_pair(a):
        return a + jnp.where(even_x, x_up(a), x_down(a))

    last3 = rows2 // 2 - 2

    def coarsen(j):
        r = 2 * j
        kx = kx2[r] + kx2[r + 1]
        kz = kz2[r] + kz2[r + 1]
        inner = ky2[r + 1] + jnp.where(even_x, kx, 0.0) + jnp.where(low, kz, 0.0)
        f3[j] = z_pair(x_pair(r2[j - 1]))
        kx3[j] = z_pair(jnp.where(even_x, x_up(kx), kx))
        ky3[j + 1] = z_pair(x_pair(ky2[r + 2]))
        kz = x_pair(kz)
        kz3[j] = jnp.where(low, z_up(kz, 4), kz)
        d3[j] = z_pair(x_pair(d2[r] + d2[r + 1] - 2.0 * inner))

    each(1, last3, 6, coarsen)
    three = Level(2, 8, kx3, ky3, kz3, d3, w3, f3, 16)
    three.weigh(1, last3)
    three.first(ua3, 1, last3)
    three.sweep(ua3, ub3, 2, last3 - 1)
    three.sweep(ub3, ua3, 3, last3 - 2)
    three.sweep(ua3, ub3, 4, last3 - 3)

    first2 = FAR * own2
    for j in range(4, last3 - 2):
        e = ub3[j]
        ua2[2 * j] = ub2[2 * j] + e
        ua2[2 * j + 1] = ub2[2 * j + 1] + e
    two.sweep(ua2, ub2, first2 - 3, first2 + own2 + 2)
    two.sweep(ub2, ua2, first2 - 2, first2 + own2 + 1)

    one = Level(1, 2, kx1, ky1, kz1, None, w1, f1, 8)
    correct(ua1, ub1, ua2, t1, quarter_x, first2 - 2, first2 + own2 + 1, 0)
    one.sweep(ub1, ua1, 1, own + 6)
    one.sweep(ua1, ub1, 2, own + 5)

    finest = Level(1, 1, kx0, ky0, kz0, d0, w0, f0)

    def corrected(j):
        part = ub1[j]
        t0[j, pl.ds(0, half_x, stride=2)] = part
        t0[j, pl.ds(1, half_x, stride=2)] = part
        both = t0[j]
        ua0[2 * j - 1] = u0[2 * j - 1] + both
        ua0[2 * j] = u0[2 * j] + both

    def sweep(j):
        ub0[2 * j - 1] = finest.swept(ua0, 2 * j - 1)
        ub0[2 * j] = finest.swept(ua0, 2 * j)

    def sweep_again(j):
        uc0[2 * j] = finest.swept(ub0, 2 * j)
        uc0[2 * j + 1] = finest.swept(ub0, 2 * j + 1)

    def finish(j):
        for r in (2 * j - 1, 2 * j):
            scaled = d0[r] * uc0[r]
            rest = f0[r] + finest.beside(uc0, r) - scaled
            for s in range(plan.gx):
                part = slice(s * plan.px, (s + 1) * plan.px)
                out[s ^ here, r - HALO, 0] = scaled[part, :LANES]
                out[s ^ here, r - HALO, 1] = rest[part, :LANES]

    wave(
        (finish, 4, own + 3, 5),
        (sweep_again, 3, own + 3, 4),
        (sweep, 3, own + 4, 2),
        (corrected, 2, own + 5, 0),
    )


def place_kernel(plan, *refs):
    parts, (scaled, residual) = refs[: plan.gx], refs[plan.gx :]
    here = lax.axis_index("gx")
    by, px = plan.by, plan.px
    for k, part in enumerate(parts):
        rows = pl.ds(plan.start_of(here ^ k), by)
        for p in range(px):
            scaled[0, p, rows, :] = part[pl.ds(p, by, stride=2 * px), :]
            residual[0, p, rows, :] = part[pl.ds(px + p, by, stride=2 * px), :]


def in_vmem(*shape):
    return pltpu.VMEM(shape, F32)


def call(kernel, out_shape, scratch=(), **more):
    return pl.pallas_call(
        kernel,
        out_shape=out_shape,
        scratch_shapes=list(scratch),
        compiler_params=pltpu.CompilerParams(vmem_limit_bytes=VMEM_LIMIT),
        **more,
    )


def pinned(*arrays, where=pltpu.VMEM):
    return [pltpu.with_memory_space_constraint(a, where) for a in arrays]


def beside_in_z(plan, a):
    count = plan.gz
    if plan.paired:
        return lax.ppermute(a, "gz", [(0, 1), (1, 0)])
    cut = LANES // 2
    right = lax.ppermute(a[..., :cut], "gz", [(i + 1, i) for i in range(count - 1)])
    left = lax.ppermute(a[..., cut:], "gz", [(i, i + 1) for i in range(count - 1)])
    return jnp.concatenate([right, left], axis=-1)


def exchange(plan, parts):
    got = [parts[0]] * plan.gx
    for k in range(plan.gx - 1, 0, -1):
        got[k] = lax.ppermute(parts[k], "gx", [(i, i ^ k) for i in range(plan.gx)])
    return got


def pairs_of(plan, k, one):
    low = [b for b in range(plan.blocks - k) if b // k % 2 == one]
    pairs = [(plan.device(b), plan.device(b + k)) for b in low]
    return pairs + [(b, a) for a, b in pairs]


def swap_blocks(plan, a, k, one):
    return lax.ppermute(a, ("gx", "gy"), pairs_of(plan, k, one))


def swap_blocks_apart(plan, a, k):
    pairs = [(2 * p + one, 2 * q + one) for one in range(2) for p, q in pairs_of(plan, k, one)]
    return lax.ppermute(a, ("gx", "gy", "gz"), pairs)


def far_blocks(plan, pack, nears):
    def line(move, near):
        parts = [move(pack, k) for k in range(FAR, 1, -1)] + [move(near, 1)]
        return jnp.concatenate(parts[::-1], axis=0)

    if plan.paired:
        mine = line(functools.partial(swap_blocks_apart, plan), nears[0])
        return mine, beside_in_z(plan, mine)
    return [line(functools.partial(swap_blocks, plan, one=one), nears[one]) for one in range(2)]


def on_device(plan, phase, density, rhs):
    nx, by, rows, px, gx = plan.nx, plan.by, plan.rows, plan.px, plan.gx
    flat = by * 2 * px
    block = (px, plan.ny, LANES)
    outside = pl.BlockSpec(memory_space=pltpu.HBM)
    parts = call(
        functools.partial(prepare_kernel, plan),
        [in_vmem(flat, LANES)] * gx,
        [pltpu.VMEM(block, jnp.int32), in_vmem(*block), in_vmem(1, *block), pltpu.SemaphoreType.DMA((3,))],
        in_specs=[outside] * 3,
    )(*pinned(phase, density, rhs, where=pltpu.HBM))
    parts = [a.reshape(by, 2, px, LANES) for a in exchange(plan, parts)]
    c, *sets = call(
        functools.partial(gather_kernel, plan),
        [in_vmem(gx, by, 2, px, LANES)] + [in_vmem(gx, HALO, 2, px, LANES)] * 2,
    )(*pinned(*parts))
    sides = jnp.concatenate([swap_blocks(plan, a, 1, one) for one, a in enumerate(sets)], axis=0)
    zc = beside_in_z(plan, c)
    zsides = beside_in_z(plan, sides)

    own, own2 = by // 2, by // 4
    size = 5 * (own2 // 2) * (nx // 4)
    side = size + 8 * (nx // 2)

    def level0(n):
        return in_vmem(n, 2, nx, LANES)

    def level1(n):
        return in_vmem(n, 2, nx // 2, LANES)

    outs = [in_vmem(size, LANES)] + [in_vmem(side, LANES)] * (1 if plan.paired else 2)
    fields = [level0(rows)] * 7 + [level1(own + 8)] * 6
    scratch = [level0(rows)] * 3 + [level0(own + 8), level1(own + 8), level1(own2), level1(own + 8)]
    scratch += [in_vmem(2, size, WIDE)]
    down = call(functools.partial(down_kernel, plan), outs + fields, scratch)(*pinned(c, zc, sides, zsides))
    pack, nears, fields = down[0], down[1 : len(outs)], down[len(outs) :]

    mine, theirs = far_blocks(plan, pack, nears)
    rows2 = (2 * FAR + 1) * own2
    scratch = [in_vmem(2 * FAR + 1, size, LANES)]
    scratch += [in_vmem(rows2 + 1, 2, nx // 4, LANES)] * 9 + [in_vmem(rows2 // 2 + 1, 2, nx // 4, LANES)] * 8
    scratch += [level1(rows2), level0(own + 8)] + [level1(own + 8)] * 3 + [level0(rows)] * 3
    (result,) = call(
        functools.partial(up_kernel, plan), [in_vmem(gx, by, 2, px, LANES)], scratch
    )(*pinned(pack, mine, theirs, *fields))

    parts = exchange(plan, [result[k].reshape(flat, LANES) for k in range(gx)])
    return call(
        functools.partial(place_kernel, plan),
        [jax.ShapeDtypeStruct((1, px, plan.ny, LANES), F32)] * 2,
    )(*pinned(*parts))


def solution(mesh):
    sizes = [mesh.shape[a] for a in ("gx", "gy", "gz")]

    def local(phase, density, rhs):
        return tuple(on_device(Plan(sizes, phase.shape), phase, density, rhs))

    in_specs = (P("gx", "gy", "gz"), P("gx", "gy", "gz"), P(None, "gx", "gy", "gz"))
    out_specs = (P(None, "gx", "gy", "gz"), P(None, "gx", "gy", "gz"))
    return jax.shard_map(local, mesh=mesh, in_specs=in_specs, out_specs=out_specs, check_vma=False)
```

```python
import functools

import jax
import jax.numpy as jnp
from jax import lax
from jax.experimental import pallas as pl
from jax.experimental.pallas import tpu as pltpu
from jax.sharding import PartitionSpec as P


DAMPING = 2.0 / 3.0
LANES = 128
WIDE = 256
HALO = 7
FAR = 3
F32 = jnp.float32
VMEM_LIMIT = 24 * 1024 * 1024


class Plan:
    def __init__(self, sizes, shape):
        self.gx, self.gy, self.gz = sizes
        self.px, self.ny, self.nz = shape
        self.nx = self.px * self.gx
        self.by = self.ny // self.gx
        self.blocks = self.gx * self.gy
        self.rows = self.by + 2 * HALO
        self.paired = self.gz == 2
        order = [0, 1, 3, 2] if self.gx == 4 else list(range(self.gx))
        self.place = [order.index(i) for i in range(self.gx)]
        self.order = order

    def device(self, block):
        j, q = divmod(block, self.gx)
        i = self.order[q if j % 2 == 0 else self.gx - 1 - q]
        return i * self.gy + j

    def look_up(self, table, i):
        return sum(jnp.where(i == k, v, 0) for k, v in enumerate(table))

    def start_of(self, i):
        q = self.look_up(self.place, i)
        q = jnp.where(lax.rem(lax.axis_index("gy"), 2) == 0, q, self.gx - 1 - q)
        return pl.multiple_of(q * self.by, self.by)

    def block_here(self):
        q = self.look_up(self.place, lax.axis_index("gx"))
        j = lax.axis_index("gy")
        return j * self.gx + jnp.where(lax.rem(j, 2) == 0, q, self.gx - 1 - q)

    def gx_of(self, block):
        block = jnp.clip(block, 0, self.blocks - 1)
        j, q = lax.div(block, self.gx), lax.rem(block, self.gx)
        return self.look_up(self.order, jnp.where(lax.rem(j, 2) == 0, q, self.gx - 1 - q))

    def is_up(self, block, k, one):
        return lax.rem(lax.div(block, k), 2) == one


def x_up(a, s=1):
    return pltpu.roll(a, a.shape[0] - s, 0)


def x_down(a, s=1):
    return pltpu.roll(a, s, 0)


def z_up(a, g):
    return pltpu.roll(a, a.shape[1] - g, 1)


def z_down(a, g):
    return pltpu.roll(a, g, 1)


def inverse(a):
    r = pl.reciprocal(a, approx=True)
    return r * (2.0 - a * r)


def each(first, last, step, body):
    count = last + 1 - first
    if count <= 2 * step:
        for i in range(first, last + 1):
            body(i)
        return

    def go(c, _):
        for k in range(step):
            body(first + c * step + k)
        return 0

    lax.fori_loop(0, count // step, go, 0)
    for i in range(first + count // step * step, last + 1):
        body(i)


def wave(*stages):
    start = min(first + delay for _, first, _, delay in stages)
    end = max(last + delay for _, _, last, delay in stages)
    full = max(first + delay for _, first, _, delay in stages)
    full_end = min(last + delay for _, _, last, delay in stages)

    def step(t):
        for body, first, last, delay in stages:
            if first <= t - delay <= last:
                body(t - delay)

    def all_of_them(t, _):
        for body, _, _, delay in stages:
            body(t - delay)
        return 0

    if full_end - full < 3:
        full = full_end = end + 1
    for t in range(start, min(full, end + 1)):
        step(t)
    if full <= end:
        lax.fori_loop(full, full_end + 1, all_of_them, 0)
        for t in range(full_end + 1, end + 1):
            step(t)


class Wide:
    def __init__(self, ref):
        self.ref = ref

    def __getitem__(self, key):
        r, xs = key if isinstance(key, tuple) else (key, slice(None))
        return jnp.concatenate([self.ref[r, 0, xs, :], self.ref[r, 1, xs, :]], axis=1)

    def __setitem__(self, key, value):
        r, xs = key if isinstance(key, tuple) else (key, slice(None))
        self.ref[r, 0, xs, :] = value[:, :LANES]
        self.ref[r, 1, xs, :] = value[:, LANES:]


class Level:
    def __init__(self, s, g, kx, ky, kz, d, w, f, step=2):
        self.s, self.g, self.step = s, g, step
        self.kx, self.ky, self.kz, self.d, self.w, self.f = kx, ky, kz, d, w, f

    def beside(self, u, r):
        here = u[r]
        kx, kz = self.kx[r], self.kz[r]
        a = kx * x_up(here, self.s) + x_down(kx * here, self.s)
        b = kz * z_up(here, self.g) + z_down(kz * here, self.g)
        return a + b + (self.ky[r + 1] * u[r + 1] + self.ky[r] * u[r - 1])

    def weigh(self, first, last):
        def body(r):
            self.w[r] = DAMPING * inverse(self.d[r])

        each(first, last, self.step, body)

    def first(self, u, first, last):
        def body(r):
            u[r] = self.w[r] * self.f[r]

        each(first, last, self.step, body)

    def swept(self, u, r):
        return (1.0 / 3.0) * u[r] + self.w[r] * (self.f[r] + self.beside(u, r))

    def sweep(self, u, v, first, last):
        def body(r):
            v[r] = self.swept(u, r)

        each(first, last, self.step, body)

    def residual(self, u, r):
        return self.f[r] + self.beside(u, r) - self.d[r] * u[r]

    def residual_pairs(self, u, out, first, count):
        def body(j):
            out[j] = self.residual(u, first + 2 * j) + self.residual(u, first + 2 * j + 1)

        each(0, count - 1, self.step // 2, body)


def z_pairs(low, g):
    return lambda a: a + jnp.where(low, z_up(a, g), z_down(a, g))


def coarse_coefficients(level, r, x_count):
    even, odd = pl.ds(0, x_count, stride=2), pl.ds(1, x_count, stride=2)
    g = level.g
    low = (lax.broadcasted_iota(jnp.int32, (x_count, WIDE), 1) & g) == 0
    z_pair = z_pairs(low, g)

    def all_x(ref, row):
        return ref[row, even] + ref[row, odd]

    kx = level.kx[r, odd] + level.kx[r + 1, odd]
    inner = level.kx[r, even] + level.kx[r + 1, even] + all_x(level.ky, r + 1)
    kz = all_x(level.kz, r) + all_x(level.kz, r + 1)
    d = all_x(level.d, r) + all_x(level.d, r + 1)
    d = d - 2.0 * (inner + jnp.where(low, kz, 0.0))
    return z_pair(kx), coarse_sum(level.ky, r + 2, x_count, g), jnp.where(low, z_up(kz, g), kz), z_pair(d)


def coarse_sum(ref, r, x_count, g):
    even, odd = pl.ds(0, x_count, stride=2), pl.ds(1, x_count, stride=2)
    low = (lax.broadcasted_iota(jnp.int32, (x_count, WIDE), 1) & g) == 0
    return z_pairs(low, g)(ref[r, even] + ref[r, odd])


def correct(u, v, e, t, x_count, first, last, to):
    def body(j):
        part = e[j]
        t[j, pl.ds(0, x_count, stride=2)] = part
        t[j, pl.ds(1, x_count, stride=2)] = part
        wide = t[j]
        r = to + 2 * (j - first)
        v[r] = u[r] + wide
        v[r + 1] = u[r + 1] + wide

    each(first, last, 2, body)


def pick_lanes(a, lanes):
    return jnp.take_along_axis(a, lanes, axis=1, mode="promise_in_bounds")


def prepare_kernel(plan, phase_in, density_in, rhs_in, *refs):
    outs, (phase, density, rhs, sems) = refs[: plan.gx], refs[plan.gx :]
    pairs = ((phase_in, phase), (density_in, density), (rhs_in, rhs))
    copies = [pltpu.make_async_copy(a, b, sems.at[k]) for k, (a, b) in enumerate(pairs)]
    for copy in copies:
        copy.start()
    for copy in copies:
        copy.wait()
    here = lax.axis_index("gx")
    by, px = plan.by, plan.px
    for k, out in enumerate(outs):
        rows = pl.ds(plan.start_of(here ^ k), by)
        for p in range(px):
            half = jnp.where(phase[p, rows, :] == 1, 500.0, 0.5).astype(F32)
            out[pl.ds(p, by, stride=2 * px), :] = half * density[p, rows, :]
            out[pl.ds(px + p, by, stride=2 * px), :] = rhs[0, p, rows, :]


def gather_kernel(plan, *refs):
    parts, (c, *sets) = refs[: plan.gx], refs[plan.gx :]
    block = plan.block_here()
    for k, part in enumerate(parts):
        c[k] = part[...]
        for one, out in enumerate(sets):
            first = jnp.where(plan.is_up(block, 1, one), plan.by - HALO, 0)
            out[k] = part[pl.ds(first, HALO)]


def down_kernel(plan, c, zc, sides, zsides, *refs):
    near_count = 1 if plan.paired else 2
    pack, nears, refs = refs[0], refs[1 : 1 + near_count], refs[1 + near_count :]
    kx0, ky0, kz0, d0, w0, f0, ub, kx1, ky1, kz1, w1, f1, u1 = [Wide(r) for r in refs[:13]]
    h0, ua, face, r0, uc, r1, d1 = [Wide(r) for r in refs[13:20]]
    stage = refs[20]
    nx, by, rows, gx, px = plan.nx, plan.by, plan.rows, plan.gx, plan.px
    shape = (nx, WIDE)
    block, here = plan.block_here(), lax.axis_index("gx")
    base = block * by - HALO
    y_count, z_count = plan.by * plan.blocks, plan.nz * plan.gz

    x = lax.broadcasted_iota(jnp.int32, shape, 0)
    lane = lax.broadcasted_iota(jnp.int32, shape, 1)
    core = lax.axis_index("gz")
    if plan.paired:
        z = lax.rem(core * LANES + lane, WIDE)
    else:
        z = core * LANES + jnp.where(lane < LANES + LANES // 2, lane, lane - WIDE)
    x_top, x_bottom = x == nx - 1, x == 0
    z_top, z_bottom = z == z_count - 1, z == 0
    z_shut = (z < 0) | (z >= z_count - 1)
    z_out = (z < 0) | (z >= z_count)

    def take(a, b, at, other, r, to):
        y = base + to
        inside = (y >= 0) & (y < y_count)
        for k in range(gx):
            xs = pl.ds(pl.multiple_of((other ^ k) * px, px), px)
            for s, ref in enumerate((a, b)):
                h = jnp.where(inside, ref[at + k, r, 0], 0.5)
                if not plan.paired:
                    h = jnp.where(z_out[:px, s * LANES : (s + 1) * LANES], 0.5, h)
                h0.ref[to, s, xs, :] = h
                f0.ref[to, s, xs, :] = ref[at + k, r, 1]

    each(0, by - 1, 4, lambda r: take(c, zc, 0, here, r, r + HALO))
    up_first = plan.is_up(block, 1, 0)
    below, above = jnp.where(up_first, gx, 0), jnp.where(up_first, 0, gx)
    gx_below, gx_above = plan.gx_of(block - 1), plan.gx_of(block + 1)
    each(0, HALO - 1, 4, lambda r: take(sides, zsides, below, gx_below, r, r))
    each(0, HALO - 1, 4, lambda r: take(sides, zsides, above, gx_above, r, r + HALO + by))

    @pl.when(block == 0)
    def _():
        h0[HALO - 1] = h0[HALO]

    @pl.when(block == plan.blocks - 1)
    def _():
        h0[HALO + by] = h0[HALO + by - 1]

    def is_open(r):
        y = base + r
        return (y >= 0) & (y < y_count - 1)

    first_face = inverse(h0[0] + h0[1])
    face[1] = first_face
    ky0[1] = jnp.where(is_open(0), first_face, 0.0)

    def faces(j):
        yd = face[2 * j - 1]
        for r in (2 * j - 1, 2 * j):
            h = h0[r]
            alone = 0.5 * inverse(h)
            xu = inverse(h + jnp.where(x_top, h, x_up(h)))
            xd = jnp.where(x_bottom, alone, x_down(xu))
            yu = inverse(h + h0[r + 1])
            zu = inverse(h + jnp.where(z_top, h, z_up(h, 1)))
            zd = jnp.where(z_bottom, alone, z_down(zu, 1))
            d = xu + xd + yu + yd + zu + zd
            w = DAMPING * inverse(d)
            kx0[r] = jnp.where(x_top, 0.0, xu)
            ky0[r + 1] = jnp.where(is_open(r), yu, 0.0)
            kz0[r] = jnp.where(z_shut, 0.0, zu)
            d0[r], w0[r] = d, w
            ua[r] = w * f0[r]
            yd = yu
        face[2 * j + 1] = yd

    fine = Level(1, 1, kx0, ky0, kz0, d0, w0, f0)

    own = by // 2
    half_x = nx // 2
    middle = Level(1, 2, kx1, ky1, kz1, d1, w1, f1, 8)
    def coarsen(j):
        kx1[j], ky1[j + 1], kz1[j], d1[j] = coarse_coefficients(fine, 2 * j - 1, half_x)

    def restrict(j):
        f1[j] = coarse_sum(r0, j, half_x, 1)

    def sweep(j):
        ub[2 * j] = fine.swept(ua, 2 * j)
        ub[2 * j + 1] = fine.swept(ua, 2 * j + 1)

    def residual(j):
        r0[j] = fine.residual(ub, 2 * j - 1) + fine.residual(ub, 2 * j)

    wave(
        (restrict, 2, own + 5, 4),
        (residual, 2, own + 5, 3),
        (sweep, 1, own + 5, 2),
        (coarsen, 1, own + 6, 1),
        (faces, 1, own + 6, 0),
    )
    ky1[1] = coarse_sum(ky0, 1, half_x, 1)
    middle.weigh(1, own + 6)
    middle.first(uc, 2, own + 5)
    middle.sweep(uc, u1, 3, own + 4)
    middle.residual_pairs(u1, r1, 4, own // 2)

    quarter_x = nx // 4
    own2 = own // 2
    part = own2 // 2
    for j in range(own2):
        fields = (coarse_sum(r1, j, quarter_x, 2),) + coarse_coefficients(middle, 4 + 2 * j, quarter_x)
        for t, a in enumerate(fields):
            stage[j // part, pl.ds((t * part + j % part) * quarter_x, quarter_x), :] = a
    cell = lax.broadcasted_iota(jnp.int32, pack.shape, 1)
    lanes = lax.rem(4 * cell, LANES)
    quarter = lax.div(4 * cell, LANES)
    total = pick_lanes(stage[0, :, :LANES], lanes)
    for k in range(1, 4):
        half = slice((k % 2) * LANES, (k % 2 + 1) * LANES)
        total = jnp.where(quarter == k, pick_lanes(stage[k // 2, :, half], lanes), total)
    pack[...] = total

    size = pack.shape[0]

    def near(out, first):
        out[pl.ds(0, size), :] = total
        for k, (ref, r) in enumerate(((u1, first), (u1, first + 1), (u1, first + 2), (f1, first + 1))):
            for s in range(2):
                out[pl.ds(size + (2 * k + s) * half_x, half_x), :] = ref.ref[r, s]

    for one, out in enumerate(nears):
        near(out, jnp.where(plan.is_up(block, 1, core if plan.paired else one), own, 5))


def up_kernel(plan, pack, mine, theirs, *refs):
    refs, out, scratch = refs[:13], refs[13], refs[14:]
    kx0, ky0, kz0, d0, w0, f0, u0, kx1, ky1, kz1, w1, f1_in, u1_in = [Wide(r) for r in refs]
    stage = scratch[0]
    wide = [Wide(r) for r in scratch[1:]]
    f2, kx2, ky2, kz2, d2, w2, ua2, ub2, r2 = wide[:9]
    f3, kx3, ky3, kz3, d3, w3, ua3, ub3 = wide[9:17]
    t1, t0, f1, ua1, ub1, ua0, ub0, uc0 = wide[17:]
    nx, by = plan.nx, plan.by
    own, own2 = by // 2, by // 4
    part = own2 // 2
    half_x, quarter_x = nx // 2, nx // 4
    size = pack.shape[0]
    side = size + 8 * half_x
    core = lax.axis_index("gz")
    block = plan.block_here()
    here = lax.axis_index("gx")
    turn = 1 if plan.paired else 0

    for r in range(2, own + 6):
        f1[r] = f1_in[r]
    for r in range(3, own + 5):
        ua1[r] = u1_in[r]

    ups = {k: plan.is_up(block, k, core if plan.paired else 0) for k in range(1, FAR + 1)}
    stage[FAR] = pack[...]
    for k, up in ups.items():
        at = 0 if k == 1 else side + (k - 2) * size
        stage[jnp.where(up, FAR + k, FAR - k)] = mine[pl.ds(at, size), :]
        stage[jnp.where(up, FAR - k, FAR + k)] = theirs[pl.ds(at, size), :]
    for ref, up, half_turn in ((mine, ups[1], 0), (theirs, jnp.logical_not(ups[1]), turn)):
        row = jnp.where(up, own + 5, 0)
        for k, (to, r) in enumerate(((ua1, row), (ua1, row + 1), (ua1, row + 2), (f1, row + 1))):
            for s in range(2):
                to.ref[r, s ^ half_turn] = ref[pl.ds(size + (2 * k + s) * half_x, half_x), :]

    lane = lax.broadcasted_iota(jnp.int32, (size, LANES), 1)
    lanes = [lax.div(lane, 4) + k * (LANES // 4) for k in range(4)]

    def expand(k):
        there = block + k - FAR
        exists = (there >= 0) & (there < plan.blocks)
        swapped = 0
        if plan.paired and k != FAR:
            swapped = jnp.where(ups[abs(k - FAR)] == (k > FAR), 0, 1)
        rows = stage[k]
        for quarter in range(4):
            part_of, half = divmod(quarter, 2)
            a = pick_lanes(rows, lanes[quarter])
            for t, ref in enumerate((f2, kx2, ky2, kz2, d2)):
                for j in range(part):
                    at = (t * part + j) * quarter_x
                    b = a[at : at + quarter_x]
                    if t == 2:
                        b = jnp.where(exists, b, 0.0)
                    r = k * own2 + part_of * part + j + (1 if t == 2 else 0)
                    ref.ref[r, swapped if half == 0 else 1 - swapped] = b

    for k in range(2 * FAR + 1):
        expand(k)

    rows2 = (2 * FAR + 1) * own2
    two = Level(1, 4, kx2, ky2, kz2, d2, w2, f2, 14)
    two.weigh(0, rows2 - 1)
    two.first(ua2, 0, rows2 - 1)
    two.sweep(ua2, ub2, 1, rows2 - 2)
    two.residual_pairs(ub2, r2, 2, rows2 // 2 - 2)

    x = lax.broadcasted_iota(jnp.int32, (quarter_x, WIDE), 0)
    even_x = (x & 1) == 0
    low = (lax.broadcasted_iota(jnp.int32, (quarter_x, WIDE), 1) & 4) == 0
    z_pair = z_pairs(low, 4)

    def x_pair(a):
        return a + jnp.where(even_x, x_up(a), x_down(a))

    last3 = rows2 // 2 - 2

    def coarsen(j):
        r = 2 * j
        kx = kx2[r] + kx2[r + 1]
        kz = kz2[r] + kz2[r + 1]
        inner = ky2[r + 1] + jnp.where(even_x, kx, 0.0) + jnp.where(low, kz, 0.0)
        f3[j] = z_pair(x_pair(r2[j - 1]))
        kx3[j] = z_pair(jnp.where(even_x, x_up(kx), kx))
        ky3[j + 1] = z_pair(x_pair(ky2[r + 2]))
        kz = x_pair(kz)
        kz3[j] = jnp.where(low, z_up(kz, 4), kz)
        d3[j] = z_pair(x_pair(d2[r] + d2[r + 1] - 2.0 * inner))

    each(1, last3, 6, coarsen)
    three = Level(2, 8, kx3, ky3, kz3, d3, w3, f3, 16)
    three.weigh(1, last3)
    three.first(ua3, 1, last3)
    three.sweep(ua3, ub3, 2, last3 - 1)
    three.sweep(ub3, ua3, 3, last3 - 2)
    three.sweep(ua3, ub3, 4, last3 - 3)

    first2 = FAR * own2
    for j in range(4, last3 - 2):
        e = ub3[j]
        ua2[2 * j] = ub2[2 * j] + e
        ua2[2 * j + 1] = ub2[2 * j + 1] + e
    two.sweep(ua2, ub2, first2 - 3, first2 + own2 + 2)
    two.sweep(ub2, ua2, first2 - 2, first2 + own2 + 1)

    one = Level(1, 2, kx1, ky1, kz1, None, w1, f1, 8)
    correct(ua1, ub1, ua2, t1, quarter_x, first2 - 2, first2 + own2 + 1, 0)
    one.sweep(ub1, ua1, 1, own + 6)
    one.sweep(ua1, ub1, 2, own + 5)

    finest = Level(1, 1, kx0, ky0, kz0, d0, w0, f0)

    def corrected(j):
        part = ub1[j]
        t0[j, pl.ds(0, half_x, stride=2)] = part
        t0[j, pl.ds(1, half_x, stride=2)] = part
        both = t0[j]
        ua0[2 * j - 1] = u0[2 * j - 1] + both
        ua0[2 * j] = u0[2 * j] + both

    def sweep(j):
        ub0[2 * j - 1] = finest.swept(ua0, 2 * j - 1)
        ub0[2 * j] = finest.swept(ua0, 2 * j)

    def sweep_again(j):
        uc0[2 * j] = finest.swept(ub0, 2 * j)
        uc0[2 * j + 1] = finest.swept(ub0, 2 * j + 1)

    def finish(j):
        for r in (2 * j - 1, 2 * j):
            scaled = d0[r] * uc0[r]
            rest = f0[r] + finest.beside(uc0, r) - scaled
            for s in range(plan.gx):
                part = slice(s * plan.px, (s + 1) * plan.px)
                out[s ^ here, r - HALO, 0] = scaled[part, :LANES]
                out[s ^ here, r - HALO, 1] = rest[part, :LANES]

    wave(
        (finish, 4, own + 3, 5),
        (sweep_again, 3, own + 3, 4),
        (sweep, 3, own + 4, 2),
        (corrected, 2, own + 5, 0),
    )


def place_kernel(plan, *refs):
    parts, (scaled, residual) = refs[: plan.gx], refs[plan.gx :]
    here = lax.axis_index("gx")
    by, px = plan.by, plan.px
    for k, part in enumerate(parts):
        rows = pl.ds(plan.start_of(here ^ k), by)
        for p in range(px):
            scaled[0, p, rows, :] = part[pl.ds(p, by, stride=2 * px), :]
            residual[0, p, rows, :] = part[pl.ds(px + p, by, stride=2 * px), :]


def in_vmem(*shape):
    return pltpu.VMEM(shape, F32)


def call(kernel, out_shape, scratch=(), **more):
    return pl.pallas_call(
        kernel,
        out_shape=out_shape,
        scratch_shapes=list(scratch),
        compiler_params=pltpu.CompilerParams(vmem_limit_bytes=VMEM_LIMIT),
        **more,
    )


def pinned(*arrays, where=pltpu.VMEM):
    return [pltpu.with_memory_space_constraint(a, where) for a in arrays]


def beside_in_z(plan, a):
    count = plan.gz
    if plan.paired:
        return lax.ppermute(a, "gz", [(0, 1), (1, 0)])
    cut = LANES // 2
    right = lax.ppermute(a[..., :cut], "gz", [(i + 1, i) for i in range(count - 1)])
    left = lax.ppermute(a[..., cut:], "gz", [(i, i + 1) for i in range(count - 1)])
    return jnp.concatenate([right, left], axis=-1)


def exchange(plan, parts):
    got = [parts[0]] * plan.gx
    for k in range(plan.gx - 1, 0, -1):
        got[k] = lax.ppermute(parts[k], "gx", [(i, i ^ k) for i in range(plan.gx)])
    return got


def pairs_of(plan, k, one):
    partner = list(range(plan.blocks))
    for b in range(plan.blocks - k):
        if b // k % 2 == one:
            partner[b], partner[b + k] = b + k, b
    return [(plan.device(a), plan.device(b)) for a, b in enumerate(partner)]


def swap_blocks(plan, a, k, one):
    return lax.ppermute(a, ("gx", "gy"), pairs_of(plan, k, one))


def swap_blocks_apart(plan, a, k):
    pairs = [(2 * p + one, 2 * q + one) for one in range(2) for p, q in pairs_of(plan, k, one)]
    return lax.ppermute(a, ("gx", "gy", "gz"), pairs)


def far_blocks(plan, pack, nears):
    def line(move, near):
        parts = [move(pack, k) for k in range(FAR, 1, -1)] + [move(near, 1)]
        return jnp.concatenate(parts[::-1], axis=0)

    if plan.paired:
        mine = line(functools.partial(swap_blocks_apart, plan), nears[0])
        return mine, beside_in_z(plan, mine)
    return [line(functools.partial(swap_blocks, plan, one=one), nears[one]) for one in range(2)]


def on_device(plan, phase, density, rhs):
    nx, by, rows, px, gx = plan.nx, plan.by, plan.rows, plan.px, plan.gx
    flat = by * 2 * px
    block = (px, plan.ny, LANES)
    outside = pl.BlockSpec(memory_space=pltpu.HBM)
    parts = call(
        functools.partial(prepare_kernel, plan),
        [in_vmem(flat, LANES)] * gx,
        [pltpu.VMEM(block, jnp.int32), in_vmem(*block), in_vmem(1, *block), pltpu.SemaphoreType.DMA((3,))],
        in_specs=[outside] * 3,
    )(*pinned(phase, density, rhs, where=pltpu.HBM))
    parts = [a.reshape(by, 2, px, LANES) for a in exchange(plan, parts)]
    c, *sets = call(
        functools.partial(gather_kernel, plan),
        [in_vmem(gx, by, 2, px, LANES)] + [in_vmem(gx, HALO, 2, px, LANES)] * 2,
    )(*pinned(*parts))
    sides = jnp.concatenate([swap_blocks(plan, a, 1, one) for one, a in enumerate(sets)], axis=0)
    zc = beside_in_z(plan, c)
    zsides = beside_in_z(plan, sides)

    own, own2 = by // 2, by // 4
    size = 5 * (own2 // 2) * (nx // 4)
    side = size + 8 * (nx // 2)

    def level0(n):
        return in_vmem(n, 2, nx, LANES)

    def level1(n):
        return in_vmem(n, 2, nx // 2, LANES)

    outs = [in_vmem(size, LANES)] + [in_vmem(side, LANES)] * (1 if plan.paired else 2)
    fields = [level0(rows)] * 7 + [level1(own + 8)] * 6
    scratch = [level0(rows)] * 3 + [level0(own + 8), level1(own + 8), level1(own2), level1(own + 8)]
    scratch += [in_vmem(2, size, WIDE)]
    down = call(functools.partial(down_kernel, plan), outs + fields, scratch)(*pinned(c, zc, sides, zsides))
    pack, nears, fields = down[0], down[1 : len(outs)], down[len(outs) :]

    mine, theirs = far_blocks(plan, pack, nears)
    rows2 = (2 * FAR + 1) * own2
    scratch = [in_vmem(2 * FAR + 1, size, LANES)]
    scratch += [in_vmem(rows2 + 1, 2, nx // 4, LANES)] * 9 + [in_vmem(rows2 // 2 + 1, 2, nx // 4, LANES)] * 8
    scratch += [level1(rows2), level0(own + 8)] + [level1(own + 8)] * 3 + [level0(rows)] * 3
    (result,) = call(
        functools.partial(up_kernel, plan), [in_vmem(gx, by, 2, px, LANES)], scratch
    )(*pinned(pack, mine, theirs, *fields))

    parts = exchange(plan, [result[k].reshape(flat, LANES) for k in range(gx)])
    return call(
        functools.partial(place_kernel, plan),
        [jax.ShapeDtypeStruct((1, px, plan.ny, LANES), F32)] * 2,
    )(*pinned(*parts))


def solution(mesh):
    sizes = [mesh.shape[a] for a in ("gx", "gy", "gz")]

    def local(phase, density, rhs):
        return tuple(on_device(Plan(sizes, phase.shape), phase, density, rhs))

    in_specs = (P("gx", "gy", "gz"), P("gx", "gy", "gz"), P(None, "gx", "gy", "gz"))
    out_specs = (P(None, "gx", "gy", "gz"), P(None, "gx", "gy", "gz"))
    return jax.shard_map(local, mesh=mesh, in_specs=in_specs, out_specs=out_specs, check_vma=False)
```

```python
import functools

import jax
import jax.numpy as jnp
from jax import lax
from jax.experimental import pallas as pl
from jax.experimental.pallas import tpu as pltpu
from jax.sharding import PartitionSpec as P


DAMPING = 2.0 / 3.0
LANES = 128
WIDE = 256
HALO = 7
FAR = 3
F32 = jnp.float32
VMEM_LIMIT = 24 * 1024 * 1024


class Plan:
    def __init__(self, sizes, shape):
        self.gx, self.gy, self.gz = sizes
        self.px, self.ny, self.nz = shape
        self.nx = self.px * self.gx
        self.by = self.ny // self.gx
        self.blocks = self.gx * self.gy
        self.rows = self.by + 2 * HALO
        self.paired = self.gz == 2
        order = [0, 1, 3, 2] if self.gx == 4 else list(range(self.gx))
        self.place = [order.index(i) for i in range(self.gx)]
        self.order = order

    def device(self, block):
        j, q = divmod(block, self.gx)
        i = self.order[q if j % 2 == 0 else self.gx - 1 - q]
        return i * self.gy + j

    def look_up(self, table, i):
        return sum(jnp.where(i == k, v, 0) for k, v in enumerate(table))

    def start_of(self, i):
        q = self.look_up(self.place, i)
        q = jnp.where(lax.rem(lax.axis_index("gy"), 2) == 0, q, self.gx - 1 - q)
        return pl.multiple_of(q * self.by, self.by)

    def block_here(self):
        q = self.look_up(self.place, lax.axis_index("gx"))
        j = lax.axis_index("gy")
        return j * self.gx + jnp.where(lax.rem(j, 2) == 0, q, self.gx - 1 - q)

    def gx_of(self, block):
        block = jnp.clip(block, 0, self.blocks - 1)
        j, q = lax.div(block, self.gx), lax.rem(block, self.gx)
        return self.look_up(self.order, jnp.where(lax.rem(j, 2) == 0, q, self.gx - 1 - q))

    def is_up(self, block, k, one):
        return lax.rem(lax.div(block, k), 2) == one


def x_up(a, s=1):
    return pltpu.roll(a, a.shape[0] - s, 0)


def x_down(a, s=1):
    return pltpu.roll(a, s, 0)


def z_up(a, g):
    return pltpu.roll(a, a.shape[1] - g, 1)


def z_down(a, g):
    return pltpu.roll(a, g, 1)


def inverse(a):
    r = pl.reciprocal(a, approx=True)
    return r * (2.0 - a * r)


def each(first, last, step, body):
    count = last + 1 - first
    if count <= 2 * step:
        for i in range(first, last + 1):
            body(i)
        return

    def go(c, _):
        for k in range(step):
            body(first + c * step + k)
        return 0

    lax.fori_loop(0, count // step, go, 0)
    for i in range(first + count // step * step, last + 1):
        body(i)


def wave(*stages):
    start = min(first + delay for _, first, _, delay in stages)
    end = max(last + delay for _, _, last, delay in stages)
    full = max(first + delay for _, first, _, delay in stages)
    full_end = min(last + delay for _, _, last, delay in stages)

    def step(t):
        for body, first, last, delay in stages:
            if first <= t - delay <= last:
                body(t - delay)

    def all_of_them(t, _):
        for body, _, _, delay in stages:
            body(t - delay)
        return 0

    if full_end - full < 3:
        full = full_end = end + 1
    for t in range(start, min(full, end + 1)):
        step(t)
    if full <= end:
        lax.fori_loop(full, full_end + 1, all_of_them, 0)
        for t in range(full_end + 1, end + 1):
            step(t)


class Wide:
    def __init__(self, ref):
        self.ref = ref

    def __getitem__(self, key):
        r, xs = key if isinstance(key, tuple) else (key, slice(None))
        return jnp.concatenate([self.ref[r, 0, xs, :], self.ref[r, 1, xs, :]], axis=1)

    def __setitem__(self, key, value):
        r, xs = key if isinstance(key, tuple) else (key, slice(None))
        self.ref[r, 0, xs, :] = value[:, :LANES]
        self.ref[r, 1, xs, :] = value[:, LANES:]


class Level:
    def __init__(self, s, g, kx, ky, kz, d, w, f, step=2):
        self.s, self.g, self.step = s, g, step
        self.kx, self.ky, self.kz, self.d, self.w, self.f = kx, ky, kz, d, w, f

    def beside(self, u, r):
        here = u[r]
        kx, kz = self.kx[r], self.kz[r]
        a = kx * x_up(here, self.s) + x_down(kx * here, self.s)
        b = kz * z_up(here, self.g) + z_down(kz * here, self.g)
        return a + b + (self.ky[r + 1] * u[r + 1] + self.ky[r] * u[r - 1])

    def weigh(self, first, last):
        def body(r):
            self.w[r] = DAMPING * inverse(self.d[r])

        each(first, last, self.step, body)

    def first(self, u, first, last):
        def body(r):
            u[r] = self.w[r] * self.f[r]

        each(first, last, self.step, body)

    def swept(self, u, r):
        return (1.0 / 3.0) * u[r] + self.w[r] * (self.f[r] + self.beside(u, r))

    def sweep(self, u, v, first, last):
        def body(r):
            v[r] = self.swept(u, r)

        each(first, last, self.step, body)

    def residual(self, u, r):
        return self.f[r] + self.beside(u, r) - self.d[r] * u[r]

    def residual_pairs(self, u, out, first, count):
        def body(j):
            out[j] = self.residual(u, first + 2 * j) + self.residual(u, first + 2 * j + 1)

        each(0, count - 1, self.step // 2, body)


def z_pairs(low, g):
    return lambda a: a + jnp.where(low, z_up(a, g), z_down(a, g))


def coarse_coefficients(level, r, x_count):
    even, odd = pl.ds(0, x_count, stride=2), pl.ds(1, x_count, stride=2)
    g = level.g
    low = (lax.broadcasted_iota(jnp.int32, (x_count, WIDE), 1) & g) == 0
    z_pair = z_pairs(low, g)

    def all_x(ref, row):
        return ref[row, even] + ref[row, odd]

    kx = level.kx[r, odd] + level.kx[r + 1, odd]
    inner = level.kx[r, even] + level.kx[r + 1, even] + all_x(level.ky, r + 1)
    kz = all_x(level.kz, r) + all_x(level.kz, r + 1)
    d = all_x(level.d, r) + all_x(level.d, r + 1)
    d = d - 2.0 * (inner + jnp.where(low, kz, 0.0))
    return z_pair(kx), coarse_sum(level.ky, r + 2, x_count, g), jnp.where(low, z_up(kz, g), kz), z_pair(d)


def coarse_sum(ref, r, x_count, g):
    even, odd = pl.ds(0, x_count, stride=2), pl.ds(1, x_count, stride=2)
    low = (lax.broadcasted_iota(jnp.int32, (x_count, WIDE), 1) & g) == 0
    return z_pairs(low, g)(ref[r, even] + ref[r, odd])


def correct(u, v, e, t, x_count, first, last, to):
    def body(j):
        part = e[j]
        t[j, pl.ds(0, x_count, stride=2)] = part
        t[j, pl.ds(1, x_count, stride=2)] = part
        wide = t[j]
        r = to + 2 * (j - first)
        v[r] = u[r] + wide
        v[r + 1] = u[r + 1] + wide

    each(first, last, 2, body)


def pick_lanes(a, lanes):
    return jnp.take_along_axis(a, lanes, axis=1, mode="promise_in_bounds")


def prepare_kernel(plan, phase_in, density_in, rhs_in, *refs):
    outs, (phase, density, rhs, sems) = refs[: plan.gx], refs[plan.gx :]
    pairs = ((phase_in, phase), (density_in, density), (rhs_in, rhs))
    copies = [pltpu.make_async_copy(a, b, sems.at[k]) for k, (a, b) in enumerate(pairs)]
    for copy in copies:
        copy.start()
    for copy in copies:
        copy.wait()
    here = lax.axis_index("gx")
    by, px = plan.by, plan.px
    for k, out in enumerate(outs):
        rows = pl.ds(plan.start_of(here ^ k), by)
        for p in range(px):
            half = jnp.where(phase[p, rows, :] == 1, 500.0, 0.5).astype(F32)
            out[pl.ds(p, by, stride=2 * px), :] = half * density[p, rows, :]
            out[pl.ds(px + p, by, stride=2 * px), :] = rhs[0, p, rows, :]


def gather_kernel(plan, *refs):
    parts, (c, *sets) = refs[: plan.gx], refs[plan.gx :]
    block = plan.block_here()
    for k, part in enumerate(parts):
        c[k] = part[...]
        for one, out in enumerate(sets):
            first = jnp.where(plan.is_up(block, 1, one), plan.by - HALO, 0)
            out[k] = part[pl.ds(first, HALO)]


def down_kernel(plan, c, zc, sides, zsides, *refs):
    near_count = 1 if plan.paired else 2
    pack, nears, refs = refs[0], refs[1 : 1 + near_count], refs[1 + near_count :]
    kx0, ky0, kz0, d0, w0, f0, ub, kx1, ky1, kz1, w1, f1, u1 = [Wide(r) for r in refs[:13]]
    h0, ua, face, r0, uc, r1, d1 = [Wide(r) for r in refs[13:20]]
    stage = refs[20]
    nx, by, rows, gx, px = plan.nx, plan.by, plan.rows, plan.gx, plan.px
    shape = (nx, WIDE)
    block, here = plan.block_here(), lax.axis_index("gx")
    base = block * by - HALO
    y_count, z_count = plan.by * plan.blocks, plan.nz * plan.gz

    x = lax.broadcasted_iota(jnp.int32, shape, 0)
    lane = lax.broadcasted_iota(jnp.int32, shape, 1)
    core = lax.axis_index("gz")
    if plan.paired:
        z = lax.rem(core * LANES + lane, WIDE)
    else:
        z = core * LANES + jnp.where(lane < LANES + LANES // 2, lane, lane - WIDE)
    x_top, x_bottom = x == nx - 1, x == 0
    z_top, z_bottom = z == z_count - 1, z == 0
    z_shut = (z < 0) | (z >= z_count - 1)
    z_out = (z < 0) | (z >= z_count)

    def take(a, b, at, other, r, to):
        y = base + to
        inside = (y >= 0) & (y < y_count)
        for k in range(gx):
            xs = pl.ds(pl.multiple_of((other ^ k) * px, px), px)
            for s, ref in enumerate((a, b)):
                h = jnp.where(inside, ref[at + k, r, 0], 0.5)
                if not plan.paired:
                    h = jnp.where(z_out[:px, s * LANES : (s + 1) * LANES], 0.5, h)
                h0.ref[to, s, xs, :] = h
                f0.ref[to, s, xs, :] = ref[at + k, r, 1]

    each(0, by - 1, 4, lambda r: take(c, zc, 0, here, r, r + HALO))
    up_first = plan.is_up(block, 1, 0)
    below, above = jnp.where(up_first, gx, 0), jnp.where(up_first, 0, gx)
    gx_below, gx_above = plan.gx_of(block - 1), plan.gx_of(block + 1)
    each(0, HALO - 1, 4, lambda r: take(sides, zsides, below, gx_below, r, r))
    each(0, HALO - 1, 4, lambda r: take(sides, zsides, above, gx_above, r, r + HALO + by))

    @pl.when(block == 0)
    def _():
        h0[HALO - 1] = h0[HALO]

    @pl.when(block == plan.blocks - 1)
    def _():
        h0[HALO + by] = h0[HALO + by - 1]

    def is_open(r):
        y = base + r
        return (y >= 0) & (y < y_count - 1)

    first_face = inverse(h0[0] + h0[1])
    face[1] = first_face
    ky0[1] = jnp.where(is_open(0), first_face, 0.0)

    def faces(j):
        yd = face[2 * j - 1]
        for r in (2 * j - 1, 2 * j):
            h = h0[r]
            alone = 0.5 * inverse(h)
            xu = inverse(h + jnp.where(x_top, h, x_up(h)))
            xd = jnp.where(x_bottom, alone, x_down(xu))
            yu = inverse(h + h0[r + 1])
            zu = inverse(h + jnp.where(z_top, h, z_up(h, 1)))
            zd = jnp.where(z_bottom, alone, z_down(zu, 1))
            d = xu + xd + yu + yd + zu + zd
            w = DAMPING * inverse(d)
            kx0[r] = jnp.where(x_top, 0.0, xu)
            ky0[r + 1] = jnp.where(is_open(r), yu, 0.0)
            kz0[r] = jnp.where(z_shut, 0.0, zu)
            d0[r], w0[r] = d, w
            ua[r] = w * f0[r]
            yd = yu
        face[2 * j + 1] = yd

    fine = Level(1, 1, kx0, ky0, kz0, d0, w0, f0)

    own = by // 2
    half_x = nx // 2
    middle = Level(1, 2, kx1, ky1, kz1, d1, w1, f1, 8)
    def coarsen(j):
        kx1[j], ky1[j + 1], kz1[j], d1[j] = coarse_coefficients(fine, 2 * j - 1, half_x)

    def restrict(j):
        f1[j] = coarse_sum(r0, j, half_x, 1)

    def sweep(j):
        ub[2 * j] = fine.swept(ua, 2 * j)
        ub[2 * j + 1] = fine.swept(ua, 2 * j + 1)

    def residual(j):
        r0[j] = fine.residual(ub, 2 * j - 1) + fine.residual(ub, 2 * j)

    wave(
        (restrict, 2, own + 5, 4),
        (residual, 2, own + 5, 3),
        (sweep, 1, own + 5, 2),
        (coarsen, 1, own + 6, 1),
        (faces, 1, own + 6, 0),
    )
    ky1[1] = coarse_sum(ky0, 1, half_x, 1)
    middle.weigh(1, own + 6)
    middle.first(uc, 2, own + 5)
    middle.sweep(uc, u1, 3, own + 4)
    middle.residual_pairs(u1, r1, 4, own // 2)

    quarter_x = nx // 4
    own2 = own // 2
    part = own2 // 2
    for j in range(own2):
        fields = (coarse_sum(r1, j, quarter_x, 2),) + coarse_coefficients(middle, 4 + 2 * j, quarter_x)
        for t, a in enumerate(fields):
            stage[j // part, pl.ds((t * part + j % part) * quarter_x, quarter_x), :] = a
    cell = lax.broadcasted_iota(jnp.int32, pack.shape, 1)
    lanes = lax.rem(4 * cell, LANES)
    quarter = lax.div(4 * cell, LANES)
    total = pick_lanes(stage[0, :, :LANES], lanes)
    for k in range(1, 4):
        half = slice((k % 2) * LANES, (k % 2 + 1) * LANES)
        total = jnp.where(quarter == k, pick_lanes(stage[k // 2, :, half], lanes), total)
    pack[...] = total

    size = pack.shape[0]

    def near(out, first):
        out[pl.ds(0, size), :] = total
        for k, (ref, r) in enumerate(((u1, first), (u1, first + 1), (u1, first + 2), (f1, first + 1))):
            for s in range(2):
                out[pl.ds(size + (2 * k + s) * half_x, half_x), :] = ref.ref[r, s]

    for one, out in enumerate(nears):
        near(out, jnp.where(plan.is_up(block, 1, core if plan.paired else one), own, 5))


def up_kernel(plan, pack, mine, theirs, *refs):
    refs, out, scratch = refs[:13], refs[13], refs[14:]
    kx0, ky0, kz0, d0, w0, f0, u0, kx1, ky1, kz1, w1, f1_in, u1_in = [Wide(r) for r in refs]
    stage = scratch[0]
    wide = [Wide(r) for r in scratch[1:]]
    f2, kx2, ky2, kz2, d2, w2, ua2, ub2, r2 = wide[:9]
    f3, kx3, ky3, kz3, d3, w3, ua3, ub3 = wide[9:17]
    t1, t0, f1, ua1, ub1, ua0, ub0, uc0 = wide[17:]
    nx, by = plan.nx, plan.by
    own, own2 = by // 2, by // 4
    part = own2 // 2
    half_x, quarter_x = nx // 2, nx // 4
    size = pack.shape[0]
    side = size + 8 * half_x
    core = lax.axis_index("gz")
    block = plan.block_here()
    here = lax.axis_index("gx")
    turn = 1 if plan.paired else 0

    for r in range(2, own + 6):
        f1[r] = f1_in[r]
    for r in range(3, own + 5):
        ua1[r] = u1_in[r]

    ups = {k: plan.is_up(block, k, core if plan.paired else 0) for k in range(1, FAR + 1)}
    stage[FAR] = pack[...]
    for k, up in ups.items():
        at = 0 if k == 1 else side + (k - 2) * size
        stage[jnp.where(up, FAR + k, FAR - k)] = mine[pl.ds(at, size), :]
        stage[jnp.where(up, FAR - k, FAR + k)] = theirs[pl.ds(at, size), :]
    for ref, up, half_turn in ((mine, ups[1], 0), (theirs, jnp.logical_not(ups[1]), turn)):
        row = jnp.where(up, own + 5, 0)
        for k, (to, r) in enumerate(((ua1, row), (ua1, row + 1), (ua1, row + 2), (f1, row + 1))):
            for s in range(2):
                to.ref[r, s ^ half_turn] = ref[pl.ds(size + (2 * k + s) * half_x, half_x), :]

    lane = lax.broadcasted_iota(jnp.int32, (size, LANES), 1)
    lanes = [lax.div(lane, 4) + k * (LANES // 4) for k in range(4)]

    def expand(k):
        there = block + k - FAR
        exists = (there >= 0) & (there < plan.blocks)
        swapped = 0
        if plan.paired and k != FAR:
            swapped = jnp.where(ups[abs(k - FAR)] == (k > FAR), 0, 1)
        rows = stage[k]
        for quarter in range(4):
            part_of, half = divmod(quarter, 2)
            a = pick_lanes(rows, lanes[quarter])
            for t, ref in enumerate((f2, kx2, ky2, kz2, d2)):
                for j in range(part):
                    at = (t * part + j) * quarter_x
                    b = a[at : at + quarter_x]
                    if t == 2:
                        b = jnp.where(exists, b, 0.0)
                    r = k * own2 + part_of * part + j + (1 if t == 2 else 0)
                    ref.ref[r, swapped if half == 0 else 1 - swapped] = b

    for k in range(2 * FAR + 1):
        expand(k)

    rows2 = (2 * FAR + 1) * own2
    two = Level(1, 4, kx2, ky2, kz2, d2, w2, f2, 14)
    two.weigh(0, rows2 - 1)
    two.first(ua2, 0, rows2 - 1)
    two.sweep(ua2, ub2, 1, rows2 - 2)
    two.residual_pairs(ub2, r2, 2, rows2 // 2 - 2)

    x = lax.broadcasted_iota(jnp.int32, (quarter_x, WIDE), 0)
    even_x = (x & 1) == 0
    low = (lax.broadcasted_iota(jnp.int32, (quarter_x, WIDE), 1) & 4) == 0
    z_pair = z_pairs(low, 4)

    def x_pair(a):
        return a + jnp.where(even_x, x_up(a), x_down(a))

    last3 = rows2 // 2 - 2

    def coarsen(j):
        r = 2 * j
        kx = kx2[r] + kx2[r + 1]
        kz = kz2[r] + kz2[r + 1]
        inner = ky2[r + 1] + jnp.where(even_x, kx, 0.0) + jnp.where(low, kz, 0.0)
        f3[j] = z_pair(x_pair(r2[j - 1]))
        kx3[j] = z_pair(jnp.where(even_x, x_up(kx), kx))
        ky3[j + 1] = z_pair(x_pair(ky2[r + 2]))
        kz = x_pair(kz)
        kz3[j] = jnp.where(low, z_up(kz, 4), kz)
        d3[j] = z_pair(x_pair(d2[r] + d2[r + 1] - 2.0 * inner))

    each(1, last3, 6, coarsen)
    three = Level(2, 8, kx3, ky3, kz3, d3, w3, f3, 16)
    three.weigh(1, last3)
    three.first(ua3, 1, last3)
    three.sweep(ua3, ub3, 2, last3 - 1)
    three.sweep(ub3, ua3, 3, last3 - 2)
    three.sweep(ua3, ub3, 4, last3 - 3)

    first2 = FAR * own2
    for j in range(4, last3 - 2):
        e = ub3[j]
        ua2[2 * j] = ub2[2 * j] + e
        ua2[2 * j + 1] = ub2[2 * j + 1] + e
    two.sweep(ua2, ub2, first2 - 3, first2 + own2 + 2)
    two.sweep(ub2, ua2, first2 - 2, first2 + own2 + 1)

    one = Level(1, 2, kx1, ky1, kz1, None, w1, f1, 8)
    correct(ua1, ub1, ua2, t1, quarter_x, first2 - 2, first2 + own2 + 1, 0)
    one.sweep(ub1, ua1, 1, own + 6)
    one.sweep(ua1, ub1, 2, own + 5)

    finest = Level(1, 1, kx0, ky0, kz0, d0, w0, f0)

    def corrected(j):
        part = ub1[j]
        t0[j, pl.ds(0, half_x, stride=2)] = part
        t0[j, pl.ds(1, half_x, stride=2)] = part
        both = t0[j]
        ua0[2 * j - 1] = u0[2 * j - 1] + both
        ua0[2 * j] = u0[2 * j] + both

    def sweep(j):
        ub0[2 * j - 1] = finest.swept(ua0, 2 * j - 1)
        ub0[2 * j] = finest.swept(ua0, 2 * j)

    def sweep_again(j):
        uc0[2 * j] = finest.swept(ub0, 2 * j)
        uc0[2 * j + 1] = finest.swept(ub0, 2 * j + 1)

    def finish(j):
        for r in (2 * j - 1, 2 * j):
            scaled = d0[r] * uc0[r]
            rest = f0[r] + finest.beside(uc0, r) - scaled
            for s in range(plan.gx):
                part = slice(s * plan.px, (s + 1) * plan.px)
                out[s ^ here, r - HALO, 0] = scaled[part, :LANES]
                out[s ^ here, r - HALO, 1] = rest[part, :LANES]

    wave(
        (finish, 4, own + 3, 5),
        (sweep_again, 3, own + 3, 4),
        (sweep, 3, own + 4, 2),
        (corrected, 2, own + 5, 0),
    )


def place_kernel(plan, *refs):
    parts, (scaled, residual) = refs[: plan.gx], refs[plan.gx :]
    here = lax.axis_index("gx")
    by, px = plan.by, plan.px
    for k, part in enumerate(parts):
        rows = pl.ds(plan.start_of(here ^ k), by)
        for p in range(px):
            scaled[0, p, rows, :] = part[pl.ds(p, by, stride=2 * px), :]
            residual[0, p, rows, :] = part[pl.ds(px + p, by, stride=2 * px), :]


def in_vmem(*shape):
    return pltpu.VMEM(shape, F32)


def call(kernel, out_shape, scratch=(), **more):
    return pl.pallas_call(
        kernel,
        out_shape=out_shape,
        scratch_shapes=list(scratch),
        compiler_params=pltpu.CompilerParams(vmem_limit_bytes=VMEM_LIMIT),
        **more,
    )


def pinned(*arrays, where=pltpu.VMEM):
    return [pltpu.with_memory_space_constraint(a, where) for a in arrays]


def beside_in_z(plan, a):
    count = plan.gz
    if plan.paired:
        return lax.ppermute(a, "gz", [(0, 1), (1, 0)])
    cut = LANES // 2
    right = lax.ppermute(a[..., :cut], "gz", [(i + 1, i) for i in range(count - 1)])
    left = lax.ppermute(a[..., cut:], "gz", [(i, i + 1) for i in range(count - 1)])
    return jnp.concatenate([right, left], axis=-1)


def exchange(plan, parts):
    got = [parts[0]] * plan.gx
    for k in range(plan.gx - 1, 0, -1):
        got[k] = lax.ppermute(parts[k], "gx", [(i, i ^ k) for i in range(plan.gx)])
    return got


def pairs_of(plan, k, one):
    partner = list(range(plan.blocks))
    for b in range(plan.blocks - k):
        if b // k % 2 == one:
            partner[b], partner[b + k] = b + k, b
    alone = [b for b in range(plan.blocks) if partner[b] == b]
    for a, b in zip(alone[::2], alone[1::2]):
        partner[a], partner[b] = b, a
    return [(plan.device(a), plan.device(b)) for a, b in enumerate(partner)]


def swap_blocks(plan, a, k, one):
    return lax.ppermute(a, ("gx", "gy"), pairs_of(plan, k, one))


def swap_blocks_apart(plan, a, k):
    pairs = [(2 * p + one, 2 * q + one) for one in range(2) for p, q in pairs_of(plan, k, one)]
    return lax.ppermute(a, ("gx", "gy", "gz"), pairs)


def far_blocks(plan, pack, nears):
    def line(move, near):
        parts = [move(pack, k) for k in range(FAR, 1, -1)] + [move(near, 1)]
        return jnp.concatenate(parts[::-1], axis=0)

    if plan.paired:
        mine = line(functools.partial(swap_blocks_apart, plan), nears[0])
        return mine, beside_in_z(plan, mine)
    return [line(functools.partial(swap_blocks, plan, one=one), nears[one]) for one in range(2)]


def on_device(plan, phase, density, rhs):
    nx, by, rows, px, gx = plan.nx, plan.by, plan.rows, plan.px, plan.gx
    flat = by * 2 * px
    block = (px, plan.ny, LANES)
    outside = pl.BlockSpec(memory_space=pltpu.HBM)
    parts = call(
        functools.partial(prepare_kernel, plan),
        [in_vmem(flat, LANES)] * gx,
        [pltpu.VMEM(block, jnp.int32), in_vmem(*block), in_vmem(1, *block), pltpu.SemaphoreType.DMA((3,))],
        in_specs=[outside] * 3,
    )(*pinned(phase, density, rhs, where=pltpu.HBM))
    parts = [a.reshape(by, 2, px, LANES) for a in exchange(plan, parts)]
    c, *sets = call(
        functools.partial(gather_kernel, plan),
        [in_vmem(gx, by, 2, px, LANES)] + [in_vmem(gx, HALO, 2, px, LANES)] * 2,
    )(*pinned(*parts))
    sides = jnp.concatenate([swap_blocks(plan, a, 1, one) for one, a in enumerate(sets)], axis=0)
    zc = beside_in_z(plan, c)
    zsides = beside_in_z(plan, sides)

    own, own2 = by // 2, by // 4
    size = 5 * (own2 // 2) * (nx // 4)
    side = size + 8 * (nx // 2)

    def level0(n):
        return in_vmem(n, 2, nx, LANES)

    def level1(n):
        return in_vmem(n, 2, nx // 2, LANES)

    outs = [in_vmem(size, LANES)] + [in_vmem(side, LANES)] * (1 if plan.paired else 2)
    fields = [level0(rows)] * 7 + [level1(own + 8)] * 6
    scratch = [level0(rows)] * 3 + [level0(own + 8), level1(own + 8), level1(own2), level1(own + 8)]
    scratch += [in_vmem(2, size, WIDE)]
    down = call(functools.partial(down_kernel, plan), outs + fields, scratch)(*pinned(c, zc, sides, zsides))
    pack, nears, fields = down[0], down[1 : len(outs)], down[len(outs) :]

    mine, theirs = far_blocks(plan, pack, nears)
    rows2 = (2 * FAR + 1) * own2
    scratch = [in_vmem(2 * FAR + 1, size, LANES)]
    scratch += [in_vmem(rows2 + 1, 2, nx // 4, LANES)] * 9 + [in_vmem(rows2 // 2 + 1, 2, nx // 4, LANES)] * 8
    scratch += [level1(rows2), level0(own + 8)] + [level1(own + 8)] * 3 + [level0(rows)] * 3
    (result,) = call(
        functools.partial(up_kernel, plan), [in_vmem(gx, by, 2, px, LANES)], scratch
    )(*pinned(pack, mine, theirs, *fields))

    parts = exchange(plan, [result[k].reshape(flat, LANES) for k in range(gx)])
    return call(
        functools.partial(place_kernel, plan),
        [jax.ShapeDtypeStruct((1, px, plan.ny, LANES), F32)] * 2,
    )(*pinned(*parts))


def solution(mesh):
    sizes = [mesh.shape[a] for a in ("gx", "gy", "gz")]

    def local(phase, density, rhs):
        return tuple(on_device(Plan(sizes, phase.shape), phase, density, rhs))

    in_specs = (P("gx", "gy", "gz"), P("gx", "gy", "gz"), P(None, "gx", "gy", "gz"))
    out_specs = (P(None, "gx", "gy", "gz"), P(None, "gx", "gy", "gz"))
    return jax.shard_map(local, mesh=mesh, in_specs=in_specs, out_specs=out_specs, check_vma=False)
```

```python
import functools

import jax
import jax.numpy as jnp
from jax import lax
from jax.experimental import pallas as pl
from jax.experimental.pallas import tpu as pltpu
from jax.sharding import PartitionSpec as P


DAMPING = 2.0 / 3.0
LANES = 128
WIDE = 256
HALO = 7
FAR = 3
F32 = jnp.float32
VMEM_LIMIT = 24 * 1024 * 1024


class Plan:
    def __init__(self, sizes, shape):
        self.gx, self.gy, self.gz = sizes
        self.px, self.ny, self.nz = shape
        self.nx = self.px * self.gx
        self.by = self.ny // self.gx
        self.blocks = self.gx * self.gy
        self.rows = self.by + 2 * HALO
        self.paired = self.gz == 2
        self.ring = [0, 1, 3, 2] if self.gx == 4 else list(range(self.gx))
        self.place = [self.ring.index(i) for i in range(self.gx)]

    def device(self, block):
        j, q = divmod(block, self.gx)
        return self.ring[(q - j) % self.gx] * self.gy + j

    def look_up(self, table, i):
        return sum(jnp.where(i == k, v, 0) for k, v in enumerate(table))

    def start_of(self, i):
        q = lax.rem(self.look_up(self.place, i) + lax.axis_index("gy"), self.gx)
        return pl.multiple_of(q * self.by, self.by)

    def block_here(self):
        j = lax.axis_index("gy")
        return j * self.gx + lax.rem(self.look_up(self.place, lax.axis_index("gx")) + j, self.gx)

    def gx_of(self, block):
        block = jnp.clip(block, 0, self.blocks - 1)
        j, q = lax.div(block, self.gx), lax.rem(block, self.gx)
        return self.look_up(self.ring, lax.rem(q + self.gx * self.gy - j, self.gx))

    def is_up(self, block, k, one):
        return lax.rem(lax.div(block, k), 2) == one


def x_up(a, s=1):
    return pltpu.roll(a, a.shape[0] - s, 0)


def x_down(a, s=1):
    return pltpu.roll(a, s, 0)


def z_up(a, g):
    return pltpu.roll(a, a.shape[1] - g, 1)


def z_down(a, g):
    return pltpu.roll(a, g, 1)


def inverse(a):
    r = pl.reciprocal(a, approx=True)
    return r * (2.0 - a * r)


def each(first, last, step, body):
    count = last + 1 - first
    if count <= 2 * step:
        for i in range(first, last + 1):
            body(i)
        return

    def go(c, _):
        for k in range(step):
            body(first + c * step + k)
        return 0

    lax.fori_loop(0, count // step, go, 0)
    for i in range(first + count // step * step, last + 1):
        body(i)


def wave(*stages):
    start = min(first + delay for _, first, _, delay in stages)
    end = max(last + delay for _, _, last, delay in stages)
    full = max(first + delay for _, first, _, delay in stages)
    full_end = min(last + delay for _, _, last, delay in stages)

    def step(t):
        for body, first, last, delay in stages:
            if first <= t - delay <= last:
                body(t - delay)

    def all_of_them(t, _):
        for body, _, _, delay in stages:
            body(t - delay)
        return 0

    if full_end - full < 3:
        full = full_end = end + 1
    for t in range(start, min(full, end + 1)):
        step(t)
    if full <= end:
        lax.fori_loop(full, full_end + 1, all_of_them, 0)
        for t in range(full_end + 1, end + 1):
            step(t)


class Wide:
    def __init__(self, ref):
        self.ref = ref

    def __getitem__(self, key):
        r, xs = key if isinstance(key, tuple) else (key, slice(None))
        return jnp.concatenate([self.ref[r, 0, xs, :], self.ref[r, 1, xs, :]], axis=1)

    def __setitem__(self, key, value):
        r, xs = key if isinstance(key, tuple) else (key, slice(None))
        self.ref[r, 0, xs, :] = value[:, :LANES]
        self.ref[r, 1, xs, :] = value[:, LANES:]


class Level:
    def __init__(self, s, g, kx, ky, kz, d, w, f, step=2):
        self.s, self.g, self.step = s, g, step
        self.kx, self.ky, self.kz, self.d, self.w, self.f = kx, ky, kz, d, w, f

    def beside(self, u, r):
        here = u[r]
        kx, kz = self.kx[r], self.kz[r]
        a = kx * x_up(here, self.s) + x_down(kx * here, self.s)
        b = kz * z_up(here, self.g) + z_down(kz * here, self.g)
        return a + b + (self.ky[r + 1] * u[r + 1] + self.ky[r] * u[r - 1])

    def weigh(self, first, last):
        def body(r):
            self.w[r] = DAMPING * inverse(self.d[r])

        each(first, last, self.step, body)

    def first(self, u, first, last):
        def body(r):
            u[r] = self.w[r] * self.f[r]

        each(first, last, self.step, body)

    def swept(self, u, r):
        return (1.0 / 3.0) * u[r] + self.w[r] * (self.f[r] + self.beside(u, r))

    def sweep(self, u, v, first, last):
        def body(r):
            v[r] = self.swept(u, r)

        each(first, last, self.step, body)

    def residual(self, u, r):
        return self.f[r] + self.beside(u, r) - self.d[r] * u[r]

    def residual_pairs(self, u, out, first, count):
        def body(j):
            out[j] = self.residual(u, first + 2 * j) + self.residual(u, first + 2 * j + 1)

        each(0, count - 1, self.step // 2, body)


def z_pairs(low, g):
    return lambda a: a + jnp.where(low, z_up(a, g), z_down(a, g))


def coarse_coefficients(level, r, x_count):
    even, odd = pl.ds(0, x_count, stride=2), pl.ds(1, x_count, stride=2)
    g = level.g
    low = (lax.broadcasted_iota(jnp.int32, (x_count, WIDE), 1) & g) == 0
    z_pair = z_pairs(low, g)

    def all_x(ref, row):
        return ref[row, even] + ref[row, odd]

    kx = level.kx[r, odd] + level.kx[r + 1, odd]
    inner = level.kx[r, even] + level.kx[r + 1, even] + all_x(level.ky, r + 1)
    kz = all_x(level.kz, r) + all_x(level.kz, r + 1)
    d = all_x(level.d, r) + all_x(level.d, r + 1)
    d = d - 2.0 * (inner + jnp.where(low, kz, 0.0))
    return z_pair(kx), coarse_sum(level.ky, r + 2, x_count, g), jnp.where(low, z_up(kz, g), kz), z_pair(d)


def coarse_sum(ref, r, x_count, g):
    even, odd = pl.ds(0, x_count, stride=2), pl.ds(1, x_count, stride=2)
    low = (lax.broadcasted_iota(jnp.int32, (x_count, WIDE), 1) & g) == 0
    return z_pairs(low, g)(ref[r, even] + ref[r, odd])


def correct(u, v, e, t, x_count, first, last, to):
    def body(j):
        part = e[j]
        t[j, pl.ds(0, x_count, stride=2)] = part
        t[j, pl.ds(1, x_count, stride=2)] = part
        wide = t[j]
        r = to + 2 * (j - first)
        v[r] = u[r] + wide
        v[r + 1] = u[r + 1] + wide

    each(first, last, 2, body)


def pick_lanes(a, lanes):
    return jnp.take_along_axis(a, lanes, axis=1, mode="promise_in_bounds")


def prepare_kernel(plan, phase_in, density_in, rhs_in, *refs):
    outs, (phase, density, rhs, sems) = refs[: plan.gx], refs[plan.gx :]
    pairs = ((phase_in, phase), (density_in, density), (rhs_in, rhs))
    copies = [pltpu.make_async_copy(a, b, sems.at[k]) for k, (a, b) in enumerate(pairs)]
    for copy in copies:
        copy.start()
    for copy in copies:
        copy.wait()
    here = lax.axis_index("gx")
    by, px = plan.by, plan.px
    for k, out in enumerate(outs):
        rows = pl.ds(plan.start_of(here ^ k), by)
        for p in range(px):
            half = jnp.where(phase[p, rows, :] == 1, 500.0, 0.5).astype(F32)
            out[pl.ds(p, by, stride=2 * px), :] = half * density[p, rows, :]
            out[pl.ds(px + p, by, stride=2 * px), :] = rhs[0, p, rows, :]


def gather_kernel(plan, *refs):
    parts, (c, *sets) = refs[: plan.gx], refs[plan.gx :]
    block = plan.block_here()
    for k, part in enumerate(parts):
        c[k] = part[...]
        for one, out in enumerate(sets):
            first = jnp.where(plan.is_up(block, 1, one), plan.by - HALO, 0)
            out[k] = part[pl.ds(first, HALO)]


def down_kernel(plan, c, zc, sides, zsides, *refs):
    near_count = 1 if plan.paired else 2
    pack, nears, refs = refs[0], refs[1 : 1 + near_count], refs[1 + near_count :]
    kx0, ky0, kz0, d0, w0, f0, ub, kx1, ky1, kz1, w1, f1, u1 = [Wide(r) for r in refs[:13]]
    h0, ua, face, r0, uc, r1, d1 = [Wide(r) for r in refs[13:20]]
    stage = refs[20]
    nx, by, rows, gx, px = plan.nx, plan.by, plan.rows, plan.gx, plan.px
    shape = (nx, WIDE)
    block, here = plan.block_here(), lax.axis_index("gx")
    base = block * by - HALO
    y_count, z_count = plan.by * plan.blocks, plan.nz * plan.gz

    x = lax.broadcasted_iota(jnp.int32, shape, 0)
    lane = lax.broadcasted_iota(jnp.int32, shape, 1)
    core = lax.axis_index("gz")
    if plan.paired:
        z = lax.rem(core * LANES + lane, WIDE)
    else:
        z = core * LANES + jnp.where(lane < LANES + LANES // 2, lane, lane - WIDE)
    x_top, x_bottom = x == nx - 1, x == 0
    z_top, z_bottom = z == z_count - 1, z == 0
    z_shut = (z < 0) | (z >= z_count - 1)
    z_out = (z < 0) | (z >= z_count)

    def take(a, b, at, other, r, to):
        y = base + to
        inside = (y >= 0) & (y < y_count)
        for k in range(gx):
            xs = pl.ds(pl.multiple_of((other ^ k) * px, px), px)
            for s, ref in enumerate((a, b)):
                h = jnp.where(inside, ref[at + k, r, 0], 0.5)
                if not plan.paired:
                    h = jnp.where(z_out[:px, s * LANES : (s + 1) * LANES], 0.5, h)
                h0.ref[to, s, xs, :] = h
                f0.ref[to, s, xs, :] = ref[at + k, r, 1]

    each(0, by - 1, 4, lambda r: take(c, zc, 0, here, r, r + HALO))
    up_first = plan.is_up(block, 1, 0)
    below, above = jnp.where(up_first, gx, 0), jnp.where(up_first, 0, gx)
    gx_below, gx_above = plan.gx_of(block - 1), plan.gx_of(block + 1)
    each(0, HALO - 1, 4, lambda r: take(sides, zsides, below, gx_below, r, r))
    each(0, HALO - 1, 4, lambda r: take(sides, zsides, above, gx_above, r, r + HALO + by))

    @pl.when(block == 0)
    def _():
        h0[HALO - 1] = h0[HALO]

    @pl.when(block == plan.blocks - 1)
    def _():
        h0[HALO + by] = h0[HALO + by - 1]

    def is_open(r):
        y = base + r
        return (y >= 0) & (y < y_count - 1)

    first_face = inverse(h0[0] + h0[1])
    face[1] = first_face
    ky0[1] = jnp.where(is_open(0), first_face, 0.0)

    def faces(j):
        yd = face[2 * j - 1]
        for r in (2 * j - 1, 2 * j):
            h = h0[r]
            alone = 0.5 * inverse(h)
            xu = inverse(h + jnp.where(x_top, h, x_up(h)))
            xd = jnp.where(x_bottom, alone, x_down(xu))
            yu = inverse(h + h0[r + 1])
            zu = inverse(h + jnp.where(z_top, h, z_up(h, 1)))
            zd = jnp.where(z_bottom, alone, z_down(zu, 1))
            d = xu + xd + yu + yd + zu + zd
            w = DAMPING * inverse(d)
            kx0[r] = jnp.where(x_top, 0.0, xu)
            ky0[r + 1] = jnp.where(is_open(r), yu, 0.0)
            kz0[r] = jnp.where(z_shut, 0.0, zu)
            d0[r], w0[r] = d, w
            ua[r] = w * f0[r]
            yd = yu
        face[2 * j + 1] = yd

    fine = Level(1, 1, kx0, ky0, kz0, d0, w0, f0)

    own = by // 2
    half_x = nx // 2
    middle = Level(1, 2, kx1, ky1, kz1, d1, w1, f1, 8)
    def coarsen(j):
        kx1[j], ky1[j + 1], kz1[j], d1[j] = coarse_coefficients(fine, 2 * j - 1, half_x)

    def restrict(j):
        f1[j] = coarse_sum(r0, j, half_x, 1)

    def sweep(j):
        ub[2 * j] = fine.swept(ua, 2 * j)
        ub[2 * j + 1] = fine.swept(ua, 2 * j + 1)

    def residual(j):
        r0[j] = fine.residual(ub, 2 * j - 1) + fine.residual(ub, 2 * j)

    wave(
        (restrict, 2, own + 5, 4),
        (residual, 2, own + 5, 3),
        (sweep, 1, own + 5, 2),
        (coarsen, 1, own + 6, 1),
        (faces, 1, own + 6, 0),
    )
    ky1[1] = coarse_sum(ky0, 1, half_x, 1)
    middle.weigh(1, own + 6)
    middle.first(uc, 2, own + 5)
    middle.sweep(uc, u1, 3, own + 4)
    middle.residual_pairs(u1, r1, 4, own // 2)

    quarter_x = nx // 4
    own2 = own // 2
    part = own2 // 2
    for j in range(own2):
        fields = (coarse_sum(r1, j, quarter_x, 2),) + coarse_coefficients(middle, 4 + 2 * j, quarter_x)
        for t, a in enumerate(fields):
            stage[j // part, pl.ds((t * part + j % part) * quarter_x, quarter_x), :] = a
    cell = lax.broadcasted_iota(jnp.int32, pack.shape, 1)
    lanes = lax.rem(4 * cell, LANES)
    quarter = lax.div(4 * cell, LANES)
    total = pick_lanes(stage[0, :, :LANES], lanes)
    for k in range(1, 4):
        half = slice((k % 2) * LANES, (k % 2 + 1) * LANES)
        total = jnp.where(quarter == k, pick_lanes(stage[k // 2, :, half], lanes), total)
    pack[...] = total

    size = pack.shape[0]

    def near(out, first):
        out[pl.ds(0, size), :] = total
        for k, (ref, r) in enumerate(((u1, first), (u1, first + 1), (u1, first + 2), (f1, first + 1))):
            for s in range(2):
                out[pl.ds(size + (2 * k + s) * half_x, half_x), :] = ref.ref[r, s]

    for one, out in enumerate(nears):
        near(out, jnp.where(plan.is_up(block, 1, core if plan.paired else one), own, 5))


def up_kernel(plan, pack, mine, theirs, *refs):
    refs, out, scratch = refs[:13], refs[13], refs[14:]
    kx0, ky0, kz0, d0, w0, f0, u0, kx1, ky1, kz1, w1, f1_in, u1_in = [Wide(r) for r in refs]
    stage = scratch[0]
    wide = [Wide(r) for r in scratch[1:]]
    f2, kx2, ky2, kz2, d2, w2, ua2, ub2, r2 = wide[:9]
    f3, kx3, ky3, kz3, d3, w3, ua3, ub3 = wide[9:17]
    t1, t0, f1, ua1, ub1, ua0, ub0, uc0 = wide[17:]
    nx, by = plan.nx, plan.by
    own, own2 = by // 2, by // 4
    part = own2 // 2
    half_x, quarter_x = nx // 2, nx // 4
    size = pack.shape[0]
    side = size + 8 * half_x
    core = lax.axis_index("gz")
    block = plan.block_here()
    here = lax.axis_index("gx")
    turn = 1 if plan.paired else 0

    for r in range(2, own + 6):
        f1[r] = f1_in[r]
    for r in range(3, own + 5):
        ua1[r] = u1_in[r]

    ups = {k: plan.is_up(block, k, core if plan.paired else 0) for k in range(1, FAR + 1)}
    stage[FAR] = pack[...]
    for k, up in ups.items():
        at = 0 if k == 1 else side + (k - 2) * size
        stage[jnp.where(up, FAR + k, FAR - k)] = mine[pl.ds(at, size), :]
        stage[jnp.where(up, FAR - k, FAR + k)] = theirs[pl.ds(at, size), :]
    for ref, up, half_turn in ((mine, ups[1], 0), (theirs, jnp.logical_not(ups[1]), turn)):
        row = jnp.where(up, own + 5, 0)
        for k, (to, r) in enumerate(((ua1, row), (ua1, row + 1), (ua1, row + 2), (f1, row + 1))):
            for s in range(2):
                to.ref[r, s ^ half_turn] = ref[pl.ds(size + (2 * k + s) * half_x, half_x), :]

    lane = lax.broadcasted_iota(jnp.int32, (size, LANES), 1)
    lanes = [lax.div(lane, 4) + k * (LANES // 4) for k in range(4)]

    def expand(k):
        there = block + k - FAR
        exists = (there >= 0) & (there < plan.blocks)
        swapped = 0
        if plan.paired and k != FAR:
            swapped = jnp.where(ups[abs(k - FAR)] == (k > FAR), 0, 1)
        rows = stage[k]
        for quarter in range(4):
            part_of, half = divmod(quarter, 2)
            a = pick_lanes(rows, lanes[quarter])
            for t, ref in enumerate((f2, kx2, ky2, kz2, d2)):
                for j in range(part):
                    at = (t * part + j) * quarter_x
                    b = a[at : at + quarter_x]
                    if t == 2:
                        b = jnp.where(exists, b, 0.0)
                    r = k * own2 + part_of * part + j + (1 if t == 2 else 0)
                    ref.ref[r, swapped if half == 0 else 1 - swapped] = b

    for k in range(2 * FAR + 1):
        expand(k)

    rows2 = (2 * FAR + 1) * own2
    two = Level(1, 4, kx2, ky2, kz2, d2, w2, f2, 14)
    two.weigh(0, rows2 - 1)
    two.first(ua2, 0, rows2 - 1)
    two.sweep(ua2, ub2, 1, rows2 - 2)
    two.residual_pairs(ub2, r2, 2, rows2 // 2 - 2)

    x = lax.broadcasted_iota(jnp.int32, (quarter_x, WIDE), 0)
    even_x = (x & 1) == 0
    low = (lax.broadcasted_iota(jnp.int32, (quarter_x, WIDE), 1) & 4) == 0
    z_pair = z_pairs(low, 4)

    def x_pair(a):
        return a + jnp.where(even_x, x_up(a), x_down(a))

    last3 = rows2 // 2 - 2

    def coarsen(j):
        r = 2 * j
        kx = kx2[r] + kx2[r + 1]
        kz = kz2[r] + kz2[r + 1]
        inner = ky2[r + 1] + jnp.where(even_x, kx, 0.0) + jnp.where(low, kz, 0.0)
        f3[j] = z_pair(x_pair(r2[j - 1]))
        kx3[j] = z_pair(jnp.where(even_x, x_up(kx), kx))
        ky3[j + 1] = z_pair(x_pair(ky2[r + 2]))
        kz = x_pair(kz)
        kz3[j] = jnp.where(low, z_up(kz, 4), kz)
        d3[j] = z_pair(x_pair(d2[r] + d2[r + 1] - 2.0 * inner))

    each(1, last3, 6, coarsen)
    three = Level(2, 8, kx3, ky3, kz3, d3, w3, f3, 16)
    three.weigh(1, last3)
    three.first(ua3, 1, last3)
    three.sweep(ua3, ub3, 2, last3 - 1)
    three.sweep(ub3, ua3, 3, last3 - 2)
    three.sweep(ua3, ub3, 4, last3 - 3)

    first2 = FAR * own2
    for j in range(4, last3 - 2):
        e = ub3[j]
        ua2[2 * j] = ub2[2 * j] + e
        ua2[2 * j + 1] = ub2[2 * j + 1] + e
    two.sweep(ua2, ub2, first2 - 3, first2 + own2 + 2)
    two.sweep(ub2, ua2, first2 - 2, first2 + own2 + 1)

    one = Level(1, 2, kx1, ky1, kz1, None, w1, f1, 8)
    correct(ua1, ub1, ua2, t1, quarter_x, first2 - 2, first2 + own2 + 1, 0)
    one.sweep(ub1, ua1, 1, own + 6)
    one.sweep(ua1, ub1, 2, own + 5)

    finest = Level(1, 1, kx0, ky0, kz0, d0, w0, f0)

    def corrected(j):
        part = ub1[j]
        t0[j, pl.ds(0, half_x, stride=2)] = part
        t0[j, pl.ds(1, half_x, stride=2)] = part
        both = t0[j]
        ua0[2 * j - 1] = u0[2 * j - 1] + both
        ua0[2 * j] = u0[2 * j] + both

    def sweep(j):
        ub0[2 * j - 1] = finest.swept(ua0, 2 * j - 1)
        ub0[2 * j] = finest.swept(ua0, 2 * j)

    def sweep_again(j):
        uc0[2 * j] = finest.swept(ub0, 2 * j)
        uc0[2 * j + 1] = finest.swept(ub0, 2 * j + 1)

    def finish(j):
        for r in (2 * j - 1, 2 * j):
            scaled = d0[r] * uc0[r]
            rest = f0[r] + finest.beside(uc0, r) - scaled
            for s in range(plan.gx):
                part = slice(s * plan.px, (s + 1) * plan.px)
                out[s ^ here, r - HALO, 0] = scaled[part, :LANES]
                out[s ^ here, r - HALO, 1] = rest[part, :LANES]

    wave(
        (finish, 4, own + 3, 5),
        (sweep_again, 3, own + 3, 4),
        (sweep, 3, own + 4, 2),
        (corrected, 2, own + 5, 0),
    )


def place_kernel(plan, *refs):
    parts, (scaled, residual) = refs[: plan.gx], refs[plan.gx :]
    here = lax.axis_index("gx")
    by, px = plan.by, plan.px
    for k, part in enumerate(parts):
        rows = pl.ds(plan.start_of(here ^ k), by)
        for p in range(px):
            scaled[0, p, rows, :] = part[pl.ds(p, by, stride=2 * px), :]
            residual[0, p, rows, :] = part[pl.ds(px + p, by, stride=2 * px), :]


def in_vmem(*shape):
    return pltpu.VMEM(shape, F32)


def call(kernel, out_shape, scratch=(), **more):
    return pl.pallas_call(
        kernel,
        out_shape=out_shape,
        scratch_shapes=list(scratch),
        compiler_params=pltpu.CompilerParams(vmem_limit_bytes=VMEM_LIMIT),
        **more,
    )


def pinned(*arrays, where=pltpu.VMEM):
    return [pltpu.with_memory_space_constraint(a, where) for a in arrays]


def beside_in_z(plan, a):
    count = plan.gz
    if plan.paired:
        return lax.ppermute(a, "gz", [(0, 1), (1, 0)])
    cut = LANES // 2
    right = lax.ppermute(a[..., :cut], "gz", [(i + 1, i) for i in range(count - 1)])
    left = lax.ppermute(a[..., cut:], "gz", [(i, i + 1) for i in range(count - 1)])
    return jnp.concatenate([right, left], axis=-1)


def exchange(plan, parts):
    got = [parts[0]] * plan.gx
    for k in range(plan.gx - 1, 0, -1):
        got[k] = lax.ppermute(parts[k], "gx", [(i, i ^ k) for i in range(plan.gx)])
    return got


def pairs_of(plan, k, one):
    partner = list(range(plan.blocks))
    for b in range(plan.blocks - k):
        if b // k % 2 == one:
            partner[b], partner[b + k] = b + k, b
    alone = [b for b in range(plan.blocks) if partner[b] == b]
    for a, b in zip(alone[::2], alone[1::2]):
        partner[a], partner[b] = b, a
    return [(plan.device(a), plan.device(b)) for a, b in enumerate(partner)]


def swap_blocks(plan, a, k, one):
    return lax.ppermute(a, ("gx", "gy"), pairs_of(plan, k, one))


def swap_blocks_apart(plan, a, k):
    pairs = [(2 * p + one, 2 * q + one) for one in range(2) for p, q in pairs_of(plan, k, one)]
    return lax.ppermute(a, ("gx", "gy", "gz"), pairs)


def far_blocks(plan, pack, nears):
    def line(move, near):
        parts = [move(pack, k) for k in range(FAR, 1, -1)] + [move(near, 1)]
        return jnp.concatenate(parts[::-1], axis=0)

    if plan.paired:
        mine = line(functools.partial(swap_blocks_apart, plan), nears[0])
        return mine, beside_in_z(plan, mine)
    return [line(functools.partial(swap_blocks, plan, one=one), nears[one]) for one in range(2)]


def on_device(plan, phase, density, rhs):
    nx, by, rows, px, gx = plan.nx, plan.by, plan.rows, plan.px, plan.gx
    flat = by * 2 * px
    block = (px, plan.ny, LANES)
    outside = pl.BlockSpec(memory_space=pltpu.HBM)
    parts = call(
        functools.partial(prepare_kernel, plan),
        [in_vmem(flat, LANES)] * gx,
        [pltpu.VMEM(block, jnp.int32), in_vmem(*block), in_vmem(1, *block), pltpu.SemaphoreType.DMA((3,))],
        in_specs=[outside] * 3,
    )(*pinned(phase, density, rhs, where=pltpu.HBM))
    parts = [a.reshape(by, 2, px, LANES) for a in exchange(plan, parts)]
    c, *sets = call(
        functools.partial(gather_kernel, plan),
        [in_vmem(gx, by, 2, px, LANES)] + [in_vmem(gx, HALO, 2, px, LANES)] * 2,
    )(*pinned(*parts))
    sides = jnp.concatenate([swap_blocks(plan, a, 1, one) for one, a in enumerate(sets)], axis=0)
    zc = beside_in_z(plan, c)
    zsides = beside_in_z(plan, sides)

    own, own2 = by // 2, by // 4
    size = 5 * (own2 // 2) * (nx // 4)
    side = size + 8 * (nx // 2)

    def level0(n):
        return in_vmem(n, 2, nx, LANES)

    def level1(n):
        return in_vmem(n, 2, nx // 2, LANES)

    outs = [in_vmem(size, LANES)] + [in_vmem(side, LANES)] * (1 if plan.paired else 2)
    fields = [level0(rows)] * 7 + [level1(own + 8)] * 6
    scratch = [level0(rows)] * 3 + [level0(own + 8), level1(own + 8), level1(own2), level1(own + 8)]
    scratch += [in_vmem(2, size, WIDE)]
    down = call(functools.partial(down_kernel, plan), outs + fields, scratch)(*pinned(c, zc, sides, zsides))
    pack, nears, fields = down[0], down[1 : len(outs)], down[len(outs) :]

    mine, theirs = far_blocks(plan, pack, nears)
    rows2 = (2 * FAR + 1) * own2
    scratch = [in_vmem(2 * FAR + 1, size, LANES)]
    scratch += [in_vmem(rows2 + 1, 2, nx // 4, LANES)] * 9 + [in_vmem(rows2 // 2 + 1, 2, nx // 4, LANES)] * 8
    scratch += [level1(rows2), level0(own + 8)] + [level1(own + 8)] * 3 + [level0(rows)] * 3
    (result,) = call(
        functools.partial(up_kernel, plan), [in_vmem(gx, by, 2, px, LANES)], scratch
    )(*pinned(pack, mine, theirs, *fields))

    parts = exchange(plan, [result[k].reshape(flat, LANES) for k in range(gx)])
    return call(
        functools.partial(place_kernel, plan),
        [jax.ShapeDtypeStruct((1, px, plan.ny, LANES), F32)] * 2,
    )(*pinned(*parts))


def solution(mesh):
    sizes = [mesh.shape[a] for a in ("gx", "gy", "gz")]

    def local(phase, density, rhs):
        return tuple(on_device(Plan(sizes, phase.shape), phase, density, rhs))

    in_specs = (P("gx", "gy", "gz"), P("gx", "gy", "gz"), P(None, "gx", "gy", "gz"))
    out_specs = (P(None, "gx", "gy", "gz"), P(None, "gx", "gy", "gz"))
    return jax.shard_map(local, mesh=mesh, in_specs=in_specs, out_specs=out_specs, check_vma=False)
```

```python
import functools

import jax
import jax.numpy as jnp
from jax import lax
from jax.experimental import pallas as pl
from jax.experimental.pallas import tpu as pltpu
from jax.sharding import PartitionSpec as P


DAMPING = 2.0 / 3.0
LANES = 128
WIDE = 256
HALO = 7
HALO_RHS = 6
FAR = 3
F32 = jnp.float32
VMEM_LIMIT = 24 * 1024 * 1024


class Plan:
    def __init__(self, sizes, shape):
        self.gx, self.gy, self.gz = sizes
        self.px, self.ny, self.nz = shape
        self.nx = self.px * self.gx
        self.by = self.ny // self.gx
        self.blocks = self.gx * self.gy
        self.rows = self.by + 2 * HALO
        self.paired = self.gz == 2
        self.ring = [0, 1, 3, 2] if self.gx == 4 else list(range(self.gx))
        self.place = [self.ring.index(i) for i in range(self.gx)]

    def device(self, block):
        j, q = divmod(block, self.gx)
        return self.ring[(q - j) % self.gx] * self.gy + j

    def look_up(self, table, i):
        return sum(jnp.where(i == k, v, 0) for k, v in enumerate(table))

    def start_of(self, i):
        q = lax.rem(self.look_up(self.place, i) + lax.axis_index("gy"), self.gx)
        return pl.multiple_of(q * self.by, self.by)

    def block_here(self):
        j = lax.axis_index("gy")
        return j * self.gx + lax.rem(self.look_up(self.place, lax.axis_index("gx")) + j, self.gx)

    def gx_of(self, block):
        block = jnp.clip(block, 0, self.blocks - 1)
        j, q = lax.div(block, self.gx), lax.rem(block, self.gx)
        return self.look_up(self.ring, lax.rem(q + self.gx * self.gy - j, self.gx))

    def is_up(self, block, k, one):
        return lax.rem(lax.div(block, k), 2) == one


def x_up(a, s=1):
    return pltpu.roll(a, a.shape[0] - s, 0)


def x_down(a, s=1):
    return pltpu.roll(a, s, 0)


def z_up(a, g):
    return pltpu.roll(a, a.shape[1] - g, 1)


def z_down(a, g):
    return pltpu.roll(a, g, 1)


def inverse(a):
    r = pl.reciprocal(a, approx=True)
    return r * (2.0 - a * r)


def each(first, last, step, body):
    count = last + 1 - first
    if count <= 2 * step:
        for i in range(first, last + 1):
            body(i)
        return

    def go(c, _):
        for k in range(step):
            body(first + c * step + k)
        return 0

    lax.fori_loop(0, count // step, go, 0)
    for i in range(first + count // step * step, last + 1):
        body(i)


def wave(*stages):
    start = min(first + delay for _, first, _, delay in stages)
    end = max(last + delay for _, _, last, delay in stages)
    full = max(first + delay for _, first, _, delay in stages)
    full_end = min(last + delay for _, _, last, delay in stages)

    def step(t):
        for body, first, last, delay in stages:
            if first <= t - delay <= last:
                body(t - delay)

    def all_of_them(t, _):
        for body, _, _, delay in stages:
            body(t - delay)
        return 0

    if full_end - full < 3:
        full = full_end = end + 1
    for t in range(start, min(full, end + 1)):
        step(t)
    if full <= end:
        lax.fori_loop(full, full_end + 1, all_of_them, 0)
        for t in range(full_end + 1, end + 1):
            step(t)


class Wide:
    def __init__(self, ref):
        self.ref = ref

    def __getitem__(self, key):
        r, xs = key if isinstance(key, tuple) else (key, slice(None))
        return jnp.concatenate([self.ref[r, 0, xs, :], self.ref[r, 1, xs, :]], axis=1)

    def __setitem__(self, key, value):
        r, xs = key if isinstance(key, tuple) else (key, slice(None))
        self.ref[r, 0, xs, :] = value[:, :LANES]
        self.ref[r, 1, xs, :] = value[:, LANES:]


class Level:
    def __init__(self, s, g, kx, ky, kz, d, w, f, step=2):
        self.s, self.g, self.step = s, g, step
        self.kx, self.ky, self.kz, self.d, self.w, self.f = kx, ky, kz, d, w, f

    def beside(self, u, r):
        here = u[r]
        kx, kz = self.kx[r], self.kz[r]
        a = kx * x_up(here, self.s) + x_down(kx * here, self.s)
        b = kz * z_up(here, self.g) + z_down(kz * here, self.g)
        return a + b + (self.ky[r + 1] * u[r + 1] + self.ky[r] * u[r - 1])

    def weigh(self, first, last):
        def body(r):
            self.w[r] = DAMPING * inverse(self.d[r])

        each(first, last, self.step, body)

    def first(self, u, first, last):
        def body(r):
            u[r] = self.w[r] * self.f[r]

        each(first, last, self.step, body)

    def swept(self, u, r):
        return (1.0 / 3.0) * u[r] + self.w[r] * (self.f[r] + self.beside(u, r))

    def sweep(self, u, v, first, last):
        def body(r):
            v[r] = self.swept(u, r)

        each(first, last, self.step, body)

    def residual(self, u, r):
        return self.f[r] + self.beside(u, r) - self.d[r] * u[r]

    def residual_pairs(self, u, out, first, count):
        def body(j):
            out[j] = self.residual(u, first + 2 * j) + self.residual(u, first + 2 * j + 1)

        each(0, count - 1, self.step // 2, body)


def z_pairs(low, g):
    return lambda a: a + jnp.where(low, z_up(a, g), z_down(a, g))


def coarse_coefficients(level, r, x_count):
    even, odd = pl.ds(0, x_count, stride=2), pl.ds(1, x_count, stride=2)
    g = level.g
    low = (lax.broadcasted_iota(jnp.int32, (x_count, WIDE), 1) & g) == 0
    z_pair = z_pairs(low, g)

    def all_x(ref, row):
        return ref[row, even] + ref[row, odd]

    kx = level.kx[r, odd] + level.kx[r + 1, odd]
    inner = level.kx[r, even] + level.kx[r + 1, even] + all_x(level.ky, r + 1)
    kz = all_x(level.kz, r) + all_x(level.kz, r + 1)
    d = all_x(level.d, r) + all_x(level.d, r + 1)
    d = d - 2.0 * (inner + jnp.where(low, kz, 0.0))
    return z_pair(kx), coarse_sum(level.ky, r + 2, x_count, g), jnp.where(low, z_up(kz, g), kz), z_pair(d)


def coarse_sum(ref, r, x_count, g):
    even, odd = pl.ds(0, x_count, stride=2), pl.ds(1, x_count, stride=2)
    low = (lax.broadcasted_iota(jnp.int32, (x_count, WIDE), 1) & g) == 0
    return z_pairs(low, g)(ref[r, even] + ref[r, odd])


def correct(u, v, e, t, x_count, first, last, to):
    def body(j):
        part = e[j]
        t[j, pl.ds(0, x_count, stride=2)] = part
        t[j, pl.ds(1, x_count, stride=2)] = part
        wide = t[j]
        r = to + 2 * (j - first)
        v[r] = u[r] + wide
        v[r + 1] = u[r + 1] + wide

    each(first, last, 2, body)


def pick_lanes(a, lanes):
    return jnp.take_along_axis(a, lanes, axis=1, mode="promise_in_bounds")


def prepare_kernel(plan, phase_in, density_in, rhs_in, *refs):
    gx = plan.gx
    halves, sources, (phase, density, rhs, sems) = refs[:gx], refs[gx : 2 * gx], refs[2 * gx :]
    pairs = ((phase_in, phase), (density_in, density), (rhs_in, rhs))
    copies = [pltpu.make_async_copy(a, b, sems.at[k]) for k, (a, b) in enumerate(pairs)]
    for copy in copies:
        copy.start()
    for copy in copies:
        copy.wait()
    here = lax.axis_index("gx")
    by, px = plan.by, plan.px
    for k, (half, source) in enumerate(zip(halves, sources)):
        rows = pl.ds(plan.start_of(here ^ k), by)
        for p in range(px):
            factor = jnp.where(phase[p, rows, :] == 1, 500.0, 0.5).astype(F32)
            half[pl.ds(p, by, stride=px), :] = factor * density[p, rows, :]
            source[pl.ds(p, by, stride=px), :] = rhs[0, p, rows, :]


def gather_kernel(plan, count, *refs):
    parts, (c, *sets) = refs[: plan.gx], refs[plan.gx :]
    block = plan.block_here()
    for k, part in enumerate(parts):
        c[k] = part[...]
        for one, out in enumerate(sets):
            first = jnp.where(plan.is_up(block, 1, one), plan.by - count, 0)
            out[k] = part[pl.ds(first, count)]


class Pieces:
    def __init__(self, plan, refs):
        self.plan = plan
        self.c, self.zc, self.sides, self.zsides = refs

    def each_row(self, count, put):
        plan = self.plan
        by, px, gx = plan.by, plan.px, plan.gx
        block = plan.block_here()

        def take(a, b, at, other, r, to):
            for k in range(gx):
                xs = pl.ds(pl.multiple_of((other ^ k) * px, px), px)
                for s, ref in enumerate((a, b)):
                    put(to, s, xs, ref[at + k, r])

        each(0, by - 1, 4, lambda r: take(self.c, self.zc, 0, lax.axis_index("gx"), r, r + HALO))
        up_first = plan.is_up(block, 1, 0)
        for at, nearby, to in (
            (jnp.where(up_first, gx, 0), plan.gx_of(block - 1), HALO - count),
            (jnp.where(up_first, 0, gx), plan.gx_of(block + 1), HALO + by),
        ):
            each(0, count - 1, 4, lambda r: take(self.sides, self.zsides, at, nearby, r, r + to))


def compress(stage, g):
    halves, _, rows, _ = stage.shape
    width = LANES // g
    cell = lax.broadcasted_iota(jnp.int32, (rows, LANES), 1)
    lanes, place = lax.rem(g * cell, LANES), lax.div(cell, width)
    total = pick_lanes(stage[0, 0], lanes)
    for k in range(1, 2 * halves):
        total = jnp.where(place == k, pick_lanes(stage[k // 2, k % 2], lanes), total)
    return total


def coefficient_kernel(plan, *refs):
    pieces, pack, refs = Pieces(plan, refs[:4]), refs[4], refs[5:]
    kx0, ky0, kz0, d0, w0, kx1, ky1, kz1, w1, d1 = [Wide(r) for r in refs[:10]]
    h0, face = [Wide(r) for r in refs[10:12]]
    stage = refs[12]
    nx, by, rows, px = plan.nx, plan.by, plan.rows, plan.px
    shape = (nx, WIDE)
    block = plan.block_here()
    base = block * by - HALO
    y_count, z_count = plan.by * plan.blocks, plan.nz * plan.gz

    x = lax.broadcasted_iota(jnp.int32, shape, 0)
    lane = lax.broadcasted_iota(jnp.int32, shape, 1)
    core = lax.axis_index("gz")
    if plan.paired:
        z = lax.rem(core * LANES + lane, WIDE)
    else:
        z = core * LANES + jnp.where(lane < LANES + LANES // 2, lane, lane - WIDE)
    x_top, x_bottom = x == nx - 1, x == 0
    z_top, z_bottom = z == z_count - 1, z == 0
    z_shut = (z < 0) | (z >= z_count - 1)
    z_out = (z < 0) | (z >= z_count)

    def put(to, s, xs, tile):
        y = base + to
        tile = jnp.where((y >= 0) & (y < y_count), tile, 0.5)
        if not plan.paired:
            tile = jnp.where(z_out[:px, s * LANES : (s + 1) * LANES], 0.5, tile)
        h0.ref[to, s, xs, :] = tile

    pieces.each_row(HALO, put)

    @pl.when(block == 0)
    def _():
        h0[HALO - 1] = h0[HALO]

    @pl.when(block == plan.blocks - 1)
    def _():
        h0[HALO + by] = h0[HALO + by - 1]

    def is_open(r):
        y = base + r
        return (y >= 0) & (y < y_count - 1)

    first_face = inverse(h0[0] + h0[1])
    face[1] = first_face
    ky0[1] = jnp.where(is_open(0), first_face, 0.0)

    def faces(j):
        yd = face[2 * j - 1]
        for r in (2 * j - 1, 2 * j):
            h = h0[r]
            alone = 0.5 * inverse(h)
            xu = inverse(h + jnp.where(x_top, h, x_up(h)))
            xd = jnp.where(x_bottom, alone, x_down(xu))
            yu = inverse(h + h0[r + 1])
            zu = inverse(h + jnp.where(z_top, h, z_up(h, 1)))
            zd = jnp.where(z_bottom, alone, z_down(zu, 1))
            d = xu + xd + yu + yd + zu + zd
            kx0[r] = jnp.where(x_top, 0.0, xu)
            ky0[r + 1] = jnp.where(is_open(r), yu, 0.0)
            kz0[r] = jnp.where(z_shut, 0.0, zu)
            d0[r], w0[r] = d, DAMPING * inverse(d)
            yd = yu
        face[2 * j + 1] = yd

    fine = Level(1, 1, kx0, ky0, kz0, d0, w0, None)
    own = by // 2
    half_x = nx // 2

    def coarsen(j):
        kx1[j], ky1[j + 1], kz1[j], d1[j] = coarse_coefficients(fine, 2 * j - 1, half_x)

    wave((coarsen, 1, own + 6, 1), (faces, 1, own + 6, 0))
    ky1[1] = coarse_sum(ky0, 1, half_x, 1)
    middle = Level(1, 2, kx1, ky1, kz1, d1, w1, None, 8)
    middle.weigh(1, own + 6)

    quarter_x = nx // 4
    part = own // 4
    for j in range(2 * part):
        for t, a in enumerate(coarse_coefficients(middle, 4 + 2 * j, quarter_x)):
            xs = pl.ds((t * part + j % part) * quarter_x, quarter_x)
            stage[j // part, 0, xs, :] = a[:, :LANES]
            stage[j // part, 1, xs, :] = a[:, LANES:]
    pack[...] = compress(stage, 4)


def smooth_kernel(plan, *refs):
    near_count = 1 if plan.paired else 2
    packed, refs = refs[0], refs[1:]
    kx0, ky0, kz0, d0, w0, kx1, ky1, kz1, w1, d1 = [Wide(r) for r in refs[:10]]
    pieces, refs = Pieces(plan, refs[10:14]), refs[4:]
    pack, nears, refs = refs[10], refs[11 : 11 + near_count], refs[11 + near_count :]
    f0, ub, f1, u1 = [Wide(r) for r in refs[:4]]
    ua, r0, uc, r1 = [Wide(r) for r in refs[4:8]]
    stage, near_stage = refs[8], refs[9]
    nx, by = plan.nx, plan.by
    own = by // 2
    half_x, quarter_x = nx // 2, nx // 4

    def put(to, s, xs, tile):
        f0.ref[to, s, xs, :] = tile

    pieces.each_row(HALO_RHS, put)
    fine = Level(1, 1, kx0, ky0, kz0, d0, w0, f0)

    def first(j):
        for r in (2 * j - 1, 2 * j):
            ua[r] = w0[r] * f0[r]

    def sweep(j):
        ub[2 * j] = fine.swept(ua, 2 * j)
        ub[2 * j + 1] = fine.swept(ua, 2 * j + 1)

    def residual(j):
        r0[j] = fine.residual(ub, 2 * j - 1) + fine.residual(ub, 2 * j)

    def restrict(j):
        f1[j] = coarse_sum(r0, j, half_x, 1)

    wave(
        (restrict, 2, own + 5, 4),
        (residual, 2, own + 5, 3),
        (sweep, 1, own + 5, 2),
        (first, 1, own + 6, 0),
    )
    middle = Level(1, 2, kx1, ky1, kz1, d1, w1, f1, 8)
    middle.first(uc, 2, own + 5)
    middle.sweep(uc, u1, 3, own + 4)

    middle.residual_pairs(u1, r1, 4, own // 2)

    own2 = own // 2
    part = own2 // 2
    for j in range(own2):
        a = coarse_sum(r1, j, quarter_x, 2)
        xs = pl.ds(j % part * quarter_x, quarter_x)
        stage[j // part, 0, xs, :] = a[:, :LANES]
        stage[j // part, 1, xs, :] = a[:, LANES:]
    size = pack.shape[0]
    total = jnp.concatenate([compress(stage, 4), packed[...]], axis=0)
    pack[...] = total

    block, core = plan.block_here(), lax.axis_index("gz")
    for one, out in enumerate(nears):
        row = jnp.where(plan.is_up(block, 1, core if plan.paired else one), own, 5)
        for k, (ref, r) in enumerate(((u1, row), (u1, row + 1), (u1, row + 2), (f1, row + 1))):
            for s in range(2):
                near_stage[0, s, pl.ds(k * half_x, half_x), :] = ref.ref[r, s]
        out[pl.ds(0, size), :] = total
        out[pl.ds(size, 4 * half_x), :] = compress(near_stage, 2)


def up_kernel(plan, pack, mine, theirs, *refs):
    refs, out, scratch = refs[:13], refs[13], refs[14:]
    kx0, ky0, kz0, d0, w0, kx1, ky1, kz1, w1, f0, u0, f1_in, u1_in = [Wide(r) for r in refs]
    stage = scratch[0]
    wide = [Wide(r) for r in scratch[1:]]
    f2, kx2, ky2, kz2, d2, w2, ua2, ub2, r2 = wide[:9]
    f3, kx3, ky3, kz3, d3, w3, ua3, ub3 = wide[9:17]
    t1, t0, f1, ua1, ub1, ua0, ub0, uc0 = wide[17:]
    nx, by = plan.nx, plan.by
    own, own2 = by // 2, by // 4
    part = own2 // 2
    half_x, quarter_x = nx // 2, nx // 4
    size = pack.shape[0]
    side = size + 4 * half_x
    core = lax.axis_index("gz")
    block = plan.block_here()
    here = lax.axis_index("gx")
    turn = 1 if plan.paired else 0

    for r in range(2, own + 6):
        f1[r] = f1_in[r]
    for r in range(3, own + 5):
        ua1[r] = u1_in[r]

    ups = {k: plan.is_up(block, k, core if plan.paired else 0) for k in range(1, FAR + 1)}
    stage[FAR] = pack[...]
    for k, up in ups.items():
        at = 0 if k == 1 else side + (k - 2) * size
        stage[jnp.where(up, FAR + k, FAR - k)] = mine[pl.ds(at, size), :]
        stage[jnp.where(up, FAR - k, FAR + k)] = theirs[pl.ds(at, size), :]
    for ref, up, half_turn in ((mine, ups[1], 0), (theirs, jnp.logical_not(ups[1]), turn)):
        row = jnp.where(up, own + 5, 0)
        for k, (to, r) in enumerate(((ua1, row), (ua1, row + 1), (ua1, row + 2), (f1, row + 1))):
            row_in = ref[pl.ds(size + k * half_x, half_x), :]
            lane = lax.broadcasted_iota(jnp.int32, row_in.shape, 1)
            for s in range(2):
                to.ref[r, s ^ half_turn] = pick_lanes(row_in, lax.div(lane, 2) + s * (LANES // 2))

    lane = lax.broadcasted_iota(jnp.int32, (size, LANES), 1)
    lanes = [lax.div(lane, 4) + k * (LANES // 4) for k in range(4)]

    def expand(k):
        there = block + k - FAR
        exists = (there >= 0) & (there < plan.blocks)
        swapped = 0
        if plan.paired and k != FAR:
            swapped = jnp.where(ups[abs(k - FAR)] == (k > FAR), 0, 1)
        rows = stage[k]
        for quarter in range(4):
            part_of, half = divmod(quarter, 2)
            a = pick_lanes(rows, lanes[quarter])
            for t, ref in enumerate((f2, kx2, ky2, kz2, d2)):
                for j in range(part):
                    at = (t * part + j) * quarter_x
                    b = a[at : at + quarter_x]
                    if t == 2:
                        b = jnp.where(exists, b, 0.0)
                    r = k * own2 + part_of * part + j + (1 if t == 2 else 0)
                    ref.ref[r, swapped if half == 0 else 1 - swapped] = b

    for k in range(2 * FAR + 1):
        expand(k)

    rows2 = (2 * FAR + 1) * own2
    two = Level(1, 4, kx2, ky2, kz2, d2, w2, f2, 14)
    two.weigh(0, rows2 - 1)
    two.first(ua2, 0, rows2 - 1)
    two.sweep(ua2, ub2, 1, rows2 - 2)
    two.residual_pairs(ub2, r2, 2, rows2 // 2 - 2)

    x = lax.broadcasted_iota(jnp.int32, (quarter_x, WIDE), 0)
    even_x = (x & 1) == 0
    low = (lax.broadcasted_iota(jnp.int32, (quarter_x, WIDE), 1) & 4) == 0
    z_pair = z_pairs(low, 4)

    def x_pair(a):
        return a + jnp.where(even_x, x_up(a), x_down(a))

    last3 = rows2 // 2 - 2

    def coarsen(j):
        r = 2 * j
        kx = kx2[r] + kx2[r + 1]
        kz = kz2[r] + kz2[r + 1]
        inner = ky2[r + 1] + jnp.where(even_x, kx, 0.0) + jnp.where(low, kz, 0.0)
        f3[j] = z_pair(x_pair(r2[j - 1]))
        kx3[j] = z_pair(jnp.where(even_x, x_up(kx), kx))
        ky3[j + 1] = z_pair(x_pair(ky2[r + 2]))
        kz = x_pair(kz)
        kz3[j] = jnp.where(low, z_up(kz, 4), kz)
        d3[j] = z_pair(x_pair(d2[r] + d2[r + 1] - 2.0 * inner))

    each(1, last3, 6, coarsen)
    three = Level(2, 8, kx3, ky3, kz3, d3, w3, f3, 16)
    three.weigh(1, last3)
    three.first(ua3, 1, last3)
    three.sweep(ua3, ub3, 2, last3 - 1)
    three.sweep(ub3, ua3, 3, last3 - 2)
    three.sweep(ua3, ub3, 4, last3 - 3)

    first2 = FAR * own2
    for j in range(4, last3 - 2):
        e = ub3[j]
        ua2[2 * j] = ub2[2 * j] + e
        ua2[2 * j + 1] = ub2[2 * j + 1] + e
    two.sweep(ua2, ub2, first2 - 3, first2 + own2 + 2)
    two.sweep(ub2, ua2, first2 - 2, first2 + own2 + 1)

    one = Level(1, 2, kx1, ky1, kz1, None, w1, f1, 8)
    correct(ua1, ub1, ua2, t1, quarter_x, first2 - 2, first2 + own2 + 1, 0)
    one.sweep(ub1, ua1, 1, own + 6)
    one.sweep(ua1, ub1, 2, own + 5)

    finest = Level(1, 1, kx0, ky0, kz0, d0, w0, f0)

    def corrected(j):
        part = ub1[j]
        t0[j, pl.ds(0, half_x, stride=2)] = part
        t0[j, pl.ds(1, half_x, stride=2)] = part
        both = t0[j]
        ua0[2 * j - 1] = u0[2 * j - 1] + both
        ua0[2 * j] = u0[2 * j] + both

    def sweep(j):
        ub0[2 * j - 1] = finest.swept(ua0, 2 * j - 1)
        ub0[2 * j] = finest.swept(ua0, 2 * j)

    def sweep_again(j):
        uc0[2 * j] = finest.swept(ub0, 2 * j)
        uc0[2 * j + 1] = finest.swept(ub0, 2 * j + 1)

    def finish(j):
        for r in (2 * j - 1, 2 * j):
            scaled = d0[r] * uc0[r]
            rest = f0[r] + finest.beside(uc0, r) - scaled
            for s in range(plan.gx):
                part = slice(s * plan.px, (s + 1) * plan.px)
                out[s ^ here, r - HALO, 0] = scaled[part, :LANES]
                out[s ^ here, r - HALO, 1] = rest[part, :LANES]

    wave(
        (finish, 4, own + 3, 5),
        (sweep_again, 3, own + 3, 4),
        (sweep, 3, own + 4, 2),
        (corrected, 2, own + 5, 0),
    )


def place_kernel(plan, *refs):
    parts, (scaled, residual) = refs[: plan.gx], refs[plan.gx :]
    here = lax.axis_index("gx")
    by, px = plan.by, plan.px
    for k, part in enumerate(parts):
        rows = pl.ds(plan.start_of(here ^ k), by)
        for p in range(px):
            scaled[0, p, rows, :] = part[pl.ds(p, by, stride=2 * px), :]
            residual[0, p, rows, :] = part[pl.ds(px + p, by, stride=2 * px), :]


def in_vmem(*shape):
    return pltpu.VMEM(shape, F32)


def call(kernel, out_shape, scratch=(), work=0, **more):
    if work:
        more["cost_estimate"] = pl.CostEstimate(flops=0, bytes_accessed=work, transcendentals=0)
    return pl.pallas_call(
        kernel,
        out_shape=out_shape,
        scratch_shapes=list(scratch),
        compiler_params=pltpu.CompilerParams(vmem_limit_bytes=VMEM_LIMIT),
        **more,
    )


def pinned(*arrays, where=pltpu.VMEM):
    return [pltpu.with_memory_space_constraint(a, where) for a in arrays]


def beside_in_z(plan, a):
    count = plan.gz
    if plan.paired:
        return lax.ppermute(a, "gz", [(0, 1), (1, 0)])
    cut = LANES // 2
    right = lax.ppermute(a[..., :cut], "gz", [(i + 1, i) for i in range(count - 1)])
    left = lax.ppermute(a[..., cut:], "gz", [(i, i + 1) for i in range(count - 1)])
    return jnp.concatenate([right, left], axis=-1)


def exchange(plan, parts):
    got = [parts[0]] * plan.gx
    for k in range(plan.gx - 1, 0, -1):
        got[k] = lax.ppermute(parts[k], "gx", [(i, i ^ k) for i in range(plan.gx)])
    return got


def pairs_of(plan, k, one):
    partner = list(range(plan.blocks))
    for b in range(plan.blocks - k):
        if b // k % 2 == one:
            partner[b], partner[b + k] = b + k, b
    alone = [b for b in range(plan.blocks) if partner[b] == b]
    for a, b in zip(alone[::2], alone[1::2]):
        partner[a], partner[b] = b, a
    return [(plan.device(a), plan.device(b)) for a, b in enumerate(partner)]


def swap_blocks(plan, a, k, one):
    return lax.ppermute(a, ("gx", "gy"), pairs_of(plan, k, one))


def swap_blocks_apart(plan, a, k):
    pairs = [(2 * p + one, 2 * q + one) for one in range(2) for p, q in pairs_of(plan, k, one)]
    return lax.ppermute(a, ("gx", "gy", "gz"), pairs)


def far_blocks(plan, pack, nears):
    def line(move, near):
        parts = [move(pack, k) for k in range(FAR, 1, -1)] + [move(near, 1)]
        return jnp.concatenate(parts[::-1], axis=0)

    if plan.paired:
        mine = line(functools.partial(swap_blocks_apart, plan), nears[0])
        return mine, beside_in_z(plan, mine)
    return [line(functools.partial(swap_blocks, plan, one=one), nears[one]) for one in range(2)]


def after(arrays, other):
    shapes = [in_vmem(*a.shape) for a in arrays]
    pairs = {k: k for k in range(len(arrays))}
    return call(lambda *refs: None, shapes, input_output_aliases=pairs)(*pinned(*arrays, other))


def pieces(plan, parts, count):
    c, *sets = call(
        functools.partial(gather_kernel, plan, count),
        [in_vmem(plan.gx, plan.by, plan.px, LANES)] + [in_vmem(plan.gx, count, plan.px, LANES)] * 2,
    )(*pinned(*[a.reshape(plan.by, plan.px, LANES) for a in parts]))
    sides = jnp.concatenate([swap_blocks(plan, a, 1, one) for one, a in enumerate(sets)], axis=0)
    return pinned(c, beside_in_z(plan, c), sides, beside_in_z(plan, sides))


def on_device(plan, phase, density, rhs):
    nx, by, rows, px, gx = plan.nx, plan.by, plan.rows, plan.px, plan.gx
    own, own2 = by // 2, by // 4
    size = 5 * (own2 // 2) * (nx // 4)
    head = size // 5
    side = size + 4 * (nx // 2)

    def level0(n):
        return in_vmem(n, 2, nx, LANES)

    def level1(n):
        return in_vmem(n, 2, nx // 2, LANES)

    block = (px, plan.ny, LANES)
    outside = pl.BlockSpec(memory_space=pltpu.HBM)
    parts = call(
        functools.partial(prepare_kernel, plan),
        [in_vmem(by * px, LANES)] * (2 * gx),
        [pltpu.VMEM(block, jnp.int32), in_vmem(*block), in_vmem(1, *block), pltpu.SemaphoreType.DMA((3,))],
        in_specs=[outside] * 3,
    )(*pinned(phase, density, rhs, where=pltpu.HBM))
    halves = exchange(plan, parts[:gx])
    sources = exchange(plan, parts[gx : gx + 1] + after(parts[gx + 1 :], halves[1]))
    halves = pieces(plan, halves, HALO)
    sources = pieces(plan, sources, HALO_RHS)

    packed, *coefs = call(
        functools.partial(coefficient_kernel, plan),
        [in_vmem(size - head, LANES)] + [level0(rows)] * 5 + [level1(own + 8)] * 5,
        [level0(rows)] * 2 + [in_vmem(2, 2, size - head, LANES)],
        work=9_000_000,
    )(*halves)
    near_count = 1 if plan.paired else 2
    pack, *rest = call(
        functools.partial(smooth_kernel, plan),
        [in_vmem(size, LANES)] + [in_vmem(side, LANES)] * near_count + [level0(rows)] * 2 + [level1(own + 8)] * 2,
        [level0(rows), level0(own + 8), level1(own + 8), level1(own2)]
        + [in_vmem(2, 2, head, LANES), in_vmem(1, 2, 4 * (nx // 2), LANES)],
        work=7_000_000,
    )(*pinned(packed, *coefs), *sources)
    nears, fields = rest[:near_count], coefs[:9] + rest[near_count:]

    mine, theirs = far_blocks(plan, pack, nears)
    rows2 = (2 * FAR + 1) * own2
    scratch = [in_vmem(2 * FAR + 1, size, LANES)]
    scratch += [in_vmem(rows2 + 1, 2, nx // 4, LANES)] * 9 + [in_vmem(rows2 // 2 + 1, 2, nx // 4, LANES)] * 8
    scratch += [level1(rows2), level0(own + 8)] + [level1(own + 8)] * 3 + [level0(rows)] * 3
    (result,) = call(
        functools.partial(up_kernel, plan), [in_vmem(gx, by, 2, px, LANES)], scratch
    )(*pinned(pack, mine, theirs, *fields))

    parts = exchange(plan, [result[k].reshape(2 * by * px, LANES) for k in range(gx)])
    return call(
        functools.partial(place_kernel, plan),
        [jax.ShapeDtypeStruct((1, px, plan.ny, LANES), F32)] * 2,
    )(*pinned(*parts))


def solution(mesh):
    sizes = [mesh.shape[a] for a in ("gx", "gy", "gz")]

    def local(phase, density, rhs):
        return tuple(on_device(Plan(sizes, phase.shape), phase, density, rhs))

    in_specs = (P("gx", "gy", "gz"), P("gx", "gy", "gz"), P(None, "gx", "gy", "gz"))
    out_specs = (P(None, "gx", "gy", "gz"), P(None, "gx", "gy", "gz"))
    return jax.shard_map(local, mesh=mesh, in_specs=in_specs, out_specs=out_specs, check_vma=False)
```

```python
import functools

import jax
import jax.numpy as jnp
from jax import lax
from jax.experimental import pallas as pl
from jax.experimental.pallas import tpu as pltpu
from jax.sharding import PartitionSpec as P


DAMPING = 2.0 / 3.0
LANES = 128
WIDE = 256
HALO = 7
HALO_RHS = 6
FAR = 3
F32 = jnp.float32
VMEM_LIMIT = 24 * 1024 * 1024


class Plan:
    def __init__(self, sizes, shape):
        self.gx, self.gy, self.gz = sizes
        self.px, self.ny, self.nz = shape
        self.nx = self.px * self.gx
        self.by = self.ny // self.gx
        self.blocks = self.gx * self.gy
        self.rows = self.by + 2 * HALO
        self.paired = self.gz == 2
        self.ring = [0, 1, 3, 2] if self.gx == 4 else list(range(self.gx))
        self.place = [self.ring.index(i) for i in range(self.gx)]

    def device(self, block):
        j, q = divmod(block, self.gx)
        return self.ring[(q - j) % self.gx] * self.gy + j

    def look_up(self, table, i):
        return sum(jnp.where(i == k, v, 0) for k, v in enumerate(table))

    def start_of(self, i):
        q = lax.rem(self.look_up(self.place, i) + lax.axis_index("gy"), self.gx)
        return pl.multiple_of(q * self.by, self.by)

    def distance(self, slot):
        if self.gx != 4 or slot not in (1, 2):
            return slot
        return jnp.where(lax.rem(lax.axis_index("gz"), 2) == 0, slot, 3 - slot)

    def block_here(self):
        j = lax.axis_index("gy")
        return j * self.gx + lax.rem(self.look_up(self.place, lax.axis_index("gx")) + j, self.gx)

    def gx_of(self, block):
        block = jnp.clip(block, 0, self.blocks - 1)
        j, q = lax.div(block, self.gx), lax.rem(block, self.gx)
        return self.look_up(self.ring, lax.rem(q + self.gx * self.gy - j, self.gx))

    def is_up(self, block, k, one):
        return lax.rem(lax.div(block, k), 2) == one


def x_up(a, s=1):
    return pltpu.roll(a, a.shape[0] - s, 0)


def x_down(a, s=1):
    return pltpu.roll(a, s, 0)


def z_up(a, g):
    return pltpu.roll(a, a.shape[1] - g, 1)


def z_down(a, g):
    return pltpu.roll(a, g, 1)


def inverse(a):
    r = pl.reciprocal(a, approx=True)
    return r * (2.0 - a * r)


def each(first, last, step, body):
    count = last + 1 - first
    if count <= 2 * step:
        for i in range(first, last + 1):
            body(i)
        return

    def go(c, _):
        for k in range(step):
            body(first + c * step + k)
        return 0

    lax.fori_loop(0, count // step, go, 0)
    for i in range(first + count // step * step, last + 1):
        body(i)


def wave(*stages):
    start = min(first + delay for _, first, _, delay in stages)
    end = max(last + delay for _, _, last, delay in stages)
    full = max(first + delay for _, first, _, delay in stages)
    full_end = min(last + delay for _, _, last, delay in stages)

    def step(t):
        for body, first, last, delay in stages:
            if first <= t - delay <= last:
                body(t - delay)

    def all_of_them(t, _):
        for body, _, _, delay in stages:
            body(t - delay)
        return 0

    if full_end - full < 3:
        full = full_end = end + 1
    for t in range(start, min(full, end + 1)):
        step(t)
    if full <= end:
        lax.fori_loop(full, full_end + 1, all_of_them, 0)
        for t in range(full_end + 1, end + 1):
            step(t)


class Wide:
    def __init__(self, ref):
        self.ref = ref

    def __getitem__(self, key):
        r, xs = key if isinstance(key, tuple) else (key, slice(None))
        return jnp.concatenate([self.ref[r, 0, xs, :], self.ref[r, 1, xs, :]], axis=1)

    def __setitem__(self, key, value):
        r, xs = key if isinstance(key, tuple) else (key, slice(None))
        self.ref[r, 0, xs, :] = value[:, :LANES]
        self.ref[r, 1, xs, :] = value[:, LANES:]


class Level:
    def __init__(self, s, g, kx, ky, kz, d, w, f, step=2):
        self.s, self.g, self.step = s, g, step
        self.kx, self.ky, self.kz, self.d, self.w, self.f = kx, ky, kz, d, w, f

    def beside(self, u, r):
        here = u[r]
        kx, kz = self.kx[r], self.kz[r]
        a = kx * x_up(here, self.s) + x_down(kx * here, self.s)
        b = kz * z_up(here, self.g) + z_down(kz * here, self.g)
        return a + b + (self.ky[r + 1] * u[r + 1] + self.ky[r] * u[r - 1])

    def weigh(self, first, last):
        def body(r):
            self.w[r] = DAMPING * inverse(self.d[r])

        each(first, last, self.step, body)

    def first(self, u, first, last):
        def body(r):
            u[r] = self.w[r] * self.f[r]

        each(first, last, self.step, body)

    def swept(self, u, r):
        return (1.0 / 3.0) * u[r] + self.w[r] * (self.f[r] + self.beside(u, r))

    def sweep(self, u, v, first, last):
        def body(r):
            v[r] = self.swept(u, r)

        each(first, last, self.step, body)

    def residual(self, u, r):
        return self.f[r] + self.beside(u, r) - self.d[r] * u[r]

    def residual_pairs(self, u, out, first, count):
        def body(j):
            out[j] = self.residual(u, first + 2 * j) + self.residual(u, first + 2 * j + 1)

        each(0, count - 1, self.step // 2, body)


def z_pairs(low, g):
    return lambda a: a + jnp.where(low, z_up(a, g), z_down(a, g))


def coarse_coefficients(level, r, x_count):
    even, odd = pl.ds(0, x_count, stride=2), pl.ds(1, x_count, stride=2)
    g = level.g
    low = (lax.broadcasted_iota(jnp.int32, (x_count, WIDE), 1) & g) == 0
    z_pair = z_pairs(low, g)

    def all_x(ref, row):
        return ref[row, even] + ref[row, odd]

    kx = level.kx[r, odd] + level.kx[r + 1, odd]
    inner = level.kx[r, even] + level.kx[r + 1, even] + all_x(level.ky, r + 1)
    kz = all_x(level.kz, r) + all_x(level.kz, r + 1)
    d = all_x(level.d, r) + all_x(level.d, r + 1)
    d = d - 2.0 * (inner + jnp.where(low, kz, 0.0))
    return z_pair(kx), coarse_sum(level.ky, r + 2, x_count, g), jnp.where(low, z_up(kz, g), kz), z_pair(d)


def coarse_sum(ref, r, x_count, g):
    even, odd = pl.ds(0, x_count, stride=2), pl.ds(1, x_count, stride=2)
    low = (lax.broadcasted_iota(jnp.int32, (x_count, WIDE), 1) & g) == 0
    return z_pairs(low, g)(ref[r, even] + ref[r, odd])


def correct(u, v, e, t, x_count, first, last, to):
    def body(j):
        part = e[j]
        t[j, pl.ds(0, x_count, stride=2)] = part
        t[j, pl.ds(1, x_count, stride=2)] = part
        wide = t[j]
        r = to + 2 * (j - first)
        v[r] = u[r] + wide
        v[r + 1] = u[r + 1] + wide

    each(first, last, 2, body)


def pick_lanes(a, lanes):
    return jnp.take_along_axis(a, lanes, axis=1, mode="promise_in_bounds")


def prepare_kernel(plan, phase_in, density_in, rhs_in, *refs):
    outs, (phase, density, rhs, sems) = refs[: plan.gx], refs[plan.gx :]
    pairs = ((phase_in, phase), (density_in, density), (rhs_in, rhs))
    copies = [pltpu.make_async_copy(a, b, sems.at[k]) for k, (a, b) in enumerate(pairs)]
    for copy in copies:
        copy.start()
    for copy in copies:
        copy.wait()
    here = lax.axis_index("gx")
    by, px = plan.by, plan.px
    for slot, out in enumerate(outs):
        rows = pl.ds(plan.start_of(here ^ plan.distance(slot)), by)
        for p in range(px):
            half = jnp.where(phase[p, rows, :] == 1, 500.0, 0.5).astype(F32)
            out[pl.ds(p, by, stride=2 * px), :] = half * density[p, rows, :]
            out[pl.ds(px + p, by, stride=2 * px), :] = rhs[0, p, rows, :]


def gather_kernel(plan, *refs):
    parts, (c, *sets) = refs[: plan.gx], refs[plan.gx :]
    block = plan.block_here()
    for slot, part in enumerate(parts):
        k = plan.distance(slot)
        c[k] = part[...]
        for one, out in enumerate(sets):
            up = plan.is_up(block, 1, one)
            for field, count, at in ((0, HALO, 0), (1, HALO_RHS, HALO)):
                first = jnp.where(up, plan.by - count, 0)
                for r in range(count):
                    out[k, at + r] = part[first + r, field]


def compress(stage, g):
    halves, _, rows, _ = stage.shape
    width = LANES // g
    cell = lax.broadcasted_iota(jnp.int32, (rows, LANES), 1)
    lanes, place = lax.rem(g * cell, LANES), lax.div(cell, width)
    total = pick_lanes(stage[0, 0], lanes)
    for k in range(1, 2 * halves):
        total = jnp.where(place == k, pick_lanes(stage[k // 2, k % 2], lanes), total)
    return total


def down_kernel(plan, c, zc, sides, zsides, *refs):
    near_count = 1 if plan.paired else 2
    pack, nears, refs = refs[0], refs[1 : 1 + near_count], refs[1 + near_count :]
    kx0, ky0, kz0, d0, w0, f0, ub, kx1, ky1, kz1, w1, f1, u1 = [Wide(r) for r in refs[:13]]
    h0, ua, face, r0, uc, r1, d1 = [Wide(r) for r in refs[13:20]]
    stage, near_stage = refs[20:22]
    nx, by, rows, gx, px = plan.nx, plan.by, plan.rows, plan.gx, plan.px
    shape = (nx, WIDE)
    block, here = plan.block_here(), lax.axis_index("gx")
    base = block * by - HALO
    y_count, z_count = plan.by * plan.blocks, plan.nz * plan.gz

    x = lax.broadcasted_iota(jnp.int32, shape, 0)
    lane = lax.broadcasted_iota(jnp.int32, shape, 1)
    core = lax.axis_index("gz")
    if plan.paired:
        z = lax.rem(core * LANES + lane, WIDE)
    else:
        z = core * LANES + jnp.where(lane < LANES + LANES // 2, lane, lane - WIDE)
    x_top, x_bottom = x == nx - 1, x == 0
    z_top, z_bottom = z == z_count - 1, z == 0
    z_shut = (z < 0) | (z >= z_count - 1)
    z_out = (z < 0) | (z >= z_count)

    def put_h(to, s, xs, tile):
        y = base + to
        tile = jnp.where((y >= 0) & (y < y_count), tile, 0.5)
        if not plan.paired:
            tile = jnp.where(z_out[:px, s * LANES : (s + 1) * LANES], 0.5, tile)
        h0.ref[to, s, xs, :] = tile

    def tiles(other):
        return [(k, pl.ds(pl.multiple_of((other ^ k) * px, px), px)) for k in range(gx)]

    def take(r):
        for k, xs in tiles(here):
            for s, ref in enumerate((c, zc)):
                put_h(r + HALO, s, xs, ref[k, r, 0])
                f0.ref[r + HALO, s, xs, :] = ref[k, r, 1]

    def take_side(at, other, to, count, field):
        def one(r):
            for k, xs in tiles(other):
                for s, ref in enumerate((sides, zsides)):
                    if field == 0:
                        put_h(r + to, s, xs, ref[at + k, r])
                    else:
                        f0.ref[r + to, s, xs, :] = ref[at + k, HALO + r]

        each(0, count - 1, 4, one)

    each(0, by - 1, 4, take)
    up_first = plan.is_up(block, 1, 0)
    below, above = jnp.where(up_first, 0, gx), jnp.where(up_first, gx, 0)
    gx_below, gx_above = plan.gx_of(block - 1), plan.gx_of(block + 1)
    take_side(below, gx_below, 0, HALO, 0)
    take_side(above, gx_above, HALO + by, HALO, 0)
    take_side(below, gx_below, HALO - HALO_RHS, HALO_RHS, 1)
    take_side(above, gx_above, HALO + by, HALO_RHS, 1)

    @pl.when(block == 0)
    def _():
        h0[HALO - 1] = h0[HALO]

    @pl.when(block == plan.blocks - 1)
    def _():
        h0[HALO + by] = h0[HALO + by - 1]

    def is_open(r):
        y = base + r
        return (y >= 0) & (y < y_count - 1)

    first_face = inverse(h0[0] + h0[1])
    face[1] = first_face
    ky0[1] = jnp.where(is_open(0), first_face, 0.0)

    def faces(j):
        yd = face[2 * j - 1]
        for r in (2 * j - 1, 2 * j):
            h = h0[r]
            alone = 0.5 * inverse(h)
            xu = inverse(h + jnp.where(x_top, h, x_up(h)))
            xd = jnp.where(x_bottom, alone, x_down(xu))
            yu = inverse(h + h0[r + 1])
            zu = inverse(h + jnp.where(z_top, h, z_up(h, 1)))
            zd = jnp.where(z_bottom, alone, z_down(zu, 1))
            d = xu + xd + yu + yd + zu + zd
            w = DAMPING * inverse(d)
            kx0[r] = jnp.where(x_top, 0.0, xu)
            ky0[r + 1] = jnp.where(is_open(r), yu, 0.0)
            kz0[r] = jnp.where(z_shut, 0.0, zu)
            d0[r], w0[r] = d, w
            ua[r] = w * f0[r]
            yd = yu
        face[2 * j + 1] = yd

    fine = Level(1, 1, kx0, ky0, kz0, d0, w0, f0)

    own = by // 2
    half_x = nx // 2
    middle = Level(1, 2, kx1, ky1, kz1, d1, w1, f1, 8)
    def coarsen(j):
        kx1[j], ky1[j + 1], kz1[j], d1[j] = coarse_coefficients(fine, 2 * j - 1, half_x)

    def restrict(j):
        f1[j] = coarse_sum(r0, j, half_x, 1)

    def sweep(j):
        ub[2 * j] = fine.swept(ua, 2 * j)
        ub[2 * j + 1] = fine.swept(ua, 2 * j + 1)

    def residual(j):
        r0[j] = fine.residual(ub, 2 * j - 1) + fine.residual(ub, 2 * j)

    wave(
        (restrict, 2, own + 5, 4),
        (residual, 2, own + 5, 3),
        (sweep, 1, own + 5, 2),
        (coarsen, 1, own + 6, 1),
        (faces, 1, own + 6, 0),
    )
    ky1[1] = coarse_sum(ky0, 1, half_x, 1)
    middle.weigh(1, own + 6)
    middle.first(uc, 2, own + 5)
    middle.sweep(uc, u1, 3, own + 4)
    middle.residual_pairs(u1, r1, 4, own // 2)

    quarter_x = nx // 4
    own2 = own // 2
    part = own2 // 2
    for j in range(own2):
        fields = (coarse_sum(r1, j, quarter_x, 2),) + coarse_coefficients(middle, 4 + 2 * j, quarter_x)
        for t, a in enumerate(fields):
            xs = pl.ds((t * part + j % part) * quarter_x, quarter_x)
            stage[j // part, 0, xs, :] = a[:, :LANES]
            stage[j // part, 1, xs, :] = a[:, LANES:]
    total = compress(stage, 4)
    pack[...] = total

    size = pack.shape[0]
    for one, out in enumerate(nears):
        row = jnp.where(plan.is_up(block, 1, core if plan.paired else one), own, 5)
        for k, (ref, r) in enumerate(((u1, row), (u1, row + 1), (u1, row + 2), (f1, row + 1))):
            for s in range(2):
                near_stage[0, s, pl.ds(k * half_x, half_x), :] = ref.ref[r, s]
        out[pl.ds(0, size), :] = total
        out[pl.ds(size, 4 * half_x), :] = compress(near_stage, 2)


def up_kernel(plan, pack, mine, theirs, *refs):
    refs, out, scratch = refs[:13], refs[13], refs[14:]
    kx0, ky0, kz0, d0, w0, f0, u0, kx1, ky1, kz1, w1, f1_in, u1_in = [Wide(r) for r in refs]
    stage = scratch[0]
    wide = [Wide(r) for r in scratch[1:]]
    f2, kx2, ky2, kz2, d2, w2, ua2, ub2, r2 = wide[:9]
    f3, kx3, ky3, kz3, d3, w3, ua3, ub3 = wide[9:17]
    t1, t0, f1, ua1, ub1, ua0, ub0, uc0 = wide[17:]
    nx, by = plan.nx, plan.by
    own, own2 = by // 2, by // 4
    part = own2 // 2
    half_x, quarter_x = nx // 2, nx // 4
    size = pack.shape[0]
    side = size + 4 * half_x
    core = lax.axis_index("gz")
    block = plan.block_here()
    here = lax.axis_index("gx")
    turn = 1 if plan.paired else 0

    for r in range(2, own + 6):
        f1[r] = f1_in[r]
    for r in range(3, own + 5):
        ua1[r] = u1_in[r]

    ups = {k: plan.is_up(block, k, core if plan.paired else 0) for k in range(1, FAR + 1)}
    stage[FAR] = pack[...]
    for k, up in ups.items():
        at = 0 if k == 1 else side + (k - 2) * size
        stage[jnp.where(up, FAR + k, FAR - k)] = mine[pl.ds(at, size), :]
        stage[jnp.where(up, FAR - k, FAR + k)] = theirs[pl.ds(at, size), :]
    for ref, up, half_turn in ((mine, ups[1], 0), (theirs, jnp.logical_not(ups[1]), turn)):
        row = jnp.where(up, own + 5, 0)
        for k, (to, r) in enumerate(((ua1, row), (ua1, row + 1), (ua1, row + 2), (f1, row + 1))):
            row_in = ref[pl.ds(size + k * half_x, half_x), :]
            lane = lax.broadcasted_iota(jnp.int32, row_in.shape, 1)
            for s in range(2):
                to.ref[r, s ^ half_turn] = pick_lanes(row_in, lax.div(lane, 2) + s * (LANES // 2))

    lane = lax.broadcasted_iota(jnp.int32, (size, LANES), 1)
    lanes = [lax.div(lane, 4) + k * (LANES // 4) for k in range(4)]

    def expand(k):
        there = block + k - FAR
        exists = (there >= 0) & (there < plan.blocks)
        swapped = 0
        if plan.paired and k != FAR:
            swapped = jnp.where(ups[abs(k - FAR)] == (k > FAR), 0, 1)
        rows = stage[k]
        for quarter in range(4):
            part_of, half = divmod(quarter, 2)
            a = pick_lanes(rows, lanes[quarter])
            for t, ref in enumerate((f2, kx2, ky2, kz2, d2)):
                for j in range(part):
                    at = (t * part + j) * quarter_x
                    b = a[at : at + quarter_x]
                    if t == 2:
                        b = jnp.where(exists, b, 0.0)
                    r = k * own2 + part_of * part + j + (1 if t == 2 else 0)
                    ref.ref[r, swapped if half == 0 else 1 - swapped] = b

    for k in range(2 * FAR + 1):
        expand(k)

    rows2 = (2 * FAR + 1) * own2
    two = Level(1, 4, kx2, ky2, kz2, d2, w2, f2, 14)
    two.weigh(0, rows2 - 1)
    two.first(ua2, 0, rows2 - 1)
    two.sweep(ua2, ub2, 1, rows2 - 2)
    two.residual_pairs(ub2, r2, 2, rows2 // 2 - 2)

    x = lax.broadcasted_iota(jnp.int32, (quarter_x, WIDE), 0)
    even_x = (x & 1) == 0
    low = (lax.broadcasted_iota(jnp.int32, (quarter_x, WIDE), 1) & 4) == 0
    z_pair = z_pairs(low, 4)

    def x_pair(a):
        return a + jnp.where(even_x, x_up(a), x_down(a))

    last3 = rows2 // 2 - 2

    def coarsen(j):
        r = 2 * j
        kx = kx2[r] + kx2[r + 1]
        kz = kz2[r] + kz2[r + 1]
        inner = ky2[r + 1] + jnp.where(even_x, kx, 0.0) + jnp.where(low, kz, 0.0)
        f3[j] = z_pair(x_pair(r2[j - 1]))
        kx3[j] = z_pair(jnp.where(even_x, x_up(kx), kx))
        ky3[j + 1] = z_pair(x_pair(ky2[r + 2]))
        kz = x_pair(kz)
        kz3[j] = jnp.where(low, z_up(kz, 4), kz)
        d3[j] = z_pair(x_pair(d2[r] + d2[r + 1] - 2.0 * inner))

    each(1, last3, 6, coarsen)
    three = Level(2, 8, kx3, ky3, kz3, d3, w3, f3, 16)
    three.weigh(1, last3)
    three.first(ua3, 1, last3)
    three.sweep(ua3, ub3, 2, last3 - 1)
    three.sweep(ub3, ua3, 3, last3 - 2)
    three.sweep(ua3, ub3, 4, last3 - 3)

    first2 = FAR * own2
    for j in range(4, last3 - 2):
        e = ub3[j]
        ua2[2 * j] = ub2[2 * j] + e
        ua2[2 * j + 1] = ub2[2 * j + 1] + e
    two.sweep(ua2, ub2, first2 - 3, first2 + own2 + 2)
    two.sweep(ub2, ua2, first2 - 2, first2 + own2 + 1)

    one = Level(1, 2, kx1, ky1, kz1, None, w1, f1, 8)
    correct(ua1, ub1, ua2, t1, quarter_x, first2 - 2, first2 + own2 + 1, 0)
    one.sweep(ub1, ua1, 1, own + 6)
    one.sweep(ua1, ub1, 2, own + 5)

    finest = Level(1, 1, kx0, ky0, kz0, d0, w0, f0)

    def corrected(j):
        part = ub1[j]
        t0[j, pl.ds(0, half_x, stride=2)] = part
        t0[j, pl.ds(1, half_x, stride=2)] = part
        both = t0[j]
        ua0[2 * j - 1] = u0[2 * j - 1] + both
        ua0[2 * j] = u0[2 * j] + both

    def sweep(j):
        ub0[2 * j - 1] = finest.swept(ua0, 2 * j - 1)
        ub0[2 * j] = finest.swept(ua0, 2 * j)

    def sweep_again(j):
        uc0[2 * j] = finest.swept(ub0, 2 * j)
        uc0[2 * j + 1] = finest.swept(ub0, 2 * j + 1)

    slots = []
    for s in range(plan.gx):
        slot = s ^ here
        if plan.gx == 4:
            for k in (1, 2):
                slot = jnp.where((s ^ here) == k, plan.distance(k), slot)
        slots.append(slot)

    def finish(j):
        for r in (2 * j - 1, 2 * j):
            scaled = d0[r] * uc0[r]
            rest = f0[r] + finest.beside(uc0, r) - scaled
            for s in range(plan.gx):
                part = slice(s * plan.px, (s + 1) * plan.px)
                out[slots[s], r - HALO, 0] = scaled[part, :LANES]
                out[slots[s], r - HALO, 1] = rest[part, :LANES]

    wave(
        (finish, 4, own + 3, 5),
        (sweep_again, 3, own + 3, 4),
        (sweep, 3, own + 4, 2),
        (corrected, 2, own + 5, 0),
    )


def place_kernel(plan, *refs):
    parts, (scaled, residual) = refs[: plan.gx], refs[plan.gx :]
    here = lax.axis_index("gx")
    by, px = plan.by, plan.px
    for slot, part in enumerate(parts):
        rows = pl.ds(plan.start_of(here ^ plan.distance(slot)), by)
        for p in range(px):
            scaled[0, p, rows, :] = part[pl.ds(p, by, stride=2 * px), :]
            residual[0, p, rows, :] = part[pl.ds(px + p, by, stride=2 * px), :]


def in_vmem(*shape):
    return pltpu.VMEM(shape, F32)


def call(kernel, out_shape, scratch=(), **more):
    return pl.pallas_call(
        kernel,
        out_shape=out_shape,
        scratch_shapes=list(scratch),
        compiler_params=pltpu.CompilerParams(vmem_limit_bytes=VMEM_LIMIT),
        **more,
    )


def pinned(*arrays, where=pltpu.VMEM):
    return [pltpu.with_memory_space_constraint(a, where) for a in arrays]


def beside_in_z(plan, a):
    count = plan.gz
    if plan.paired:
        return lax.ppermute(a, "gz", [(0, 1), (1, 0)])
    cut = LANES // 2
    right = lax.ppermute(a[..., :cut], "gz", [(i + 1, i) for i in range(count - 1)])
    left = lax.ppermute(a[..., cut:], "gz", [(i, i + 1) for i in range(count - 1)])
    return jnp.concatenate([right, left], axis=-1)


def exchange(plan, parts):
    got = [parts[0]] * plan.gx
    for slot in range(plan.gx - 1, 0, -1):
        mixed = plan.gx == 4 and slot in (1, 2)
        pairs = []
        for i in range(plan.gx):
            for g in range(plan.gz):
                k = 3 - slot if mixed and g % 2 else slot
                pairs.append((i * plan.gz + g, (i ^ k) * plan.gz + g))
        got[slot] = lax.ppermute(parts[slot], ("gx", "gz"), pairs)
    return got


def pairs_of(plan, k, one):
    partner = list(range(plan.blocks))
    for b in range(plan.blocks - k):
        if b // k % 2 == one:
            partner[b], partner[b + k] = b + k, b
    alone = [b for b in range(plan.blocks) if partner[b] == b]
    for a, b in zip(alone[::2], alone[1::2]):
        partner[a], partner[b] = b, a
    return [(plan.device(a), plan.device(b)) for a, b in enumerate(partner)]


def swap_blocks(plan, a, k, one):
    return lax.ppermute(a, ("gx", "gy"), pairs_of(plan, k, one))


def swap_blocks_apart(plan, a, k):
    pairs = [(2 * p + one, 2 * q + one) for one in range(2) for p, q in pairs_of(plan, k, one)]
    return lax.ppermute(a, ("gx", "gy", "gz"), pairs)


def far_blocks(plan, pack, nears):
    def line(move, near):
        parts = [move(pack, k) for k in range(FAR, 1, -1)] + [move(near, 1)]
        return jnp.concatenate(parts[::-1], axis=0)

    if plan.paired:
        mine = line(functools.partial(swap_blocks_apart, plan), nears[0])
        return mine, beside_in_z(plan, mine)
    return [line(functools.partial(swap_blocks, plan, one=one), nears[one]) for one in range(2)]


def on_device(plan, phase, density, rhs):
    nx, by, rows, px, gx = plan.nx, plan.by, plan.rows, plan.px, plan.gx
    flat = by * 2 * px
    block = (px, plan.ny, LANES)
    outside = pl.BlockSpec(memory_space=pltpu.HBM)
    parts = call(
        functools.partial(prepare_kernel, plan),
        [in_vmem(flat, LANES)] * gx,
        [pltpu.VMEM(block, jnp.int32), in_vmem(*block), in_vmem(1, *block), pltpu.SemaphoreType.DMA((3,))],
        in_specs=[outside] * 3,
    )(*pinned(phase, density, rhs, where=pltpu.HBM))
    parts = [a.reshape(by, 2, px, LANES) for a in exchange(plan, parts)]
    c, *sets = call(
        functools.partial(gather_kernel, plan),
        [in_vmem(gx, by, 2, px, LANES)] + [in_vmem(gx, HALO + HALO_RHS, px, LANES)] * 2,
    )(*pinned(*parts))
    sides = jnp.concatenate([swap_blocks(plan, sets[one], 1, one) for one in (1, 0)], axis=0)
    zc = beside_in_z(plan, c)
    zsides = beside_in_z(plan, sides)

    own, own2 = by // 2, by // 4
    size = 5 * (own2 // 2) * (nx // 4)
    side = size + 4 * (nx // 2)

    def level0(n):
        return in_vmem(n, 2, nx, LANES)

    def level1(n):
        return in_vmem(n, 2, nx // 2, LANES)

    outs = [in_vmem(size, LANES)] + [in_vmem(side, LANES)] * (1 if plan.paired else 2)
    fields = [level0(rows)] * 7 + [level1(own + 8)] * 6
    scratch = [level0(rows)] * 3 + [level0(own + 8), level1(own + 8), level1(own2), level1(own + 8)]
    scratch += [in_vmem(2, 2, size, LANES), in_vmem(1, 2, 4 * (nx // 2), LANES)]
    down = call(functools.partial(down_kernel, plan), outs + fields, scratch)(*pinned(c, zc, sides, zsides))
    pack, nears, fields = down[0], down[1 : len(outs)], down[len(outs) :]

    mine, theirs = far_blocks(plan, pack, nears)
    rows2 = (2 * FAR + 1) * own2
    scratch = [in_vmem(2 * FAR + 1, size, LANES)]
    scratch += [in_vmem(rows2 + 1, 2, nx // 4, LANES)] * 9 + [in_vmem(rows2 // 2 + 1, 2, nx // 4, LANES)] * 8
    scratch += [level1(rows2), level0(own + 8)] + [level1(own + 8)] * 3 + [level0(rows)] * 3
    (result,) = call(
        functools.partial(up_kernel, plan), [in_vmem(gx, by, 2, px, LANES)], scratch
    )(*pinned(pack, mine, theirs, *fields))

    parts = exchange(plan, [result[k].reshape(flat, LANES) for k in range(gx)])
    return call(
        functools.partial(place_kernel, plan),
        [jax.ShapeDtypeStruct((1, px, plan.ny, LANES), F32)] * 2,
    )(*pinned(*parts))


def solution(mesh):
    sizes = [mesh.shape[a] for a in ("gx", "gy", "gz")]

    def local(phase, density, rhs):
        return tuple(on_device(Plan(sizes, phase.shape), phase, density, rhs))

    in_specs = (P("gx", "gy", "gz"), P("gx", "gy", "gz"), P(None, "gx", "gy", "gz"))
    out_specs = (P(None, "gx", "gy", "gz"), P(None, "gx", "gy", "gz"))
    return jax.shard_map(local, mesh=mesh, in_specs=in_specs, out_specs=out_specs, check_vma=False)
```

```python
import functools

import jax
import jax.numpy as jnp
from jax import lax
from jax.experimental import pallas as pl
from jax.experimental.pallas import tpu as pltpu
from jax.sharding import PartitionSpec as P


DAMPING = 2.0 / 3.0
LANES = 128
WIDE = 256
HALO = 7
HALO_RHS = 6
FAR = 3
F32 = jnp.float32
VMEM_LIMIT = 24 * 1024 * 1024


class Plan:
    def __init__(self, sizes, shape):
        self.gx, self.gy, self.gz = sizes
        self.px, self.ny, self.nz = shape
        self.nx = self.px * self.gx
        self.by = self.ny // self.gx
        self.blocks = self.gx * self.gy
        self.rows = self.by + 2 * HALO
        self.paired = self.gz == 2
        self.ring = [0, 1, 3, 2] if self.gx == 4 else list(range(self.gx))
        self.place = [self.ring.index(i) for i in range(self.gx)]

    def device(self, block):
        j, q = divmod(block, self.gx)
        return self.ring[(q - j) % self.gx] * self.gy + j

    def look_up(self, table, i):
        return sum(jnp.where(i == k, v, 0) for k, v in enumerate(table))

    def start_of(self, i):
        q = lax.rem(self.look_up(self.place, i) + lax.axis_index("gy"), self.gx)
        return pl.multiple_of(q * self.by, self.by)

    def distance(self, slot):
        if self.gx != 4 or slot not in (1, 2):
            return slot
        return jnp.where(lax.rem(lax.axis_index("gz"), 2) == 0, slot, 3 - slot)

    def block_here(self):
        j = lax.axis_index("gy")
        return j * self.gx + lax.rem(self.look_up(self.place, lax.axis_index("gx")) + j, self.gx)

    def gx_of(self, block):
        block = jnp.clip(block, 0, self.blocks - 1)
        j, q = lax.div(block, self.gx), lax.rem(block, self.gx)
        return self.look_up(self.ring, lax.rem(q + self.gx * self.gy - j, self.gx))

    def is_up(self, block, k, one):
        return lax.rem(lax.div(block, k), 2) == one


def x_up(a, s=1):
    return pltpu.roll(a, a.shape[0] - s, 0)


def x_down(a, s=1):
    return pltpu.roll(a, s, 0)


def z_up(a, g):
    return pltpu.roll(a, a.shape[1] - g, 1)


def z_down(a, g):
    return pltpu.roll(a, g, 1)


def inverse(a):
    r = pl.reciprocal(a, approx=True)
    return r * (2.0 - a * r)


def each(first, last, step, body):
    count = last + 1 - first
    if count <= 2 * step:
        for i in range(first, last + 1):
            body(i)
        return

    def go(c, _):
        for k in range(step):
            body(first + c * step + k)
        return 0

    lax.fori_loop(0, count // step, go, 0)
    for i in range(first + count // step * step, last + 1):
        body(i)


def wave(*stages):
    start = min(first + delay for _, first, _, delay in stages)
    end = max(last + delay for _, _, last, delay in stages)
    full = max(first + delay for _, first, _, delay in stages)
    full_end = min(last + delay for _, _, last, delay in stages)

    def step(t):
        for body, first, last, delay in stages:
            if first <= t - delay <= last:
                body(t - delay)

    def all_of_them(t, _):
        for body, _, _, delay in stages:
            body(t - delay)
        return 0

    if full_end - full < 3:
        full = full_end = end + 1
    for t in range(start, min(full, end + 1)):
        step(t)
    if full <= end:
        lax.fori_loop(full, full_end + 1, all_of_them, 0)
        for t in range(full_end + 1, end + 1):
            step(t)


class Wide:
    def __init__(self, ref):
        self.ref = ref

    def __getitem__(self, key):
        r, xs = key if isinstance(key, tuple) else (key, slice(None))
        return jnp.concatenate([self.ref[r, 0, xs, :], self.ref[r, 1, xs, :]], axis=1)

    def __setitem__(self, key, value):
        r, xs = key if isinstance(key, tuple) else (key, slice(None))
        self.ref[r, 0, xs, :] = value[:, :LANES]
        self.ref[r, 1, xs, :] = value[:, LANES:]


class Level:
    def __init__(self, s, g, kx, ky, kz, d, w, f, step=2):
        self.s, self.g, self.step = s, g, step
        self.kx, self.ky, self.kz, self.d, self.w, self.f = kx, ky, kz, d, w, f

    def beside(self, u, r):
        here = u[r]
        kx, kz = self.kx[r], self.kz[r]
        a = kx * x_up(here, self.s) + x_down(kx * here, self.s)
        b = kz * z_up(here, self.g) + z_down(kz * here, self.g)
        return a + b + (self.ky[r + 1] * u[r + 1] + self.ky[r] * u[r - 1])

    def weigh(self, first, last):
        def body(r):
            self.w[r] = DAMPING * inverse(self.d[r])

        each(first, last, self.step, body)

    def first(self, u, first, last):
        def body(r):
            u[r] = self.w[r] * self.f[r]

        each(first, last, self.step, body)

    def swept(self, u, r):
        return (1.0 / 3.0) * u[r] + self.w[r] * (self.f[r] + self.beside(u, r))

    def sweep(self, u, v, first, last):
        def body(r):
            v[r] = self.swept(u, r)

        each(first, last, self.step, body)

    def residual(self, u, r):
        return self.f[r] + self.beside(u, r) - self.d[r] * u[r]

    def residual_pairs(self, u, out, first, count):
        def body(j):
            out[j] = self.residual(u, first + 2 * j) + self.residual(u, first + 2 * j + 1)

        each(0, count - 1, self.step // 2, body)


def z_pairs(low, g):
    return lambda a: a + jnp.where(low, z_up(a, g), z_down(a, g))


def coarse_coefficients(level, r, x_count):
    even, odd = pl.ds(0, x_count, stride=2), pl.ds(1, x_count, stride=2)
    g = level.g
    low = (lax.broadcasted_iota(jnp.int32, (x_count, WIDE), 1) & g) == 0
    z_pair = z_pairs(low, g)

    def all_x(ref, row):
        return ref[row, even] + ref[row, odd]

    kx = level.kx[r, odd] + level.kx[r + 1, odd]
    inner = level.kx[r, even] + level.kx[r + 1, even] + all_x(level.ky, r + 1)
    kz = all_x(level.kz, r) + all_x(level.kz, r + 1)
    d = all_x(level.d, r) + all_x(level.d, r + 1)
    d = d - 2.0 * (inner + jnp.where(low, kz, 0.0))
    return z_pair(kx), coarse_sum(level.ky, r + 2, x_count, g), jnp.where(low, z_up(kz, g), kz), z_pair(d)


def coarse_sum(ref, r, x_count, g):
    even, odd = pl.ds(0, x_count, stride=2), pl.ds(1, x_count, stride=2)
    low = (lax.broadcasted_iota(jnp.int32, (x_count, WIDE), 1) & g) == 0
    return z_pairs(low, g)(ref[r, even] + ref[r, odd])


def correct(u, v, e, t, x_count, first, last, to):
    def body(j):
        part = e[j]
        t[j, pl.ds(0, x_count, stride=2)] = part
        t[j, pl.ds(1, x_count, stride=2)] = part
        wide = t[j]
        r = to + 2 * (j - first)
        v[r] = u[r] + wide
        v[r + 1] = u[r + 1] + wide

    each(first, last, 2, body)


def pick_lanes(a, lanes):
    return jnp.take_along_axis(a, lanes, axis=1, mode="promise_in_bounds")


def prepare_kernel(plan, phase_in, density_in, rhs_in, *refs):
    outs, (phase, density, rhs, sems) = refs[: plan.gx], refs[plan.gx :]
    pairs = ((phase_in, phase), (density_in, density), (rhs_in, rhs))
    copies = [pltpu.make_async_copy(a, b, sems.at[k]) for k, (a, b) in enumerate(pairs)]
    for copy in copies:
        copy.start()
    for copy in copies:
        copy.wait()
    here = lax.axis_index("gx")
    by, px = plan.by, plan.px
    for slot, out in enumerate(outs):
        rows = pl.ds(plan.start_of(here ^ plan.distance(slot)), by)
        for p in range(px):
            half = jnp.where(phase[p, rows, :] == 1, 500.0, 0.5).astype(F32)
            out[pl.ds(p, by, stride=2 * px), :] = half * density[p, rows, :]
            out[pl.ds(px + p, by, stride=2 * px), :] = rhs[0, p, rows, :]


def gather_kernel(plan, *refs):
    parts, (c, *sets) = refs[: plan.gx], refs[plan.gx :]
    block = plan.block_here()
    for slot, part in enumerate(parts):
        k = plan.distance(slot)
        c[k] = part[...]
        for one, out in enumerate(sets):
            up = plan.is_up(block, 1, one)
            for field, count, at in ((0, HALO, 0), (1, HALO_RHS, HALO)):
                first = jnp.where(up, plan.by - count, 0)
                for r in range(count):
                    out[k, at + r] = part[first + r, field]


def compress(stage, g):
    halves, _, rows, _ = stage.shape
    width = LANES // g
    cell = lax.broadcasted_iota(jnp.int32, (rows, LANES), 1)
    lanes, place = lax.rem(g * cell, LANES), lax.div(cell, width)
    total = pick_lanes(stage[0, 0], lanes)
    for k in range(1, 2 * halves):
        total = jnp.where(place == k, pick_lanes(stage[k // 2, k % 2], lanes), total)
    return total


def down_kernel(plan, c, zc, sides, zsides, *refs):
    near_count = 1 if plan.paired else 2
    pack, nears, refs = refs[0], refs[1 : 1 + near_count], refs[1 + near_count :]
    kx0, ky0, kz0, d0, w0, f0, ub, kx1, ky1, kz1, w1, f1, u1 = [Wide(r) for r in refs[:13]]
    h0, ua, face, r0, uc, r1, d1 = [Wide(r) for r in refs[13:20]]
    stage, near_stage = refs[20:22]
    nx, by, rows, gx, px = plan.nx, plan.by, plan.rows, plan.gx, plan.px
    shape = (nx, WIDE)
    block, here = plan.block_here(), lax.axis_index("gx")
    base = block * by - HALO
    y_count, z_count = plan.by * plan.blocks, plan.nz * plan.gz

    x = lax.broadcasted_iota(jnp.int32, shape, 0)
    lane = lax.broadcasted_iota(jnp.int32, shape, 1)
    core = lax.axis_index("gz")
    if plan.paired:
        z = lax.rem(core * LANES + lane, WIDE)
    else:
        z = core * LANES + jnp.where(lane < LANES + LANES // 2, lane, lane - WIDE)
    x_top, x_bottom = x == nx - 1, x == 0
    z_top, z_bottom = z == z_count - 1, z == 0
    z_shut = (z < 0) | (z >= z_count - 1)
    z_out = (z < 0) | (z >= z_count)

    def put_h(to, s, xs, tile):
        y = base + to
        tile = jnp.where((y >= 0) & (y < y_count), tile, 0.5)
        if not plan.paired:
            tile = jnp.where(z_out[:px, s * LANES : (s + 1) * LANES], 0.5, tile)
        h0.ref[to, s, xs, :] = tile

    def tiles(other):
        return [(k, pl.ds(pl.multiple_of((other ^ k) * px, px), px)) for k in range(gx)]

    def take(r):
        for k, xs in tiles(here):
            for s, ref in enumerate((c, zc)):
                put_h(r + HALO, s, xs, ref[k, r, 0])
                f0.ref[r + HALO, s, xs, :] = ref[k, r, 1]

    def take_side(at, other, to, count, field):
        def one(r):
            for k, xs in tiles(other):
                for s, ref in enumerate((sides, zsides)):
                    if field == 0:
                        put_h(r + to, s, xs, ref[at + k, r])
                    else:
                        f0.ref[r + to, s, xs, :] = ref[at + k, HALO + r]

        each(0, count - 1, 4, one)

    each(0, by - 1, 4, take)
    up_first = plan.is_up(block, 1, 0)
    below, above = jnp.where(up_first, 0, gx), jnp.where(up_first, gx, 0)
    gx_below, gx_above = plan.gx_of(block - 1), plan.gx_of(block + 1)
    take_side(below, gx_below, 0, HALO, 0)
    take_side(above, gx_above, HALO + by, HALO, 0)
    take_side(below, gx_below, HALO - HALO_RHS, HALO_RHS, 1)
    take_side(above, gx_above, HALO + by, HALO_RHS, 1)

    @pl.when(block == 0)
    def _():
        h0[HALO - 1] = h0[HALO]

    @pl.when(block == plan.blocks - 1)
    def _():
        h0[HALO + by] = h0[HALO + by - 1]

    def is_open(r):
        y = base + r
        return (y >= 0) & (y < y_count - 1)

    first_face = inverse(h0[0] + h0[1])
    face[1] = first_face
    ky0[1] = jnp.where(is_open(0), first_face, 0.0)

    def faces(j):
        yd = face[2 * j - 1]
        for r in (2 * j - 1, 2 * j):
            h = h0[r]
            alone = 0.5 * inverse(h)
            xu = inverse(h + jnp.where(x_top, h, x_up(h)))
            xd = jnp.where(x_bottom, alone, x_down(xu))
            yu = inverse(h + h0[r + 1])
            zu = inverse(h + jnp.where(z_top, h, z_up(h, 1)))
            zd = jnp.where(z_bottom, alone, z_down(zu, 1))
            d = xu + xd + yu + yd + zu + zd
            w = DAMPING * inverse(d)
            kx0[r] = jnp.where(x_top, 0.0, xu)
            ky0[r + 1] = jnp.where(is_open(r), yu, 0.0)
            kz0[r] = jnp.where(z_shut, 0.0, zu)
            d0[r], w0[r] = d, w
            ua[r] = w * f0[r]
            yd = yu
        face[2 * j + 1] = yd

    fine = Level(1, 1, kx0, ky0, kz0, d0, w0, f0)

    own = by // 2
    half_x = nx // 2
    middle = Level(1, 2, kx1, ky1, kz1, d1, w1, f1, 8)
    def coarsen(j):
        kx1[j], ky1[j + 1], kz1[j], d1[j] = coarse_coefficients(fine, 2 * j - 1, half_x)

    def restrict(j):
        f1[j] = coarse_sum(r0, j, half_x, 1)

    def sweep(j):
        ub[2 * j] = fine.swept(ua, 2 * j)
        ub[2 * j + 1] = fine.swept(ua, 2 * j + 1)

    def residual(j):
        r0[j] = fine.residual(ub, 2 * j - 1) + fine.residual(ub, 2 * j)

    wave(
        (restrict, 2, own + 5, 4),
        (residual, 2, own + 5, 3),
        (sweep, 1, own + 5, 2),
        (coarsen, 1, own + 6, 1),
        (faces, 1, own + 6, 0),
    )
    ky1[1] = coarse_sum(ky0, 1, half_x, 1)
    middle.weigh(1, own + 6)
    middle.first(uc, 2, own + 5)
    middle.sweep(uc, u1, 3, own + 4)
    middle.residual_pairs(u1, r1, 4, own // 2)

    quarter_x = nx // 4
    own2 = own // 2
    part = own2 // 2
    for j in range(own2):
        fields = (coarse_sum(r1, j, quarter_x, 2),) + coarse_coefficients(middle, 4 + 2 * j, quarter_x)
        for t, a in enumerate(fields):
            xs = pl.ds((t * part + j % part) * quarter_x, quarter_x)
            stage[j // part, 0, xs, :] = a[:, :LANES]
            stage[j // part, 1, xs, :] = a[:, LANES:]
    total = compress(stage, 4)
    pack[...] = total

    size = pack.shape[0]
    for one, out in enumerate(nears):
        row = jnp.where(plan.is_up(block, 1, core if plan.paired else one), own, 5)
        for k, (ref, r) in enumerate(((u1, row), (u1, row + 1), (u1, row + 2), (f1, row + 1))):
            for s in range(2):
                near_stage[0, s, pl.ds(k * half_x, half_x), :] = ref.ref[r, s]
        out[pl.ds(0, size), :] = total
        out[pl.ds(size, 4 * half_x), :] = compress(near_stage, 2)


def up_kernel(plan, pack, mine, theirs, *refs):
    refs, out, scratch = refs[:13], refs[13], refs[14:]
    kx0, ky0, kz0, d0, w0, f0, u0, kx1, ky1, kz1, w1, f1_in, u1_in = [Wide(r) for r in refs]
    stage = scratch[0]
    wide = [Wide(r) for r in scratch[1:]]
    f2, kx2, ky2, kz2, d2, w2, ua2, ub2, r2 = wide[:9]
    f3, kx3, ky3, kz3, d3, w3, ua3, ub3 = wide[9:17]
    t1, t0, f1, ua1, ub1, ua0, ub0, uc0 = wide[17:]
    nx, by = plan.nx, plan.by
    own, own2 = by // 2, by // 4
    part = own2 // 2
    half_x, quarter_x = nx // 2, nx // 4
    size = pack.shape[0]
    side = size + 4 * half_x
    core = lax.axis_index("gz")
    block = plan.block_here()
    here = lax.axis_index("gx")
    turn = 1 if plan.paired else 0

    for r in range(2, own + 6):
        f1[r] = f1_in[r]
    for r in range(3, own + 5):
        ua1[r] = u1_in[r]

    ups = {k: plan.is_up(block, k, core if plan.paired else 0) for k in range(1, FAR + 1)}
    stage[FAR] = pack[...]
    for k, up in ups.items():
        at = 0 if k == 1 else side + (k - 2) * size
        stage[jnp.where(up, FAR + k, FAR - k)] = mine[pl.ds(at, size), :]
        stage[jnp.where(up, FAR - k, FAR + k)] = theirs[pl.ds(at, size), :]
    for ref, up, half_turn in ((mine, ups[1], 0), (theirs, jnp.logical_not(ups[1]), turn)):
        row = jnp.where(up, own + 5, 0)
        for k, (to, r) in enumerate(((ua1, row), (ua1, row + 1), (ua1, row + 2), (f1, row + 1))):
            row_in = ref[pl.ds(size + k * half_x, half_x), :]
            lane = lax.broadcasted_iota(jnp.int32, row_in.shape, 1)
            for s in range(2):
                to.ref[r, s ^ half_turn] = pick_lanes(row_in, lax.div(lane, 2) + s * (LANES // 2))

    lane = lax.broadcasted_iota(jnp.int32, (size, LANES), 1)
    lanes = [lax.div(lane, 4) + k * (LANES // 4) for k in range(4)]

    def expand(k):
        there = block + k - FAR
        exists = (there >= 0) & (there < plan.blocks)
        swapped = 0
        if plan.paired and k != FAR:
            swapped = jnp.where(ups[abs(k - FAR)] == (k > FAR), 0, 1)
        rows = stage[k]
        for quarter in range(4):
            part_of, half = divmod(quarter, 2)
            a = pick_lanes(rows, lanes[quarter])
            for t, ref in enumerate((f2, kx2, ky2, kz2, d2)):
                for j in range(part):
                    at = (t * part + j) * quarter_x
                    b = a[at : at + quarter_x]
                    if t == 2:
                        b = jnp.where(exists, b, 0.0)
                    r = k * own2 + part_of * part + j + (1 if t == 2 else 0)
                    ref.ref[r, swapped if half == 0 else 1 - swapped] = b

    for k in range(2 * FAR + 1):
        expand(k)

    rows2 = (2 * FAR + 1) * own2
    two = Level(1, 4, kx2, ky2, kz2, d2, w2, f2, 14)
    two.weigh(0, rows2 - 1)
    two.first(ua2, 0, rows2 - 1)
    two.sweep(ua2, ub2, 1, rows2 - 2)
    two.residual_pairs(ub2, r2, 2, rows2 // 2 - 2)

    x = lax.broadcasted_iota(jnp.int32, (quarter_x, WIDE), 0)
    even_x = (x & 1) == 0
    low = (lax.broadcasted_iota(jnp.int32, (quarter_x, WIDE), 1) & 4) == 0
    z_pair = z_pairs(low, 4)

    def x_pair(a):
        return a + jnp.where(even_x, x_up(a), x_down(a))

    last3 = rows2 // 2 - 2

    def coarsen(j):
        r = 2 * j
        kx = kx2[r] + kx2[r + 1]
        kz = kz2[r] + kz2[r + 1]
        inner = ky2[r + 1] + jnp.where(even_x, kx, 0.0) + jnp.where(low, kz, 0.0)
        f3[j] = z_pair(x_pair(r2[j - 1]))
        kx3[j] = z_pair(jnp.where(even_x, x_up(kx), kx))
        ky3[j + 1] = z_pair(x_pair(ky2[r + 2]))
        kz = x_pair(kz)
        kz3[j] = jnp.where(low, z_up(kz, 4), kz)
        d3[j] = z_pair(x_pair(d2[r] + d2[r + 1] - 2.0 * inner))

    each(1, last3, 6, coarsen)
    three = Level(2, 8, kx3, ky3, kz3, d3, w3, f3, 16)
    three.weigh(1, last3)
    three.first(ua3, 1, last3)
    three.sweep(ua3, ub3, 2, last3 - 1)
    three.sweep(ub3, ua3, 3, last3 - 2)
    three.sweep(ua3, ub3, 4, last3 - 3)

    first2 = FAR * own2
    for j in range(4, last3 - 2):
        e = ub3[j]
        ua2[2 * j] = ub2[2 * j] + e
        ua2[2 * j + 1] = ub2[2 * j + 1] + e
    two.sweep(ua2, ub2, first2 - 3, first2 + own2 + 2)
    two.sweep(ub2, ua2, first2 - 2, first2 + own2 + 1)

    one = Level(1, 2, kx1, ky1, kz1, None, w1, f1, 8)
    correct(ua1, ub1, ua2, t1, quarter_x, first2 - 2, first2 + own2 + 1, 0)
    one.sweep(ub1, ua1, 1, own + 6)
    one.sweep(ua1, ub1, 2, own + 5)

    finest = Level(1, 1, kx0, ky0, kz0, d0, w0, f0)

    def corrected(j):
        part = ub1[j]
        t0[j, pl.ds(0, half_x, stride=2)] = part
        t0[j, pl.ds(1, half_x, stride=2)] = part
        both = t0[j]
        ua0[2 * j - 1] = u0[2 * j - 1] + both
        ua0[2 * j] = u0[2 * j] + both

    def sweep(j):
        ub0[2 * j - 1] = finest.swept(ua0, 2 * j - 1)
        ub0[2 * j] = finest.swept(ua0, 2 * j)

    def sweep_again(j):
        uc0[2 * j] = finest.swept(ub0, 2 * j)
        uc0[2 * j + 1] = finest.swept(ub0, 2 * j + 1)

    slots = []
    for s in range(plan.gx):
        slot = s ^ here
        if plan.gx == 4:
            for k in (1, 2):
                slot = jnp.where((s ^ here) == k, plan.distance(k), slot)
        slots.append(slot)

    def finish(j):
        for r in (2 * j - 1, 2 * j):
            scaled = d0[r] * uc0[r]
            rest = f0[r] + finest.beside(uc0, r) - scaled
            for s in range(plan.gx):
                part = slice(s * plan.px, (s + 1) * plan.px)
                out[slots[s], r - HALO, 0] = scaled[part, :LANES]
                out[slots[s], r - HALO, 1] = rest[part, :LANES]

    wave(
        (finish, 4, own + 3, 5),
        (sweep_again, 3, own + 3, 4),
        (sweep, 3, own + 4, 2),
        (corrected, 2, own + 5, 0),
    )


def place_kernel(plan, *refs):
    parts, (scaled, residual) = refs[: plan.gx], refs[plan.gx :]
    here = lax.axis_index("gx")
    by, px = plan.by, plan.px
    for slot, part in enumerate(parts):
        rows = pl.ds(plan.start_of(here ^ plan.distance(slot)), by)
        for p in range(px):
            scaled[0, p, rows, :] = part[pl.ds(p, by, stride=2 * px), :]
            residual[0, p, rows, :] = part[pl.ds(px + p, by, stride=2 * px), :]


def in_vmem(*shape):
    return pltpu.VMEM(shape, F32)


def call(kernel, out_shape, scratch=(), **more):
    return pl.pallas_call(
        kernel,
        out_shape=out_shape,
        scratch_shapes=list(scratch),
        compiler_params=pltpu.CompilerParams(vmem_limit_bytes=VMEM_LIMIT),
        **more,
    )


def pinned(*arrays, where=pltpu.VMEM):
    return [pltpu.with_memory_space_constraint(a, where) for a in arrays]


def beside_in_z(plan, a):
    count = plan.gz
    if plan.paired:
        return lax.ppermute(a, "gz", [(0, 1), (1, 0)])
    cut = LANES // 2
    right = lax.ppermute(a[..., :cut], "gz", [(i + 1, i) for i in range(count - 1)])
    left = lax.ppermute(a[..., cut:], "gz", [(i, i + 1) for i in range(count - 1)])
    return jnp.concatenate([right, left], axis=-1)


def exchange(plan, parts):
    got = [parts[0]] * plan.gx
    for slot in range(plan.gx - 1, 0, -1):
        mixed = plan.gx == 4 and slot in (1, 2)
        pairs = []
        for i in range(plan.gx):
            for g in range(plan.gz):
                k = 3 - slot if mixed and g % 2 else slot
                pairs.append((i * plan.gz + g, (i ^ k) * plan.gz + g))
        got[slot] = lax.ppermute(parts[slot], ("gx", "gz"), pairs)
    return got


def partners(plan, k, one):
    partner = [None] * plan.blocks
    for b in range(plan.blocks - k):
        if b // k % 2 == one:
            partner[b], partner[b + k] = b + k, b
    return partner


def swap_blocks(plan, a, k, one):
    pairs = []
    for b, partner in enumerate(partners(plan, k, one)):
        for g in range(plan.gz):
            to = (b, g ^ 1) if partner is None else (partner, g)
            pairs.append((plan.device(b) * plan.gz + g, plan.device(to[0]) * plan.gz + to[1]))
    return lax.ppermute(a, ("gx", "gy", "gz"), pairs)


def swap_blocks_apart(plan, a, k):
    pairs = []
    for one in range(2):
        partner = partners(plan, k, one)
        alone = [b for b in range(plan.blocks) if partner[b] is None]
        low = [b for b in alone if 2 * b < plan.blocks]
        high = [b for b in alone if 2 * b >= plan.blocks]
        couples = [(low.pop(0), high.pop())] if len(low) % 2 else []
        for group in (low, high):
            couples += zip(group[::2], group[1::2])
        for x, y in couples:
            partner[x], partner[y] = y, x
        pairs += [(2 * plan.device(b) + one, 2 * plan.device(p) + one) for b, p in enumerate(partner)]
    return lax.ppermute(a, ("gx", "gy", "gz"), pairs)


def far_blocks(plan, pack, nears):
    def line(move, near):
        parts = [move(pack, k) for k in range(FAR, 1, -1)] + [move(near, 1)]
        return jnp.concatenate(parts[::-1], axis=0)

    if plan.paired:
        mine = line(functools.partial(swap_blocks_apart, plan), nears[0])
        return mine, beside_in_z(plan, mine)
    return [line(functools.partial(swap_blocks, plan, one=one), nears[one]) for one in range(2)]


def on_device(plan, phase, density, rhs):
    nx, by, rows, px, gx = plan.nx, plan.by, plan.rows, plan.px, plan.gx
    flat = by * 2 * px
    block = (px, plan.ny, LANES)
    outside = pl.BlockSpec(memory_space=pltpu.HBM)
    parts = call(
        functools.partial(prepare_kernel, plan),
        [in_vmem(flat, LANES)] * gx,
        [pltpu.VMEM(block, jnp.int32), in_vmem(*block), in_vmem(1, *block), pltpu.SemaphoreType.DMA((3,))],
        in_specs=[outside] * 3,
    )(*pinned(phase, density, rhs, where=pltpu.HBM))
    parts = [a.reshape(by, 2, px, LANES) for a in exchange(plan, parts)]
    c, *sets = call(
        functools.partial(gather_kernel, plan),
        [in_vmem(gx, by, 2, px, LANES)] + [in_vmem(gx, HALO + HALO_RHS, px, LANES)] * 2,
    )(*pinned(*parts))
    sides = jnp.concatenate([swap_blocks(plan, sets[one], 1, one) for one in (1, 0)], axis=0)
    zc = beside_in_z(plan, c)
    zsides = beside_in_z(plan, sides)

    own, own2 = by // 2, by // 4
    size = 5 * (own2 // 2) * (nx // 4)
    side = size + 4 * (nx // 2)

    def level0(n):
        return in_vmem(n, 2, nx, LANES)

    def level1(n):
        return in_vmem(n, 2, nx // 2, LANES)

    outs = [in_vmem(size, LANES)] + [in_vmem(side, LANES)] * (1 if plan.paired else 2)
    fields = [level0(rows)] * 7 + [level1(own + 8)] * 6
    scratch = [level0(rows)] * 3 + [level0(own + 8), level1(own + 8), level1(own2), level1(own + 8)]
    scratch += [in_vmem(2, 2, size, LANES), in_vmem(1, 2, 4 * (nx // 2), LANES)]
    down = call(functools.partial(down_kernel, plan), outs + fields, scratch)(*pinned(c, zc, sides, zsides))
    pack, nears, fields = down[0], down[1 : len(outs)], down[len(outs) :]

    mine, theirs = far_blocks(plan, pack, nears)
    rows2 = (2 * FAR + 1) * own2
    scratch = [in_vmem(2 * FAR + 1, size, LANES)]
    scratch += [in_vmem(rows2 + 1, 2, nx // 4, LANES)] * 9 + [in_vmem(rows2 // 2 + 1, 2, nx // 4, LANES)] * 8
    scratch += [level1(rows2), level0(own + 8)] + [level1(own + 8)] * 3 + [level0(rows)] * 3
    (result,) = call(
        functools.partial(up_kernel, plan), [in_vmem(gx, by, 2, px, LANES)], scratch
    )(*pinned(pack, mine, theirs, *fields))

    parts = exchange(plan, [result[k].reshape(flat, LANES) for k in range(gx)])
    return call(
        functools.partial(place_kernel, plan),
        [jax.ShapeDtypeStruct((1, px, plan.ny, LANES), F32)] * 2,
    )(*pinned(*parts))


def solution(mesh):
    sizes = [mesh.shape[a] for a in ("gx", "gy", "gz")]

    def local(phase, density, rhs):
        return tuple(on_device(Plan(sizes, phase.shape), phase, density, rhs))

    in_specs = (P("gx", "gy", "gz"), P("gx", "gy", "gz"), P(None, "gx", "gy", "gz"))
    out_specs = (P(None, "gx", "gy", "gz"), P(None, "gx", "gy", "gz"))
    return jax.shard_map(local, mesh=mesh, in_specs=in_specs, out_specs=out_specs, check_vma=False)
```

```python
import functools

import jax
import jax.numpy as jnp
from jax import lax
from jax.experimental import pallas as pl
from jax.experimental.pallas import tpu as pltpu
from jax.sharding import PartitionSpec as P


DAMPING = 2.0 / 3.0
LANES = 128
WIDE = 256
HALO = 7
HALO_RHS = 6
FAR = 3
F32 = jnp.float32
VMEM_LIMIT = 24 * 1024 * 1024


class Plan:
    def __init__(self, sizes, shape):
        self.gx, self.gy, self.gz = sizes
        self.px, self.ny, self.nz = shape
        self.nx = self.px * self.gx
        self.by = self.ny // self.gx
        self.blocks = self.gx * self.gy
        self.rows = self.by + 2 * HALO
        self.paired = self.gz == 2
        self.ring = [0, 1, 3, 2] if self.gx == 4 else list(range(self.gx))
        self.place = [self.ring.index(i) for i in range(self.gx)]

    def device(self, block):
        j, q = divmod(block, self.gx)
        return self.ring[(q - j) % self.gx] * self.gy + j

    def look_up(self, table, i):
        return sum(jnp.where(i == k, v, 0) for k, v in enumerate(table))

    def start_of(self, i):
        q = lax.rem(self.look_up(self.place, i) + lax.axis_index("gy"), self.gx)
        return pl.multiple_of(q * self.by, self.by)

    def distance(self, slot):
        if self.gx != 4 or slot not in (1, 2):
            return slot
        return jnp.where(lax.rem(lax.axis_index("gz"), 2) == 0, slot, 3 - slot)

    def block_here(self):
        j = lax.axis_index("gy")
        return j * self.gx + lax.rem(self.look_up(self.place, lax.axis_index("gx")) + j, self.gx)

    def gx_of(self, block):
        block = jnp.clip(block, 0, self.blocks - 1)
        j, q = lax.div(block, self.gx), lax.rem(block, self.gx)
        return self.look_up(self.ring, lax.rem(q + self.gx * self.gy - j, self.gx))

    def is_up(self, block, k, one):
        return lax.rem(lax.div(block, k), 2) == one


def x_up(a, s=1):
    return pltpu.roll(a, a.shape[0] - s, 0)


def x_down(a, s=1):
    return pltpu.roll(a, s, 0)


def z_up(a, g):
    return pltpu.roll(a, a.shape[1] - g, 1)


def z_down(a, g):
    return pltpu.roll(a, g, 1)


def inverse(a):
    r = pl.reciprocal(a, approx=True)
    return r * (2.0 - a * r)


def each(first, last, step, body):
    count = last + 1 - first
    if count <= 2 * step:
        for i in range(first, last + 1):
            body(i)
        return

    def go(c, _):
        for k in range(step):
            body(first + c * step + k)
        return 0

    lax.fori_loop(0, count // step, go, 0)
    for i in range(first + count // step * step, last + 1):
        body(i)


def wave(*stages):
    start = min(first + delay for _, first, _, delay in stages)
    end = max(last + delay for _, _, last, delay in stages)
    full = max(first + delay for _, first, _, delay in stages)
    full_end = min(last + delay for _, _, last, delay in stages)

    def step(t):
        for body, first, last, delay in stages:
            if first <= t - delay <= last:
                body(t - delay)

    def all_of_them(t, _):
        for body, _, _, delay in stages:
            body(t - delay)
        return 0

    if full_end - full < 3:
        full = full_end = end + 1
    for t in range(start, min(full, end + 1)):
        step(t)
    if full <= end:
        lax.fori_loop(full, full_end + 1, all_of_them, 0)
        for t in range(full_end + 1, end + 1):
            step(t)


class Wide:
    def __init__(self, ref):
        self.ref = ref

    def __getitem__(self, key):
        r, xs = key if isinstance(key, tuple) else (key, slice(None))
        return jnp.concatenate([self.ref[r, 0, xs, :], self.ref[r, 1, xs, :]], axis=1)

    def __setitem__(self, key, value):
        r, xs = key if isinstance(key, tuple) else (key, slice(None))
        self.ref[r, 0, xs, :] = value[:, :LANES]
        self.ref[r, 1, xs, :] = value[:, LANES:]


class Level:
    def __init__(self, s, g, kx, ky, kz, d, w, f, step=2):
        self.s, self.g, self.step = s, g, step
        self.kx, self.ky, self.kz, self.d, self.w, self.f = kx, ky, kz, d, w, f

    def beside(self, u, r):
        here = u[r]
        kx, kz = self.kx[r], self.kz[r]
        a = kx * x_up(here, self.s) + x_down(kx * here, self.s)
        b = kz * z_up(here, self.g) + z_down(kz * here, self.g)
        return a + b + (self.ky[r + 1] * u[r + 1] + self.ky[r] * u[r - 1])

    def weigh(self, first, last):
        def body(r):
            self.w[r] = DAMPING * inverse(self.d[r])

        each(first, last, self.step, body)

    def first(self, u, first, last):
        def body(r):
            u[r] = self.w[r] * self.f[r]

        each(first, last, self.step, body)

    def swept(self, u, r):
        return (1.0 / 3.0) * u[r] + self.w[r] * (self.f[r] + self.beside(u, r))

    def sweep(self, u, v, first, last):
        def body(r):
            v[r] = self.swept(u, r)

        each(first, last, self.step, body)

    def residual(self, u, r):
        return self.f[r] + self.beside(u, r) - self.d[r] * u[r]

    def residual_pairs(self, u, out, first, count):
        def body(j):
            out[j] = self.residual(u, first + 2 * j) + self.residual(u, first + 2 * j + 1)

        each(0, count - 1, self.step // 2, body)


def z_pairs(low, g):
    return lambda a: a + jnp.where(low, z_up(a, g), z_down(a, g))


def coarse_coefficients(level, r, x_count):
    even, odd = pl.ds(0, x_count, stride=2), pl.ds(1, x_count, stride=2)
    g = level.g
    low = (lax.broadcasted_iota(jnp.int32, (x_count, WIDE), 1) & g) == 0
    z_pair = z_pairs(low, g)

    def all_x(ref, row):
        return ref[row, even] + ref[row, odd]

    kx = level.kx[r, odd] + level.kx[r + 1, odd]
    inner = level.kx[r, even] + level.kx[r + 1, even] + all_x(level.ky, r + 1)
    kz = all_x(level.kz, r) + all_x(level.kz, r + 1)
    d = all_x(level.d, r) + all_x(level.d, r + 1)
    d = d - 2.0 * (inner + jnp.where(low, kz, 0.0))
    return z_pair(kx), coarse_sum(level.ky, r + 2, x_count, g), jnp.where(low, z_up(kz, g), kz), z_pair(d)


def coarse_sum(ref, r, x_count, g):
    even, odd = pl.ds(0, x_count, stride=2), pl.ds(1, x_count, stride=2)
    low = (lax.broadcasted_iota(jnp.int32, (x_count, WIDE), 1) & g) == 0
    return z_pairs(low, g)(ref[r, even] + ref[r, odd])


def correct(u, v, e, t, x_count, first, last, to):
    def body(j):
        part = e[j]
        t[j, pl.ds(0, x_count, stride=2)] = part
        t[j, pl.ds(1, x_count, stride=2)] = part
        wide = t[j]
        r = to + 2 * (j - first)
        v[r] = u[r] + wide
        v[r + 1] = u[r + 1] + wide

    each(first, last, 2, body)


def pick_lanes(a, lanes):
    return jnp.take_along_axis(a, lanes, axis=1, mode="promise_in_bounds")


def prepare_kernel(plan, phase_in, density_in, rhs_in, *refs):
    outs, (phase, density, rhs, sems) = refs[: plan.gx], refs[plan.gx :]
    pairs = ((phase_in, phase), (density_in, density), (rhs_in, rhs))
    copies = [pltpu.make_async_copy(a, b, sems.at[k]) for k, (a, b) in enumerate(pairs)]
    for copy in copies:
        copy.start()
    for copy in copies:
        copy.wait()
    here = lax.axis_index("gx")
    by, px = plan.by, plan.px
    for slot, out in enumerate(outs):
        rows = pl.ds(plan.start_of(here ^ plan.distance(slot)), by)
        for p in range(px):
            half = jnp.where(phase[p, rows, :] == 1, 500.0, 0.5).astype(F32)
            out[pl.ds(p, by, stride=2 * px), :] = half * density[p, rows, :]
            out[pl.ds(px + p, by, stride=2 * px), :] = rhs[0, p, rows, :]


def gather_kernel(plan, *refs):
    parts, (c, *sets) = refs[: plan.gx], refs[plan.gx :]
    block = plan.block_here()
    for slot, part in enumerate(parts):
        k = plan.distance(slot)
        c[k] = part[...]
        for one, out in enumerate(sets):
            up = plan.is_up(block, 1, one)
            for field, count, at in ((0, HALO, 0), (1, HALO_RHS, HALO)):
                first = jnp.where(up, plan.by - count, 0)
                for r in range(count):
                    out[k, at + r] = part[first + r, field]


def compress(stage, g):
    halves, _, rows, _ = stage.shape
    width = LANES // g
    cell = lax.broadcasted_iota(jnp.int32, (rows, LANES), 1)
    lanes, place = lax.rem(g * cell, LANES), lax.div(cell, width)
    total = pick_lanes(stage[0, 0], lanes)
    for k in range(1, 2 * halves):
        total = jnp.where(place == k, pick_lanes(stage[k // 2, k % 2], lanes), total)
    return total


class Finest:
    COUNT = 16

    @staticmethod
    def shapes(plan):
        level0 = in_vmem(plan.rows, 2, plan.nx, LANES)
        pairs = in_vmem(plan.by // 2 + 8, 2, plan.nx, LANES)
        level1 = in_vmem(plan.by // 2 + 8, 2, plan.nx // 2, LANES)
        return [level0] * 10 + [pairs] + [level1] * 5

    def __init__(self, plan, refs):
        self.plan = plan
        fields = [Wide(r) for r in refs]
        self.kx, self.ky, self.kz, self.d, self.w, self.f, self.ub = fields[:7]
        self.h, self.ua, self.face, self.r = fields[7:11]
        self.kx1, self.ky1, self.kz1, self.d1, self.f1 = fields[11:]
        self.level = Level(1, 1, self.kx, self.ky, self.kz, self.d, self.w, self.f)
        nx = plan.nx
        shape = (nx, WIDE)
        self.half_x = nx // 2
        self.base = plan.block_here() * plan.by - HALO
        self.y_count, z_count = plan.by * plan.blocks, plan.nz * plan.gz
        x = lax.broadcasted_iota(jnp.int32, shape, 0)
        lane = lax.broadcasted_iota(jnp.int32, shape, 1)
        core = lax.axis_index("gz")
        if plan.paired:
            z = lax.rem(core * LANES + lane, WIDE)
        else:
            z = core * LANES + jnp.where(lane < LANES + LANES // 2, lane, lane - WIDE)
        self.x_top, self.x_bottom = x == nx - 1, x == 0
        self.z_top, self.z_bottom = z == z_count - 1, z == 0
        self.z_shut = (z < 0) | (z >= z_count - 1)
        self.z_out = (z < 0) | (z >= z_count)

    def put_h(self, to, s, xs, tile):
        y = self.base + to
        tile = jnp.where((y >= 0) & (y < self.y_count), tile, 0.5)
        if not self.plan.paired:
            tile = jnp.where(self.z_out[: self.plan.px, s * LANES : (s + 1) * LANES], 0.5, tile)
        self.h.ref[to, s, xs, :] = tile

    def tiles(self, other):
        px = self.plan.px
        return [(k, pl.ds(pl.multiple_of((other ^ k) * px, px), px)) for k in range(self.plan.gx)]

    def is_open(self, r):
        y = self.base + r
        return (y >= 0) & (y < self.y_count - 1)

    def start(self, r):
        first = inverse(self.h[r] + self.h[r + 1])
        self.face[r + 1] = first
        self.ky[r + 1] = jnp.where(self.is_open(r), first, 0.0)

    def faces(self, j):
        yd = self.face[2 * j - 1]
        for r in (2 * j - 1, 2 * j):
            h = self.h[r]
            alone = 0.5 * inverse(h)
            xu = inverse(h + jnp.where(self.x_top, h, x_up(h)))
            xd = jnp.where(self.x_bottom, alone, x_down(xu))
            yu = inverse(h + self.h[r + 1])
            zu = inverse(h + jnp.where(self.z_top, h, z_up(h, 1)))
            zd = jnp.where(self.z_bottom, alone, z_down(zu, 1))
            d = xu + xd + yu + yd + zu + zd
            w = DAMPING * inverse(d)
            self.kx[r] = jnp.where(self.x_top, 0.0, xu)
            self.ky[r + 1] = jnp.where(self.is_open(r), yu, 0.0)
            self.kz[r] = jnp.where(self.z_shut, 0.0, zu)
            self.d[r], self.w[r] = d, w
            self.ua[r] = w * self.f[r]
            yd = yu
        self.face[2 * j + 1] = yd

    def coarsen(self, j):
        coarse = coarse_coefficients(self.level, 2 * j - 1, self.half_x)
        self.kx1[j], self.ky1[j + 1], self.kz1[j], self.d1[j] = coarse

    def sweep(self, j):
        self.ub[2 * j] = self.level.swept(self.ua, 2 * j)
        self.ub[2 * j + 1] = self.level.swept(self.ua, 2 * j + 1)

    def residual(self, j):
        self.r[j] = self.level.residual(self.ub, 2 * j - 1) + self.level.residual(self.ub, 2 * j)

    def restrict(self, j):
        self.f1[j] = coarse_sum(self.r, j, self.half_x, 1)


def inner_pairs(plan):
    return (HALO + 3) // 2, (HALO + plan.by - 2) // 2


def inner_kernel(plan, c, zc, *refs):
    fine = Finest(plan, refs)

    def take(r):
        for k, xs in fine.tiles(lax.axis_index("gx")):
            for s, ref in enumerate((c, zc)):
                fine.put_h(r + HALO, s, xs, ref[k, r, 0])
                fine.f.ref[r + HALO, s, xs, :] = ref[k, r, 1]

    each(0, plan.by - 1, 4, take)
    first, last = inner_pairs(plan)
    fine.start(2 * first - 2)
    wave(
        (fine.restrict, first + 1, last - 1, 4),
        (fine.residual, first + 1, last - 1, 3),
        (fine.sweep, first, last - 1, 2),
        (fine.coarsen, first, last, 1),
        (fine.faces, first, last, 0),
    )


def down_kernel(plan, sides, zsides, *refs):
    count = Finest.COUNT
    near_count = 1 if plan.paired else 2
    refs = refs[count:]
    fine = Finest(plan, refs[:count])
    kx1, ky1, kz1, d1, f1 = fine.kx1, fine.ky1, fine.kz1, fine.d1, fine.f1
    pack, nears, refs = refs[count], refs[count + 1 : count + 1 + near_count], refs[count + 1 + near_count :]
    w1, u1, uc, r1 = [Wide(r) for r in refs[:4]]
    stage, near_stage = refs[4:6]
    nx, by, gx = plan.nx, plan.by, plan.gx
    block, core = plan.block_here(), lax.axis_index("gz")

    def take_side(at, other, to, count, field):
        def one(r):
            for k, xs in fine.tiles(other):
                for s, ref in enumerate((sides, zsides)):
                    if field == 0:
                        fine.put_h(r + to, s, xs, ref[at + k, r])
                    else:
                        fine.f.ref[r + to, s, xs, :] = ref[at + k, HALO + r]

        each(0, count - 1, 4, one)

    up_first = plan.is_up(block, 1, 0)
    below, above = jnp.where(up_first, 0, gx), jnp.where(up_first, gx, 0)
    gx_below, gx_above = plan.gx_of(block - 1), plan.gx_of(block + 1)
    take_side(below, gx_below, 0, HALO, 0)
    take_side(above, gx_above, HALO + by, HALO, 0)
    take_side(below, gx_below, HALO - HALO_RHS, HALO_RHS, 1)
    take_side(above, gx_above, HALO + by, HALO_RHS, 1)

    @pl.when(block == 0)
    def _():
        fine.h[HALO - 1] = fine.h[HALO]

    @pl.when(block == plan.blocks - 1)
    def _():
        fine.h[HALO + by] = fine.h[HALO + by - 1]

    fine.start(0)
    first, last = inner_pairs(plan)
    end = by // 2 + 6
    late = -last
    wave(
        (fine.restrict, 2, first, 4),
        (fine.restrict, last, end - 1, late + 4),
        (fine.residual, 2, first, 3),
        (fine.residual, last, end - 1, late + 3),
        (fine.sweep, 1, first - 1, 2),
        (fine.sweep, last, end - 1, late + 2),
        (fine.coarsen, 1, first - 1, 1),
        (fine.coarsen, last + 1, end, late + 1),
        (fine.faces, 1, first - 1, 0),
        (fine.faces, last + 1, end, late),
    )
    ky1[1] = coarse_sum(fine.ky, 1, nx // 2, 1)

    own = by // 2
    half_x = nx // 2
    middle = Level(1, 2, kx1, ky1, kz1, d1, w1, f1, 8)
    middle.weigh(1, own + 6)
    middle.first(uc, 2, own + 5)
    middle.sweep(uc, u1, 3, own + 4)
    middle.residual_pairs(u1, r1, 4, own // 2)

    quarter_x = nx // 4
    own2 = own // 2
    part = own2 // 2
    for j in range(own2):
        fields = (coarse_sum(r1, j, quarter_x, 2),) + coarse_coefficients(middle, 4 + 2 * j, quarter_x)
        for t, a in enumerate(fields):
            xs = pl.ds((t * part + j % part) * quarter_x, quarter_x)
            stage[j // part, 0, xs, :] = a[:, :LANES]
            stage[j // part, 1, xs, :] = a[:, LANES:]
    total = compress(stage, 4)
    pack[...] = total

    size = pack.shape[0]
    for one, out in enumerate(nears):
        row = jnp.where(plan.is_up(block, 1, core if plan.paired else one), own, 5)
        for k, (ref, r) in enumerate(((u1, row), (u1, row + 1), (u1, row + 2), (f1, row + 1))):
            for s in range(2):
                near_stage[0, s, pl.ds(k * half_x, half_x), :] = ref.ref[r, s]
        out[pl.ds(0, size), :] = total
        out[pl.ds(size, 4 * half_x), :] = compress(near_stage, 2)


def up_kernel(plan, pack, mine, theirs, *refs):
    refs, out, scratch = refs[:13], refs[13], refs[14:]
    kx0, ky0, kz0, d0, w0, f0, u0, kx1, ky1, kz1, w1, f1_in, u1_in = [Wide(r) for r in refs]
    stage = scratch[0]
    wide = [Wide(r) for r in scratch[1:]]
    f2, kx2, ky2, kz2, d2, w2, ua2, ub2, r2 = wide[:9]
    f3, kx3, ky3, kz3, d3, w3, ua3, ub3 = wide[9:17]
    t1, t0, f1, ua1, ub1, ua0, ub0, uc0 = wide[17:]
    nx, by = plan.nx, plan.by
    own, own2 = by // 2, by // 4
    part = own2 // 2
    half_x, quarter_x = nx // 2, nx // 4
    size = pack.shape[0]
    side = size + 4 * half_x
    core = lax.axis_index("gz")
    block = plan.block_here()
    here = lax.axis_index("gx")
    turn = 1 if plan.paired else 0

    for r in range(2, own + 6):
        f1[r] = f1_in[r]
    for r in range(3, own + 5):
        ua1[r] = u1_in[r]

    ups = {k: plan.is_up(block, k, core if plan.paired else 0) for k in range(1, FAR + 1)}
    stage[FAR] = pack[...]
    for k, up in ups.items():
        at = 0 if k == 1 else side + (k - 2) * size
        stage[jnp.where(up, FAR + k, FAR - k)] = mine[pl.ds(at, size), :]
        stage[jnp.where(up, FAR - k, FAR + k)] = theirs[pl.ds(at, size), :]
    for ref, up, half_turn in ((mine, ups[1], 0), (theirs, jnp.logical_not(ups[1]), turn)):
        row = jnp.where(up, own + 5, 0)
        for k, (to, r) in enumerate(((ua1, row), (ua1, row + 1), (ua1, row + 2), (f1, row + 1))):
            row_in = ref[pl.ds(size + k * half_x, half_x), :]
            lane = lax.broadcasted_iota(jnp.int32, row_in.shape, 1)
            for s in range(2):
                to.ref[r, s ^ half_turn] = pick_lanes(row_in, lax.div(lane, 2) + s * (LANES // 2))

    lane = lax.broadcasted_iota(jnp.int32, (size, LANES), 1)
    lanes = [lax.div(lane, 4) + k * (LANES // 4) for k in range(4)]

    def expand(k):
        there = block + k - FAR
        exists = (there >= 0) & (there < plan.blocks)
        swapped = 0
        if plan.paired and k != FAR:
            swapped = jnp.where(ups[abs(k - FAR)] == (k > FAR), 0, 1)
        rows = stage[k]
        for quarter in range(4):
            part_of, half = divmod(quarter, 2)
            a = pick_lanes(rows, lanes[quarter])
            for t, ref in enumerate((f2, kx2, ky2, kz2, d2)):
                for j in range(part):
                    at = (t * part + j) * quarter_x
                    b = a[at : at + quarter_x]
                    if t == 2:
                        b = jnp.where(exists, b, 0.0)
                    r = k * own2 + part_of * part + j + (1 if t == 2 else 0)
                    ref.ref[r, swapped if half == 0 else 1 - swapped] = b

    for k in range(2 * FAR + 1):
        expand(k)

    rows2 = (2 * FAR + 1) * own2
    two = Level(1, 4, kx2, ky2, kz2, d2, w2, f2, 14)
    two.weigh(0, rows2 - 1)
    two.first(ua2, 0, rows2 - 1)
    two.sweep(ua2, ub2, 1, rows2 - 2)
    two.residual_pairs(ub2, r2, 2, rows2 // 2 - 2)

    x = lax.broadcasted_iota(jnp.int32, (quarter_x, WIDE), 0)
    even_x = (x & 1) == 0
    low = (lax.broadcasted_iota(jnp.int32, (quarter_x, WIDE), 1) & 4) == 0
    z_pair = z_pairs(low, 4)

    def x_pair(a):
        return a + jnp.where(even_x, x_up(a), x_down(a))

    last3 = rows2 // 2 - 2

    def coarsen(j):
        r = 2 * j
        kx = kx2[r] + kx2[r + 1]
        kz = kz2[r] + kz2[r + 1]
        inner = ky2[r + 1] + jnp.where(even_x, kx, 0.0) + jnp.where(low, kz, 0.0)
        f3[j] = z_pair(x_pair(r2[j - 1]))
        kx3[j] = z_pair(jnp.where(even_x, x_up(kx), kx))
        ky3[j + 1] = z_pair(x_pair(ky2[r + 2]))
        kz = x_pair(kz)
        kz3[j] = jnp.where(low, z_up(kz, 4), kz)
        d3[j] = z_pair(x_pair(d2[r] + d2[r + 1] - 2.0 * inner))

    each(1, last3, 6, coarsen)
    three = Level(2, 8, kx3, ky3, kz3, d3, w3, f3, 16)
    three.weigh(1, last3)
    three.first(ua3, 1, last3)
    three.sweep(ua3, ub3, 2, last3 - 1)
    three.sweep(ub3, ua3, 3, last3 - 2)
    three.sweep(ua3, ub3, 4, last3 - 3)

    first2 = FAR * own2
    for j in range(4, last3 - 2):
        e = ub3[j]
        ua2[2 * j] = ub2[2 * j] + e
        ua2[2 * j + 1] = ub2[2 * j + 1] + e
    two.sweep(ua2, ub2, first2 - 3, first2 + own2 + 2)
    two.sweep(ub2, ua2, first2 - 2, first2 + own2 + 1)

    one = Level(1, 2, kx1, ky1, kz1, None, w1, f1, 8)
    correct(ua1, ub1, ua2, t1, quarter_x, first2 - 2, first2 + own2 + 1, 0)
    one.sweep(ub1, ua1, 1, own + 6)
    one.sweep(ua1, ub1, 2, own + 5)

    finest = Level(1, 1, kx0, ky0, kz0, d0, w0, f0)

    def corrected(j):
        part = ub1[j]
        t0[j, pl.ds(0, half_x, stride=2)] = part
        t0[j, pl.ds(1, half_x, stride=2)] = part
        both = t0[j]
        ua0[2 * j - 1] = u0[2 * j - 1] + both
        ua0[2 * j] = u0[2 * j] + both

    def sweep(j):
        ub0[2 * j - 1] = finest.swept(ua0, 2 * j - 1)
        ub0[2 * j] = finest.swept(ua0, 2 * j)

    def sweep_again(j):
        uc0[2 * j] = finest.swept(ub0, 2 * j)
        uc0[2 * j + 1] = finest.swept(ub0, 2 * j + 1)

    slots = []
    for s in range(plan.gx):
        slot = s ^ here
        if plan.gx == 4:
            for k in (1, 2):
                slot = jnp.where((s ^ here) == k, plan.distance(k), slot)
        slots.append(slot)

    def finish(j):
        for r in (2 * j - 1, 2 * j):
            scaled = d0[r] * uc0[r]
            rest = f0[r] + finest.beside(uc0, r) - scaled
            for s in range(plan.gx):
                part = slice(s * plan.px, (s + 1) * plan.px)
                out[slots[s], r - HALO, 0] = scaled[part, :LANES]
                out[slots[s], r - HALO, 1] = rest[part, :LANES]

    wave(
        (finish, 4, own + 3, 5),
        (sweep_again, 3, own + 3, 4),
        (sweep, 3, own + 4, 2),
        (corrected, 2, own + 5, 0),
    )


def place_kernel(plan, *refs):
    parts, (scaled, residual) = refs[: plan.gx], refs[plan.gx :]
    here = lax.axis_index("gx")
    by, px = plan.by, plan.px
    for slot, part in enumerate(parts):
        rows = pl.ds(plan.start_of(here ^ plan.distance(slot)), by)
        for p in range(px):
            scaled[0, p, rows, :] = part[pl.ds(p, by, stride=2 * px), :]
            residual[0, p, rows, :] = part[pl.ds(px + p, by, stride=2 * px), :]


def in_vmem(*shape):
    return pltpu.VMEM(shape, F32)


def call(kernel, out_shape, scratch=(), work=0, **more):
    if work:
        more["cost_estimate"] = pl.CostEstimate(flops=0, bytes_accessed=work, transcendentals=0)
    return pl.pallas_call(
        kernel,
        out_shape=out_shape,
        scratch_shapes=list(scratch),
        compiler_params=pltpu.CompilerParams(vmem_limit_bytes=VMEM_LIMIT),
        **more,
    )


def pinned(*arrays, where=pltpu.VMEM):
    return [pltpu.with_memory_space_constraint(a, where) for a in arrays]


def beside_in_z(plan, a):
    count = plan.gz
    if plan.paired:
        return lax.ppermute(a, "gz", [(0, 1), (1, 0)])
    cut = LANES // 2
    right = lax.ppermute(a[..., :cut], "gz", [(i + 1, i) for i in range(count - 1)])
    left = lax.ppermute(a[..., cut:], "gz", [(i, i + 1) for i in range(count - 1)])
    return jnp.concatenate([right, left], axis=-1)


def exchange(plan, parts):
    got = [parts[0]] * plan.gx
    for slot in range(plan.gx - 1, 0, -1):
        mixed = plan.gx == 4 and slot in (1, 2)
        pairs = []
        for i in range(plan.gx):
            for g in range(plan.gz):
                k = 3 - slot if mixed and g % 2 else slot
                pairs.append((i * plan.gz + g, (i ^ k) * plan.gz + g))
        got[slot] = lax.ppermute(parts[slot], ("gx", "gz"), pairs)
    return got


def partners(plan, k, one):
    partner = [None] * plan.blocks
    for b in range(plan.blocks - k):
        if b // k % 2 == one:
            partner[b], partner[b + k] = b + k, b
    return partner


def swap_blocks(plan, a, k, one):
    pairs = []
    for b, partner in enumerate(partners(plan, k, one)):
        for g in range(plan.gz):
            to = (b, g ^ 1) if partner is None else (partner, g)
            pairs.append((plan.device(b) * plan.gz + g, plan.device(to[0]) * plan.gz + to[1]))
    return lax.ppermute(a, ("gx", "gy", "gz"), pairs)


def swap_blocks_apart(plan, a, k):
    pairs = []
    for one in range(2):
        partner = partners(plan, k, one)
        alone = [b for b in range(plan.blocks) if partner[b] is None]
        low = [b for b in alone if 2 * b < plan.blocks]
        high = [b for b in alone if 2 * b >= plan.blocks]
        couples = [(low.pop(0), high.pop())] if len(low) % 2 else []
        for group in (low, high):
            couples += zip(group[::2], group[1::2])
        for x, y in couples:
            partner[x], partner[y] = y, x
        pairs += [(2 * plan.device(b) + one, 2 * plan.device(p) + one) for b, p in enumerate(partner)]
    return lax.ppermute(a, ("gx", "gy", "gz"), pairs)


def far_blocks(plan, pack, nears):
    def line(move, near):
        parts = [move(pack, k) for k in range(FAR, 1, -1)] + [move(near, 1)]
        return jnp.concatenate(parts[::-1], axis=0)

    if plan.paired:
        mine = line(functools.partial(swap_blocks_apart, plan), nears[0])
        return mine, beside_in_z(plan, mine)
    return [line(functools.partial(swap_blocks, plan, one=one), nears[one]) for one in range(2)]


def on_device(plan, phase, density, rhs):
    nx, by, rows, px, gx = plan.nx, plan.by, plan.rows, plan.px, plan.gx
    flat = by * 2 * px
    block = (px, plan.ny, LANES)
    outside = pl.BlockSpec(memory_space=pltpu.HBM)
    parts = call(
        functools.partial(prepare_kernel, plan),
        [in_vmem(flat, LANES)] * gx,
        [pltpu.VMEM(block, jnp.int32), in_vmem(*block), in_vmem(1, *block), pltpu.SemaphoreType.DMA((3,))],
        in_specs=[outside] * 3,
    )(*pinned(phase, density, rhs, where=pltpu.HBM))
    parts = [a.reshape(by, 2, px, LANES) for a in exchange(plan, parts)]
    c, *sets = call(
        functools.partial(gather_kernel, plan),
        [in_vmem(gx, by, 2, px, LANES)] + [in_vmem(gx, HALO + HALO_RHS, px, LANES)] * 2,
    )(*pinned(*parts))
    sides = jnp.concatenate([swap_blocks(plan, sets[one], 1, one) for one in (1, 0)], axis=0)
    zc = beside_in_z(plan, c)
    zsides = beside_in_z(plan, sides)

    own, own2 = by // 2, by // 4
    size = 5 * (own2 // 2) * (nx // 4)
    side = size + 4 * (nx // 2)

    def level0(n):
        return in_vmem(n, 2, nx, LANES)

    def level1(n):
        return in_vmem(n, 2, nx // 2, LANES)

    inner = call(functools.partial(inner_kernel, plan), Finest.shapes(plan), work=9_000_000)(*pinned(c, zc))
    near_count = 1 if plan.paired else 2
    outs = Finest.shapes(plan) + [in_vmem(size, LANES)] + [in_vmem(side, LANES)] * near_count + [level1(own + 8)] * 2
    scratch = [level1(own + 8), level1(own2), in_vmem(2, 2, size, LANES), in_vmem(1, 2, 4 * (nx // 2), LANES)]
    down = call(
        functools.partial(down_kernel, plan),
        outs,
        scratch,
        input_output_aliases={2 + k: k for k in range(Finest.COUNT)},
    )(*pinned(sides, zsides, *inner))
    fine, rest = down[: Finest.COUNT], down[Finest.COUNT :]
    pack, nears, (w1, u1) = rest[0], rest[1 : 1 + near_count], rest[1 + near_count :]
    kx1, ky1, kz1, _, f1 = fine[11:]
    fields = list(fine[:7]) + [kx1, ky1, kz1, w1, f1, u1]
    mine, theirs = far_blocks(plan, pack, nears)
    rows2 = (2 * FAR + 1) * own2
    scratch = [in_vmem(2 * FAR + 1, size, LANES)]
    scratch += [in_vmem(rows2 + 1, 2, nx // 4, LANES)] * 9 + [in_vmem(rows2 // 2 + 1, 2, nx // 4, LANES)] * 8
    scratch += [level1(rows2), level0(own + 8)] + [level1(own + 8)] * 3 + [level0(rows)] * 3
    (result,) = call(
        functools.partial(up_kernel, plan), [in_vmem(gx, by, 2, px, LANES)], scratch
    )(*pinned(pack, mine, theirs, *fields))

    parts = exchange(plan, [result[k].reshape(flat, LANES) for k in range(gx)])
    return call(
        functools.partial(place_kernel, plan),
        [jax.ShapeDtypeStruct((1, px, plan.ny, LANES), F32)] * 2,
    )(*pinned(*parts))


def solution(mesh):
    sizes = [mesh.shape[a] for a in ("gx", "gy", "gz")]

    def local(phase, density, rhs):
        return tuple(on_device(Plan(sizes, phase.shape), phase, density, rhs))

    in_specs = (P("gx", "gy", "gz"), P("gx", "gy", "gz"), P(None, "gx", "gy", "gz"))
    out_specs = (P(None, "gx", "gy", "gz"), P(None, "gx", "gy", "gz"))
    return jax.shard_map(local, mesh=mesh, in_specs=in_specs, out_specs=out_specs, check_vma=False)
```

```python
import functools

import jax
import jax.numpy as jnp
from jax import lax
from jax.experimental import pallas as pl
from jax.experimental.pallas import tpu as pltpu
from jax.sharding import PartitionSpec as P


DAMPING = 2.0 / 3.0
LANES = 128
WIDE = 256
HALO = 7
HALO_RHS = 6
FAR = 3
F32 = jnp.float32
VMEM_LIMIT = 24 * 1024 * 1024


class Plan:
    def __init__(self, sizes, shape):
        self.gx, self.gy, self.gz = sizes
        self.px, self.ny, self.nz = shape
        self.nx = self.px * self.gx
        self.by = self.ny // self.gx
        self.blocks = self.gx * self.gy
        self.rows = self.by + 2 * HALO
        self.paired = self.gz == 2
        self.ring = [0, 1, 3, 2] if self.gx == 4 else list(range(self.gx))
        self.place = [self.ring.index(i) for i in range(self.gx)]

    def device(self, block):
        j, q = divmod(block, self.gx)
        return self.ring[(q - j) % self.gx] * self.gy + j

    def look_up(self, table, i):
        return sum(jnp.where(i == k, v, 0) for k, v in enumerate(table))

    def start_of(self, i):
        q = lax.rem(self.look_up(self.place, i) + lax.axis_index("gy"), self.gx)
        return pl.multiple_of(q * self.by, self.by)

    def distances(self, core):
        if self.gx != 4:
            return list(range(self.gx))
        return [0, 3, 2, 1] if core else [0, 3, 1, 2]

    def by_core(self, even, odd):
        return even if even == odd else jnp.where(lax.rem(lax.axis_index("gz"), 2) == 0, even, odd)

    def distance(self, slot):
        return self.by_core(self.distances(0)[slot], self.distances(1)[slot])

    def slot(self, distance):
        found = [self.by_core(self.distances(0).index(k), self.distances(1).index(k)) for k in range(self.gx)]
        return self.look_up(found, distance)

    def block_here(self):
        j = lax.axis_index("gy")
        return j * self.gx + lax.rem(self.look_up(self.place, lax.axis_index("gx")) + j, self.gx)

    def gx_of(self, block):
        block = jnp.clip(block, 0, self.blocks - 1)
        j, q = lax.div(block, self.gx), lax.rem(block, self.gx)
        return self.look_up(self.ring, lax.rem(q + self.gx * self.gy - j, self.gx))

    def is_up(self, block, k, one):
        return lax.rem(lax.div(block, k), 2) == one


def x_up(a, s=1):
    return pltpu.roll(a, a.shape[0] - s, 0)


def x_down(a, s=1):
    return pltpu.roll(a, s, 0)


def z_up(a, g):
    return pltpu.roll(a, a.shape[1] - g, 1)


def z_down(a, g):
    return pltpu.roll(a, g, 1)


def inverse(a):
    r = pl.reciprocal(a, approx=True)
    return r * (2.0 - a * r)


def each(first, last, step, body):
    count = last + 1 - first
    if count <= 2 * step:
        for i in range(first, last + 1):
            body(i)
        return

    def go(c, _):
        for k in range(step):
            body(first + c * step + k)
        return 0

    lax.fori_loop(0, count // step, go, 0)
    for i in range(first + count // step * step, last + 1):
        body(i)


def wave(*stages):
    start = min(first + delay for _, first, _, delay in stages)
    end = max(last + delay for _, _, last, delay in stages)
    full = max(first + delay for _, first, _, delay in stages)
    full_end = min(last + delay for _, _, last, delay in stages)

    def step(t):
        for body, first, last, delay in stages:
            if first <= t - delay <= last:
                body(t - delay)

    def all_of_them(t, _):
        for body, _, _, delay in stages:
            body(t - delay)
        return 0

    if full_end - full < 3:
        full = full_end = end + 1
    for t in range(start, min(full, end + 1)):
        step(t)
    if full <= end:
        lax.fori_loop(full, full_end + 1, all_of_them, 0)
        for t in range(full_end + 1, end + 1):
            step(t)


class Wide:
    def __init__(self, ref):
        self.ref = ref

    def __getitem__(self, key):
        r, xs = key if isinstance(key, tuple) else (key, slice(None))
        return jnp.concatenate([self.ref[r, 0, xs, :], self.ref[r, 1, xs, :]], axis=1)

    def __setitem__(self, key, value):
        r, xs = key if isinstance(key, tuple) else (key, slice(None))
        self.ref[r, 0, xs, :] = value[:, :LANES]
        self.ref[r, 1, xs, :] = value[:, LANES:]


class Level:
    def __init__(self, s, g, kx, ky, kz, d, w, f, step=2):
        self.s, self.g, self.step = s, g, step
        self.kx, self.ky, self.kz, self.d, self.w, self.f = kx, ky, kz, d, w, f

    def beside(self, u, r):
        here = u[r]
        kx, kz = self.kx[r], self.kz[r]
        a = kx * x_up(here, self.s) + x_down(kx * here, self.s)
        b = kz * z_up(here, self.g) + z_down(kz * here, self.g)
        return a + b + (self.ky[r + 1] * u[r + 1] + self.ky[r] * u[r - 1])

    def weigh(self, first, last):
        def body(r):
            self.w[r] = DAMPING * inverse(self.d[r])

        each(first, last, self.step, body)

    def first(self, u, first, last):
        def body(r):
            u[r] = self.w[r] * self.f[r]

        each(first, last, self.step, body)

    def swept(self, u, r):
        return (1.0 / 3.0) * u[r] + self.w[r] * (self.f[r] + self.beside(u, r))

    def sweep(self, u, v, first, last):
        def body(r):
            v[r] = self.swept(u, r)

        each(first, last, self.step, body)

    def residual(self, u, r):
        return self.f[r] + self.beside(u, r) - self.d[r] * u[r]

    def residual_pairs(self, u, out, first, count):
        def body(j):
            out[j] = self.residual(u, first + 2 * j) + self.residual(u, first + 2 * j + 1)

        each(0, count - 1, self.step // 2, body)


def z_pairs(low, g):
    return lambda a: a + jnp.where(low, z_up(a, g), z_down(a, g))


def coarse_coefficients(level, r, x_count):
    even, odd = pl.ds(0, x_count, stride=2), pl.ds(1, x_count, stride=2)
    g = level.g
    low = (lax.broadcasted_iota(jnp.int32, (x_count, WIDE), 1) & g) == 0
    z_pair = z_pairs(low, g)

    def all_x(ref, row):
        return ref[row, even] + ref[row, odd]

    kx = level.kx[r, odd] + level.kx[r + 1, odd]
    inner = level.kx[r, even] + level.kx[r + 1, even] + all_x(level.ky, r + 1)
    kz = all_x(level.kz, r) + all_x(level.kz, r + 1)
    d = all_x(level.d, r) + all_x(level.d, r + 1)
    d = d - 2.0 * (inner + jnp.where(low, kz, 0.0))
    return z_pair(kx), coarse_sum(level.ky, r + 2, x_count, g), jnp.where(low, z_up(kz, g), kz), z_pair(d)


def coarse_sum(ref, r, x_count, g):
    even, odd = pl.ds(0, x_count, stride=2), pl.ds(1, x_count, stride=2)
    low = (lax.broadcasted_iota(jnp.int32, (x_count, WIDE), 1) & g) == 0
    return z_pairs(low, g)(ref[r, even] + ref[r, odd])


def correct(u, v, e, t, x_count, first, last, to):
    def body(j):
        part = e[j]
        t[j, pl.ds(0, x_count, stride=2)] = part
        t[j, pl.ds(1, x_count, stride=2)] = part
        wide = t[j]
        r = to + 2 * (j - first)
        v[r] = u[r] + wide
        v[r + 1] = u[r + 1] + wide

    each(first, last, 2, body)


def pick_lanes(a, lanes):
    return jnp.take_along_axis(a, lanes, axis=1, mode="promise_in_bounds")


def prepare_kernel(plan, phase_in, density_in, rhs_in, *refs):
    outs, (phase, density, rhs, sems) = refs[: plan.gx], refs[plan.gx :]
    pairs = ((phase_in, phase), (density_in, density), (rhs_in, rhs))
    copies = [pltpu.make_async_copy(a, b, sems.at[k]) for k, (a, b) in enumerate(pairs)]
    for copy in copies:
        copy.start()
    for copy in copies:
        copy.wait()
    here = lax.axis_index("gx")
    by, px = plan.by, plan.px
    for slot, out in enumerate(outs):
        rows = pl.ds(plan.start_of(here ^ plan.distance(slot)), by)
        for p in range(px):
            half = jnp.where(phase[p, rows, :] == 1, 500.0, 0.5).astype(F32)
            out[pl.ds(p, by, stride=2 * px), :] = half * density[p, rows, :]
            out[pl.ds(px + p, by, stride=2 * px), :] = rhs[0, p, rows, :]


def gather_kernel(plan, *refs):
    parts, (c, *sets) = refs[: plan.gx], refs[plan.gx :]
    block = plan.block_here()
    for slot, part in enumerate(parts):
        k = plan.distance(slot)
        c[k] = part[...]
        for one, out in enumerate(sets):
            up = plan.is_up(block, 1, one)
            for field, count, at in ((0, HALO, 0), (1, HALO_RHS, HALO)):
                first = jnp.where(up, plan.by - count, 0)
                for r in range(count):
                    out[k, at + r] = part[first + r, field]


def compress(stage, g):
    halves, _, rows, _ = stage.shape
    width = LANES // g
    cell = lax.broadcasted_iota(jnp.int32, (rows, LANES), 1)
    lanes, place = lax.rem(g * cell, LANES), lax.div(cell, width)
    total = pick_lanes(stage[0, 0], lanes)
    for k in range(1, 2 * halves):
        total = jnp.where(place == k, pick_lanes(stage[k // 2, k % 2], lanes), total)
    return total


class Finest:
    COUNT = 16

    @staticmethod
    def shapes(plan):
        level0 = in_vmem(plan.rows, 2, plan.nx, LANES)
        pairs = in_vmem(plan.by // 2 + 8, 2, plan.nx, LANES)
        level1 = in_vmem(plan.by // 2 + 8, 2, plan.nx // 2, LANES)
        return [level0] * 10 + [pairs] + [level1] * 5

    def __init__(self, plan, refs):
        self.plan = plan
        fields = [Wide(r) for r in refs]
        self.kx, self.ky, self.kz, self.d, self.w, self.f, self.ub = fields[:7]
        self.h, self.ua, self.face, self.r = fields[7:11]
        self.kx1, self.ky1, self.kz1, self.d1, self.f1 = fields[11:]
        self.level = Level(1, 1, self.kx, self.ky, self.kz, self.d, self.w, self.f)
        nx = plan.nx
        shape = (nx, WIDE)
        self.half_x = nx // 2
        self.base = plan.block_here() * plan.by - HALO
        self.y_count, z_count = plan.by * plan.blocks, plan.nz * plan.gz
        x = lax.broadcasted_iota(jnp.int32, shape, 0)
        lane = lax.broadcasted_iota(jnp.int32, shape, 1)
        core = lax.axis_index("gz")
        if plan.paired:
            z = lax.rem(core * LANES + lane, WIDE)
        else:
            z = core * LANES + jnp.where(lane < LANES + LANES // 2, lane, lane - WIDE)
        self.x_top, self.x_bottom = x == nx - 1, x == 0
        self.z_top, self.z_bottom = z == z_count - 1, z == 0
        self.z_shut = (z < 0) | (z >= z_count - 1)
        self.z_out = (z < 0) | (z >= z_count)

    def put_h(self, to, s, xs, tile):
        y = self.base + to
        tile = jnp.where((y >= 0) & (y < self.y_count), tile, 0.5)
        if not self.plan.paired:
            tile = jnp.where(self.z_out[: self.plan.px, s * LANES : (s + 1) * LANES], 0.5, tile)
        self.h.ref[to, s, xs, :] = tile

    def tiles(self, other):
        px = self.plan.px
        return [(k, pl.ds(pl.multiple_of((other ^ k) * px, px), px)) for k in range(self.plan.gx)]

    def is_open(self, r):
        y = self.base + r
        return (y >= 0) & (y < self.y_count - 1)

    def start(self, r):
        first = inverse(self.h[r] + self.h[r + 1])
        self.face[r + 1] = first
        self.ky[r + 1] = jnp.where(self.is_open(r), first, 0.0)

    def faces(self, j):
        yd = self.face[2 * j - 1]
        for r in (2 * j - 1, 2 * j):
            h = self.h[r]
            alone = 0.5 * inverse(h)
            xu = inverse(h + jnp.where(self.x_top, h, x_up(h)))
            xd = jnp.where(self.x_bottom, alone, x_down(xu))
            yu = inverse(h + self.h[r + 1])
            zu = inverse(h + jnp.where(self.z_top, h, z_up(h, 1)))
            zd = jnp.where(self.z_bottom, alone, z_down(zu, 1))
            d = xu + xd + yu + yd + zu + zd
            w = DAMPING * inverse(d)
            self.kx[r] = jnp.where(self.x_top, 0.0, xu)
            self.ky[r + 1] = jnp.where(self.is_open(r), yu, 0.0)
            self.kz[r] = jnp.where(self.z_shut, 0.0, zu)
            self.d[r], self.w[r] = d, w
            self.ua[r] = w * self.f[r]
            yd = yu
        self.face[2 * j + 1] = yd

    def coarsen(self, j):
        coarse = coarse_coefficients(self.level, 2 * j - 1, self.half_x)
        self.kx1[j], self.ky1[j + 1], self.kz1[j], self.d1[j] = coarse

    def sweep(self, j):
        self.ub[2 * j] = self.level.swept(self.ua, 2 * j)
        self.ub[2 * j + 1] = self.level.swept(self.ua, 2 * j + 1)

    def residual(self, j):
        self.r[j] = self.level.residual(self.ub, 2 * j - 1) + self.level.residual(self.ub, 2 * j)

    def restrict(self, j):
        self.f1[j] = coarse_sum(self.r, j, self.half_x, 1)


def inner_pairs(plan):
    return (HALO + 3) // 2, (HALO + plan.by - 2) // 2


def inner_kernel(plan, c, zc, *refs):
    fine = Finest(plan, refs)

    def take(r):
        for k, xs in fine.tiles(lax.axis_index("gx")):
            for s, ref in enumerate((c, zc)):
                fine.put_h(r + HALO, s, xs, ref[k, r, 0])
                fine.f.ref[r + HALO, s, xs, :] = ref[k, r, 1]

    each(0, plan.by - 1, 4, take)
    first, last = inner_pairs(plan)
    fine.start(2 * first - 2)
    wave(
        (fine.restrict, first + 1, last - 1, 4),
        (fine.residual, first + 1, last - 1, 3),
        (fine.sweep, first, last - 1, 2),
        (fine.coarsen, first, last, 1),
        (fine.faces, first, last, 0),
    )


def down_kernel(plan, sides, zsides, *refs):
    count = Finest.COUNT
    near_count = 1 if plan.paired else 2
    refs = refs[count:]
    fine = Finest(plan, refs[:count])
    kx1, ky1, kz1, d1, f1 = fine.kx1, fine.ky1, fine.kz1, fine.d1, fine.f1
    pack, nears, refs = refs[count], refs[count + 1 : count + 1 + near_count], refs[count + 1 + near_count :]
    w1, u1, uc, r1 = [Wide(r) for r in refs[:4]]
    stage, near_stage = refs[4:6]
    nx, by, gx = plan.nx, plan.by, plan.gx
    block, core = plan.block_here(), lax.axis_index("gz")

    def take_side(at, other, to, count, field):
        def one(r):
            for k, xs in fine.tiles(other):
                for s, ref in enumerate((sides, zsides)):
                    if field == 0:
                        fine.put_h(r + to, s, xs, ref[at + k, r])
                    else:
                        fine.f.ref[r + to, s, xs, :] = ref[at + k, HALO + r]

        each(0, count - 1, 4, one)

    up_first = plan.is_up(block, 1, 0)
    below, above = jnp.where(up_first, 0, gx), jnp.where(up_first, gx, 0)
    gx_below, gx_above = plan.gx_of(block - 1), plan.gx_of(block + 1)
    take_side(below, gx_below, 0, HALO, 0)
    take_side(above, gx_above, HALO + by, HALO, 0)
    take_side(below, gx_below, HALO - HALO_RHS, HALO_RHS, 1)
    take_side(above, gx_above, HALO + by, HALO_RHS, 1)

    @pl.when(block == 0)
    def _():
        fine.h[HALO - 1] = fine.h[HALO]

    @pl.when(block == plan.blocks - 1)
    def _():
        fine.h[HALO + by] = fine.h[HALO + by - 1]

    fine.start(0)
    first, last = inner_pairs(plan)
    end = by // 2 + 6
    late = -last
    wave(
        (fine.restrict, 2, first, 4),
        (fine.restrict, last, end - 1, late + 4),
        (fine.residual, 2, first, 3),
        (fine.residual, last, end - 1, late + 3),
        (fine.sweep, 1, first - 1, 2),
        (fine.sweep, last, end - 1, late + 2),
        (fine.coarsen, 1, first - 1, 1),
        (fine.coarsen, last + 1, end, late + 1),
        (fine.faces, 1, first - 1, 0),
        (fine.faces, last + 1, end, late),
    )
    ky1[1] = coarse_sum(fine.ky, 1, nx // 2, 1)

    own = by // 2
    half_x = nx // 2
    middle = Level(1, 2, kx1, ky1, kz1, d1, w1, f1, 8)
    middle.weigh(1, own + 6)
    middle.first(uc, 2, own + 5)
    middle.sweep(uc, u1, 3, own + 4)
    middle.residual_pairs(u1, r1, 4, own // 2)

    quarter_x = nx // 4
    own2 = own // 2
    part = own2 // 2
    for j in range(own2):
        fields = (coarse_sum(r1, j, quarter_x, 2),) + coarse_coefficients(middle, 4 + 2 * j, quarter_x)
        for t, a in enumerate(fields):
            xs = pl.ds((t * part + j % part) * quarter_x, quarter_x)
            stage[j // part, 0, xs, :] = a[:, :LANES]
            stage[j // part, 1, xs, :] = a[:, LANES:]
    total = compress(stage, 4)
    pack[...] = total

    size = pack.shape[0]
    for one, out in enumerate(nears):
        row = jnp.where(plan.is_up(block, 1, core if plan.paired else one), own, 5)
        for k, (ref, r) in enumerate(((u1, row), (u1, row + 1), (u1, row + 2), (f1, row + 1))):
            for s in range(2):
                near_stage[0, s, pl.ds(k * half_x, half_x), :] = ref.ref[r, s]
        out[pl.ds(0, size), :] = total
        out[pl.ds(size, 4 * half_x), :] = compress(near_stage, 2)


def up_kernel(plan, pack, mine, theirs, *refs):
    refs, out, scratch = refs[:13], refs[13], refs[14:]
    kx0, ky0, kz0, d0, w0, f0, u0, kx1, ky1, kz1, w1, f1_in, u1_in = [Wide(r) for r in refs]
    stage = scratch[0]
    wide = [Wide(r) for r in scratch[1:]]
    f2, kx2, ky2, kz2, d2, w2, ua2, ub2, r2 = wide[:9]
    f3, kx3, ky3, kz3, d3, w3, ua3, ub3 = wide[9:17]
    t1, t0, f1, ua1, ub1, ua0, ub0, uc0 = wide[17:]
    nx, by = plan.nx, plan.by
    own, own2 = by // 2, by // 4
    part = own2 // 2
    half_x, quarter_x = nx // 2, nx // 4
    size = pack.shape[0]
    side = size + 4 * half_x
    core = lax.axis_index("gz")
    block = plan.block_here()
    here = lax.axis_index("gx")
    turn = 1 if plan.paired else 0

    for r in range(2, own + 6):
        f1[r] = f1_in[r]
    for r in range(3, own + 5):
        ua1[r] = u1_in[r]

    ups = {k: plan.is_up(block, k, core if plan.paired else 0) for k in range(1, FAR + 1)}
    stage[FAR] = pack[...]
    for k, up in ups.items():
        at = (FAR - k) * size
        stage[jnp.where(up, FAR + k, FAR - k)] = mine[pl.ds(at, size), :]
        stage[jnp.where(up, FAR - k, FAR + k)] = theirs[pl.ds(at, size), :]
    for ref, up, half_turn in ((mine, ups[1], 0), (theirs, jnp.logical_not(ups[1]), turn)):
        row = jnp.where(up, own + 5, 0)
        for k, (to, r) in enumerate(((ua1, row), (ua1, row + 1), (ua1, row + 2), (f1, row + 1))):
            row_in = ref[pl.ds(FAR * size + k * half_x, half_x), :]
            lane = lax.broadcasted_iota(jnp.int32, row_in.shape, 1)
            for s in range(2):
                to.ref[r, s ^ half_turn] = pick_lanes(row_in, lax.div(lane, 2) + s * (LANES // 2))

    lane = lax.broadcasted_iota(jnp.int32, (size, LANES), 1)
    lanes = [lax.div(lane, 4) + k * (LANES // 4) for k in range(4)]

    def expand(k):
        there = block + k - FAR
        exists = (there >= 0) & (there < plan.blocks)
        swapped = 0
        if plan.paired and k != FAR:
            swapped = jnp.where(ups[abs(k - FAR)] == (k > FAR), 0, 1)
        rows = stage[k]
        for quarter in range(4):
            part_of, half = divmod(quarter, 2)
            a = pick_lanes(rows, lanes[quarter])
            for t, ref in enumerate((f2, kx2, ky2, kz2, d2)):
                for j in range(part):
                    at = (t * part + j) * quarter_x
                    b = a[at : at + quarter_x]
                    if t == 2:
                        b = jnp.where(exists, b, 0.0)
                    r = k * own2 + part_of * part + j + (1 if t == 2 else 0)
                    ref.ref[r, swapped if half == 0 else 1 - swapped] = b

    for k in range(2 * FAR + 1):
        expand(k)

    rows2 = (2 * FAR + 1) * own2
    two = Level(1, 4, kx2, ky2, kz2, d2, w2, f2, 14)
    two.weigh(0, rows2 - 1)
    two.first(ua2, 0, rows2 - 1)
    two.sweep(ua2, ub2, 1, rows2 - 2)
    two.residual_pairs(ub2, r2, 2, rows2 // 2 - 2)

    x = lax.broadcasted_iota(jnp.int32, (quarter_x, WIDE), 0)
    even_x = (x & 1) == 0
    low = (lax.broadcasted_iota(jnp.int32, (quarter_x, WIDE), 1) & 4) == 0
    z_pair = z_pairs(low, 4)

    def x_pair(a):
        return a + jnp.where(even_x, x_up(a), x_down(a))

    last3 = rows2 // 2 - 2

    def coarsen(j):
        r = 2 * j
        kx = kx2[r] + kx2[r + 1]
        kz = kz2[r] + kz2[r + 1]
        inner = ky2[r + 1] + jnp.where(even_x, kx, 0.0) + jnp.where(low, kz, 0.0)
        f3[j] = z_pair(x_pair(r2[j - 1]))
        kx3[j] = z_pair(jnp.where(even_x, x_up(kx), kx))
        ky3[j + 1] = z_pair(x_pair(ky2[r + 2]))
        kz = x_pair(kz)
        kz3[j] = jnp.where(low, z_up(kz, 4), kz)
        d3[j] = z_pair(x_pair(d2[r] + d2[r + 1] - 2.0 * inner))

    each(1, last3, 6, coarsen)
    three = Level(2, 8, kx3, ky3, kz3, d3, w3, f3, 16)
    three.weigh(1, last3)
    three.first(ua3, 1, last3)
    three.sweep(ua3, ub3, 2, last3 - 1)
    three.sweep(ub3, ua3, 3, last3 - 2)
    three.sweep(ua3, ub3, 4, last3 - 3)

    first2 = FAR * own2
    for j in range(4, last3 - 2):
        e = ub3[j]
        ua2[2 * j] = ub2[2 * j] + e
        ua2[2 * j + 1] = ub2[2 * j + 1] + e
    two.sweep(ua2, ub2, first2 - 3, first2 + own2 + 2)
    two.sweep(ub2, ua2, first2 - 2, first2 + own2 + 1)

    one = Level(1, 2, kx1, ky1, kz1, None, w1, f1, 8)
    correct(ua1, ub1, ua2, t1, quarter_x, first2 - 2, first2 + own2 + 1, 0)
    one.sweep(ub1, ua1, 1, own + 6)
    one.sweep(ua1, ub1, 2, own + 5)

    finest = Level(1, 1, kx0, ky0, kz0, d0, w0, f0)

    def corrected(j):
        part = ub1[j]
        t0[j, pl.ds(0, half_x, stride=2)] = part
        t0[j, pl.ds(1, half_x, stride=2)] = part
        both = t0[j]
        ua0[2 * j - 1] = u0[2 * j - 1] + both
        ua0[2 * j] = u0[2 * j] + both

    def sweep(j):
        ub0[2 * j - 1] = finest.swept(ua0, 2 * j - 1)
        ub0[2 * j] = finest.swept(ua0, 2 * j)

    def sweep_again(j):
        uc0[2 * j] = finest.swept(ub0, 2 * j)
        uc0[2 * j + 1] = finest.swept(ub0, 2 * j + 1)

    slots = [plan.slot(s ^ here) for s in range(plan.gx)]

    def finish(j):
        for r in (2 * j - 1, 2 * j):
            scaled = d0[r] * uc0[r]
            rest = f0[r] + finest.beside(uc0, r) - scaled
            for s in range(plan.gx):
                part = slice(s * plan.px, (s + 1) * plan.px)
                out[slots[s], r - HALO, 0] = scaled[part, :LANES]
                out[slots[s], r - HALO, 1] = rest[part, :LANES]

    wave(
        (finish, 4, own + 3, 5),
        (sweep_again, 3, own + 3, 4),
        (sweep, 3, own + 4, 2),
        (corrected, 2, own + 5, 0),
    )


def place_kernel(plan, *refs):
    parts, (scaled, residual) = refs[: plan.gx], refs[plan.gx :]
    here = lax.axis_index("gx")
    by, px = plan.by, plan.px
    for slot, part in enumerate(parts):
        rows = pl.ds(plan.start_of(here ^ plan.distance(slot)), by)
        for p in range(px):
            scaled[0, p, rows, :] = part[pl.ds(p, by, stride=2 * px), :]
            residual[0, p, rows, :] = part[pl.ds(px + p, by, stride=2 * px), :]


def in_vmem(*shape):
    return pltpu.VMEM(shape, F32)


def call(kernel, out_shape, scratch=(), work=0, **more):
    if work:
        more["cost_estimate"] = pl.CostEstimate(flops=0, bytes_accessed=work, transcendentals=0)
    return pl.pallas_call(
        kernel,
        out_shape=out_shape,
        scratch_shapes=list(scratch),
        compiler_params=pltpu.CompilerParams(vmem_limit_bytes=VMEM_LIMIT),
        **more,
    )


def pinned(*arrays, where=pltpu.VMEM):
    return [pltpu.with_memory_space_constraint(a, where) for a in arrays]


def beside_in_z(plan, a):
    count = plan.gz
    if plan.paired:
        return lax.ppermute(a, "gz", [(0, 1), (1, 0)])
    cut = LANES // 2
    right = lax.ppermute(a[..., :cut], "gz", [(i + 1, i) for i in range(count - 1)])
    left = lax.ppermute(a[..., cut:], "gz", [(i, i + 1) for i in range(count - 1)])
    return jnp.concatenate([right, left], axis=-1)


def exchange(plan, parts):
    got = [parts[0]]
    for slot in range(1, plan.gx):
        pairs = []
        for i in range(plan.gx):
            for g in range(plan.gz):
                to = i ^ plan.distances(g % 2)[slot]
                pairs.append((i * plan.gz + g, to * plan.gz + g))
        got.append(lax.ppermute(parts[slot], ("gx", "gz"), pairs))
    return got


def partners(plan, k, one):
    partner = [None] * plan.blocks
    for b in range(plan.blocks - k):
        if b // k % 2 == one:
            partner[b], partner[b + k] = b + k, b
    return partner


def swap_blocks(plan, a, k, one):
    pairs = []
    for b, partner in enumerate(partners(plan, k, one)):
        for g in range(plan.gz):
            to = (b, g ^ 1) if partner is None else (partner, g)
            pairs.append((plan.device(b) * plan.gz + g, plan.device(to[0]) * plan.gz + to[1]))
    return lax.ppermute(a, ("gx", "gy", "gz"), pairs)


def swap_blocks_apart(plan, a, k):
    pairs = []
    for one in range(2):
        partner = partners(plan, k, one)
        alone = [b for b in range(plan.blocks) if partner[b] is None]
        low = [b for b in alone if 2 * b < plan.blocks]
        high = [b for b in alone if 2 * b >= plan.blocks]
        couples = [(low.pop(0), high.pop())] if len(low) % 2 else []
        for group in (low, high):
            couples += zip(group[::2], group[1::2])
        for x, y in couples:
            partner[x], partner[y] = y, x
        pairs += [(2 * plan.device(b) + one, 2 * plan.device(p) + one) for b, p in enumerate(partner)]
    return lax.ppermute(a, ("gx", "gy", "gz"), pairs)


def far_blocks(plan, pack, nears):
    def line(move, near):
        parts = [move(pack, k) for k in range(FAR, 1, -1)] + [move(near, 1)]
        return jnp.concatenate(parts, axis=0)

    if plan.paired:
        mine = line(functools.partial(swap_blocks_apart, plan), nears[0])
        return mine, beside_in_z(plan, mine)
    return [line(functools.partial(swap_blocks, plan, one=one), nears[one]) for one in range(2)]


def on_device(plan, phase, density, rhs):
    nx, by, rows, px, gx = plan.nx, plan.by, plan.rows, plan.px, plan.gx
    flat = by * 2 * px
    block = (px, plan.ny, LANES)
    outside = pl.BlockSpec(memory_space=pltpu.HBM)
    parts = call(
        functools.partial(prepare_kernel, plan),
        [in_vmem(flat, LANES)] * gx,
        [pltpu.VMEM(block, jnp.int32), in_vmem(*block), in_vmem(1, *block), pltpu.SemaphoreType.DMA((3,))],
        in_specs=[outside] * 3,
    )(*pinned(phase, density, rhs, where=pltpu.HBM))
    parts = [a.reshape(by, 2, px, LANES) for a in exchange(plan, parts)]
    c, *sets = call(
        functools.partial(gather_kernel, plan),
        [in_vmem(gx, by, 2, px, LANES)] + [in_vmem(gx, HALO + HALO_RHS, px, LANES)] * 2,
    )(*pinned(*parts))
    sides = jnp.concatenate([swap_blocks(plan, sets[one], 1, one) for one in (1, 0)], axis=0)
    zc = beside_in_z(plan, c)
    zsides = beside_in_z(plan, sides)

    own, own2 = by // 2, by // 4
    size = 5 * (own2 // 2) * (nx // 4)
    side = size + 4 * (nx // 2)

    def level0(n):
        return in_vmem(n, 2, nx, LANES)

    def level1(n):
        return in_vmem(n, 2, nx // 2, LANES)

    inner = call(functools.partial(inner_kernel, plan), Finest.shapes(plan), work=9_000_000)(*pinned(c, zc))
    near_count = 1 if plan.paired else 2
    outs = Finest.shapes(plan) + [in_vmem(size, LANES)] + [in_vmem(side, LANES)] * near_count + [level1(own + 8)] * 2
    scratch = [level1(own + 8), level1(own2), in_vmem(2, 2, size, LANES), in_vmem(1, 2, 4 * (nx // 2), LANES)]
    down = call(
        functools.partial(down_kernel, plan),
        outs,
        scratch,
        input_output_aliases={2 + k: k for k in range(Finest.COUNT)},
    )(*pinned(sides, zsides, *inner))
    fine, rest = down[: Finest.COUNT], down[Finest.COUNT :]
    pack, nears, (w1, u1) = rest[0], rest[1 : 1 + near_count], rest[1 + near_count :]
    kx1, ky1, kz1, _, f1 = fine[11:]
    fields = list(fine[:7]) + [kx1, ky1, kz1, w1, f1, u1]
    mine, theirs = far_blocks(plan, pack, nears)
    rows2 = (2 * FAR + 1) * own2
    scratch = [in_vmem(2 * FAR + 1, size, LANES)]
    scratch += [in_vmem(rows2 + 1, 2, nx // 4, LANES)] * 9 + [in_vmem(rows2 // 2 + 1, 2, nx // 4, LANES)] * 8
    scratch += [level1(rows2), level0(own + 8)] + [level1(own + 8)] * 3 + [level0(rows)] * 3
    (result,) = call(
        functools.partial(up_kernel, plan), [in_vmem(gx, by, 2, px, LANES)], scratch
    )(*pinned(pack, mine, theirs, *fields))

    parts = exchange(plan, [result[k].reshape(flat, LANES) for k in range(gx)])
    return call(
        functools.partial(place_kernel, plan),
        [jax.ShapeDtypeStruct((1, px, plan.ny, LANES), F32)] * 2,
    )(*pinned(*parts))


def solution(mesh):
    sizes = [mesh.shape[a] for a in ("gx", "gy", "gz")]

    def local(phase, density, rhs):
        return tuple(on_device(Plan(sizes, phase.shape), phase, density, rhs))

    in_specs = (P("gx", "gy", "gz"), P("gx", "gy", "gz"), P(None, "gx", "gy", "gz"))
    out_specs = (P(None, "gx", "gy", "gz"), P(None, "gx", "gy", "gz"))
    return jax.shard_map(local, mesh=mesh, in_specs=in_specs, out_specs=out_specs, check_vma=False)
```

```python
import functools

import jax
import jax.numpy as jnp
from jax import lax
from jax.experimental import pallas as pl
from jax.experimental.pallas import tpu as pltpu
from jax.sharding import PartitionSpec as P


DAMPING = 2.0 / 3.0
LANES = 128
WIDE = 256
HALO = 7
HALO_RHS = 6
FAR = 3
F32 = jnp.float32
VMEM_LIMIT = 24 * 1024 * 1024


class Plan:
    def __init__(self, sizes, shape):
        self.gx, self.gy, self.gz = sizes
        self.px, self.ny, self.nz = shape
        self.nx = self.px * self.gx
        self.by = self.ny // self.gx
        self.blocks = self.gx * self.gy
        self.rows = self.by + 2 * HALO
        self.paired = self.gz == 2
        self.ring = [0, 1, 3, 2] if self.gx == 4 else list(range(self.gx))
        self.place = [self.ring.index(i) for i in range(self.gx)]
        self.back = [0, 2, 1, 3] if self.gx == 4 else list(range(self.gx))

    def device(self, block):
        j, q = divmod(block, self.gx)
        return self.ring[(q - j) % self.gx] * self.gy + j

    def look_up(self, table, i):
        return sum(jnp.where(i == k, v, 0) for k, v in enumerate(table))

    def start_of(self, i):
        q = lax.rem(self.look_up(self.place, i) + lax.axis_index("gy"), self.gx)
        return pl.multiple_of(q * self.by, self.by)

    def distances(self, core):
        if self.gx != 4:
            return list(range(self.gx))
        return [0, 3, 2, 1] if core else [0, 3, 1, 2]

    def by_core(self, even, odd):
        return even if even == odd else jnp.where(lax.rem(lax.axis_index("gz"), 2) == 0, even, odd)

    def distance(self, slot):
        return self.by_core(self.distances(0)[slot], self.distances(1)[slot])

    def slot(self, distance):
        found = [self.by_core(self.distances(0).index(k), self.distances(1).index(k)) for k in range(self.gx)]
        return self.look_up(found, distance)

    def block_here(self):
        j = lax.axis_index("gy")
        return j * self.gx + lax.rem(self.look_up(self.place, lax.axis_index("gx")) + j, self.gx)

    def gx_of(self, block):
        block = jnp.clip(block, 0, self.blocks - 1)
        j, q = lax.div(block, self.gx), lax.rem(block, self.gx)
        return self.look_up(self.ring, lax.rem(q + self.gx * self.gy - j, self.gx))

    def is_up(self, block, k, one):
        return lax.rem(lax.div(block, k), 2) == one


def x_up(a, s=1):
    return pltpu.roll(a, a.shape[0] - s, 0)


def x_down(a, s=1):
    return pltpu.roll(a, s, 0)


def z_up(a, g):
    return pltpu.roll(a, a.shape[1] - g, 1)


def z_down(a, g):
    return pltpu.roll(a, g, 1)


def inverse(a):
    r = pl.reciprocal(a, approx=True)
    return r * (2.0 - a * r)


def each(first, last, step, body):
    count = last + 1 - first
    if count <= 2 * step:
        for i in range(first, last + 1):
            body(i)
        return

    def go(c, _):
        for k in range(step):
            body(first + c * step + k)
        return 0

    lax.fori_loop(0, count // step, go, 0)
    for i in range(first + count // step * step, last + 1):
        body(i)


def wave(*stages):
    start = min(first + delay for _, first, _, delay in stages)
    end = max(last + delay for _, _, last, delay in stages)
    full = max(first + delay for _, first, _, delay in stages)
    full_end = min(last + delay for _, _, last, delay in stages)

    def step(t):
        for body, first, last, delay in stages:
            if first <= t - delay <= last:
                body(t - delay)

    def all_of_them(t, _):
        for body, _, _, delay in stages:
            body(t - delay)
        return 0

    if full_end - full < 3:
        full = full_end = end + 1
    for t in range(start, min(full, end + 1)):
        step(t)
    if full <= end:
        lax.fori_loop(full, full_end + 1, all_of_them, 0)
        for t in range(full_end + 1, end + 1):
            step(t)


class Wide:
    def __init__(self, ref):
        self.ref = ref

    def __getitem__(self, key):
        r, xs = key if isinstance(key, tuple) else (key, slice(None))
        return jnp.concatenate([self.ref[r, 0, xs, :], self.ref[r, 1, xs, :]], axis=1)

    def __setitem__(self, key, value):
        r, xs = key if isinstance(key, tuple) else (key, slice(None))
        self.ref[r, 0, xs, :] = value[:, :LANES]
        self.ref[r, 1, xs, :] = value[:, LANES:]


class Level:
    def __init__(self, s, g, kx, ky, kz, d, w, f, step=2):
        self.s, self.g, self.step = s, g, step
        self.kx, self.ky, self.kz, self.d, self.w, self.f = kx, ky, kz, d, w, f

    def beside(self, u, r):
        here = u[r]
        kx, kz = self.kx[r], self.kz[r]
        a = kx * x_up(here, self.s) + x_down(kx * here, self.s)
        b = kz * z_up(here, self.g) + z_down(kz * here, self.g)
        return a + b + (self.ky[r + 1] * u[r + 1] + self.ky[r] * u[r - 1])

    def weigh(self, first, last):
        def body(r):
            self.w[r] = DAMPING * inverse(self.d[r])

        each(first, last, self.step, body)

    def first(self, u, first, last):
        def body(r):
            u[r] = self.w[r] * self.f[r]

        each(first, last, self.step, body)

    def swept(self, u, r):
        return (1.0 / 3.0) * u[r] + self.w[r] * (self.f[r] + self.beside(u, r))

    def sweep(self, u, v, first, last):
        def body(r):
            v[r] = self.swept(u, r)

        each(first, last, self.step, body)

    def residual(self, u, r):
        return self.f[r] + self.beside(u, r) - self.d[r] * u[r]

    def residual_pairs(self, u, out, first, count):
        def body(j):
            out[j] = self.residual(u, first + 2 * j) + self.residual(u, first + 2 * j + 1)

        each(0, count - 1, self.step // 2, body)


def z_pairs(low, g):
    return lambda a: a + jnp.where(low, z_up(a, g), z_down(a, g))


def coarse_coefficients(level, r, x_count):
    even, odd = pl.ds(0, x_count, stride=2), pl.ds(1, x_count, stride=2)
    g = level.g
    low = (lax.broadcasted_iota(jnp.int32, (x_count, WIDE), 1) & g) == 0
    z_pair = z_pairs(low, g)

    def all_x(ref, row):
        return ref[row, even] + ref[row, odd]

    kx = level.kx[r, odd] + level.kx[r + 1, odd]
    inner = level.kx[r, even] + level.kx[r + 1, even] + all_x(level.ky, r + 1)
    kz = all_x(level.kz, r) + all_x(level.kz, r + 1)
    d = all_x(level.d, r) + all_x(level.d, r + 1)
    d = d - 2.0 * (inner + jnp.where(low, kz, 0.0))
    return z_pair(kx), coarse_sum(level.ky, r + 2, x_count, g), jnp.where(low, z_up(kz, g), kz), z_pair(d)


def coarse_sum(ref, r, x_count, g):
    even, odd = pl.ds(0, x_count, stride=2), pl.ds(1, x_count, stride=2)
    low = (lax.broadcasted_iota(jnp.int32, (x_count, WIDE), 1) & g) == 0
    return z_pairs(low, g)(ref[r, even] + ref[r, odd])


def correct(u, v, e, t, x_count, first, last, to):
    def body(j):
        part = e[j]
        t[j, pl.ds(0, x_count, stride=2)] = part
        t[j, pl.ds(1, x_count, stride=2)] = part
        wide = t[j]
        r = to + 2 * (j - first)
        v[r] = u[r] + wide
        v[r + 1] = u[r + 1] + wide

    each(first, last, 2, body)


def pick_lanes(a, lanes):
    return jnp.take_along_axis(a, lanes, axis=1, mode="promise_in_bounds")


def prepare_kernel(plan, phase_in, density_in, rhs_in, *refs):
    outs, (phase, density, rhs, sems) = refs[: plan.gx], refs[plan.gx :]
    pairs = ((phase_in, phase), (density_in, density), (rhs_in, rhs))
    copies = [pltpu.make_async_copy(a, b, sems.at[k]) for k, (a, b) in enumerate(pairs)]
    for copy in copies:
        copy.start()
    for copy in copies:
        copy.wait()
    here = lax.axis_index("gx")
    by, px = plan.by, plan.px
    for slot, out in enumerate(outs):
        rows = pl.ds(plan.start_of(here ^ plan.distance(slot)), by)
        for p in range(px):
            half = jnp.where(phase[p, rows, :] == 1, 500.0, 0.5).astype(F32)
            out[pl.ds(p, by, stride=2 * px), :] = half * density[p, rows, :]
            out[pl.ds(px + p, by, stride=2 * px), :] = rhs[0, p, rows, :]


def gather_kernel(plan, *refs):
    parts, (c, *sets) = refs[: plan.gx], refs[plan.gx :]
    block = plan.block_here()
    for slot, part in enumerate(parts):
        k = plan.distance(slot)
        c[k] = part[...]
        for one, out in enumerate(sets):
            up = plan.is_up(block, 1, one)
            for field, count, at in ((0, HALO, 0), (1, HALO_RHS, HALO)):
                first = jnp.where(up, plan.by - count, 0)
                for r in range(count):
                    out[k, at + r] = part[first + r, field]


def compress(stage, g):
    halves, _, rows, _ = stage.shape
    width = LANES // g
    cell = lax.broadcasted_iota(jnp.int32, (rows, LANES), 1)
    lanes, place = lax.rem(g * cell, LANES), lax.div(cell, width)
    total = pick_lanes(stage[0, 0], lanes)
    for k in range(1, 2 * halves):
        total = jnp.where(place == k, pick_lanes(stage[k // 2, k % 2], lanes), total)
    return total


class Finest:
    COUNT = 16

    @staticmethod
    def shapes(plan):
        level0 = in_vmem(plan.rows, 2, plan.nx, LANES)
        pairs = in_vmem(plan.by // 2 + 8, 2, plan.nx, LANES)
        level1 = in_vmem(plan.by // 2 + 8, 2, plan.nx // 2, LANES)
        return [level0] * 10 + [pairs] + [level1] * 5

    def __init__(self, plan, refs):
        self.plan = plan
        fields = [Wide(r) for r in refs]
        self.kx, self.ky, self.kz, self.d, self.w, self.f, self.ub = fields[:7]
        self.h, self.ua, self.face, self.r = fields[7:11]
        self.kx1, self.ky1, self.kz1, self.d1, self.f1 = fields[11:]
        self.level = Level(1, 1, self.kx, self.ky, self.kz, self.d, self.w, self.f)
        nx = plan.nx
        shape = (nx, WIDE)
        self.half_x = nx // 2
        self.base = plan.block_here() * plan.by - HALO
        self.y_count, z_count = plan.by * plan.blocks, plan.nz * plan.gz
        x = lax.broadcasted_iota(jnp.int32, shape, 0)
        lane = lax.broadcasted_iota(jnp.int32, shape, 1)
        core = lax.axis_index("gz")
        if plan.paired:
            z = lax.rem(core * LANES + lane, WIDE)
        else:
            z = core * LANES + jnp.where(lane < LANES + LANES // 2, lane, lane - WIDE)
        self.x_top, self.x_bottom = x == nx - 1, x == 0
        self.z_top, self.z_bottom = z == z_count - 1, z == 0
        self.z_shut = (z < 0) | (z >= z_count - 1)
        self.z_out = (z < 0) | (z >= z_count)

    def put_h(self, to, s, xs, tile):
        y = self.base + to
        tile = jnp.where((y >= 0) & (y < self.y_count), tile, 0.5)
        if not self.plan.paired:
            tile = jnp.where(self.z_out[: self.plan.px, s * LANES : (s + 1) * LANES], 0.5, tile)
        self.h.ref[to, s, xs, :] = tile

    def tiles(self, other):
        px = self.plan.px
        return [(k, pl.ds(pl.multiple_of((other ^ k) * px, px), px)) for k in range(self.plan.gx)]

    def is_open(self, r):
        y = self.base + r
        return (y >= 0) & (y < self.y_count - 1)

    def start(self, r):
        first = inverse(self.h[r] + self.h[r + 1])
        self.face[r + 1] = first
        self.ky[r + 1] = jnp.where(self.is_open(r), first, 0.0)

    def faces(self, j):
        yd = self.face[2 * j - 1]
        for r in (2 * j - 1, 2 * j):
            h = self.h[r]
            alone = 0.5 * inverse(h)
            xu = inverse(h + jnp.where(self.x_top, h, x_up(h)))
            xd = jnp.where(self.x_bottom, alone, x_down(xu))
            yu = inverse(h + self.h[r + 1])
            zu = inverse(h + jnp.where(self.z_top, h, z_up(h, 1)))
            zd = jnp.where(self.z_bottom, alone, z_down(zu, 1))
            d = xu + xd + yu + yd + zu + zd
            w = DAMPING * inverse(d)
            self.kx[r] = jnp.where(self.x_top, 0.0, xu)
            self.ky[r + 1] = jnp.where(self.is_open(r), yu, 0.0)
            self.kz[r] = jnp.where(self.z_shut, 0.0, zu)
            self.d[r], self.w[r] = d, w
            self.ua[r] = w * self.f[r]
            yd = yu
        self.face[2 * j + 1] = yd

    def coarsen(self, j):
        coarse = coarse_coefficients(self.level, 2 * j - 1, self.half_x)
        self.kx1[j], self.ky1[j + 1], self.kz1[j], self.d1[j] = coarse

    def sweep(self, j):
        self.ub[2 * j] = self.level.swept(self.ua, 2 * j)
        self.ub[2 * j + 1] = self.level.swept(self.ua, 2 * j + 1)

    def residual(self, j):
        self.r[j] = self.level.residual(self.ub, 2 * j - 1) + self.level.residual(self.ub, 2 * j)

    def restrict(self, j):
        self.f1[j] = coarse_sum(self.r, j, self.half_x, 1)


def inner_pairs(plan):
    return (HALO + 3) // 2, (HALO + plan.by - 2) // 2


def inner_kernel(plan, c, zc, *refs):
    fine = Finest(plan, refs)

    def take(r):
        for k, xs in fine.tiles(lax.axis_index("gx")):
            for s, ref in enumerate((c, zc)):
                fine.put_h(r + HALO, s, xs, ref[k, r, 0])
                fine.f.ref[r + HALO, s, xs, :] = ref[k, r, 1]

    each(0, plan.by - 1, 4, take)
    first, last = inner_pairs(plan)
    fine.start(2 * first - 2)
    wave(
        (fine.restrict, first + 1, last - 1, 4),
        (fine.residual, first + 1, last - 1, 3),
        (fine.sweep, first, last - 1, 2),
        (fine.coarsen, first, last, 1),
        (fine.faces, first, last, 0),
    )


def down_kernel(plan, sides, zsides, *refs):
    count = Finest.COUNT
    near_count = 1 if plan.paired else 2
    refs = refs[count:]
    fine = Finest(plan, refs[:count])
    kx1, ky1, kz1, d1, f1 = fine.kx1, fine.ky1, fine.kz1, fine.d1, fine.f1
    pack, nears, refs = refs[count], refs[count + 1 : count + 1 + near_count], refs[count + 1 + near_count :]
    w1, u1, uc, r1 = [Wide(r) for r in refs[:4]]
    stage, near_stage = refs[4:6]
    nx, by, gx = plan.nx, plan.by, plan.gx
    block, core = plan.block_here(), lax.axis_index("gz")

    def take_side(at, other, to, count, field):
        def one(r):
            for k, xs in fine.tiles(other):
                for s, ref in enumerate((sides, zsides)):
                    if field == 0:
                        fine.put_h(r + to, s, xs, ref[at + k, r])
                    else:
                        fine.f.ref[r + to, s, xs, :] = ref[at + k, HALO + r]

        each(0, count - 1, 4, one)

    up_first = plan.is_up(block, 1, 0)
    below, above = jnp.where(up_first, 0, gx), jnp.where(up_first, gx, 0)
    gx_below, gx_above = plan.gx_of(block - 1), plan.gx_of(block + 1)
    take_side(below, gx_below, 0, HALO, 0)
    take_side(above, gx_above, HALO + by, HALO, 0)
    take_side(below, gx_below, HALO - HALO_RHS, HALO_RHS, 1)
    take_side(above, gx_above, HALO + by, HALO_RHS, 1)

    @pl.when(block == 0)
    def _():
        fine.h[HALO - 1] = fine.h[HALO]

    @pl.when(block == plan.blocks - 1)
    def _():
        fine.h[HALO + by] = fine.h[HALO + by - 1]

    fine.start(0)
    first, last = inner_pairs(plan)
    end = by // 2 + 6
    late = -last
    wave(
        (fine.restrict, 2, first, 4),
        (fine.restrict, last, end - 1, late + 4),
        (fine.residual, 2, first, 3),
        (fine.residual, last, end - 1, late + 3),
        (fine.sweep, 1, first - 1, 2),
        (fine.sweep, last, end - 1, late + 2),
        (fine.coarsen, 1, first - 1, 1),
        (fine.coarsen, last + 1, end, late + 1),
        (fine.faces, 1, first - 1, 0),
        (fine.faces, last + 1, end, late),
    )
    ky1[1] = coarse_sum(fine.ky, 1, nx // 2, 1)

    own = by // 2
    half_x = nx // 2
    middle = Level(1, 2, kx1, ky1, kz1, d1, w1, f1, 8)
    middle.weigh(1, own + 6)
    middle.first(uc, 2, own + 5)
    middle.sweep(uc, u1, 3, own + 4)
    middle.residual_pairs(u1, r1, 4, own // 2)

    quarter_x = nx // 4
    own2 = own // 2
    part = own2 // 2
    for j in range(own2):
        fields = (coarse_sum(r1, j, quarter_x, 2),) + coarse_coefficients(middle, 4 + 2 * j, quarter_x)
        for t, a in enumerate(fields):
            xs = pl.ds((t * part + j % part) * quarter_x, quarter_x)
            stage[j // part, 0, xs, :] = a[:, :LANES]
            stage[j // part, 1, xs, :] = a[:, LANES:]
    total = compress(stage, 4)
    pack[...] = total

    size = pack.shape[0]
    for one, out in enumerate(nears):
        row = jnp.where(plan.is_up(block, 1, core if plan.paired else one), own, 5)
        for k, (ref, r) in enumerate(((u1, row), (u1, row + 1), (u1, row + 2), (f1, row + 1))):
            for s in range(2):
                near_stage[0, s, pl.ds(k * half_x, half_x), :] = ref.ref[r, s]
        out[pl.ds(0, size), :] = total
        out[pl.ds(size, 4 * half_x), :] = compress(near_stage, 2)


class Coarse:
    COUNT = 9

    @staticmethod
    def shapes(plan):
        rows = (2 * FAR + 1) * (plan.by // 4) + 1
        level2 = in_vmem(rows, 2, plan.nx // 4, LANES)
        level1 = in_vmem(plan.by // 2 + 8, 2, plan.nx // 2, LANES)
        return [level2] * 7 + [level1] * 2

    def __init__(self, plan, refs):
        self.plan = plan
        self.fields = [Wide(r) for r in refs[:5]]
        self.f, self.kx, self.ky, self.kz, self.d = self.fields
        self.w, self.u, self.f1, self.u1 = [Wide(r) for r in refs[5:]]
        self.block = plan.block_here()

    def spread(self, packed, at, turned):
        plan = self.plan
        own2, quarter_x = plan.by // 4, plan.nx // 4
        part = own2 // 2
        there = self.block + at - FAR
        exists = (there >= 0) & (there < plan.blocks)
        lane = lax.broadcasted_iota(jnp.int32, packed.shape, 1)
        for quarter in range(4):
            part_of, half = divmod(quarter, 2)
            s = half ^ turned
            a = pick_lanes(packed, lax.div(lane, 4) + quarter * (LANES // 4))
            for j in range(part):
                r = at * own2 + part_of * part + j
                tiles = [a[(t * part + j) * quarter_x : (t * part + j + 1) * quarter_x] for t in range(5)]
                for t, ref in enumerate(self.fields):
                    if t == 2:
                        ref.ref[r + 1, s] = jnp.where(exists, tiles[t], 0.0)
                    else:
                        ref.ref[r, s] = tiles[t]
                w = DAMPING * inverse(tiles[4])
                self.w.ref[r, s] = w
                self.u.ref[r, s] = w * tiles[0]

    def side(self, ref, ups, turned):
        plan = self.plan
        own, half_x = plan.by // 2, plan.nx // 2
        size = 5 * (plan.by // 8) * (plan.nx // 4)
        nearest = size + 4 * half_x
        for k, up in ups.items():
            first = 0 if k == 1 else nearest + (k - 2) * size
            self.spread(ref[pl.ds(first, size), :], jnp.where(up, FAR + k, FAR - k), turned)
        row = jnp.where(ups[1], own + 5, 0)
        for k, (to, r) in enumerate(((self.u1, row), (self.u1, row + 1), (self.u1, row + 2), (self.f1, row + 1))):
            row_in = ref[pl.ds(size + k * half_x, half_x), :]
            lane = lax.broadcasted_iota(jnp.int32, row_in.shape, 1)
            for s in range(2):
                to.ref[r, s ^ turned] = pick_lanes(row_in, lax.div(lane, 2) + s * (LANES // 2))

    def ups(self, opposite):
        one = lax.axis_index("gz") if self.plan.paired else 0
        one = 1 - one if opposite else one
        return {k: self.plan.is_up(self.block, k, one) for k in range(1, FAR + 1)}


def spread_kernel(plan, pack, mine, f1, u1, *refs):
    coarse = Coarse(plan, refs)
    own = plan.by // 2
    for r in range(2, own + 6):
        coarse.f1.ref[r] = f1[r]
    for r in range(3, own + 5):
        coarse.u1.ref[r] = u1[r]
    coarse.spread(pack[...], FAR, 0)
    coarse.side(mine, coarse.ups(False), 0)


def up_kernel(plan, theirs, *refs):
    count = Coarse.COUNT
    refs = refs[count:]
    kx0, ky0, kz0, d0, w0, f0, u0, kx1, ky1, kz1, w1 = [Wide(r) for r in refs[:11]]
    out, coarse, scratch = refs[11], Coarse(plan, refs[12 : 12 + count]), refs[12 + count :]
    f2, kx2, ky2, kz2, d2, w2, ua2 = *coarse.fields, coarse.w, coarse.u
    f1, ua1 = coarse.f1, coarse.u1
    wide = [Wide(r) for r in scratch]
    ub2, r2, f3, kx3, ky3, kz3, d3, w3, ua3, ub3 = wide[:10]
    t1, t0, ub1, ua0, ub0, uc0 = wide[10:]
    nx, by = plan.nx, plan.by
    own, own2 = by // 2, by // 4
    half_x, quarter_x = nx // 2, nx // 4
    here = lax.axis_index("gx")
    coarse.side(theirs, coarse.ups(True), 1 if plan.paired else 0)

    rows2 = (2 * FAR + 1) * own2
    two = Level(1, 4, kx2, ky2, kz2, d2, w2, f2, 14)
    two.sweep(ua2, ub2, 1, rows2 - 2)
    two.residual_pairs(ub2, r2, 2, rows2 // 2 - 2)

    x = lax.broadcasted_iota(jnp.int32, (quarter_x, WIDE), 0)
    even_x = (x & 1) == 0
    low = (lax.broadcasted_iota(jnp.int32, (quarter_x, WIDE), 1) & 4) == 0
    z_pair = z_pairs(low, 4)

    def x_pair(a):
        return a + jnp.where(even_x, x_up(a), x_down(a))

    last3 = rows2 // 2 - 2

    def coarsen(j):
        r = 2 * j
        kx = kx2[r] + kx2[r + 1]
        kz = kz2[r] + kz2[r + 1]
        inner = ky2[r + 1] + jnp.where(even_x, kx, 0.0) + jnp.where(low, kz, 0.0)
        f3[j] = z_pair(x_pair(r2[j - 1]))
        kx3[j] = z_pair(jnp.where(even_x, x_up(kx), kx))
        ky3[j + 1] = z_pair(x_pair(ky2[r + 2]))
        kz = x_pair(kz)
        kz3[j] = jnp.where(low, z_up(kz, 4), kz)
        d3[j] = z_pair(x_pair(d2[r] + d2[r + 1] - 2.0 * inner))

    each(1, last3, 6, coarsen)
    three = Level(2, 8, kx3, ky3, kz3, d3, w3, f3, 16)
    three.weigh(1, last3)
    three.first(ua3, 1, last3)
    three.sweep(ua3, ub3, 2, last3 - 1)
    three.sweep(ub3, ua3, 3, last3 - 2)
    three.sweep(ua3, ub3, 4, last3 - 3)

    first2 = FAR * own2
    for j in range(4, last3 - 2):
        e = ub3[j]
        ua2[2 * j] = ub2[2 * j] + e
        ua2[2 * j + 1] = ub2[2 * j + 1] + e
    two.sweep(ua2, ub2, first2 - 3, first2 + own2 + 2)
    two.sweep(ub2, ua2, first2 - 2, first2 + own2 + 1)

    one = Level(1, 2, kx1, ky1, kz1, None, w1, f1, 8)
    correct(ua1, ub1, ua2, t1, quarter_x, first2 - 2, first2 + own2 + 1, 0)
    one.sweep(ub1, ua1, 1, own + 6)
    one.sweep(ua1, ub1, 2, own + 5)

    finest = Level(1, 1, kx0, ky0, kz0, d0, w0, f0)

    def corrected(j):
        part = ub1[j]
        t0[j, pl.ds(0, half_x, stride=2)] = part
        t0[j, pl.ds(1, half_x, stride=2)] = part
        both = t0[j]
        ua0[2 * j - 1] = u0[2 * j - 1] + both
        ua0[2 * j] = u0[2 * j] + both

    def sweep(j):
        ub0[2 * j - 1] = finest.swept(ua0, 2 * j - 1)
        ub0[2 * j] = finest.swept(ua0, 2 * j)

    def sweep_again(j):
        uc0[2 * j] = finest.swept(ub0, 2 * j)
        uc0[2 * j + 1] = finest.swept(ub0, 2 * j + 1)

    slots = [plan.slot(s ^ here) for s in range(plan.gx)]

    def finish(j):
        for r in (2 * j - 1, 2 * j):
            scaled = d0[r] * uc0[r]
            rest = f0[r] + finest.beside(uc0, r) - scaled
            for s in range(plan.gx):
                part = slice(s * plan.px, (s + 1) * plan.px)
                out[slots[s], r - HALO, 0] = scaled[part, :LANES]
                out[slots[s], r - HALO, 1] = rest[part, :LANES]

    wave(
        (finish, 4, own + 3, 5),
        (sweep_again, 3, own + 3, 4),
        (sweep, 3, own + 4, 2),
        (corrected, 2, own + 5, 0),
    )


def place_kernel(plan, *refs):
    parts, (scaled, residual) = refs[: plan.gx], refs[plan.gx :]
    here = lax.axis_index("gx")
    by, px = plan.by, plan.px
    for slot, part in zip(plan.back, parts):
        rows = pl.ds(plan.start_of(here ^ plan.distance(slot)), by)
        for p in range(px):
            scaled[0, p, rows, :] = part[pl.ds(p, by, stride=2 * px), :]
            residual[0, p, rows, :] = part[pl.ds(px + p, by, stride=2 * px), :]


def in_vmem(*shape):
    return pltpu.VMEM(shape, F32)


def call(kernel, out_shape, scratch=(), work=0, **more):
    if work:
        more["cost_estimate"] = pl.CostEstimate(flops=0, bytes_accessed=work, transcendentals=0)
    return pl.pallas_call(
        kernel,
        out_shape=out_shape,
        scratch_shapes=list(scratch),
        compiler_params=pltpu.CompilerParams(vmem_limit_bytes=VMEM_LIMIT),
        **more,
    )


def pinned(*arrays, where=pltpu.VMEM):
    return [pltpu.with_memory_space_constraint(a, where) for a in arrays]


def beside_in_z(plan, a):
    count = plan.gz
    if plan.paired:
        return lax.ppermute(a, "gz", [(0, 1), (1, 0)])
    cut = LANES // 2
    right = lax.ppermute(a[..., :cut], "gz", [(i + 1, i) for i in range(count - 1)])
    left = lax.ppermute(a[..., cut:], "gz", [(i, i + 1) for i in range(count - 1)])
    return jnp.concatenate([right, left], axis=-1)


def exchange(plan, parts):
    got = [parts[0]]
    for slot in range(1, plan.gx):
        pairs = []
        for i in range(plan.gx):
            for g in range(plan.gz):
                to = i ^ plan.distances(g % 2)[slot]
                pairs.append((i * plan.gz + g, to * plan.gz + g))
        got.append(lax.ppermute(parts[slot], ("gx", "gz"), pairs))
    return got


def partners(plan, k, one):
    partner = [None] * plan.blocks
    for b in range(plan.blocks - k):
        if b // k % 2 == one:
            partner[b], partner[b + k] = b + k, b
    return partner


def swap_blocks(plan, a, k, one):
    pairs = []
    for b, partner in enumerate(partners(plan, k, one)):
        for g in range(plan.gz):
            to = (b, g ^ 1) if partner is None else (partner, g)
            pairs.append((plan.device(b) * plan.gz + g, plan.device(to[0]) * plan.gz + to[1]))
    return lax.ppermute(a, ("gx", "gy", "gz"), pairs)


def swap_blocks_apart(plan, a, k):
    pairs = []
    for one in range(2):
        partner = partners(plan, k, one)
        alone = [b for b in range(plan.blocks) if partner[b] is None]
        low = [b for b in alone if 2 * b < plan.blocks]
        high = [b for b in alone if 2 * b >= plan.blocks]
        couples = [(low.pop(0), high.pop())] if len(low) % 2 else []
        for group in (low, high):
            couples += zip(group[::2], group[1::2])
        for x, y in couples:
            partner[x], partner[y] = y, x
        pairs += [(2 * plan.device(b) + one, 2 * plan.device(p) + one) for b, p in enumerate(partner)]
    return lax.ppermute(a, ("gx", "gy", "gz"), pairs)


def far_blocks(plan, pack, nears):
    def line(move, near):
        parts = [move(pack, k) for k in range(FAR, 1, -1)] + [move(near, 1)]
        return jnp.concatenate(parts[::-1], axis=0)

    if plan.paired:
        mine = line(functools.partial(swap_blocks_apart, plan), nears[0])
        return mine, beside_in_z(plan, mine)
    return [line(functools.partial(swap_blocks, plan, one=one), nears[one]) for one in range(2)]


def on_device(plan, phase, density, rhs):
    nx, by, rows, px, gx = plan.nx, plan.by, plan.rows, plan.px, plan.gx
    flat = by * 2 * px
    block = (px, plan.ny, LANES)
    outside = pl.BlockSpec(memory_space=pltpu.HBM)
    parts = call(
        functools.partial(prepare_kernel, plan),
        [in_vmem(flat, LANES)] * gx,
        [pltpu.VMEM(block, jnp.int32), in_vmem(*block), in_vmem(1, *block), pltpu.SemaphoreType.DMA((3,))],
        in_specs=[outside] * 3,
    )(*pinned(phase, density, rhs, where=pltpu.HBM))
    parts = [a.reshape(by, 2, px, LANES) for a in exchange(plan, parts)]
    c, *sets = call(
        functools.partial(gather_kernel, plan),
        [in_vmem(gx, by, 2, px, LANES)] + [in_vmem(gx, HALO + HALO_RHS, px, LANES)] * 2,
    )(*pinned(*parts))
    sides = jnp.concatenate([swap_blocks(plan, sets[one], 1, one) for one in (1, 0)], axis=0)
    zc = beside_in_z(plan, c)
    zsides = beside_in_z(plan, sides)

    own, own2 = by // 2, by // 4
    size = 5 * (own2 // 2) * (nx // 4)
    side = size + 4 * (nx // 2)

    def level0(n):
        return in_vmem(n, 2, nx, LANES)

    def level1(n):
        return in_vmem(n, 2, nx // 2, LANES)

    inner = call(functools.partial(inner_kernel, plan), Finest.shapes(plan), work=9_000_000)(*pinned(c, zc))
    near_count = 1 if plan.paired else 2
    outs = Finest.shapes(plan) + [in_vmem(size, LANES)] + [in_vmem(side, LANES)] * near_count + [level1(own + 8)] * 2
    scratch = [level1(own + 8), level1(own2), in_vmem(2, 2, size, LANES), in_vmem(1, 2, 4 * (nx // 2), LANES)]
    down = call(
        functools.partial(down_kernel, plan),
        outs,
        scratch,
        input_output_aliases={2 + k: k for k in range(Finest.COUNT)},
    )(*pinned(sides, zsides, *inner))
    fine, rest = down[: Finest.COUNT], down[Finest.COUNT :]
    pack, nears, (w1, u1) = rest[0], rest[1 : 1 + near_count], rest[1 + near_count :]
    kx1, ky1, kz1, _, f1 = fine[11:]
    mine, theirs = far_blocks(plan, pack, nears)
    coarse = call(functools.partial(spread_kernel, plan), Coarse.shapes(plan), work=3_000_000)(
        *pinned(pack, mine, f1, u1)
    )
    rows2 = (2 * FAR + 1) * own2
    level2, level3 = in_vmem(rows2 + 1, 2, nx // 4, LANES), in_vmem(rows2 // 2 + 1, 2, nx // 4, LANES)
    scratch = [level2] * 2 + [level3] * 8 + [level1(rows2), level0(own + 8), level1(own + 8)] + [level0(rows)] * 3
    result = call(
        functools.partial(up_kernel, plan),
        [in_vmem(gx, by, 2, px, LANES)] + Coarse.shapes(plan),
        scratch,
        input_output_aliases={1 + k: 1 + k for k in range(Coarse.COUNT)},
    )(*pinned(theirs, *coarse, *fine[:7], kx1, ky1, kz1, w1))[0]

    parts = exchange(plan, [result[k].reshape(flat, LANES) for k in range(gx)])
    return call(
        functools.partial(place_kernel, plan),
        [jax.ShapeDtypeStruct((1, px, plan.ny, LANES), F32)] * 2,
    )(*pinned(*[parts[slot] for slot in plan.back]))


def solution(mesh):
    sizes = [mesh.shape[a] for a in ("gx", "gy", "gz")]

    def local(phase, density, rhs):
        return tuple(on_device(Plan(sizes, phase.shape), phase, density, rhs))

    in_specs = (P("gx", "gy", "gz"), P("gx", "gy", "gz"), P(None, "gx", "gy", "gz"))
    out_specs = (P(None, "gx", "gy", "gz"), P(None, "gx", "gy", "gz"))
    return jax.shard_map(local, mesh=mesh, in_specs=in_specs, out_specs=out_specs, check_vma=False)
```

```python
import functools

import jax
import jax.numpy as jnp
from jax import lax
from jax.experimental import pallas as pl
from jax.experimental.pallas import tpu as pltpu
from jax.sharding import PartitionSpec as P


DAMPING = 2.0 / 3.0
LANES = 128
WIDE = 256
HALO = 7
HALO_RHS = 6
FAR = 3
F32 = jnp.float32
VMEM_LIMIT = 24 * 1024 * 1024


class Plan:
    def __init__(self, sizes, shape):
        self.gx, self.gy, self.gz = sizes
        self.px, self.ny, self.nz = shape
        self.nx = self.px * self.gx
        self.by = self.ny // self.gx
        self.blocks = self.gx * self.gy
        self.rows = self.by + 2 * HALO
        self.paired = self.gz == 2
        self.ring = [0, 1, 3, 2] if self.gx == 4 else list(range(self.gx))
        self.place = [self.ring.index(i) for i in range(self.gx)]
        self.back = [0, 2, 3, 1] if self.gx == 4 else list(range(self.gx))

    def device(self, block):
        j, q = divmod(block, self.gx)
        return self.ring[(q - j) % self.gx] * self.gy + j

    def look_up(self, table, i):
        return sum(jnp.where(i == k, v, 0) for k, v in enumerate(table))

    def start_of(self, i):
        q = lax.rem(self.look_up(self.place, i) + lax.axis_index("gy"), self.gx)
        return pl.multiple_of(q * self.by, self.by)

    def distances(self, core):
        if self.gx != 4:
            return list(range(self.gx))
        return [0, 3, 2, 1] if core else [0, 3, 1, 2]

    def by_core(self, even, odd):
        return even if even == odd else jnp.where(lax.rem(lax.axis_index("gz"), 2) == 0, even, odd)

    def distance(self, slot):
        return self.by_core(self.distances(0)[slot], self.distances(1)[slot])

    def slot(self, distance):
        found = [self.by_core(self.distances(0).index(k), self.distances(1).index(k)) for k in range(self.gx)]
        return self.look_up(found, distance)

    def block_here(self):
        j = lax.axis_index("gy")
        return j * self.gx + lax.rem(self.look_up(self.place, lax.axis_index("gx")) + j, self.gx)

    def gx_of(self, block):
        block = jnp.clip(block, 0, self.blocks - 1)
        j, q = lax.div(block, self.gx), lax.rem(block, self.gx)
        return self.look_up(self.ring, lax.rem(q + self.gx * self.gy - j, self.gx))

    def is_up(self, block, k, one):
        return lax.rem(lax.div(block, k), 2) == one


def x_up(a, s=1):
    return pltpu.roll(a, a.shape[0] - s, 0)


def x_down(a, s=1):
    return pltpu.roll(a, s, 0)


def z_up(a, g):
    return pltpu.roll(a, a.shape[1] - g, 1)


def z_down(a, g):
    return pltpu.roll(a, g, 1)


def inverse(a):
    r = pl.reciprocal(a, approx=True)
    return r * (2.0 - a * r)


def each(first, last, step, body):
    count = last + 1 - first
    if count <= 2 * step:
        for i in range(first, last + 1):
            body(i)
        return

    def go(c, _):
        for k in range(step):
            body(first + c * step + k)
        return 0

    lax.fori_loop(0, count // step, go, 0)
    for i in range(first + count // step * step, last + 1):
        body(i)


def wave(*stages):
    start = min(first + delay for _, first, _, delay in stages)
    end = max(last + delay for _, _, last, delay in stages)
    full = max(first + delay for _, first, _, delay in stages)
    full_end = min(last + delay for _, _, last, delay in stages)

    def step(t):
        for body, first, last, delay in stages:
            if first <= t - delay <= last:
                body(t - delay)

    def all_of_them(t, _):
        for body, _, _, delay in stages:
            body(t - delay)
        return 0

    if full_end - full < 3:
        full = full_end = end + 1
    for t in range(start, min(full, end + 1)):
        step(t)
    if full <= end:
        lax.fori_loop(full, full_end + 1, all_of_them, 0)
        for t in range(full_end + 1, end + 1):
            step(t)


class Wide:
    def __init__(self, ref):
        self.ref = ref

    def __getitem__(self, key):
        r, xs = key if isinstance(key, tuple) else (key, slice(None))
        return jnp.concatenate([self.ref[r, 0, xs, :], self.ref[r, 1, xs, :]], axis=1)

    def __setitem__(self, key, value):
        r, xs = key if isinstance(key, tuple) else (key, slice(None))
        self.ref[r, 0, xs, :] = value[:, :LANES]
        self.ref[r, 1, xs, :] = value[:, LANES:]


class Level:
    def __init__(self, s, g, kx, ky, kz, d, w, f, step=2):
        self.s, self.g, self.step = s, g, step
        self.kx, self.ky, self.kz, self.d, self.w, self.f = kx, ky, kz, d, w, f

    def beside(self, u, r):
        here = u[r]
        kx, kz = self.kx[r], self.kz[r]
        a = kx * x_up(here, self.s) + x_down(kx * here, self.s)
        b = kz * z_up(here, self.g) + z_down(kz * here, self.g)
        return a + b + (self.ky[r + 1] * u[r + 1] + self.ky[r] * u[r - 1])

    def weigh(self, first, last):
        def body(r):
            self.w[r] = DAMPING * inverse(self.d[r])

        each(first, last, self.step, body)

    def first(self, u, first, last):
        def body(r):
            u[r] = self.w[r] * self.f[r]

        each(first, last, self.step, body)

    def swept(self, u, r):
        return (1.0 / 3.0) * u[r] + self.w[r] * (self.f[r] + self.beside(u, r))

    def sweep(self, u, v, first, last):
        def body(r):
            v[r] = self.swept(u, r)

        each(first, last, self.step, body)

    def residual(self, u, r):
        return self.f[r] + self.beside(u, r) - self.d[r] * u[r]

    def residual_pairs(self, u, out, first, count):
        def body(j):
            out[j] = self.residual(u, first + 2 * j) + self.residual(u, first + 2 * j + 1)

        each(0, count - 1, self.step // 2, body)


def z_pairs(low, g):
    return lambda a: a + jnp.where(low, z_up(a, g), z_down(a, g))


def coarse_coefficients(level, r, x_count):
    even, odd = pl.ds(0, x_count, stride=2), pl.ds(1, x_count, stride=2)
    g = level.g
    low = (lax.broadcasted_iota(jnp.int32, (x_count, WIDE), 1) & g) == 0
    z_pair = z_pairs(low, g)

    def all_x(ref, row):
        return ref[row, even] + ref[row, odd]

    kx = level.kx[r, odd] + level.kx[r + 1, odd]
    inner = level.kx[r, even] + level.kx[r + 1, even] + all_x(level.ky, r + 1)
    kz = all_x(level.kz, r) + all_x(level.kz, r + 1)
    d = all_x(level.d, r) + all_x(level.d, r + 1)
    d = d - 2.0 * (inner + jnp.where(low, kz, 0.0))
    return z_pair(kx), coarse_sum(level.ky, r + 2, x_count, g), jnp.where(low, z_up(kz, g), kz), z_pair(d)


def coarse_sum(ref, r, x_count, g):
    even, odd = pl.ds(0, x_count, stride=2), pl.ds(1, x_count, stride=2)
    low = (lax.broadcasted_iota(jnp.int32, (x_count, WIDE), 1) & g) == 0
    return z_pairs(low, g)(ref[r, even] + ref[r, odd])


def correct(u, v, e, t, x_count, first, last, to):
    def body(j):
        part = e[j]
        t[j, pl.ds(0, x_count, stride=2)] = part
        t[j, pl.ds(1, x_count, stride=2)] = part
        wide = t[j]
        r = to + 2 * (j - first)
        v[r] = u[r] + wide
        v[r + 1] = u[r + 1] + wide

    each(first, last, 2, body)


def pick_lanes(a, lanes):
    return jnp.take_along_axis(a, lanes, axis=1, mode="promise_in_bounds")


def prepare_kernel(plan, phase_in, density_in, rhs_in, *refs):
    outs, (phase, density, rhs, sems) = refs[: plan.gx], refs[plan.gx :]
    pairs = ((phase_in, phase), (density_in, density), (rhs_in, rhs))
    copies = [pltpu.make_async_copy(a, b, sems.at[k]) for k, (a, b) in enumerate(pairs)]
    for copy in copies:
        copy.start()
    for copy in copies:
        copy.wait()
    here = lax.axis_index("gx")
    by, px = plan.by, plan.px
    for slot, out in enumerate(outs):
        rows = pl.ds(plan.start_of(here ^ plan.distance(slot)), by)
        for p in range(px):
            half = jnp.where(phase[p, rows, :] == 1, 500.0, 0.5).astype(F32)
            out[pl.ds(p, by, stride=2 * px), :] = half * density[p, rows, :]
            out[pl.ds(px + p, by, stride=2 * px), :] = rhs[0, p, rows, :]


def gather_kernel(plan, *refs):
    parts, (c, *sets) = refs[: plan.gx], refs[plan.gx :]
    block = plan.block_here()
    for slot, part in enumerate(parts):
        k = plan.distance(slot)
        c[k] = part[...]
        for one, out in enumerate(sets):
            up = plan.is_up(block, 1, one)
            for field, count, at in ((0, HALO, 0), (1, HALO_RHS, HALO)):
                first = jnp.where(up, plan.by - count, 0)
                for r in range(count):
                    out[k, at + r] = part[first + r, field]


def compress(stage, g):
    halves, _, rows, _ = stage.shape
    width = LANES // g
    cell = lax.broadcasted_iota(jnp.int32, (rows, LANES), 1)
    lanes, place = lax.rem(g * cell, LANES), lax.div(cell, width)
    total = pick_lanes(stage[0, 0], lanes)
    for k in range(1, 2 * halves):
        total = jnp.where(place == k, pick_lanes(stage[k // 2, k % 2], lanes), total)
    return total


class Finest:
    COUNT = 16

    @staticmethod
    def shapes(plan):
        level0 = in_vmem(plan.rows, 2, plan.nx, LANES)
        pairs = in_vmem(plan.by // 2 + 8, 2, plan.nx, LANES)
        level1 = in_vmem(plan.by // 2 + 8, 2, plan.nx // 2, LANES)
        return [level0] * 10 + [pairs] + [level1] * 5

    def __init__(self, plan, refs):
        self.plan = plan
        fields = [Wide(r) for r in refs]
        self.kx, self.ky, self.kz, self.d, self.w, self.f, self.ub = fields[:7]
        self.h, self.ua, self.face, self.r = fields[7:11]
        self.kx1, self.ky1, self.kz1, self.d1, self.f1 = fields[11:]
        self.level = Level(1, 1, self.kx, self.ky, self.kz, self.d, self.w, self.f)
        nx = plan.nx
        shape = (nx, WIDE)
        self.half_x = nx // 2
        self.base = plan.block_here() * plan.by - HALO
        self.y_count, z_count = plan.by * plan.blocks, plan.nz * plan.gz
        x = lax.broadcasted_iota(jnp.int32, shape, 0)
        lane = lax.broadcasted_iota(jnp.int32, shape, 1)
        core = lax.axis_index("gz")
        if plan.paired:
            z = lax.rem(core * LANES + lane, WIDE)
        else:
            z = core * LANES + jnp.where(lane < LANES + LANES // 2, lane, lane - WIDE)
        self.x_top, self.x_bottom = x == nx - 1, x == 0
        self.z_top, self.z_bottom = z == z_count - 1, z == 0
        self.z_shut = (z < 0) | (z >= z_count - 1)
        self.z_out = (z < 0) | (z >= z_count)

    def put_h(self, to, s, xs, tile):
        y = self.base + to
        tile = jnp.where((y >= 0) & (y < self.y_count), tile, 0.5)
        if not self.plan.paired:
            tile = jnp.where(self.z_out[: self.plan.px, s * LANES : (s + 1) * LANES], 0.5, tile)
        self.h.ref[to, s, xs, :] = tile

    def tiles(self, other):
        px = self.plan.px
        return [(k, pl.ds(pl.multiple_of((other ^ k) * px, px), px)) for k in range(self.plan.gx)]

    def is_open(self, r):
        y = self.base + r
        return (y >= 0) & (y < self.y_count - 1)

    def start(self, r):
        first = inverse(self.h[r] + self.h[r + 1])
        self.face[r + 1] = first
        self.ky[r + 1] = jnp.where(self.is_open(r), first, 0.0)

    def faces(self, j):
        yd = self.face[2 * j - 1]
        for r in (2 * j - 1, 2 * j):
            h = self.h[r]
            alone = 0.5 * inverse(h)
            xu = inverse(h + jnp.where(self.x_top, h, x_up(h)))
            xd = jnp.where(self.x_bottom, alone, x_down(xu))
            yu = inverse(h + self.h[r + 1])
            zu = inverse(h + jnp.where(self.z_top, h, z_up(h, 1)))
            zd = jnp.where(self.z_bottom, alone, z_down(zu, 1))
            d = xu + xd + yu + yd + zu + zd
            w = DAMPING * inverse(d)
            self.kx[r] = jnp.where(self.x_top, 0.0, xu)
            self.ky[r + 1] = jnp.where(self.is_open(r), yu, 0.0)
            self.kz[r] = jnp.where(self.z_shut, 0.0, zu)
            self.d[r], self.w[r] = d, w
            self.ua[r] = w * self.f[r]
            yd = yu
        self.face[2 * j + 1] = yd

    def coarsen(self, j):
        coarse = coarse_coefficients(self.level, 2 * j - 1, self.half_x)
        self.kx1[j], self.ky1[j + 1], self.kz1[j], self.d1[j] = coarse

    def sweep(self, j):
        self.ub[2 * j] = self.level.swept(self.ua, 2 * j)
        self.ub[2 * j + 1] = self.level.swept(self.ua, 2 * j + 1)

    def residual(self, j):
        self.r[j] = self.level.residual(self.ub, 2 * j - 1) + self.level.residual(self.ub, 2 * j)

    def restrict(self, j):
        self.f1[j] = coarse_sum(self.r, j, self.half_x, 1)


def inner_pairs(plan):
    return (HALO + 3) // 2, (HALO + plan.by - 2) // 2


def inner_kernel(plan, c, zc, *refs):
    fine = Finest(plan, refs)

    def take(r):
        for k, xs in fine.tiles(lax.axis_index("gx")):
            for s, ref in enumerate((c, zc)):
                fine.put_h(r + HALO, s, xs, ref[k, r, 0])
                fine.f.ref[r + HALO, s, xs, :] = ref[k, r, 1]

    each(0, plan.by - 1, 4, take)
    first, last = inner_pairs(plan)
    fine.start(2 * first - 2)
    wave(
        (fine.restrict, first + 1, last - 1, 4),
        (fine.residual, first + 1, last - 1, 3),
        (fine.sweep, first, last - 1, 2),
        (fine.coarsen, first, last, 1),
        (fine.faces, first, last, 0),
    )


def down_kernel(plan, sides, zsides, *refs):
    count = Finest.COUNT
    near_count = 1 if plan.paired else 2
    refs = refs[count:]
    fine = Finest(plan, refs[:count])
    kx1, ky1, kz1, d1, f1 = fine.kx1, fine.ky1, fine.kz1, fine.d1, fine.f1
    pack, nears, refs = refs[count], refs[count + 1 : count + 1 + near_count], refs[count + 1 + near_count :]
    w1, u1, uc, r1 = [Wide(r) for r in refs[:4]]
    stage, near_stage = refs[4:6]
    nx, by, gx = plan.nx, plan.by, plan.gx
    block, core = plan.block_here(), lax.axis_index("gz")

    def take_side(at, other, to, count, field):
        def one(r):
            for k, xs in fine.tiles(other):
                for s, ref in enumerate((sides, zsides)):
                    if field == 0:
                        fine.put_h(r + to, s, xs, ref[at + k, r])
                    else:
                        fine.f.ref[r + to, s, xs, :] = ref[at + k, HALO + r]

        each(0, count - 1, 4, one)

    up_first = plan.is_up(block, 1, 0)
    below, above = jnp.where(up_first, 0, gx), jnp.where(up_first, gx, 0)
    gx_below, gx_above = plan.gx_of(block - 1), plan.gx_of(block + 1)
    take_side(below, gx_below, 0, HALO, 0)
    take_side(above, gx_above, HALO + by, HALO, 0)
    take_side(below, gx_below, HALO - HALO_RHS, HALO_RHS, 1)
    take_side(above, gx_above, HALO + by, HALO_RHS, 1)

    @pl.when(block == 0)
    def _():
        fine.h[HALO - 1] = fine.h[HALO]

    @pl.when(block == plan.blocks - 1)
    def _():
        fine.h[HALO + by] = fine.h[HALO + by - 1]

    fine.start(0)
    first, last = inner_pairs(plan)
    end = by // 2 + 6
    late = -last
    wave(
        (fine.restrict, 2, first, 4),
        (fine.restrict, last, end - 1, late + 4),
        (fine.residual, 2, first, 3),
        (fine.residual, last, end - 1, late + 3),
        (fine.sweep, 1, first - 1, 2),
        (fine.sweep, last, end - 1, late + 2),
        (fine.coarsen, 1, first - 1, 1),
        (fine.coarsen, last + 1, end, late + 1),
        (fine.faces, 1, first - 1, 0),
        (fine.faces, last + 1, end, late),
    )
    ky1[1] = coarse_sum(fine.ky, 1, nx // 2, 1)

    own = by // 2
    half_x = nx // 2
    middle = Level(1, 2, kx1, ky1, kz1, d1, w1, f1, 8)
    middle.weigh(1, own + 6)
    middle.first(uc, 2, own + 5)
    middle.sweep(uc, u1, 3, own + 4)
    middle.residual_pairs(u1, r1, 4, own // 2)

    quarter_x = nx // 4
    own2 = own // 2
    part = own2 // 2
    for j in range(own2):
        fields = (coarse_sum(r1, j, quarter_x, 2),) + coarse_coefficients(middle, 4 + 2 * j, quarter_x)
        for t, a in enumerate(fields):
            xs = pl.ds((t * part + j % part) * quarter_x, quarter_x)
            stage[j // part, 0, xs, :] = a[:, :LANES]
            stage[j // part, 1, xs, :] = a[:, LANES:]
    total = compress(stage, 4)
    pack[...] = total

    size = pack.shape[0]
    for one, out in enumerate(nears):
        row = jnp.where(plan.is_up(block, 1, core if plan.paired else one), own, 5)
        for k, (ref, r) in enumerate(((u1, row), (u1, row + 1), (u1, row + 2), (f1, row + 1))):
            for s in range(2):
                near_stage[0, s, pl.ds(k * half_x, half_x), :] = ref.ref[r, s]
        out[pl.ds(0, size), :] = total
        out[pl.ds(size, 4 * half_x), :] = compress(near_stage, 2)


class Coarse:
    COUNT = 9

    @staticmethod
    def shapes(plan):
        rows = (2 * FAR + 1) * (plan.by // 4) + 1
        level2 = in_vmem(rows, 2, plan.nx // 4, LANES)
        level1 = in_vmem(plan.by // 2 + 8, 2, plan.nx // 2, LANES)
        return [level2] * 7 + [level1] * 2

    def __init__(self, plan, refs):
        self.plan = plan
        self.fields = [Wide(r) for r in refs[:5]]
        self.f, self.kx, self.ky, self.kz, self.d = self.fields
        self.w, self.u, self.f1, self.u1 = [Wide(r) for r in refs[5:]]
        self.block = plan.block_here()

    def spread(self, packed, at, turned):
        plan = self.plan
        own2, quarter_x = plan.by // 4, plan.nx // 4
        part = own2 // 2
        there = self.block + at - FAR
        exists = (there >= 0) & (there < plan.blocks)
        lane = lax.broadcasted_iota(jnp.int32, packed.shape, 1)
        for quarter in range(4):
            part_of, half = divmod(quarter, 2)
            s = half ^ turned
            a = pick_lanes(packed, lax.div(lane, 4) + quarter * (LANES // 4))
            for j in range(part):
                r = at * own2 + part_of * part + j
                tiles = [a[(t * part + j) * quarter_x : (t * part + j + 1) * quarter_x] for t in range(5)]
                for t, ref in enumerate(self.fields):
                    if t == 2:
                        ref.ref[r + 1, s] = jnp.where(exists, tiles[t], 0.0)
                    else:
                        ref.ref[r, s] = tiles[t]
                w = DAMPING * inverse(tiles[4])
                self.w.ref[r, s] = w
                self.u.ref[r, s] = w * tiles[0]

    def side(self, ref, ups, turned):
        plan = self.plan
        own, half_x = plan.by // 2, plan.nx // 2
        size = 5 * (plan.by // 8) * (plan.nx // 4)
        nearest = size + 4 * half_x
        for k, up in ups.items():
            first = 0 if k == 1 else nearest + (k - 2) * size
            self.spread(ref[pl.ds(first, size), :], jnp.where(up, FAR + k, FAR - k), turned)
        row = jnp.where(ups[1], own + 5, 0)
        for k, (to, r) in enumerate(((self.u1, row), (self.u1, row + 1), (self.u1, row + 2), (self.f1, row + 1))):
            row_in = ref[pl.ds(size + k * half_x, half_x), :]
            lane = lax.broadcasted_iota(jnp.int32, row_in.shape, 1)
            for s in range(2):
                to.ref[r, s ^ turned] = pick_lanes(row_in, lax.div(lane, 2) + s * (LANES // 2))

    def ups(self, opposite):
        one = lax.axis_index("gz") if self.plan.paired else 0
        one = 1 - one if opposite else one
        return {k: self.plan.is_up(self.block, k, one) for k in range(1, FAR + 1)}


def spread_kernel(plan, pack, mine, f1, u1, *refs):
    coarse = Coarse(plan, refs)
    own = plan.by // 2
    for r in range(2, own + 6):
        coarse.f1.ref[r] = f1[r]
    for r in range(3, own + 5):
        coarse.u1.ref[r] = u1[r]
    coarse.spread(pack[...], FAR, 0)
    coarse.side(mine, coarse.ups(False), 0)


def up_kernel(plan, theirs, *refs):
    count = Coarse.COUNT
    refs = refs[count:]
    kx0, ky0, kz0, d0, w0, f0, u0, kx1, ky1, kz1, w1 = [Wide(r) for r in refs[:11]]
    out, coarse, scratch = refs[11], Coarse(plan, refs[12 : 12 + count]), refs[12 + count :]
    f2, kx2, ky2, kz2, d2, w2, ua2 = *coarse.fields, coarse.w, coarse.u
    f1, ua1 = coarse.f1, coarse.u1
    wide = [Wide(r) for r in scratch]
    ub2, r2, f3, kx3, ky3, kz3, d3, w3, ua3, ub3 = wide[:10]
    t1, t0, ub1, ua0, ub0, uc0 = wide[10:]
    nx, by = plan.nx, plan.by
    own, own2 = by // 2, by // 4
    half_x, quarter_x = nx // 2, nx // 4
    here = lax.axis_index("gx")
    coarse.side(theirs, coarse.ups(True), 1 if plan.paired else 0)

    rows2 = (2 * FAR + 1) * own2
    two = Level(1, 4, kx2, ky2, kz2, d2, w2, f2, 14)
    two.sweep(ua2, ub2, 1, rows2 - 2)
    two.residual_pairs(ub2, r2, 2, rows2 // 2 - 2)

    x = lax.broadcasted_iota(jnp.int32, (quarter_x, WIDE), 0)
    even_x = (x & 1) == 0
    low = (lax.broadcasted_iota(jnp.int32, (quarter_x, WIDE), 1) & 4) == 0
    z_pair = z_pairs(low, 4)

    def x_pair(a):
        return a + jnp.where(even_x, x_up(a), x_down(a))

    last3 = rows2 // 2 - 2

    def coarsen(j):
        r = 2 * j
        kx = kx2[r] + kx2[r + 1]
        kz = kz2[r] + kz2[r + 1]
        inner = ky2[r + 1] + jnp.where(even_x, kx, 0.0) + jnp.where(low, kz, 0.0)
        f3[j] = z_pair(x_pair(r2[j - 1]))
        kx3[j] = z_pair(jnp.where(even_x, x_up(kx), kx))
        ky3[j + 1] = z_pair(x_pair(ky2[r + 2]))
        kz = x_pair(kz)
        kz3[j] = jnp.where(low, z_up(kz, 4), kz)
        d3[j] = z_pair(x_pair(d2[r] + d2[r + 1] - 2.0 * inner))

    each(1, last3, 6, coarsen)
    three = Level(2, 8, kx3, ky3, kz3, d3, w3, f3, 16)
    three.weigh(1, last3)
    three.first(ua3, 1, last3)
    three.sweep(ua3, ub3, 2, last3 - 1)
    three.sweep(ub3, ua3, 3, last3 - 2)
    three.sweep(ua3, ub3, 4, last3 - 3)

    first2 = FAR * own2
    for j in range(4, last3 - 2):
        e = ub3[j]
        ua2[2 * j] = ub2[2 * j] + e
        ua2[2 * j + 1] = ub2[2 * j + 1] + e
    two.sweep(ua2, ub2, first2 - 3, first2 + own2 + 2)
    two.sweep(ub2, ua2, first2 - 2, first2 + own2 + 1)

    one = Level(1, 2, kx1, ky1, kz1, None, w1, f1, 8)
    correct(ua1, ub1, ua2, t1, quarter_x, first2 - 2, first2 + own2 + 1, 0)
    one.sweep(ub1, ua1, 1, own + 6)
    one.sweep(ua1, ub1, 2, own + 5)

    finest = Level(1, 1, kx0, ky0, kz0, d0, w0, f0)

    def corrected(j):
        part = ub1[j]
        t0[j, pl.ds(0, half_x, stride=2)] = part
        t0[j, pl.ds(1, half_x, stride=2)] = part
        both = t0[j]
        ua0[2 * j - 1] = u0[2 * j - 1] + both
        ua0[2 * j] = u0[2 * j] + both

    def sweep(j):
        ub0[2 * j - 1] = finest.swept(ua0, 2 * j - 1)
        ub0[2 * j] = finest.swept(ua0, 2 * j)

    def sweep_again(j):
        uc0[2 * j] = finest.swept(ub0, 2 * j)
        uc0[2 * j + 1] = finest.swept(ub0, 2 * j + 1)

    slots = [plan.slot(s ^ here) for s in range(plan.gx)]

    def finish(j):
        for r in (2 * j - 1, 2 * j):
            scaled = d0[r] * uc0[r]
            rest = f0[r] + finest.beside(uc0, r) - scaled
            for s in range(plan.gx):
                part = slice(s * plan.px, (s + 1) * plan.px)
                out[slots[s], r - HALO, 0] = scaled[part, :LANES]
                out[slots[s], r - HALO, 1] = rest[part, :LANES]

    wave(
        (finish, 4, own + 3, 5),
        (sweep_again, 3, own + 3, 4),
        (sweep, 3, own + 4, 2),
        (corrected, 2, own + 5, 0),
    )


def place_kernel(plan, *refs):
    parts, (scaled, residual) = refs[: plan.gx], refs[plan.gx :]
    here = lax.axis_index("gx")
    by, px = plan.by, plan.px
    for slot, part in zip(plan.back, parts):
        rows = pl.ds(plan.start_of(here ^ plan.distance(slot)), by)
        for p in range(px):
            scaled[0, p, rows, :] = part[pl.ds(p, by, stride=2 * px), :]
            residual[0, p, rows, :] = part[pl.ds(px + p, by, stride=2 * px), :]


def in_vmem(*shape):
    return pltpu.VMEM(shape, F32)


def call(kernel, out_shape, scratch=(), work=0, **more):
    if work:
        more["cost_estimate"] = pl.CostEstimate(flops=0, bytes_accessed=work, transcendentals=0)
    return pl.pallas_call(
        kernel,
        out_shape=out_shape,
        scratch_shapes=list(scratch),
        compiler_params=pltpu.CompilerParams(vmem_limit_bytes=VMEM_LIMIT),
        **more,
    )


def pinned(*arrays, where=pltpu.VMEM):
    return [pltpu.with_memory_space_constraint(a, where) for a in arrays]


def beside_in_z(plan, a):
    count = plan.gz
    if plan.paired:
        return lax.ppermute(a, "gz", [(0, 1), (1, 0)])
    cut = LANES // 2
    right = lax.ppermute(a[..., :cut], "gz", [(i + 1, i) for i in range(count - 1)])
    left = lax.ppermute(a[..., cut:], "gz", [(i, i + 1) for i in range(count - 1)])
    return jnp.concatenate([right, left], axis=-1)


def exchange(plan, parts):
    got = [parts[0]]
    for slot in range(1, plan.gx):
        pairs = []
        for i in range(plan.gx):
            for g in range(plan.gz):
                to = i ^ plan.distances(g % 2)[slot]
                pairs.append((i * plan.gz + g, to * plan.gz + g))
        got.append(lax.ppermute(parts[slot], ("gx", "gz"), pairs))
    return got


def partners(plan, k, one):
    partner = [None] * plan.blocks
    for b in range(plan.blocks - k):
        if b // k % 2 == one:
            partner[b], partner[b + k] = b + k, b
    return partner


def swap_blocks(plan, a, k, one):
    pairs = []
    for b, partner in enumerate(partners(plan, k, one)):
        for g in range(plan.gz):
            to = (b, g ^ 1) if partner is None else (partner, g)
            pairs.append((plan.device(b) * plan.gz + g, plan.device(to[0]) * plan.gz + to[1]))
    return lax.ppermute(a, ("gx", "gy", "gz"), pairs)


def swap_blocks_apart(plan, a, k):
    pairs = []
    for one in range(2):
        partner = partners(plan, k, one)
        alone = [b for b in range(plan.blocks) if partner[b] is None]
        low = [b for b in alone if 2 * b < plan.blocks]
        high = [b for b in alone if 2 * b >= plan.blocks]
        couples = [(low.pop(0), high.pop())] if len(low) % 2 else []
        for group in (low, high):
            couples += zip(group[::2], group[1::2])
        for x, y in couples:
            partner[x], partner[y] = y, x
        pairs += [(2 * plan.device(b) + one, 2 * plan.device(p) + one) for b, p in enumerate(partner)]
    return lax.ppermute(a, ("gx", "gy", "gz"), pairs)


def far_blocks(plan, pack, nears):
    def line(move, near):
        parts = [move(pack, k) for k in range(FAR, 1, -1)] + [move(near, 1)]
        return jnp.concatenate(parts[::-1], axis=0)

    if plan.paired:
        mine = line(functools.partial(swap_blocks_apart, plan), nears[0])
        return mine, beside_in_z(plan, mine)
    return [line(functools.partial(swap_blocks, plan, one=one), nears[one]) for one in range(2)]


def on_device(plan, phase, density, rhs):
    nx, by, rows, px, gx = plan.nx, plan.by, plan.rows, plan.px, plan.gx
    flat = by * 2 * px
    block = (px, plan.ny, LANES)
    outside = pl.BlockSpec(memory_space=pltpu.HBM)
    parts = call(
        functools.partial(prepare_kernel, plan),
        [in_vmem(flat, LANES)] * gx,
        [pltpu.VMEM(block, jnp.int32), in_vmem(*block), in_vmem(1, *block), pltpu.SemaphoreType.DMA((3,))],
        in_specs=[outside] * 3,
    )(*pinned(phase, density, rhs, where=pltpu.HBM))
    parts = [a.reshape(by, 2, px, LANES) for a in exchange(plan, parts)]
    c, *sets = call(
        functools.partial(gather_kernel, plan),
        [in_vmem(gx, by, 2, px, LANES)] + [in_vmem(gx, HALO + HALO_RHS, px, LANES)] * 2,
    )(*pinned(*parts))
    sides = jnp.concatenate([swap_blocks(plan, sets[one], 1, one) for one in (1, 0)], axis=0)
    zc = beside_in_z(plan, c)
    zsides = beside_in_z(plan, sides)

    own, own2 = by // 2, by // 4
    size = 5 * (own2 // 2) * (nx // 4)
    side = size + 4 * (nx // 2)

    def level0(n):
        return in_vmem(n, 2, nx, LANES)

    def level1(n):
        return in_vmem(n, 2, nx // 2, LANES)

    inner = call(functools.partial(inner_kernel, plan), Finest.shapes(plan), work=9_000_000)(*pinned(c, zc))
    near_count = 1 if plan.paired else 2
    outs = Finest.shapes(plan) + [in_vmem(size, LANES)] + [in_vmem(side, LANES)] * near_count + [level1(own + 8)] * 2
    scratch = [level1(own + 8), level1(own2), in_vmem(2, 2, size, LANES), in_vmem(1, 2, 4 * (nx // 2), LANES)]
    down = call(
        functools.partial(down_kernel, plan),
        outs,
        scratch,
        input_output_aliases={2 + k: k for k in range(Finest.COUNT)},
    )(*pinned(sides, zsides, *inner))
    fine, rest = down[: Finest.COUNT], down[Finest.COUNT :]
    pack, nears, (w1, u1) = rest[0], rest[1 : 1 + near_count], rest[1 + near_count :]
    kx1, ky1, kz1, _, f1 = fine[11:]
    mine, theirs = far_blocks(plan, pack, nears)
    coarse = call(functools.partial(spread_kernel, plan), Coarse.shapes(plan), work=3_000_000)(
        *pinned(pack, mine, f1, u1)
    )
    rows2 = (2 * FAR + 1) * own2
    level2, level3 = in_vmem(rows2 + 1, 2, nx // 4, LANES), in_vmem(rows2 // 2 + 1, 2, nx // 4, LANES)
    scratch = [level2] * 2 + [level3] * 8 + [level1(rows2), level0(own + 8), level1(own + 8)] + [level0(rows)] * 3
    result = call(
        functools.partial(up_kernel, plan),
        [in_vmem(gx, by, 2, px, LANES)] + Coarse.shapes(plan),
        scratch,
        input_output_aliases={1 + k: 1 + k for k in range(Coarse.COUNT)},
    )(*pinned(theirs, *coarse, *fine[:7], kx1, ky1, kz1, w1))[0]

    parts = exchange(plan, [result[k].reshape(flat, LANES) for k in range(gx)])
    return call(
        functools.partial(place_kernel, plan),
        [jax.ShapeDtypeStruct((1, px, plan.ny, LANES), F32)] * 2,
    )(*pinned(*[parts[slot] for slot in plan.back]))


def solution(mesh):
    sizes = [mesh.shape[a] for a in ("gx", "gy", "gz")]

    def local(phase, density, rhs):
        return tuple(on_device(Plan(sizes, phase.shape), phase, density, rhs))

    in_specs = (P("gx", "gy", "gz"), P("gx", "gy", "gz"), P(None, "gx", "gy", "gz"))
    out_specs = (P(None, "gx", "gy", "gz"), P(None, "gx", "gy", "gz"))
    return jax.shard_map(local, mesh=mesh, in_specs=in_specs, out_specs=out_specs, check_vma=False)
```

```python
import functools

import jax
import jax.numpy as jnp
from jax import lax
from jax.experimental import pallas as pl
from jax.experimental.pallas import tpu as pltpu
from jax.sharding import PartitionSpec as P


DAMPING = 2.0 / 3.0
LANES = 128
WIDE = 256
HALO = 7
HALO_RHS = 6
FAR = 3
F32 = jnp.float32
VMEM_LIMIT = 24 * 1024 * 1024


class Plan:
    def __init__(self, sizes, shape):
        self.gx, self.gy, self.gz = sizes
        self.px, self.ny, self.nz = shape
        self.nx = self.px * self.gx
        self.by = self.ny // self.gx
        self.blocks = self.gx * self.gy
        self.rows = self.by + 2 * HALO
        self.paired = self.gz == 2
        self.ring = [0, 1, 3, 2] if self.gx == 4 else list(range(self.gx))
        self.place = [self.ring.index(i) for i in range(self.gx)]
        self.back = [0, 2, 3, 1] if self.gx == 4 else list(range(self.gx))

    def device(self, block):
        j, q = divmod(block, self.gx)
        return self.ring[(q - j) % self.gx] * self.gy + j

    def look_up(self, table, i):
        return sum(jnp.where(i == k, v, 0) for k, v in enumerate(table))

    def start_of(self, i):
        q = lax.rem(self.look_up(self.place, i) + lax.axis_index("gy"), self.gx)
        return pl.multiple_of(q * self.by, self.by)

    def distances(self, core):
        if self.gx != 4:
            return list(range(self.gx))
        return [0, 3, 2, 1] if core else [0, 3, 1, 2]

    def by_core(self, even, odd):
        return even if even == odd else jnp.where(lax.rem(lax.axis_index("gz"), 2) == 0, even, odd)

    def distance(self, slot):
        return self.by_core(self.distances(0)[slot], self.distances(1)[slot])

    def slot(self, distance):
        found = [self.by_core(self.distances(0).index(k), self.distances(1).index(k)) for k in range(self.gx)]
        return self.look_up(found, distance)

    def block_here(self):
        j = lax.axis_index("gy")
        return j * self.gx + lax.rem(self.look_up(self.place, lax.axis_index("gx")) + j, self.gx)

    def gx_of(self, block):
        block = jnp.clip(block, 0, self.blocks - 1)
        j, q = lax.div(block, self.gx), lax.rem(block, self.gx)
        return self.look_up(self.ring, lax.rem(q + self.gx * self.gy - j, self.gx))

    def is_up(self, block, k, one):
        return lax.rem(lax.div(block, k), 2) == one


def x_up(a, s=1):
    return pltpu.roll(a, a.shape[0] - s, 0)


def x_down(a, s=1):
    return pltpu.roll(a, s, 0)


def z_up(a, g):
    return pltpu.roll(a, a.shape[1] - g, 1)


def z_down(a, g):
    return pltpu.roll(a, g, 1)


def inverse(a):
    r = pl.reciprocal(a, approx=True)
    return r * (2.0 - a * r)


def each(first, last, step, body):
    count = last + 1 - first
    if count <= 2 * step:
        for i in range(first, last + 1):
            body(i)
        return

    def go(c, _):
        for k in range(step):
            body(first + c * step + k)
        return 0

    lax.fori_loop(0, count // step, go, 0)
    for i in range(first + count // step * step, last + 1):
        body(i)


def wave(*stages):
    start = min(first + delay for _, first, _, delay in stages)
    end = max(last + delay for _, _, last, delay in stages)
    full = max(first + delay for _, first, _, delay in stages)
    full_end = min(last + delay for _, _, last, delay in stages)

    def step(t):
        for body, first, last, delay in stages:
            if first <= t - delay <= last:
                body(t - delay)

    def all_of_them(t, _):
        for body, _, _, delay in stages:
            body(t - delay)
        return 0

    if full_end - full < 3:
        full = full_end = end + 1
    for t in range(start, min(full, end + 1)):
        step(t)
    if full <= end:
        lax.fori_loop(full, full_end + 1, all_of_them, 0)
        for t in range(full_end + 1, end + 1):
            step(t)


class Wide:
    def __init__(self, ref):
        self.ref = ref

    def __getitem__(self, key):
        r, xs = key if isinstance(key, tuple) else (key, slice(None))
        return jnp.concatenate([self.ref[r, 0, xs, :], self.ref[r, 1, xs, :]], axis=1)

    def __setitem__(self, key, value):
        r, xs = key if isinstance(key, tuple) else (key, slice(None))
        self.ref[r, 0, xs, :] = value[:, :LANES]
        self.ref[r, 1, xs, :] = value[:, LANES:]


class Level:
    def __init__(self, s, g, kx, ky, kz, d, w, f, step=2):
        self.s, self.g, self.step = s, g, step
        self.kx, self.ky, self.kz, self.d, self.w, self.f = kx, ky, kz, d, w, f

    def beside(self, u, r):
        here = u[r]
        kx, kz = self.kx[r], self.kz[r]
        a = kx * x_up(here, self.s) + x_down(kx * here, self.s)
        b = kz * z_up(here, self.g) + z_down(kz * here, self.g)
        return a + b + (self.ky[r + 1] * u[r + 1] + self.ky[r] * u[r - 1])

    def weigh(self, first, last):
        def body(r):
            self.w[r] = DAMPING * inverse(self.d[r])

        each(first, last, self.step, body)

    def first(self, u, first, last):
        def body(r):
            u[r] = self.w[r] * self.f[r]

        each(first, last, self.step, body)

    def swept(self, u, r):
        return (1.0 / 3.0) * u[r] + self.w[r] * (self.f[r] + self.beside(u, r))

    def sweep(self, u, v, first, last):
        def body(r):
            v[r] = self.swept(u, r)

        each(first, last, self.step, body)

    def residual(self, u, r):
        return self.f[r] + self.beside(u, r) - self.d[r] * u[r]

    def residual_pairs(self, u, out, first, count):
        def body(j):
            out[j] = self.residual(u, first + 2 * j) + self.residual(u, first + 2 * j + 1)

        each(0, count - 1, self.step // 2, body)


def z_pairs(low, g):
    return lambda a: a + jnp.where(low, z_up(a, g), z_down(a, g))


def coarse_coefficients(level, r, x_count):
    even, odd = pl.ds(0, x_count, stride=2), pl.ds(1, x_count, stride=2)
    g = level.g
    low = (lax.broadcasted_iota(jnp.int32, (x_count, WIDE), 1) & g) == 0
    z_pair = z_pairs(low, g)

    def all_x(ref, row):
        return ref[row, even] + ref[row, odd]

    kx = level.kx[r, odd] + level.kx[r + 1, odd]
    inner = level.kx[r, even] + level.kx[r + 1, even] + all_x(level.ky, r + 1)
    kz = all_x(level.kz, r) + all_x(level.kz, r + 1)
    d = all_x(level.d, r) + all_x(level.d, r + 1)
    d = d - 2.0 * (inner + jnp.where(low, kz, 0.0))
    return z_pair(kx), coarse_sum(level.ky, r + 2, x_count, g), jnp.where(low, z_up(kz, g), kz), z_pair(d)


def coarse_sum(ref, r, x_count, g):
    even, odd = pl.ds(0, x_count, stride=2), pl.ds(1, x_count, stride=2)
    low = (lax.broadcasted_iota(jnp.int32, (x_count, WIDE), 1) & g) == 0
    return z_pairs(low, g)(ref[r, even] + ref[r, odd])


def correct(u, v, e, t, x_count, first, last, to):
    def body(j):
        part = e[j]
        t[j, pl.ds(0, x_count, stride=2)] = part
        t[j, pl.ds(1, x_count, stride=2)] = part
        wide = t[j]
        r = to + 2 * (j - first)
        v[r] = u[r] + wide
        v[r + 1] = u[r + 1] + wide

    each(first, last, 2, body)


def pick_lanes(a, lanes):
    return jnp.take_along_axis(a, lanes, axis=1, mode="promise_in_bounds")


def prepare_kernel(plan, phase_in, density_in, rhs_in, *refs):
    outs, (phase, density, rhs, sems) = refs[: plan.gx], refs[plan.gx :]
    pairs = ((phase_in, phase), (density_in, density), (rhs_in, rhs))
    copies = [pltpu.make_async_copy(a, b, sems.at[k]) for k, (a, b) in enumerate(pairs)]
    for copy in copies:
        copy.start()
    for copy in copies:
        copy.wait()
    here = lax.axis_index("gx")
    by, px = plan.by, plan.px
    for slot, out in enumerate(outs):
        rows = pl.ds(plan.start_of(here ^ plan.distance(slot)), by)
        for p in range(px):
            half = jnp.where(phase[p, rows, :] == 1, 500.0, 0.5).astype(F32)
            out[pl.ds(p, by, stride=2 * px), :] = half * density[p, rows, :]
            out[pl.ds(px + p, by, stride=2 * px), :] = rhs[0, p, rows, :]


def gather_kernel(plan, *refs):
    parts, (c, *sets) = refs[: plan.gx], refs[plan.gx :]
    block = plan.block_here()
    for slot, part in enumerate(parts):
        k = plan.distance(slot)
        c[k] = part[...]
        for one, out in enumerate(sets):
            up = plan.is_up(block, 1, one)
            for field, count, at in ((0, HALO, 0), (1, HALO_RHS, HALO)):
                first = jnp.where(up, plan.by - count, 0)
                for r in range(count):
                    out[k, at + r] = part[first + r, field]


def compress(stage, g):
    halves, _, rows, _ = stage.shape
    width = LANES // g
    cell = lax.broadcasted_iota(jnp.int32, (rows, LANES), 1)
    lanes, place = lax.rem(g * cell, LANES), lax.div(cell, width)
    total = pick_lanes(stage[0, 0], lanes)
    for k in range(1, 2 * halves):
        total = jnp.where(place == k, pick_lanes(stage[k // 2, k % 2], lanes), total)
    return total


class Finest:
    COUNT = 16

    @staticmethod
    def shapes(plan):
        level0 = in_vmem(plan.rows, 2, plan.nx, LANES)
        pairs = in_vmem(plan.by // 2 + 8, 2, plan.nx, LANES)
        level1 = in_vmem(plan.by // 2 + 8, 2, plan.nx // 2, LANES)
        return [level0] * 10 + [pairs] + [level1] * 5

    def __init__(self, plan, refs):
        self.plan = plan
        fields = [Wide(r) for r in refs]
        self.kx, self.ky, self.kz, self.d, self.w, self.f, self.ub = fields[:7]
        self.h, self.ua, self.face, self.r = fields[7:11]
        self.kx1, self.ky1, self.kz1, self.d1, self.f1 = fields[11:]
        self.level = Level(1, 1, self.kx, self.ky, self.kz, self.d, self.w, self.f)
        nx = plan.nx
        shape = (nx, WIDE)
        self.half_x = nx // 2
        self.base = plan.block_here() * plan.by - HALO
        self.y_count, z_count = plan.by * plan.blocks, plan.nz * plan.gz
        x = lax.broadcasted_iota(jnp.int32, shape, 0)
        lane = lax.broadcasted_iota(jnp.int32, shape, 1)
        core = lax.axis_index("gz")
        if plan.paired:
            z = lax.rem(core * LANES + lane, WIDE)
        else:
            z = core * LANES + jnp.where(lane < LANES + LANES // 2, lane, lane - WIDE)
        self.x_top, self.x_bottom = x == nx - 1, x == 0
        self.z_top, self.z_bottom = z == z_count - 1, z == 0
        self.z_shut = (z < 0) | (z >= z_count - 1)
        self.z_out = (z < 0) | (z >= z_count)

    def put_h(self, to, s, xs, tile):
        y = self.base + to
        tile = jnp.where((y >= 0) & (y < self.y_count), tile, 0.5)
        if not self.plan.paired:
            tile = jnp.where(self.z_out[: self.plan.px, s * LANES : (s + 1) * LANES], 0.5, tile)
        self.h.ref[to, s, xs, :] = tile

    def tiles(self, other):
        px = self.plan.px
        return [(k, pl.ds(pl.multiple_of((other ^ k) * px, px), px)) for k in range(self.plan.gx)]

    def is_open(self, r):
        y = self.base + r
        return (y >= 0) & (y < self.y_count - 1)

    def start(self, r):
        first = inverse(self.h[r] + self.h[r + 1])
        self.face[r + 1] = first
        self.ky[r + 1] = jnp.where(self.is_open(r), first, 0.0)

    def faces(self, j):
        yd = self.face[2 * j - 1]
        for r in (2 * j - 1, 2 * j):
            h = self.h[r]
            alone = 0.5 * inverse(h)
            xu = inverse(h + jnp.where(self.x_top, h, x_up(h)))
            xd = jnp.where(self.x_bottom, alone, x_down(xu))
            yu = inverse(h + self.h[r + 1])
            zu = inverse(h + jnp.where(self.z_top, h, z_up(h, 1)))
            zd = jnp.where(self.z_bottom, alone, z_down(zu, 1))
            d = xu + xd + yu + yd + zu + zd
            w = DAMPING * inverse(d)
            self.kx[r] = jnp.where(self.x_top, 0.0, xu)
            self.ky[r + 1] = jnp.where(self.is_open(r), yu, 0.0)
            self.kz[r] = jnp.where(self.z_shut, 0.0, zu)
            self.d[r], self.w[r] = d, w
            self.ua[r] = w * self.f[r]
            yd = yu
        self.face[2 * j + 1] = yd

    def coarsen(self, j):
        coarse = coarse_coefficients(self.level, 2 * j - 1, self.half_x)
        self.kx1[j], self.ky1[j + 1], self.kz1[j], self.d1[j] = coarse

    def sweep(self, j):
        self.ub[2 * j] = self.level.swept(self.ua, 2 * j)
        self.ub[2 * j + 1] = self.level.swept(self.ua, 2 * j + 1)

    def residual(self, j):
        self.r[j] = self.level.residual(self.ub, 2 * j - 1) + self.level.residual(self.ub, 2 * j)

    def restrict(self, j):
        self.f1[j] = coarse_sum(self.r, j, self.half_x, 1)


def inner_pairs(plan):
    return (HALO + 3) // 2, (HALO + plan.by - 2) // 2


def inner_kernel(plan, c, zc, *refs):
    fine = Finest(plan, refs)

    def take(r):
        for k, xs in fine.tiles(lax.axis_index("gx")):
            for s, ref in enumerate((c, zc)):
                fine.put_h(r + HALO, s, xs, ref[k, r, 0])
                fine.f.ref[r + HALO, s, xs, :] = ref[k, r, 1]

    each(0, plan.by - 1, 4, take)
    first, last = inner_pairs(plan)
    fine.start(2 * first - 2)
    wave(
        (fine.restrict, first + 1, last - 1, 4),
        (fine.residual, first + 1, last - 1, 3),
        (fine.sweep, first, last - 1, 2),
        (fine.coarsen, first, last, 1),
        (fine.faces, first, last, 0),
    )


def down_kernel(plan, sides, zsides, *refs):
    count = Finest.COUNT
    near_count = 1 if plan.paired else 2
    refs = refs[count:]
    fine = Finest(plan, refs[:count])
    kx1, ky1, kz1, d1, f1 = fine.kx1, fine.ky1, fine.kz1, fine.d1, fine.f1
    pack, nears, refs = refs[count], refs[count + 1 : count + 1 + near_count], refs[count + 1 + near_count :]
    w1, u1, uc, r1 = [Wide(r) for r in refs[:4]]
    stage, near_stage = refs[4:6]
    nx, by, gx = plan.nx, plan.by, plan.gx
    block, core = plan.block_here(), lax.axis_index("gz")

    def take_side(at, other, to, count, field):
        def one(r):
            for k, xs in fine.tiles(other):
                for s, ref in enumerate((sides, zsides)):
                    if field == 0:
                        fine.put_h(r + to, s, xs, ref[at + k, r])
                    else:
                        fine.f.ref[r + to, s, xs, :] = ref[at + k, HALO + r]

        each(0, count - 1, 4, one)

    up_first = plan.is_up(block, 1, 0)
    below, above = jnp.where(up_first, 0, gx), jnp.where(up_first, gx, 0)
    gx_below, gx_above = plan.gx_of(block - 1), plan.gx_of(block + 1)
    take_side(below, gx_below, 0, HALO, 0)
    take_side(above, gx_above, HALO + by, HALO, 0)
    take_side(below, gx_below, HALO - HALO_RHS, HALO_RHS, 1)
    take_side(above, gx_above, HALO + by, HALO_RHS, 1)

    @pl.when(block == 0)
    def _():
        fine.h[HALO - 1] = fine.h[HALO]

    @pl.when(block == plan.blocks - 1)
    def _():
        fine.h[HALO + by] = fine.h[HALO + by - 1]

    fine.start(0)
    first, last = inner_pairs(plan)
    end = by // 2 + 6
    late = -last
    wave(
        (fine.restrict, 2, first, 4),
        (fine.restrict, last, end - 1, late + 4),
        (fine.residual, 2, first, 3),
        (fine.residual, last, end - 1, late + 3),
        (fine.sweep, 1, first - 1, 2),
        (fine.sweep, last, end - 1, late + 2),
        (fine.coarsen, 1, first - 1, 1),
        (fine.coarsen, last + 1, end, late + 1),
        (fine.faces, 1, first - 1, 0),
        (fine.faces, last + 1, end, late),
    )
    ky1[1] = coarse_sum(fine.ky, 1, nx // 2, 1)

    own = by // 2
    half_x = nx // 2
    middle = Level(1, 2, kx1, ky1, kz1, d1, w1, f1, 8)
    middle.weigh(1, own + 6)
    middle.first(uc, 2, own + 5)
    middle.sweep(uc, u1, 3, own + 4)
    middle.residual_pairs(u1, r1, 4, own // 2)

    quarter_x = nx // 4
    own2 = own // 2
    part = own2 // 2
    for j in range(own2):
        fields = (coarse_sum(r1, j, quarter_x, 2),) + coarse_coefficients(middle, 4 + 2 * j, quarter_x)
        for t, a in enumerate(fields):
            xs = pl.ds((t * part + j % part) * quarter_x, quarter_x)
            stage[j // part, 0, xs, :] = a[:, :LANES]
            stage[j // part, 1, xs, :] = a[:, LANES:]
    total = compress(stage, 4)
    pack[...] = total

    size = pack.shape[0]
    for one, out in enumerate(nears):
        row = jnp.where(plan.is_up(block, 1, core if plan.paired else one), own, 5)
        for k, (ref, r) in enumerate(((u1, row), (u1, row + 1), (u1, row + 2), (f1, row + 1))):
            for s in range(2):
                near_stage[0, s, pl.ds(k * half_x, half_x), :] = ref.ref[r, s]
        out[pl.ds(0, size), :] = total
        out[pl.ds(size, 4 * half_x), :] = compress(near_stage, 2)


class Coarse:
    COUNT = 9

    @staticmethod
    def shapes(plan):
        rows = (2 * FAR + 1) * (plan.by // 4) + 1
        level2 = in_vmem(rows, 2, plan.nx // 4, LANES)
        level1 = in_vmem(plan.by // 2 + 8, 2, plan.nx // 2, LANES)
        return [level2] * 7 + [level1] * 2

    def __init__(self, plan, refs):
        self.plan = plan
        self.fields = [Wide(r) for r in refs[:5]]
        self.f, self.kx, self.ky, self.kz, self.d = self.fields
        self.w, self.u, self.f1, self.u1 = [Wide(r) for r in refs[5:]]
        self.block = plan.block_here()

    def spread(self, packed, at, turned):
        plan = self.plan
        own2, quarter_x = plan.by // 4, plan.nx // 4
        part = own2 // 2
        there = self.block + at - FAR
        exists = (there >= 0) & (there < plan.blocks)
        lane = lax.broadcasted_iota(jnp.int32, packed.shape, 1)
        for quarter in range(4):
            part_of, half = divmod(quarter, 2)
            s = half ^ turned
            a = pick_lanes(packed, lax.div(lane, 4) + quarter * (LANES // 4))
            for j in range(part):
                r = at * own2 + part_of * part + j
                tiles = [a[(t * part + j) * quarter_x : (t * part + j + 1) * quarter_x] for t in range(5)]
                for t, ref in enumerate(self.fields):
                    if t == 2:
                        ref.ref[r + 1, s] = jnp.where(exists, tiles[t], 0.0)
                    else:
                        ref.ref[r, s] = tiles[t]
                w = DAMPING * inverse(tiles[4])
                self.w.ref[r, s] = w
                self.u.ref[r, s] = w * tiles[0]

    def side(self, ref, ups, turned):
        plan = self.plan
        own, half_x = plan.by // 2, plan.nx // 2
        size = 5 * (plan.by // 8) * (plan.nx // 4)
        nearest = size + 4 * half_x
        for k, up in ups.items():
            first = 0 if k == 1 else nearest + (k - 2) * size
            self.spread(ref[pl.ds(first, size), :], jnp.where(up, FAR + k, FAR - k), turned)
        row = jnp.where(ups[1], own + 5, 0)
        for k, (to, r) in enumerate(((self.u1, row), (self.u1, row + 1), (self.u1, row + 2), (self.f1, row + 1))):
            row_in = ref[pl.ds(size + k * half_x, half_x), :]
            lane = lax.broadcasted_iota(jnp.int32, row_in.shape, 1)
            for s in range(2):
                to.ref[r, s ^ turned] = pick_lanes(row_in, lax.div(lane, 2) + s * (LANES // 2))

    def ups(self, opposite):
        one = lax.axis_index("gz") if self.plan.paired else 0
        one = 1 - one if opposite else one
        return {k: self.plan.is_up(self.block, k, one) for k in range(1, FAR + 1)}


def spread_kernel(plan, pack, mine, f1, u1, *refs):
    coarse = Coarse(plan, refs)
    own = plan.by // 2
    for r in range(2, own + 6):
        coarse.f1.ref[r] = f1[r]
    for r in range(3, own + 5):
        coarse.u1.ref[r] = u1[r]
    coarse.spread(pack[...], FAR, 0)
    coarse.side(mine, coarse.ups(False), 0)


def up_kernel(plan, theirs, *refs):
    count = Coarse.COUNT
    refs = refs[count:]
    kx0, ky0, kz0, d0, w0, f0, u0, kx1, ky1, kz1, w1 = [Wide(r) for r in refs[:11]]
    out, coarse, scratch = refs[11], Coarse(plan, refs[12 : 12 + count]), refs[12 + count :]
    f2, kx2, ky2, kz2, d2, w2, ua2 = *coarse.fields, coarse.w, coarse.u
    f1, ua1 = coarse.f1, coarse.u1
    wide = [Wide(r) for r in scratch]
    ub2, r2, f3, kx3, ky3, kz3, d3, w3, ua3, ub3 = wide[:10]
    t1, t0, ub1, ua0, ub0, uc0 = wide[10:]
    nx, by = plan.nx, plan.by
    own, own2 = by // 2, by // 4
    half_x, quarter_x = nx // 2, nx // 4
    here = lax.axis_index("gx")
    coarse.side(theirs, coarse.ups(True), 1 if plan.paired else 0)

    rows2 = (2 * FAR + 1) * own2
    two = Level(1, 4, kx2, ky2, kz2, d2, w2, f2, 14)
    two.sweep(ua2, ub2, 1, rows2 - 2)
    two.residual_pairs(ub2, r2, 2, rows2 // 2 - 2)

    x = lax.broadcasted_iota(jnp.int32, (quarter_x, WIDE), 0)
    even_x = (x & 1) == 0
    low = (lax.broadcasted_iota(jnp.int32, (quarter_x, WIDE), 1) & 4) == 0
    z_pair = z_pairs(low, 4)

    def x_pair(a):
        return a + jnp.where(even_x, x_up(a), x_down(a))

    last3 = rows2 // 2 - 2

    def coarsen(j):
        r = 2 * j
        kx = kx2[r] + kx2[r + 1]
        kz = kz2[r] + kz2[r + 1]
        inner = ky2[r + 1] + jnp.where(even_x, kx, 0.0) + jnp.where(low, kz, 0.0)
        f3[j] = z_pair(x_pair(r2[j - 1]))
        kx3[j] = z_pair(jnp.where(even_x, x_up(kx), kx))
        ky3[j + 1] = z_pair(x_pair(ky2[r + 2]))
        kz = x_pair(kz)
        kz3[j] = jnp.where(low, z_up(kz, 4), kz)
        d3[j] = z_pair(x_pair(d2[r] + d2[r + 1] - 2.0 * inner))

    each(1, last3, 6, coarsen)
    three = Level(2, 8, kx3, ky3, kz3, d3, w3, f3, 16)
    three.weigh(1, last3)
    three.first(ua3, 1, last3)
    three.sweep(ua3, ub3, 2, last3 - 1)
    three.sweep(ub3, ua3, 3, last3 - 2)
    three.sweep(ua3, ub3, 4, last3 - 3)

    first2 = FAR * own2
    for j in range(4, last3 - 2):
        e = ub3[j]
        ua2[2 * j] = ub2[2 * j] + e
        ua2[2 * j + 1] = ub2[2 * j + 1] + e
    two.sweep(ua2, ub2, first2 - 3, first2 + own2 + 2)
    two.sweep(ub2, ua2, first2 - 2, first2 + own2 + 1)

    one = Level(1, 2, kx1, ky1, kz1, None, w1, f1, 8)
    correct(ua1, ub1, ua2, t1, quarter_x, first2 - 2, first2 + own2 + 1, 0)
    one.sweep(ub1, ua1, 1, own + 6)
    one.sweep(ua1, ub1, 2, own + 5)

    finest = Level(1, 1, kx0, ky0, kz0, d0, w0, f0)

    def corrected(j):
        part = ub1[j]
        t0[j, pl.ds(0, half_x, stride=2)] = part
        t0[j, pl.ds(1, half_x, stride=2)] = part
        both = t0[j]
        ua0[2 * j - 1] = u0[2 * j - 1] + both
        ua0[2 * j] = u0[2 * j] + both

    def sweep(j):
        ub0[2 * j - 1] = finest.swept(ua0, 2 * j - 1)
        ub0[2 * j] = finest.swept(ua0, 2 * j)

    def sweep_again(j):
        uc0[2 * j] = finest.swept(ub0, 2 * j)
        uc0[2 * j + 1] = finest.swept(ub0, 2 * j + 1)

    slots = [plan.slot(s ^ here) for s in range(plan.gx)]

    def finish(j):
        for r in (2 * j - 1, 2 * j):
            scaled = d0[r] * uc0[r]
            rest = f0[r] + finest.beside(uc0, r) - scaled
            for s in range(plan.gx):
                part = slice(s * plan.px, (s + 1) * plan.px)
                out[slots[s], r - HALO, 0] = scaled[part, :LANES]
                out[slots[s], r - HALO, 1] = rest[part, :LANES]

    wave(
        (finish, 4, own + 3, 5),
        (sweep_again, 3, own + 3, 4),
        (sweep, 3, own + 4, 2),
        (corrected, 2, own + 5, 0),
    )


def place_kernel(plan, *refs):
    parts, (scaled, residual) = refs[: plan.gx], refs[plan.gx :]
    here = lax.axis_index("gx")
    by, px = plan.by, plan.px
    for slot, part in zip(plan.back, parts):
        rows = pl.ds(plan.start_of(here ^ plan.distance(slot)), by)
        for p in range(px):
            scaled[0, p, rows, :] = part[pl.ds(p, by, stride=2 * px), :]
            residual[0, p, rows, :] = part[pl.ds(px + p, by, stride=2 * px), :]


def in_vmem(*shape):
    return pltpu.VMEM(shape, F32)


def call(kernel, out_shape, scratch=(), work=0, **more):
    if work:
        more["cost_estimate"] = pl.CostEstimate(flops=0, bytes_accessed=work, transcendentals=0)
    return pl.pallas_call(
        kernel,
        out_shape=out_shape,
        scratch_shapes=list(scratch),
        compiler_params=pltpu.CompilerParams(vmem_limit_bytes=VMEM_LIMIT),
        **more,
    )


def pinned(*arrays, where=pltpu.VMEM):
    return [pltpu.with_memory_space_constraint(a, where) for a in arrays]


def beside_in_z(plan, a):
    count = plan.gz
    if plan.paired:
        return lax.ppermute(a, "gz", [(0, 1), (1, 0)])
    cut = LANES // 2
    right = lax.ppermute(a[..., :cut], "gz", [(i + 1, i) for i in range(count - 1)])
    left = lax.ppermute(a[..., cut:], "gz", [(i, i + 1) for i in range(count - 1)])
    return jnp.concatenate([right, left], axis=-1)


def exchange(plan, parts):
    got = [parts[0]]
    for slot in range(1, plan.gx):
        pairs = []
        for i in range(plan.gx):
            for g in range(plan.gz):
                to = i ^ plan.distances(g % 2)[slot]
                pairs.append((i * plan.gz + g, to * plan.gz + g))
        got.append(lax.ppermute(parts[slot], ("gx", "gz"), pairs))
    return got


def after(arrays, other):
    shapes = [in_vmem(*a.shape) for a in arrays]
    pairs = {k: k for k in range(len(arrays))}
    return call(lambda *refs: None, shapes, input_output_aliases=pairs)(*pinned(*arrays, other))


def partners(plan, k, one):
    partner = [None] * plan.blocks
    for b in range(plan.blocks - k):
        if b // k % 2 == one:
            partner[b], partner[b + k] = b + k, b
    return partner


def swap_blocks(plan, a, k, one):
    pairs = []
    for b, partner in enumerate(partners(plan, k, one)):
        for g in range(plan.gz):
            to = (b, g ^ 1) if partner is None else (partner, g)
            pairs.append((plan.device(b) * plan.gz + g, plan.device(to[0]) * plan.gz + to[1]))
    return lax.ppermute(a, ("gx", "gy", "gz"), pairs)


def swap_blocks_apart(plan, a, k):
    pairs = []
    for one in range(2):
        partner = partners(plan, k, one)
        alone = [b for b in range(plan.blocks) if partner[b] is None]
        low = [b for b in alone if 2 * b < plan.blocks]
        high = [b for b in alone if 2 * b >= plan.blocks]
        couples = [(low.pop(0), high.pop())] if len(low) % 2 else []
        for group in (low, high):
            couples += zip(group[::2], group[1::2])
        for x, y in couples:
            partner[x], partner[y] = y, x
        pairs += [(2 * plan.device(b) + one, 2 * plan.device(p) + one) for b, p in enumerate(partner)]
    return lax.ppermute(a, ("gx", "gy", "gz"), pairs)


def far_blocks(plan, pack, nears):
    def line(move, near):
        parts = [move(pack, k) for k in range(FAR, 1, -1)] + [move(near, 1)]
        return jnp.concatenate(parts[::-1], axis=0)

    if plan.paired:
        mine = line(functools.partial(swap_blocks_apart, plan), nears[0])
        return mine, beside_in_z(plan, mine)
    return [line(functools.partial(swap_blocks, plan, one=one), nears[one]) for one in range(2)]


def on_device(plan, phase, density, rhs):
    nx, by, rows, px, gx = plan.nx, plan.by, plan.rows, plan.px, plan.gx
    flat = by * 2 * px
    block = (px, plan.ny, LANES)
    outside = pl.BlockSpec(memory_space=pltpu.HBM)
    parts = call(
        functools.partial(prepare_kernel, plan),
        [in_vmem(flat, LANES)] * gx,
        [pltpu.VMEM(block, jnp.int32), in_vmem(*block), in_vmem(1, *block), pltpu.SemaphoreType.DMA((3,))],
        in_specs=[outside] * 3,
    )(*pinned(phase, density, rhs, where=pltpu.HBM))
    parts = [a.reshape(by, 2, px, LANES) for a in exchange(plan, parts)]
    c, *sets = call(
        functools.partial(gather_kernel, plan),
        [in_vmem(gx, by, 2, px, LANES)] + [in_vmem(gx, HALO + HALO_RHS, px, LANES)] * 2,
    )(*pinned(*parts))
    sides = [swap_blocks(plan, sets[one], 1, one) for one in (1, 0)]
    zc = beside_in_z(plan, c)
    inner = call(functools.partial(inner_kernel, plan), Finest.shapes(plan), work=9_000_000)(*pinned(c, zc))
    sides = jnp.concatenate(after(sides, inner[-1]), axis=0)
    zsides = beside_in_z(plan, sides)

    own, own2 = by // 2, by // 4
    size = 5 * (own2 // 2) * (nx // 4)
    side = size + 4 * (nx // 2)

    def level0(n):
        return in_vmem(n, 2, nx, LANES)

    def level1(n):
        return in_vmem(n, 2, nx // 2, LANES)

    near_count = 1 if plan.paired else 2
    outs = Finest.shapes(plan) + [in_vmem(size, LANES)] + [in_vmem(side, LANES)] * near_count + [level1(own + 8)] * 2
    scratch = [level1(own + 8), level1(own2), in_vmem(2, 2, size, LANES), in_vmem(1, 2, 4 * (nx // 2), LANES)]
    down = call(
        functools.partial(down_kernel, plan),
        outs,
        scratch,
        input_output_aliases={2 + k: k for k in range(Finest.COUNT)},
    )(*pinned(sides, zsides, *inner))
    fine, rest = down[: Finest.COUNT], down[Finest.COUNT :]
    pack, nears, (w1, u1) = rest[0], rest[1 : 1 + near_count], rest[1 + near_count :]
    kx1, ky1, kz1, _, f1 = fine[11:]
    mine, theirs = far_blocks(plan, pack, nears)
    coarse = call(functools.partial(spread_kernel, plan), Coarse.shapes(plan), work=3_000_000)(
        *pinned(pack, mine, f1, u1)
    )
    rows2 = (2 * FAR + 1) * own2
    level2, level3 = in_vmem(rows2 + 1, 2, nx // 4, LANES), in_vmem(rows2 // 2 + 1, 2, nx // 4, LANES)
    scratch = [level2] * 2 + [level3] * 8 + [level1(rows2), level0(own + 8), level1(own + 8)] + [level0(rows)] * 3
    result = call(
        functools.partial(up_kernel, plan),
        [in_vmem(gx, by, 2, px, LANES)] + Coarse.shapes(plan),
        scratch,
        input_output_aliases={1 + k: 1 + k for k in range(Coarse.COUNT)},
    )(*pinned(theirs, *coarse, *fine[:7], kx1, ky1, kz1, w1))[0]

    parts = exchange(plan, [result[k].reshape(flat, LANES) for k in range(gx)])
    return call(
        functools.partial(place_kernel, plan),
        [jax.ShapeDtypeStruct((1, px, plan.ny, LANES), F32)] * 2,
    )(*pinned(*[parts[slot] for slot in plan.back]))


def solution(mesh):
    sizes = [mesh.shape[a] for a in ("gx", "gy", "gz")]

    def local(phase, density, rhs):
        return tuple(on_device(Plan(sizes, phase.shape), phase, density, rhs))

    in_specs = (P("gx", "gy", "gz"), P("gx", "gy", "gz"), P(None, "gx", "gy", "gz"))
    out_specs = (P(None, "gx", "gy", "gz"), P(None, "gx", "gy", "gz"))
    return jax.shard_map(local, mesh=mesh, in_specs=in_specs, out_specs=out_specs, check_vma=False)
```

```python
import functools

import jax
import jax.numpy as jnp
from jax import lax
from jax.experimental import pallas as pl
from jax.experimental.pallas import tpu as pltpu
from jax.sharding import PartitionSpec as P


DAMPING = 2.0 / 3.0
LANES = 128
WIDE = 256
HALO = 7
HALO_RHS = 6
FAR = 3
F32 = jnp.float32
VMEM_LIMIT = 24 * 1024 * 1024


class Plan:
    def __init__(self, sizes, shape):
        self.gx, self.gy, self.gz = sizes
        self.px, self.ny, self.nz = shape
        self.nx = self.px * self.gx
        self.by = self.ny // self.gx
        self.blocks = self.gx * self.gy
        self.rows = self.by + 2 * HALO
        self.paired = self.gz == 2
        self.ring = [0, 1, 3, 2] if self.gx == 4 else list(range(self.gx))
        self.place = [self.ring.index(i) for i in range(self.gx)]
        self.back = [0, 2, 3, 1] if self.gx == 4 else list(range(self.gx))

    def device(self, block):
        j, q = divmod(block, self.gx)
        return self.ring[(q - j) % self.gx] * self.gy + j

    def look_up(self, table, i):
        return sum(jnp.where(i == k, v, 0) for k, v in enumerate(table))

    def start_of(self, i):
        q = lax.rem(self.look_up(self.place, i) + lax.axis_index("gy"), self.gx)
        return pl.multiple_of(q * self.by, self.by)

    def distances(self, core):
        if self.gx != 4:
            return list(range(self.gx))
        return [0, 3, 2, 1] if core else [0, 3, 1, 2]

    def by_core(self, even, odd):
        return even if even == odd else jnp.where(lax.rem(lax.axis_index("gz"), 2) == 0, even, odd)

    def distance(self, slot):
        return self.by_core(self.distances(0)[slot], self.distances(1)[slot])

    def slot(self, distance):
        found = [self.by_core(self.distances(0).index(k), self.distances(1).index(k)) for k in range(self.gx)]
        return self.look_up(found, distance)

    def block_here(self):
        j = lax.axis_index("gy")
        return j * self.gx + lax.rem(self.look_up(self.place, lax.axis_index("gx")) + j, self.gx)

    def gx_of(self, block):
        block = jnp.clip(block, 0, self.blocks - 1)
        j, q = lax.div(block, self.gx), lax.rem(block, self.gx)
        return self.look_up(self.ring, lax.rem(q + self.gx * self.gy - j, self.gx))

    def is_up(self, block, k, one):
        return lax.rem(lax.div(block, k), 2) == one


def x_up(a, s=1):
    return pltpu.roll(a, a.shape[0] - s, 0)


def x_down(a, s=1):
    return pltpu.roll(a, s, 0)


def z_up(a, g):
    return pltpu.roll(a, a.shape[1] - g, 1)


def z_down(a, g):
    return pltpu.roll(a, g, 1)


def inverse(a):
    r = pl.reciprocal(a, approx=True)
    return r * (2.0 - a * r)


def each(first, last, step, body):
    count = last + 1 - first
    if count <= 2 * step:
        for i in range(first, last + 1):
            body(i)
        return

    def go(c, _):
        for k in range(step):
            body(first + c * step + k)
        return 0

    lax.fori_loop(0, count // step, go, 0)
    for i in range(first + count // step * step, last + 1):
        body(i)


def wave(*stages):
    start = min(first + delay for _, first, _, delay in stages)
    end = max(last + delay for _, _, last, delay in stages)
    full = max(first + delay for _, first, _, delay in stages)
    full_end = min(last + delay for _, _, last, delay in stages)

    def step(t):
        for body, first, last, delay in stages:
            if first <= t - delay <= last:
                body(t - delay)

    def all_of_them(t, _):
        for body, _, _, delay in stages:
            body(t - delay)
        return 0

    if full_end - full < 3:
        full = full_end = end + 1
    for t in range(start, min(full, end + 1)):
        step(t)
    if full <= end:
        lax.fori_loop(full, full_end + 1, all_of_them, 0)
        for t in range(full_end + 1, end + 1):
            step(t)


class Wide:
    def __init__(self, ref):
        self.ref = ref

    def __getitem__(self, key):
        r, xs = key if isinstance(key, tuple) else (key, slice(None))
        return jnp.concatenate([self.ref[r, 0, xs, :], self.ref[r, 1, xs, :]], axis=1)

    def __setitem__(self, key, value):
        r, xs = key if isinstance(key, tuple) else (key, slice(None))
        self.ref[r, 0, xs, :] = value[:, :LANES]
        self.ref[r, 1, xs, :] = value[:, LANES:]


class Level:
    def __init__(self, s, g, kx, ky, kz, d, w, f, step=2):
        self.s, self.g, self.step = s, g, step
        self.kx, self.ky, self.kz, self.d, self.w, self.f = kx, ky, kz, d, w, f

    def beside(self, u, r):
        here = u[r]
        kx, kz = self.kx[r], self.kz[r]
        a = kx * x_up(here, self.s) + x_down(kx * here, self.s)
        b = kz * z_up(here, self.g) + z_down(kz * here, self.g)
        return a + b + (self.ky[r + 1] * u[r + 1] + self.ky[r] * u[r - 1])

    def weigh(self, first, last):
        def body(r):
            self.w[r] = DAMPING * inverse(self.d[r])

        each(first, last, self.step, body)

    def first(self, u, first, last):
        def body(r):
            u[r] = self.w[r] * self.f[r]

        each(first, last, self.step, body)

    def swept(self, u, r):
        return (1.0 / 3.0) * u[r] + self.w[r] * (self.f[r] + self.beside(u, r))

    def sweep(self, u, v, first, last):
        def body(r):
            v[r] = self.swept(u, r)

        each(first, last, self.step, body)

    def residual(self, u, r):
        return self.f[r] + self.beside(u, r) - self.d[r] * u[r]

    def residual_pairs(self, u, out, first, count):
        def body(j):
            out[j] = self.residual(u, first + 2 * j) + self.residual(u, first + 2 * j + 1)

        each(0, count - 1, self.step // 2, body)


def z_pairs(low, g):
    return lambda a: a + jnp.where(low, z_up(a, g), z_down(a, g))


def coarse_coefficients(level, r, x_count):
    even, odd = pl.ds(0, x_count, stride=2), pl.ds(1, x_count, stride=2)
    g = level.g
    low = (lax.broadcasted_iota(jnp.int32, (x_count, WIDE), 1) & g) == 0
    z_pair = z_pairs(low, g)

    def all_x(ref, row):
        return ref[row, even] + ref[row, odd]

    kx = level.kx[r, odd] + level.kx[r + 1, odd]
    inner = level.kx[r, even] + level.kx[r + 1, even] + all_x(level.ky, r + 1)
    kz = all_x(level.kz, r) + all_x(level.kz, r + 1)
    d = all_x(level.d, r) + all_x(level.d, r + 1)
    d = d - 2.0 * (inner + jnp.where(low, kz, 0.0))
    return z_pair(kx), coarse_sum(level.ky, r + 2, x_count, g), jnp.where(low, z_up(kz, g), kz), z_pair(d)


def coarse_sum(ref, r, x_count, g):
    even, odd = pl.ds(0, x_count, stride=2), pl.ds(1, x_count, stride=2)
    low = (lax.broadcasted_iota(jnp.int32, (x_count, WIDE), 1) & g) == 0
    return z_pairs(low, g)(ref[r, even] + ref[r, odd])


def correct(u, v, e, t, x_count, first, last, to):
    def body(j):
        part = e[j]
        t[j, pl.ds(0, x_count, stride=2)] = part
        t[j, pl.ds(1, x_count, stride=2)] = part
        wide = t[j]
        r = to + 2 * (j - first)
        v[r] = u[r] + wide
        v[r + 1] = u[r + 1] + wide

    each(first, last, 2, body)


def pick_lanes(a, lanes):
    return jnp.take_along_axis(a, lanes, axis=1, mode="promise_in_bounds")


def prepare_kernel(plan, phase_in, density_in, rhs_in, *refs):
    outs, (phase, density, rhs, sems) = refs[: plan.gx], refs[plan.gx :]
    pairs = ((phase_in, phase), (density_in, density), (rhs_in, rhs))
    copies = [pltpu.make_async_copy(a, b, sems.at[k]) for k, (a, b) in enumerate(pairs)]
    for copy in copies:
        copy.start()
    here = lax.axis_index("gx")
    by, px = plan.by, plan.px
    places = [pl.ds(plan.start_of(here ^ plan.distance(slot)), by) for slot in range(plan.gx)]
    copies[0].wait()
    copies[1].wait()
    for out, rows in zip(outs, places):
        for p in range(px):
            half = jnp.where(phase[p, rows, :] == 1, 500.0, 0.5).astype(F32)
            out[pl.ds(p, by, stride=2 * px), :] = half * density[p, rows, :]
    copies[2].wait()
    for out, rows in zip(outs, places):
        for p in range(px):
            out[pl.ds(px + p, by, stride=2 * px), :] = rhs[0, p, rows, :]


def gather_kernel(plan, *refs):
    parts, (c, *sets) = refs[: plan.gx], refs[plan.gx :]
    block = plan.block_here()
    for slot, part in enumerate(parts):
        k = plan.distance(slot)
        c[k] = part[...]
        for one, out in enumerate(sets):
            up = plan.is_up(block, 1, one)
            for field, count, at in ((0, HALO, 0), (1, HALO_RHS, HALO)):
                first = jnp.where(up, plan.by - count, 0)
                for r in range(count):
                    out[k, at + r] = part[first + r, field]


def compress(stage, g):
    halves, _, rows, _ = stage.shape
    width = LANES // g
    cell = lax.broadcasted_iota(jnp.int32, (rows, LANES), 1)
    lanes, place = lax.rem(g * cell, LANES), lax.div(cell, width)
    total = pick_lanes(stage[0, 0], lanes)
    for k in range(1, 2 * halves):
        total = jnp.where(place == k, pick_lanes(stage[k // 2, k % 2], lanes), total)
    return total


class Finest:
    COUNT = 16

    @staticmethod
    def shapes(plan):
        level0 = in_vmem(plan.rows, 2, plan.nx, LANES)
        pairs = in_vmem(plan.by // 2 + 8, 2, plan.nx, LANES)
        level1 = in_vmem(plan.by // 2 + 8, 2, plan.nx // 2, LANES)
        return [level0] * 10 + [pairs] + [level1] * 5

    def __init__(self, plan, refs):
        self.plan = plan
        fields = [Wide(r) for r in refs]
        self.kx, self.ky, self.kz, self.d, self.w, self.f, self.ub = fields[:7]
        self.h, self.ua, self.face, self.r = fields[7:11]
        self.kx1, self.ky1, self.kz1, self.d1, self.f1 = fields[11:]
        self.level = Level(1, 1, self.kx, self.ky, self.kz, self.d, self.w, self.f)
        nx = plan.nx
        shape = (nx, WIDE)
        self.half_x = nx // 2
        self.base = plan.block_here() * plan.by - HALO
        self.y_count, z_count = plan.by * plan.blocks, plan.nz * plan.gz
        x = lax.broadcasted_iota(jnp.int32, shape, 0)
        lane = lax.broadcasted_iota(jnp.int32, shape, 1)
        core = lax.axis_index("gz")
        if plan.paired:
            z = lax.rem(core * LANES + lane, WIDE)
        else:
            z = core * LANES + jnp.where(lane < LANES + LANES // 2, lane, lane - WIDE)
        self.x_top, self.x_bottom = x == nx - 1, x == 0
        self.z_top, self.z_bottom = z == z_count - 1, z == 0
        self.z_shut = (z < 0) | (z >= z_count - 1)
        self.z_out = (z < 0) | (z >= z_count)

    def put_h(self, to, s, xs, tile):
        y = self.base + to
        tile = jnp.where((y >= 0) & (y < self.y_count), tile, 0.5)
        if not self.plan.paired:
            tile = jnp.where(self.z_out[: self.plan.px, s * LANES : (s + 1) * LANES], 0.5, tile)
        self.h.ref[to, s, xs, :] = tile

    def tiles(self, other):
        px = self.plan.px
        return [(k, pl.ds(pl.multiple_of((other ^ k) * px, px), px)) for k in range(self.plan.gx)]

    def is_open(self, r):
        y = self.base + r
        return (y >= 0) & (y < self.y_count - 1)

    def start(self, r):
        first = inverse(self.h[r] + self.h[r + 1])
        self.face[r + 1] = first
        self.ky[r + 1] = jnp.where(self.is_open(r), first, 0.0)

    def faces(self, j):
        yd = self.face[2 * j - 1]
        for r in (2 * j - 1, 2 * j):
            h = self.h[r]
            alone = 0.5 * inverse(h)
            xu = inverse(h + jnp.where(self.x_top, h, x_up(h)))
            xd = jnp.where(self.x_bottom, alone, x_down(xu))
            yu = inverse(h + self.h[r + 1])
            zu = inverse(h + jnp.where(self.z_top, h, z_up(h, 1)))
            zd = jnp.where(self.z_bottom, alone, z_down(zu, 1))
            d = xu + xd + yu + yd + zu + zd
            w = DAMPING * inverse(d)
            self.kx[r] = jnp.where(self.x_top, 0.0, xu)
            self.ky[r + 1] = jnp.where(self.is_open(r), yu, 0.0)
            self.kz[r] = jnp.where(self.z_shut, 0.0, zu)
            self.d[r], self.w[r] = d, w
            self.ua[r] = w * self.f[r]
            yd = yu
        self.face[2 * j + 1] = yd

    def coarsen(self, j):
        coarse = coarse_coefficients(self.level, 2 * j - 1, self.half_x)
        self.kx1[j], self.ky1[j + 1], self.kz1[j], self.d1[j] = coarse

    def sweep(self, j):
        self.ub[2 * j] = self.level.swept(self.ua, 2 * j)
        self.ub[2 * j + 1] = self.level.swept(self.ua, 2 * j + 1)

    def residual(self, j):
        self.r[j] = self.level.residual(self.ub, 2 * j - 1) + self.level.residual(self.ub, 2 * j)

    def restrict(self, j):
        self.f1[j] = coarse_sum(self.r, j, self.half_x, 1)


def inner_pairs(plan):
    return (HALO + 3) // 2, (HALO + plan.by - 2) // 2


def inner_kernel(plan, c, zc, *refs):
    fine = Finest(plan, refs)

    def take(r):
        for k, xs in fine.tiles(lax.axis_index("gx")):
            for s, ref in enumerate((c, zc)):
                fine.put_h(r + HALO, s, xs, ref[k, r, 0])
                fine.f.ref[r + HALO, s, xs, :] = ref[k, r, 1]

    each(0, plan.by - 1, 4, take)
    first, last = inner_pairs(plan)
    fine.start(2 * first - 2)
    wave(
        (fine.restrict, first + 1, last - 1, 4),
        (fine.residual, first + 1, last - 1, 3),
        (fine.sweep, first, last - 1, 2),
        (fine.coarsen, first, last, 1),
        (fine.faces, first, last, 0),
    )


def down_kernel(plan, sides, zsides, *refs):
    count = Finest.COUNT
    near_count = 1 if plan.paired else 2
    refs = refs[count:]
    fine = Finest(plan, refs[:count])
    kx1, ky1, kz1, d1, f1 = fine.kx1, fine.ky1, fine.kz1, fine.d1, fine.f1
    pack, nears, refs = refs[count], refs[count + 1 : count + 1 + near_count], refs[count + 1 + near_count :]
    w1, u1, uc, r1 = [Wide(r) for r in refs[:4]]
    stage, near_stage = refs[4:6]
    nx, by, gx = plan.nx, plan.by, plan.gx
    block, core = plan.block_here(), lax.axis_index("gz")

    def take_side(at, other, to, count, field):
        def one(r):
            for k, xs in fine.tiles(other):
                for s, ref in enumerate((sides, zsides)):
                    if field == 0:
                        fine.put_h(r + to, s, xs, ref[at + k, r])
                    else:
                        fine.f.ref[r + to, s, xs, :] = ref[at + k, HALO + r]

        each(0, count - 1, 4, one)

    up_first = plan.is_up(block, 1, 0)
    below, above = jnp.where(up_first, 0, gx), jnp.where(up_first, gx, 0)
    gx_below, gx_above = plan.gx_of(block - 1), plan.gx_of(block + 1)
    take_side(below, gx_below, 0, HALO, 0)
    take_side(above, gx_above, HALO + by, HALO, 0)
    take_side(below, gx_below, HALO - HALO_RHS, HALO_RHS, 1)
    take_side(above, gx_above, HALO + by, HALO_RHS, 1)

    @pl.when(block == 0)
    def _():
        fine.h[HALO - 1] = fine.h[HALO]

    @pl.when(block == plan.blocks - 1)
    def _():
        fine.h[HALO + by] = fine.h[HALO + by - 1]

    fine.start(0)
    first, last = inner_pairs(plan)
    end = by // 2 + 6
    late = -last
    wave(
        (fine.restrict, 2, first, 4),
        (fine.restrict, last, end - 1, late + 4),
        (fine.residual, 2, first, 3),
        (fine.residual, last, end - 1, late + 3),
        (fine.sweep, 1, first - 1, 2),
        (fine.sweep, last, end - 1, late + 2),
        (fine.coarsen, 1, first - 1, 1),
        (fine.coarsen, last + 1, end, late + 1),
        (fine.faces, 1, first - 1, 0),
        (fine.faces, last + 1, end, late),
    )
    ky1[1] = coarse_sum(fine.ky, 1, nx // 2, 1)

    own = by // 2
    half_x = nx // 2
    middle = Level(1, 2, kx1, ky1, kz1, d1, w1, f1, 8)
    middle.weigh(1, own + 6)
    middle.first(uc, 2, own + 5)
    middle.sweep(uc, u1, 3, own + 4)
    middle.residual_pairs(u1, r1, 4, own // 2)

    quarter_x = nx // 4
    own2 = own // 2
    part = own2 // 2
    for j in range(own2):
        fields = (coarse_sum(r1, j, quarter_x, 2),) + coarse_coefficients(middle, 4 + 2 * j, quarter_x)
        for t, a in enumerate(fields):
            xs = pl.ds((t * part + j % part) * quarter_x, quarter_x)
            stage[j // part, 0, xs, :] = a[:, :LANES]
            stage[j // part, 1, xs, :] = a[:, LANES:]
    total = compress(stage, 4)
    pack[...] = total

    size = pack.shape[0]
    for one, out in enumerate(nears):
        row = jnp.where(plan.is_up(block, 1, core if plan.paired else one), own, 5)
        for k, (ref, r) in enumerate(((u1, row), (u1, row + 1), (u1, row + 2), (f1, row + 1))):
            for s in range(2):
                near_stage[0, s, pl.ds(k * half_x, half_x), :] = ref.ref[r, s]
        out[pl.ds(0, size), :] = total
        out[pl.ds(size, 4 * half_x), :] = compress(near_stage, 2)


class Coarse:
    COUNT = 9

    @staticmethod
    def shapes(plan):
        rows = (2 * FAR + 1) * (plan.by // 4) + 1
        level2 = in_vmem(rows, 2, plan.nx // 4, LANES)
        level1 = in_vmem(plan.by // 2 + 8, 2, plan.nx // 2, LANES)
        return [level2] * 7 + [level1] * 2

    def __init__(self, plan, refs):
        self.plan = plan
        self.fields = [Wide(r) for r in refs[:5]]
        self.f, self.kx, self.ky, self.kz, self.d = self.fields
        self.w, self.u, self.f1, self.u1 = [Wide(r) for r in refs[5:]]
        self.block = plan.block_here()

    def spread(self, packed, at, turned):
        plan = self.plan
        own2, quarter_x = plan.by // 4, plan.nx // 4
        part = own2 // 2
        there = self.block + at - FAR
        exists = (there >= 0) & (there < plan.blocks)
        lane = lax.broadcasted_iota(jnp.int32, packed.shape, 1)
        for quarter in range(4):
            part_of, half = divmod(quarter, 2)
            s = half ^ turned
            a = pick_lanes(packed, lax.div(lane, 4) + quarter * (LANES // 4))
            for j in range(part):
                r = at * own2 + part_of * part + j
                tiles = [a[(t * part + j) * quarter_x : (t * part + j + 1) * quarter_x] for t in range(5)]
                for t, ref in enumerate(self.fields):
                    if t == 2:
                        ref.ref[r + 1, s] = jnp.where(exists, tiles[t], 0.0)
                    else:
                        ref.ref[r, s] = tiles[t]
                w = DAMPING * inverse(tiles[4])
                self.w.ref[r, s] = w
                self.u.ref[r, s] = w * tiles[0]

    def side(self, ref, ups, turned):
        plan = self.plan
        own, half_x = plan.by // 2, plan.nx // 2
        size = 5 * (plan.by // 8) * (plan.nx // 4)
        nearest = size + 4 * half_x
        for k, up in ups.items():
            first = 0 if k == 1 else nearest + (k - 2) * size
            self.spread(ref[pl.ds(first, size), :], jnp.where(up, FAR + k, FAR - k), turned)
        row = jnp.where(ups[1], own + 5, 0)
        for k, (to, r) in enumerate(((self.u1, row), (self.u1, row + 1), (self.u1, row + 2), (self.f1, row + 1))):
            row_in = ref[pl.ds(size + k * half_x, half_x), :]
            lane = lax.broadcasted_iota(jnp.int32, row_in.shape, 1)
            for s in range(2):
                to.ref[r, s ^ turned] = pick_lanes(row_in, lax.div(lane, 2) + s * (LANES // 2))

    def ups(self, opposite):
        one = lax.axis_index("gz") if self.plan.paired else 0
        one = 1 - one if opposite else one
        return {k: self.plan.is_up(self.block, k, one) for k in range(1, FAR + 1)}


def spread_kernel(plan, pack, mine, f1, u1, *refs):
    coarse = Coarse(plan, refs)
    own = plan.by // 2
    for r in range(2, own + 6):
        coarse.f1.ref[r] = f1[r]
    for r in range(3, own + 5):
        coarse.u1.ref[r] = u1[r]
    coarse.spread(pack[...], FAR, 0)
    coarse.side(mine, coarse.ups(False), 0)


def up_kernel(plan, theirs, *refs):
    count = Coarse.COUNT
    refs = refs[count:]
    kx0, ky0, kz0, d0, w0, f0, u0, kx1, ky1, kz1, w1 = [Wide(r) for r in refs[:11]]
    out, coarse, scratch = refs[11], Coarse(plan, refs[12 : 12 + count]), refs[12 + count :]
    f2, kx2, ky2, kz2, d2, w2, ua2 = *coarse.fields, coarse.w, coarse.u
    f1, ua1 = coarse.f1, coarse.u1
    wide = [Wide(r) for r in scratch]
    ub2, r2, f3, kx3, ky3, kz3, d3, w3, ua3, ub3 = wide[:10]
    t1, t0, ub1, ua0, ub0, uc0 = wide[10:]
    nx, by = plan.nx, plan.by
    own, own2 = by // 2, by // 4
    half_x, quarter_x = nx // 2, nx // 4
    here = lax.axis_index("gx")
    coarse.side(theirs, coarse.ups(True), 1 if plan.paired else 0)

    rows2 = (2 * FAR + 1) * own2
    two = Level(1, 4, kx2, ky2, kz2, d2, w2, f2, 14)
    two.sweep(ua2, ub2, 1, rows2 - 2)
    two.residual_pairs(ub2, r2, 2, rows2 // 2 - 2)

    x = lax.broadcasted_iota(jnp.int32, (quarter_x, WIDE), 0)
    even_x = (x & 1) == 0
    low = (lax.broadcasted_iota(jnp.int32, (quarter_x, WIDE), 1) & 4) == 0
    z_pair = z_pairs(low, 4)

    def x_pair(a):
        return a + jnp.where(even_x, x_up(a), x_down(a))

    last3 = rows2 // 2 - 2

    def coarsen(j):
        r = 2 * j
        kx = kx2[r] + kx2[r + 1]
        kz = kz2[r] + kz2[r + 1]
        inner = ky2[r + 1] + jnp.where(even_x, kx, 0.0) + jnp.where(low, kz, 0.0)
        f3[j] = z_pair(x_pair(r2[j - 1]))
        kx3[j] = z_pair(jnp.where(even_x, x_up(kx), kx))
        ky3[j + 1] = z_pair(x_pair(ky2[r + 2]))
        kz = x_pair(kz)
        kz3[j] = jnp.where(low, z_up(kz, 4), kz)
        d3[j] = z_pair(x_pair(d2[r] + d2[r + 1] - 2.0 * inner))

    each(1, last3, 6, coarsen)
    three = Level(2, 8, kx3, ky3, kz3, d3, w3, f3, 16)
    three.weigh(1, last3)
    three.first(ua3, 1, last3)
    three.sweep(ua3, ub3, 2, last3 - 1)
    three.sweep(ub3, ua3, 3, last3 - 2)
    three.sweep(ua3, ub3, 4, last3 - 3)

    first2 = FAR * own2
    for j in range(4, last3 - 2):
        e = ub3[j]
        ua2[2 * j] = ub2[2 * j] + e
        ua2[2 * j + 1] = ub2[2 * j + 1] + e
    two.sweep(ua2, ub2, first2 - 3, first2 + own2 + 2)
    two.sweep(ub2, ua2, first2 - 2, first2 + own2 + 1)

    one = Level(1, 2, kx1, ky1, kz1, None, w1, f1, 8)
    correct(ua1, ub1, ua2, t1, quarter_x, first2 - 2, first2 + own2 + 1, 0)
    one.sweep(ub1, ua1, 1, own + 6)
    one.sweep(ua1, ub1, 2, own + 5)

    finest = Level(1, 1, kx0, ky0, kz0, d0, w0, f0)

    def corrected(j):
        part = ub1[j]
        t0[j, pl.ds(0, half_x, stride=2)] = part
        t0[j, pl.ds(1, half_x, stride=2)] = part
        both = t0[j]
        ua0[2 * j - 1] = u0[2 * j - 1] + both
        ua0[2 * j] = u0[2 * j] + both

    def sweep(j):
        ub0[2 * j - 1] = finest.swept(ua0, 2 * j - 1)
        ub0[2 * j] = finest.swept(ua0, 2 * j)

    def sweep_again(j):
        uc0[2 * j] = finest.swept(ub0, 2 * j)
        uc0[2 * j + 1] = finest.swept(ub0, 2 * j + 1)

    slots = [plan.slot(s ^ here) for s in range(plan.gx)]

    def finish(j):
        for r in (2 * j - 1, 2 * j):
            scaled = d0[r] * uc0[r]
            rest = f0[r] + finest.beside(uc0, r) - scaled
            for s in range(plan.gx):
                part = slice(s * plan.px, (s + 1) * plan.px)
                out[slots[s], r - HALO, 0] = scaled[part, :LANES]
                out[slots[s], r - HALO, 1] = rest[part, :LANES]

    wave(
        (finish, 4, own + 3, 5),
        (sweep_again, 3, own + 3, 4),
        (sweep, 3, own + 4, 2),
        (corrected, 2, own + 5, 0),
    )


def place_kernel(plan, *refs):
    parts, outs, (fields, sems) = refs[: plan.gx], refs[plan.gx : plan.gx + 2], refs[plan.gx + 2 :]
    here = lax.axis_index("gx")
    by, px = plan.by, plan.px
    copies = []
    for slot, part in zip(plan.back, parts):
        rows = pl.ds(plan.start_of(here ^ plan.distance(slot)), by)
        for t, out in enumerate(outs):
            for p in range(px):
                fields[t, p, rows, :] = part[pl.ds(t * px + p, by, stride=2 * px), :]
            copy = pltpu.make_async_copy(fields.at[t, :, rows, :], out.at[0, :, rows, :], sems.at[t, slot])
            copy.start()
            copies.append(copy)
    for copy in copies:
        copy.wait()


def in_vmem(*shape):
    return pltpu.VMEM(shape, F32)


def call(kernel, out_shape, scratch=(), work=0, **more):
    if work:
        more["cost_estimate"] = pl.CostEstimate(flops=0, bytes_accessed=work, transcendentals=0)
    return pl.pallas_call(
        kernel,
        out_shape=out_shape,
        scratch_shapes=list(scratch),
        compiler_params=pltpu.CompilerParams(vmem_limit_bytes=VMEM_LIMIT),
        **more,
    )


def pinned(*arrays, where=pltpu.VMEM):
    return [pltpu.with_memory_space_constraint(a, where) for a in arrays]


def beside_in_z(plan, a):
    count = plan.gz
    if plan.paired:
        return lax.ppermute(a, "gz", [(0, 1), (1, 0)])
    cut = LANES // 2
    right = lax.ppermute(a[..., :cut], "gz", [(i + 1, i) for i in range(count - 1)])
    left = lax.ppermute(a[..., cut:], "gz", [(i, i + 1) for i in range(count - 1)])
    return jnp.concatenate([right, left], axis=-1)


def exchange(plan, parts):
    got = [parts[0]]
    for slot in range(1, plan.gx):
        pairs = []
        for i in range(plan.gx):
            for g in range(plan.gz):
                to = i ^ plan.distances(g % 2)[slot]
                pairs.append((i * plan.gz + g, to * plan.gz + g))
        got.append(lax.ppermute(parts[slot], ("gx", "gz"), pairs))
    return got


def partners(plan, k, one):
    partner = [None] * plan.blocks
    for b in range(plan.blocks - k):
        if b // k % 2 == one:
            partner[b], partner[b + k] = b + k, b
    return partner


def swap_blocks(plan, a, k, one):
    pairs = []
    for b, partner in enumerate(partners(plan, k, one)):
        for g in range(plan.gz):
            to = (b, g ^ 1) if partner is None else (partner, g)
            pairs.append((plan.device(b) * plan.gz + g, plan.device(to[0]) * plan.gz + to[1]))
    return lax.ppermute(a, ("gx", "gy", "gz"), pairs)


def swap_blocks_apart(plan, a, k):
    pairs = []
    for one in range(2):
        partner = partners(plan, k, one)
        alone = [b for b in range(plan.blocks) if partner[b] is None]
        low = [b for b in alone if 2 * b < plan.blocks]
        high = [b for b in alone if 2 * b >= plan.blocks]
        couples = [(low.pop(0), high.pop())] if len(low) % 2 else []
        for group in (low, high):
            couples += zip(group[::2], group[1::2])
        for x, y in couples:
            partner[x], partner[y] = y, x
        pairs += [(2 * plan.device(b) + one, 2 * plan.device(p) + one) for b, p in enumerate(partner)]
    return lax.ppermute(a, ("gx", "gy", "gz"), pairs)


def far_blocks(plan, pack, nears):
    def line(move, near):
        parts = [move(pack, k) for k in range(FAR, 1, -1)] + [move(near, 1)]
        return jnp.concatenate(parts[::-1], axis=0)

    if plan.paired:
        mine = line(functools.partial(swap_blocks_apart, plan), nears[0])
        return mine, beside_in_z(plan, mine)
    return [line(functools.partial(swap_blocks, plan, one=one), nears[one]) for one in range(2)]


def on_device(plan, phase, density, rhs):
    nx, by, rows, px, gx = plan.nx, plan.by, plan.rows, plan.px, plan.gx
    flat = by * 2 * px
    block = (px, plan.ny, LANES)
    outside = pl.BlockSpec(memory_space=pltpu.HBM)
    parts = call(
        functools.partial(prepare_kernel, plan),
        [in_vmem(flat, LANES)] * gx,
        [pltpu.VMEM(block, jnp.int32), in_vmem(*block), in_vmem(1, *block), pltpu.SemaphoreType.DMA((3,))],
        in_specs=[outside] * 3,
    )(*pinned(phase, density, rhs, where=pltpu.HBM))
    parts = [a.reshape(by, 2, px, LANES) for a in exchange(plan, parts)]
    c, *sets = call(
        functools.partial(gather_kernel, plan),
        [in_vmem(gx, by, 2, px, LANES)] + [in_vmem(gx, HALO + HALO_RHS, px, LANES)] * 2,
    )(*pinned(*parts))
    sides = jnp.concatenate([swap_blocks(plan, sets[one], 1, one) for one in (1, 0)], axis=0)
    zc = beside_in_z(plan, c)
    zsides = beside_in_z(plan, sides)

    own, own2 = by // 2, by // 4
    size = 5 * (own2 // 2) * (nx // 4)
    side = size + 4 * (nx // 2)

    def level0(n):
        return in_vmem(n, 2, nx, LANES)

    def level1(n):
        return in_vmem(n, 2, nx // 2, LANES)

    inner = call(functools.partial(inner_kernel, plan), Finest.shapes(plan), work=9_000_000)(*pinned(c, zc))
    near_count = 1 if plan.paired else 2
    outs = Finest.shapes(plan) + [in_vmem(size, LANES)] + [in_vmem(side, LANES)] * near_count + [level1(own + 8)] * 2
    scratch = [level1(own + 8), level1(own2), in_vmem(2, 2, size, LANES), in_vmem(1, 2, 4 * (nx // 2), LANES)]
    down = call(
        functools.partial(down_kernel, plan),
        outs,
        scratch,
        input_output_aliases={2 + k: k for k in range(Finest.COUNT)},
    )(*pinned(sides, zsides, *inner))
    fine, rest = down[: Finest.COUNT], down[Finest.COUNT :]
    pack, nears, (w1, u1) = rest[0], rest[1 : 1 + near_count], rest[1 + near_count :]
    kx1, ky1, kz1, _, f1 = fine[11:]
    mine, theirs = far_blocks(plan, pack, nears)
    coarse = call(functools.partial(spread_kernel, plan), Coarse.shapes(plan), work=3_000_000)(
        *pinned(pack, mine, f1, u1)
    )
    rows2 = (2 * FAR + 1) * own2
    level2, level3 = in_vmem(rows2 + 1, 2, nx // 4, LANES), in_vmem(rows2 // 2 + 1, 2, nx // 4, LANES)
    scratch = [level2] * 2 + [level3] * 8 + [level1(rows2), level0(own + 8), level1(own + 8)] + [level0(rows)] * 3
    result = call(
        functools.partial(up_kernel, plan),
        [in_vmem(gx, by, 2, px, LANES)] + Coarse.shapes(plan),
        scratch,
        input_output_aliases={1 + k: 1 + k for k in range(Coarse.COUNT)},
    )(*pinned(theirs, *coarse, *fine[:7], kx1, ky1, kz1, w1))[0]

    parts = exchange(plan, [result[k].reshape(flat, LANES) for k in range(gx)])
    return call(
        functools.partial(place_kernel, plan),
        [jax.ShapeDtypeStruct((1, px, plan.ny, LANES), F32)] * 2,
        [in_vmem(2, px, plan.ny, LANES), pltpu.SemaphoreType.DMA((2, gx))],
        out_specs=[outside] * 2,
    )(*pinned(*[parts[slot] for slot in plan.back]))


def solution(mesh):
    sizes = [mesh.shape[a] for a in ("gx", "gy", "gz")]

    def local(phase, density, rhs):
        return tuple(on_device(Plan(sizes, phase.shape), phase, density, rhs))

    in_specs = (P("gx", "gy", "gz"), P("gx", "gy", "gz"), P(None, "gx", "gy", "gz"))
    out_specs = (P(None, "gx", "gy", "gz"), P(None, "gx", "gy", "gz"))
    return jax.shard_map(local, mesh=mesh, in_specs=in_specs, out_specs=out_specs, check_vma=False)
```

```python
import functools

import jax
import jax.numpy as jnp
from jax import lax
from jax.experimental import pallas as pl
from jax.experimental.pallas import tpu as pltpu
from jax.sharding import PartitionSpec as P


DAMPING = 2.0 / 3.0
LANES = 128
WIDE = 256
HALO = 7
HALO_RHS = 6
FAR = 3
F32 = jnp.float32
VMEM_LIMIT = 24 * 1024 * 1024


class Plan:
    def __init__(self, sizes, shape):
        self.gx, self.gy, self.gz = sizes
        self.px, self.ny, self.nz = shape
        self.nx = self.px * self.gx
        self.by = self.ny // self.gx
        self.blocks = self.gx * self.gy
        self.rows = self.by + 2 * HALO
        self.paired = self.gz == 2
        self.ring = [0, 1, 3, 2] if self.gx == 4 else list(range(self.gx))
        self.place = [self.ring.index(i) for i in range(self.gx)]
        self.back = [0, 2, 3, 1] if self.gx == 4 else list(range(self.gx))

    def device(self, block):
        j, q = divmod(block, self.gx)
        return self.ring[(q - j) % self.gx] * self.gy + j

    def look_up(self, table, i):
        return sum(jnp.where(i == k, v, 0) for k, v in enumerate(table))

    def start_of(self, i):
        q = lax.rem(self.look_up(self.place, i) + lax.axis_index("gy"), self.gx)
        return pl.multiple_of(q * self.by, self.by)

    def distances(self, core):
        if self.gx != 4:
            return list(range(self.gx))
        return [0, 3, 2, 1] if core else [0, 3, 1, 2]

    def by_core(self, even, odd):
        return even if even == odd else jnp.where(lax.rem(lax.axis_index("gz"), 2) == 0, even, odd)

    def distance(self, slot):
        return self.by_core(self.distances(0)[slot], self.distances(1)[slot])

    def slot(self, distance):
        found = [self.by_core(self.distances(0).index(k), self.distances(1).index(k)) for k in range(self.gx)]
        return self.look_up(found, distance)

    def block_here(self):
        j = lax.axis_index("gy")
        return j * self.gx + lax.rem(self.look_up(self.place, lax.axis_index("gx")) + j, self.gx)

    def gx_of(self, block):
        block = jnp.clip(block, 0, self.blocks - 1)
        j, q = lax.div(block, self.gx), lax.rem(block, self.gx)
        return self.look_up(self.ring, lax.rem(q + self.gx * self.gy - j, self.gx))

    def is_up(self, block, k, one):
        return lax.rem(lax.div(block, k), 2) == one


def x_up(a, s=1):
    return pltpu.roll(a, a.shape[0] - s, 0)


def x_down(a, s=1):
    return pltpu.roll(a, s, 0)


def z_up(a, g):
    return pltpu.roll(a, a.shape[1] - g, 1)


def z_down(a, g):
    return pltpu.roll(a, g, 1)


def inverse(a):
    r = pl.reciprocal(a, approx=True)
    return r * (2.0 - a * r)


def each(first, last, step, body):
    count = last + 1 - first
    if count <= 2 * step:
        for i in range(first, last + 1):
            body(i)
        return

    def go(c, _):
        for k in range(step):
            body(first + c * step + k)
        return 0

    lax.fori_loop(0, count // step, go, 0)
    for i in range(first + count // step * step, last + 1):
        body(i)


def wave(*stages):
    start = min(first + delay for _, first, _, delay in stages)
    end = max(last + delay for _, _, last, delay in stages)
    full = max(first + delay for _, first, _, delay in stages)
    full_end = min(last + delay for _, _, last, delay in stages)

    def step(t):
        for body, first, last, delay in stages:
            if first <= t - delay <= last:
                body(t - delay)

    def all_of_them(t, _):
        for body, _, _, delay in stages:
            body(t - delay)
        return 0

    if full_end - full < 3:
        full = full_end = end + 1
    for t in range(start, min(full, end + 1)):
        step(t)
    if full <= end:
        lax.fori_loop(full, full_end + 1, all_of_them, 0)
        for t in range(full_end + 1, end + 1):
            step(t)


class Wide:
    def __init__(self, ref):
        self.ref = ref

    def __getitem__(self, key):
        r, xs = key if isinstance(key, tuple) else (key, slice(None))
        return jnp.concatenate([self.ref[r, 0, xs, :], self.ref[r, 1, xs, :]], axis=1)

    def __setitem__(self, key, value):
        r, xs = key if isinstance(key, tuple) else (key, slice(None))
        self.ref[r, 0, xs, :] = value[:, :LANES]
        self.ref[r, 1, xs, :] = value[:, LANES:]


class Level:
    def __init__(self, s, g, kx, ky, kz, d, w, f, step=2):
        self.s, self.g, self.step = s, g, step
        self.kx, self.ky, self.kz, self.d, self.w, self.f = kx, ky, kz, d, w, f

    def beside(self, u, r):
        here = u[r]
        kx, kz = self.kx[r], self.kz[r]
        a = kx * x_up(here, self.s) + x_down(kx * here, self.s)
        b = kz * z_up(here, self.g) + z_down(kz * here, self.g)
        return a + b + (self.ky[r + 1] * u[r + 1] + self.ky[r] * u[r - 1])

    def weigh(self, first, last):
        def body(r):
            self.w[r] = DAMPING * inverse(self.d[r])

        each(first, last, self.step, body)

    def first(self, u, first, last):
        def body(r):
            u[r] = self.w[r] * self.f[r]

        each(first, last, self.step, body)

    def swept(self, u, r):
        return (1.0 / 3.0) * u[r] + self.w[r] * (self.f[r] + self.beside(u, r))

    def sweep(self, u, v, first, last):
        def body(r):
            v[r] = self.swept(u, r)

        each(first, last, self.step, body)

    def residual(self, u, r):
        return self.f[r] + self.beside(u, r) - self.d[r] * u[r]

    def residual_pairs(self, u, out, first, count):
        def body(j):
            out[j] = self.residual(u, first + 2 * j) + self.residual(u, first + 2 * j + 1)

        each(0, count - 1, self.step // 2, body)


def z_pairs(low, g):
    return lambda a: a + jnp.where(low, z_up(a, g), z_down(a, g))


def coarse_coefficients(level, r, x_count):
    even, odd = pl.ds(0, x_count, stride=2), pl.ds(1, x_count, stride=2)
    g = level.g
    low = (lax.broadcasted_iota(jnp.int32, (x_count, WIDE), 1) & g) == 0
    z_pair = z_pairs(low, g)

    def all_x(ref, row):
        return ref[row, even] + ref[row, odd]

    kx = level.kx[r, odd] + level.kx[r + 1, odd]
    inner = level.kx[r, even] + level.kx[r + 1, even] + all_x(level.ky, r + 1)
    kz = all_x(level.kz, r) + all_x(level.kz, r + 1)
    d = all_x(level.d, r) + all_x(level.d, r + 1)
    d = d - 2.0 * (inner + jnp.where(low, kz, 0.0))
    return z_pair(kx), coarse_sum(level.ky, r + 2, x_count, g), jnp.where(low, z_up(kz, g), kz), z_pair(d)


def coarse_sum(ref, r, x_count, g):
    even, odd = pl.ds(0, x_count, stride=2), pl.ds(1, x_count, stride=2)
    low = (lax.broadcasted_iota(jnp.int32, (x_count, WIDE), 1) & g) == 0
    return z_pairs(low, g)(ref[r, even] + ref[r, odd])


def correct(u, v, e, t, x_count, first, last, to):
    def body(j):
        part = e[j]
        t[j, pl.ds(0, x_count, stride=2)] = part
        t[j, pl.ds(1, x_count, stride=2)] = part
        wide = t[j]
        r = to + 2 * (j - first)
        v[r] = u[r] + wide
        v[r + 1] = u[r + 1] + wide

    each(first, last, 2, body)


def pick_lanes(a, lanes):
    return jnp.take_along_axis(a, lanes, axis=1, mode="promise_in_bounds")


def prepare_kernel(plan, phase_in, density_in, rhs_in, *refs):
    outs, (phase, density, rhs, sems) = refs[: plan.gx], refs[plan.gx :]
    pairs = ((phase_in, phase), (density_in, density), (rhs_in, rhs))
    copies = [pltpu.make_async_copy(a, b, sems.at[k]) for k, (a, b) in enumerate(pairs)]
    for copy in copies:
        copy.start()
    here = lax.axis_index("gx")
    by, px = plan.by, plan.px
    places = [pl.ds(plan.start_of(here ^ plan.distance(slot)), by) for slot in range(plan.gx)]
    copies[0].wait()
    copies[1].wait()
    for out, rows in zip(outs, places):
        for p in range(px):
            half = jnp.where(phase[p, rows, :] == 1, 500.0, 0.5).astype(F32)
            out[pl.ds(p, by, stride=2 * px), :] = half * density[p, rows, :]
    copies[2].wait()
    for out, rows in zip(outs, places):
        for p in range(px):
            out[pl.ds(px + p, by, stride=2 * px), :] = rhs[0, p, rows, :]


def gather_kernel(plan, *refs):
    parts, (c, *sets) = refs[: plan.gx], refs[plan.gx :]
    block = plan.block_here()
    for slot, part in enumerate(parts):
        k = plan.distance(slot)
        c[k] = part[...]
        for one, out in enumerate(sets):
            up = plan.is_up(block, 1, one)
            for field, count, at in ((0, HALO, 0), (1, HALO_RHS, HALO)):
                first = jnp.where(up, plan.by - count, 0)
                for r in range(count):
                    out[k, at + r] = part[first + r, field]


def compress(stage, g):
    halves, _, rows, _ = stage.shape
    width = LANES // g
    cell = lax.broadcasted_iota(jnp.int32, (rows, LANES), 1)
    lanes, place = lax.rem(g * cell, LANES), lax.div(cell, width)
    total = pick_lanes(stage[0, 0], lanes)
    for k in range(1, 2 * halves):
        total = jnp.where(place == k, pick_lanes(stage[k // 2, k % 2], lanes), total)
    return total


class Finest:
    COUNT = 16

    @staticmethod
    def shapes(plan):
        level0 = in_vmem(plan.rows, 2, plan.nx, LANES)
        pairs = in_vmem(plan.by // 2 + 8, 2, plan.nx, LANES)
        level1 = in_vmem(plan.by // 2 + 8, 2, plan.nx // 2, LANES)
        return [level0] * 10 + [pairs] + [level1] * 5

    def __init__(self, plan, refs):
        self.plan = plan
        fields = [Wide(r) for r in refs]
        self.kx, self.ky, self.kz, self.d, self.w, self.f, self.ub = fields[:7]
        self.h, self.ua, self.face, self.r = fields[7:11]
        self.kx1, self.ky1, self.kz1, self.d1, self.f1 = fields[11:]
        self.level = Level(1, 1, self.kx, self.ky, self.kz, self.d, self.w, self.f)
        nx = plan.nx
        shape = (nx, WIDE)
        self.half_x = nx // 2
        self.base = plan.block_here() * plan.by - HALO
        self.y_count, z_count = plan.by * plan.blocks, plan.nz * plan.gz
        x = lax.broadcasted_iota(jnp.int32, shape, 0)
        lane = lax.broadcasted_iota(jnp.int32, shape, 1)
        core = lax.axis_index("gz")
        if plan.paired:
            z = lax.rem(core * LANES + lane, WIDE)
        else:
            z = core * LANES + jnp.where(lane < LANES + LANES // 2, lane, lane - WIDE)
        self.x_top, self.x_bottom = x == nx - 1, x == 0
        self.z_top, self.z_bottom = z == z_count - 1, z == 0
        self.z_shut = (z < 0) | (z >= z_count - 1)
        self.z_out = (z < 0) | (z >= z_count)

    def put_h(self, to, s, xs, tile):
        y = self.base + to
        tile = jnp.where((y >= 0) & (y < self.y_count), tile, 0.5)
        if not self.plan.paired:
            tile = jnp.where(self.z_out[: self.plan.px, s * LANES : (s + 1) * LANES], 0.5, tile)
        self.h.ref[to, s, xs, :] = tile

    def tiles(self, other):
        px = self.plan.px
        return [(k, pl.ds(pl.multiple_of((other ^ k) * px, px), px)) for k in range(self.plan.gx)]

    def is_open(self, r):
        y = self.base + r
        return (y >= 0) & (y < self.y_count - 1)

    def start(self, r):
        first = inverse(self.h[r] + self.h[r + 1])
        self.face[r + 1] = first
        self.ky[r + 1] = jnp.where(self.is_open(r), first, 0.0)

    def faces(self, j):
        yd = self.face[2 * j - 1]
        for r in (2 * j - 1, 2 * j):
            h = self.h[r]
            alone = 0.5 * inverse(h)
            xu = inverse(h + jnp.where(self.x_top, h, x_up(h)))
            xd = jnp.where(self.x_bottom, alone, x_down(xu))
            yu = inverse(h + self.h[r + 1])
            zu = inverse(h + jnp.where(self.z_top, h, z_up(h, 1)))
            zd = jnp.where(self.z_bottom, alone, z_down(zu, 1))
            d = xu + xd + yu + yd + zu + zd
            w = DAMPING * inverse(d)
            self.kx[r] = jnp.where(self.x_top, 0.0, xu)
            self.ky[r + 1] = jnp.where(self.is_open(r), yu, 0.0)
            self.kz[r] = jnp.where(self.z_shut, 0.0, zu)
            self.d[r], self.w[r] = d, w
            self.ua[r] = w * self.f[r]
            yd = yu
        self.face[2 * j + 1] = yd

    def coarsen(self, j):
        coarse = coarse_coefficients(self.level, 2 * j - 1, self.half_x)
        self.kx1[j], self.ky1[j + 1], self.kz1[j], self.d1[j] = coarse

    def sweep(self, j):
        self.ub[2 * j] = self.level.swept(self.ua, 2 * j)
        self.ub[2 * j + 1] = self.level.swept(self.ua, 2 * j + 1)

    def residual(self, j):
        self.r[j] = self.level.residual(self.ub, 2 * j - 1) + self.level.residual(self.ub, 2 * j)

    def restrict(self, j):
        self.f1[j] = coarse_sum(self.r, j, self.half_x, 1)


def inner_pairs(plan):
    return (HALO + 3) // 2, (HALO + plan.by - 2) // 2


def inner_kernel(plan, c, zc, *refs):
    fine = Finest(plan, refs)

    def take(r):
        for k, xs in fine.tiles(lax.axis_index("gx")):
            for s, ref in enumerate((c, zc)):
                fine.put_h(r + HALO, s, xs, ref[k, r, 0])
                fine.f.ref[r + HALO, s, xs, :] = ref[k, r, 1]

    each(0, plan.by - 1, 4, take)
    first, last = inner_pairs(plan)
    fine.start(2 * first - 2)
    wave(
        (fine.restrict, first + 1, last - 1, 4),
        (fine.residual, first + 1, last - 1, 3),
        (fine.sweep, first, last - 1, 2),
        (fine.coarsen, first, last, 1),
        (fine.faces, first, last, 0),
    )


def down_kernel(plan, sides, zsides, *refs):
    count = Finest.COUNT
    near_count = 1 if plan.paired else 2
    refs = refs[count:]
    fine = Finest(plan, refs[:count])
    kx1, ky1, kz1, d1, f1 = fine.kx1, fine.ky1, fine.kz1, fine.d1, fine.f1
    pack, nears, refs = refs[count], refs[count + 1 : count + 1 + near_count], refs[count + 1 + near_count :]
    w1, u1, uc, r1 = [Wide(r) for r in refs[:4]]
    stage, near_stage = refs[4:6]
    nx, by, gx = plan.nx, plan.by, plan.gx
    block, core = plan.block_here(), lax.axis_index("gz")

    def take_side(at, other, to, count, field):
        def one(r):
            for k, xs in fine.tiles(other):
                for s, ref in enumerate((sides, zsides)):
                    if field == 0:
                        fine.put_h(r + to, s, xs, ref[at + k, r])
                    else:
                        fine.f.ref[r + to, s, xs, :] = ref[at + k, HALO + r]

        each(0, count - 1, 4, one)

    up_first = plan.is_up(block, 1, 0)
    below, above = jnp.where(up_first, gx, 0), jnp.where(up_first, 0, gx)
    gx_below, gx_above = plan.gx_of(block - 1), plan.gx_of(block + 1)
    take_side(below, gx_below, 0, HALO, 0)
    take_side(above, gx_above, HALO + by, HALO, 0)
    take_side(below, gx_below, HALO - HALO_RHS, HALO_RHS, 1)
    take_side(above, gx_above, HALO + by, HALO_RHS, 1)

    @pl.when(block == 0)
    def _():
        fine.h[HALO - 1] = fine.h[HALO]

    @pl.when(block == plan.blocks - 1)
    def _():
        fine.h[HALO + by] = fine.h[HALO + by - 1]

    fine.start(0)
    first, last = inner_pairs(plan)
    end = by // 2 + 6
    late = -last
    wave(
        (fine.restrict, 2, first, 4),
        (fine.restrict, last, end - 1, late + 4),
        (fine.residual, 2, first, 3),
        (fine.residual, last, end - 1, late + 3),
        (fine.sweep, 1, first - 1, 2),
        (fine.sweep, last, end - 1, late + 2),
        (fine.coarsen, 1, first - 1, 1),
        (fine.coarsen, last + 1, end, late + 1),
        (fine.faces, 1, first - 1, 0),
        (fine.faces, last + 1, end, late),
    )
    ky1[1] = coarse_sum(fine.ky, 1, nx // 2, 1)

    own = by // 2
    half_x = nx // 2
    middle = Level(1, 2, kx1, ky1, kz1, d1, w1, f1, 8)
    middle.weigh(1, own + 6)
    middle.first(uc, 2, own + 5)
    middle.sweep(uc, u1, 3, own + 4)
    middle.residual_pairs(u1, r1, 4, own // 2)

    quarter_x = nx // 4
    own2 = own // 2
    part = own2 // 2
    for j in range(own2):
        fields = (coarse_sum(r1, j, quarter_x, 2),) + coarse_coefficients(middle, 4 + 2 * j, quarter_x)
        for t, a in enumerate(fields):
            xs = pl.ds((t * part + j % part) * quarter_x, quarter_x)
            stage[j // part, 0, xs, :] = a[:, :LANES]
            stage[j // part, 1, xs, :] = a[:, LANES:]
    total = compress(stage, 4)
    pack[...] = total

    size = pack.shape[0]
    for one, out in enumerate(nears):
        row = jnp.where(plan.is_up(block, 1, core if plan.paired else one), own, 5)
        for k, (ref, r) in enumerate(((u1, row), (u1, row + 1), (u1, row + 2), (f1, row + 1))):
            for s in range(2):
                near_stage[0, s, pl.ds(k * half_x, half_x), :] = ref.ref[r, s]
        out[pl.ds(0, size), :] = total
        out[pl.ds(size, 4 * half_x), :] = compress(near_stage, 2)


class Coarse:
    COUNT = 9

    @staticmethod
    def shapes(plan):
        rows = (2 * FAR + 1) * (plan.by // 4) + 1
        level2 = in_vmem(rows, 2, plan.nx // 4, LANES)
        level1 = in_vmem(plan.by // 2 + 8, 2, plan.nx // 2, LANES)
        return [level2] * 7 + [level1] * 2

    def __init__(self, plan, refs):
        self.plan = plan
        self.fields = [Wide(r) for r in refs[:5]]
        self.f, self.kx, self.ky, self.kz, self.d = self.fields
        self.w, self.u, self.f1, self.u1 = [Wide(r) for r in refs[5:]]
        self.block = plan.block_here()

    def spread(self, packed, at, turned):
        plan = self.plan
        own2, quarter_x = plan.by // 4, plan.nx // 4
        part = own2 // 2
        there = self.block + at - FAR
        exists = (there >= 0) & (there < plan.blocks)
        lane = lax.broadcasted_iota(jnp.int32, packed.shape, 1)
        for quarter in range(4):
            part_of, half = divmod(quarter, 2)
            s = half ^ turned
            a = pick_lanes(packed, lax.div(lane, 4) + quarter * (LANES // 4))
            for j in range(part):
                r = at * own2 + part_of * part + j
                tiles = [a[(t * part + j) * quarter_x : (t * part + j + 1) * quarter_x] for t in range(5)]
                for t, ref in enumerate(self.fields):
                    if t == 2:
                        ref.ref[r + 1, s] = jnp.where(exists, tiles[t], 0.0)
                    else:
                        ref.ref[r, s] = tiles[t]
                w = DAMPING * inverse(tiles[4])
                self.w.ref[r, s] = w
                self.u.ref[r, s] = w * tiles[0]

    def side(self, ref, ups, turned):
        plan = self.plan
        own, half_x = plan.by // 2, plan.nx // 2
        size = 5 * (plan.by // 8) * (plan.nx // 4)
        nearest = size + 4 * half_x
        for k, up in ups.items():
            first = 0 if k == 1 else nearest + (k - 2) * size
            self.spread(ref[pl.ds(first, size), :], jnp.where(up, FAR + k, FAR - k), turned)
        row = jnp.where(ups[1], own + 5, 0)
        for k, (to, r) in enumerate(((self.u1, row), (self.u1, row + 1), (self.u1, row + 2), (self.f1, row + 1))):
            row_in = ref[pl.ds(size + k * half_x, half_x), :]
            lane = lax.broadcasted_iota(jnp.int32, row_in.shape, 1)
            for s in range(2):
                to.ref[r, s ^ turned] = pick_lanes(row_in, lax.div(lane, 2) + s * (LANES // 2))

    def ups(self, opposite):
        one = lax.axis_index("gz") if self.plan.paired else 0
        one = 1 - one if opposite else one
        return {k: self.plan.is_up(self.block, k, one) for k in range(1, FAR + 1)}


def spread_kernel(plan, pack, mine, f1, u1, *refs):
    coarse = Coarse(plan, refs)
    own = plan.by // 2
    for r in range(2, own + 6):
        coarse.f1.ref[r] = f1[r]
    for r in range(3, own + 5):
        coarse.u1.ref[r] = u1[r]
    coarse.spread(pack[...], FAR, 0)
    coarse.side(mine, coarse.ups(False), 0)


def up_kernel(plan, theirs, *refs):
    count = Coarse.COUNT
    refs = refs[count:]
    kx0, ky0, kz0, d0, w0, f0, u0, kx1, ky1, kz1, w1 = [Wide(r) for r in refs[:11]]
    out, coarse, scratch = refs[11], Coarse(plan, refs[12 : 12 + count]), refs[12 + count :]
    f2, kx2, ky2, kz2, d2, w2, ua2 = *coarse.fields, coarse.w, coarse.u
    f1, ua1 = coarse.f1, coarse.u1
    wide = [Wide(r) for r in scratch]
    ub2, r2, f3, kx3, ky3, kz3, d3, w3, ua3, ub3 = wide[:10]
    t1, t0, ub1, ua0, ub0, uc0 = wide[10:]
    nx, by = plan.nx, plan.by
    own, own2 = by // 2, by // 4
    half_x, quarter_x = nx // 2, nx // 4
    here = lax.axis_index("gx")
    coarse.side(theirs, coarse.ups(True), 1 if plan.paired else 0)

    rows2 = (2 * FAR + 1) * own2
    two = Level(1, 4, kx2, ky2, kz2, d2, w2, f2, 14)
    two.sweep(ua2, ub2, 1, rows2 - 2)
    two.residual_pairs(ub2, r2, 2, rows2 // 2 - 2)

    x = lax.broadcasted_iota(jnp.int32, (quarter_x, WIDE), 0)
    even_x = (x & 1) == 0
    low = (lax.broadcasted_iota(jnp.int32, (quarter_x, WIDE), 1) & 4) == 0
    z_pair = z_pairs(low, 4)

    def x_pair(a):
        return a + jnp.where(even_x, x_up(a), x_down(a))

    last3 = rows2 // 2 - 2

    def coarsen(j):
        r = 2 * j
        kx = kx2[r] + kx2[r + 1]
        kz = kz2[r] + kz2[r + 1]
        inner = ky2[r + 1] + jnp.where(even_x, kx, 0.0) + jnp.where(low, kz, 0.0)
        f3[j] = z_pair(x_pair(r2[j - 1]))
        kx3[j] = z_pair(jnp.where(even_x, x_up(kx), kx))
        ky3[j + 1] = z_pair(x_pair(ky2[r + 2]))
        kz = x_pair(kz)
        kz3[j] = jnp.where(low, z_up(kz, 4), kz)
        d3[j] = z_pair(x_pair(d2[r] + d2[r + 1] - 2.0 * inner))

    each(1, last3, 6, coarsen)
    three = Level(2, 8, kx3, ky3, kz3, d3, w3, f3, 16)
    three.weigh(1, last3)
    three.first(ua3, 1, last3)
    three.sweep(ua3, ub3, 2, last3 - 1)
    three.sweep(ub3, ua3, 3, last3 - 2)
    three.sweep(ua3, ub3, 4, last3 - 3)

    first2 = FAR * own2
    for j in range(4, last3 - 2):
        e = ub3[j]
        ua2[2 * j] = ub2[2 * j] + e
        ua2[2 * j + 1] = ub2[2 * j + 1] + e
    two.sweep(ua2, ub2, first2 - 3, first2 + own2 + 2)
    two.sweep(ub2, ua2, first2 - 2, first2 + own2 + 1)

    one = Level(1, 2, kx1, ky1, kz1, None, w1, f1, 8)
    correct(ua1, ub1, ua2, t1, quarter_x, first2 - 2, first2 + own2 + 1, 0)
    one.sweep(ub1, ua1, 1, own + 6)
    one.sweep(ua1, ub1, 2, own + 5)

    finest = Level(1, 1, kx0, ky0, kz0, d0, w0, f0)

    def corrected(j):
        part = ub1[j]
        t0[j, pl.ds(0, half_x, stride=2)] = part
        t0[j, pl.ds(1, half_x, stride=2)] = part
        both = t0[j]
        ua0[2 * j - 1] = u0[2 * j - 1] + both
        ua0[2 * j] = u0[2 * j] + both

    def sweep(j):
        ub0[2 * j - 1] = finest.swept(ua0, 2 * j - 1)
        ub0[2 * j] = finest.swept(ua0, 2 * j)

    def sweep_again(j):
        uc0[2 * j] = finest.swept(ub0, 2 * j)
        uc0[2 * j + 1] = finest.swept(ub0, 2 * j + 1)

    slots = [plan.slot(s ^ here) for s in range(plan.gx)]

    def finish(j):
        for r in (2 * j - 1, 2 * j):
            scaled = d0[r] * uc0[r]
            rest = f0[r] + finest.beside(uc0, r) - scaled
            for s in range(plan.gx):
                part = slice(s * plan.px, (s + 1) * plan.px)
                out[slots[s], r - HALO, 0] = scaled[part, :LANES]
                out[slots[s], r - HALO, 1] = rest[part, :LANES]

    wave(
        (finish, 4, own + 3, 5),
        (sweep_again, 3, own + 3, 4),
        (sweep, 3, own + 4, 2),
        (corrected, 2, own + 5, 0),
    )


def place_kernel(plan, *refs):
    parts, outs, (fields, sems) = refs[: plan.gx], refs[plan.gx : plan.gx + 2], refs[plan.gx + 2 :]
    here = lax.axis_index("gx")
    by, px = plan.by, plan.px
    copies = []
    for slot, part in zip(plan.back, parts):
        rows = pl.ds(plan.start_of(here ^ plan.distance(slot)), by)
        for t, out in enumerate(outs):
            for p in range(px):
                fields[t, p, rows, :] = part[pl.ds(t * px + p, by, stride=2 * px), :]
            copy = pltpu.make_async_copy(fields.at[t, :, rows, :], out.at[0, :, rows, :], sems.at[t, slot])
            copy.start()
            copies.append(copy)
    for copy in copies:
        copy.wait()


def in_vmem(*shape):
    return pltpu.VMEM(shape, F32)


def call(kernel, out_shape, scratch=(), work=0, **more):
    if work:
        more["cost_estimate"] = pl.CostEstimate(flops=0, bytes_accessed=work, transcendentals=0)
    return pl.pallas_call(
        kernel,
        out_shape=out_shape,
        scratch_shapes=list(scratch),
        compiler_params=pltpu.CompilerParams(vmem_limit_bytes=VMEM_LIMIT),
        **more,
    )


def pinned(*arrays, where=pltpu.VMEM):
    return [pltpu.with_memory_space_constraint(a, where) for a in arrays]


def beside_in_z(plan, a):
    count = plan.gz
    if plan.paired:
        return lax.ppermute(a, "gz", [(0, 1), (1, 0)])
    cut = LANES // 2
    right = lax.ppermute(a[..., :cut], "gz", [(i + 1, i) for i in range(count - 1)])
    left = lax.ppermute(a[..., cut:], "gz", [(i, i + 1) for i in range(count - 1)])
    return jnp.concatenate([right, left], axis=-1)


def exchange(plan, parts):
    got = [parts[0]]
    for slot in range(1, plan.gx):
        pairs = []
        for i in range(plan.gx):
            for g in range(plan.gz):
                to = i ^ plan.distances(g % 2)[slot]
                pairs.append((i * plan.gz + g, to * plan.gz + g))
        got.append(lax.ppermute(parts[slot], ("gx", "gz"), pairs))
    return got


def partners(plan, k, one):
    partner = [None] * plan.blocks
    for b in range(plan.blocks - k):
        if b // k % 2 == one:
            partner[b], partner[b + k] = b + k, b
    return partner


def swap_blocks(plan, a, k, one):
    pairs = []
    for b, partner in enumerate(partners(plan, k, one)):
        for g in range(plan.gz):
            to = (b, g ^ 1) if partner is None else (partner, g)
            pairs.append((plan.device(b) * plan.gz + g, plan.device(to[0]) * plan.gz + to[1]))
    return lax.ppermute(a, ("gx", "gy", "gz"), pairs)


def swap_blocks_apart(plan, a, k):
    pairs = []
    for one in range(2):
        partner = partners(plan, k, one)
        alone = [b for b in range(plan.blocks) if partner[b] is None]
        low = [b for b in alone if 2 * b < plan.blocks]
        high = [b for b in alone if 2 * b >= plan.blocks]
        couples = [(low.pop(0), high.pop())] if len(low) % 2 else []
        for group in (low, high):
            couples += zip(group[::2], group[1::2])
        for x, y in couples:
            partner[x], partner[y] = y, x
        pairs += [(2 * plan.device(b) + one, 2 * plan.device(p) + one) for b, p in enumerate(partner)]
    return lax.ppermute(a, ("gx", "gy", "gz"), pairs)


def far_blocks(plan, pack, nears):
    def line(move, near):
        parts = [move(pack, k) for k in range(FAR, 1, -1)] + [move(near, 1)]
        return jnp.concatenate(parts[::-1], axis=0)

    if plan.paired:
        mine = line(functools.partial(swap_blocks_apart, plan), nears[0])
        return mine, beside_in_z(plan, mine)
    return [line(functools.partial(swap_blocks, plan, one=one), nears[one]) for one in range(2)]


def on_device(plan, phase, density, rhs):
    nx, by, rows, px, gx = plan.nx, plan.by, plan.rows, plan.px, plan.gx
    flat = by * 2 * px
    block = (px, plan.ny, LANES)
    outside = pl.BlockSpec(memory_space=pltpu.HBM)
    parts = call(
        functools.partial(prepare_kernel, plan),
        [in_vmem(flat, LANES)] * gx,
        [pltpu.VMEM(block, jnp.int32), in_vmem(*block), in_vmem(1, *block), pltpu.SemaphoreType.DMA((3,))],
        in_specs=[outside] * 3,
    )(*pinned(phase, density, rhs, where=pltpu.HBM))
    parts = [a.reshape(by, 2, px, LANES) for a in exchange(plan, parts)]
    c, *sets = call(
        functools.partial(gather_kernel, plan),
        [in_vmem(gx, by, 2, px, LANES)] + [in_vmem(gx, HALO + HALO_RHS, px, LANES)] * 2,
    )(*pinned(*parts))
    sides = jnp.concatenate([swap_blocks(plan, sets[one], 1, one) for one in (0, 1)], axis=0)
    zc = beside_in_z(plan, c)
    zsides = beside_in_z(plan, sides)

    own, own2 = by // 2, by // 4
    size = 5 * (own2 // 2) * (nx // 4)
    side = size + 4 * (nx // 2)

    def level0(n):
        return in_vmem(n, 2, nx, LANES)

    def level1(n):
        return in_vmem(n, 2, nx // 2, LANES)

    inner = call(functools.partial(inner_kernel, plan), Finest.shapes(plan), work=9_000_000)(*pinned(c, zc))
    near_count = 1 if plan.paired else 2
    outs = Finest.shapes(plan) + [in_vmem(size, LANES)] + [in_vmem(side, LANES)] * near_count + [level1(own + 8)] * 2
    scratch = [level1(own + 8), level1(own2), in_vmem(2, 2, size, LANES), in_vmem(1, 2, 4 * (nx // 2), LANES)]
    down = call(
        functools.partial(down_kernel, plan),
        outs,
        scratch,
        input_output_aliases={2 + k: k for k in range(Finest.COUNT)},
    )(*pinned(sides, zsides, *inner))
    fine, rest = down[: Finest.COUNT], down[Finest.COUNT :]
    pack, nears, (w1, u1) = rest[0], rest[1 : 1 + near_count], rest[1 + near_count :]
    kx1, ky1, kz1, _, f1 = fine[11:]
    mine, theirs = far_blocks(plan, pack, nears)
    coarse = call(functools.partial(spread_kernel, plan), Coarse.shapes(plan), work=3_000_000)(
        *pinned(pack, mine, f1, u1)
    )
    rows2 = (2 * FAR + 1) * own2
    level2, level3 = in_vmem(rows2 + 1, 2, nx // 4, LANES), in_vmem(rows2 // 2 + 1, 2, nx // 4, LANES)
    scratch = [level2] * 2 + [level3] * 8 + [level1(rows2), level0(own + 8), level1(own + 8)] + [level0(rows)] * 3
    result = call(
        functools.partial(up_kernel, plan),
        [in_vmem(gx, by, 2, px, LANES)] + Coarse.shapes(plan),
        scratch,
        input_output_aliases={1 + k: 1 + k for k in range(Coarse.COUNT)},
    )(*pinned(theirs, *coarse, *fine[:7], kx1, ky1, kz1, w1))[0]

    parts = exchange(plan, [result[k].reshape(flat, LANES) for k in range(gx)])
    return call(
        functools.partial(place_kernel, plan),
        [jax.ShapeDtypeStruct((1, px, plan.ny, LANES), F32)] * 2,
        [in_vmem(2, px, plan.ny, LANES), pltpu.SemaphoreType.DMA((2, gx))],
        out_specs=[outside] * 2,
    )(*pinned(*[parts[slot] for slot in plan.back]))


def solution(mesh):
    sizes = [mesh.shape[a] for a in ("gx", "gy", "gz")]

    def local(phase, density, rhs):
        return tuple(on_device(Plan(sizes, phase.shape), phase, density, rhs))

    in_specs = (P("gx", "gy", "gz"), P("gx", "gy", "gz"), P(None, "gx", "gy", "gz"))
    out_specs = (P(None, "gx", "gy", "gz"), P(None, "gx", "gy", "gz"))
    return jax.shard_map(local, mesh=mesh, in_specs=in_specs, out_specs=out_specs, check_vma=False)
```

```python
import functools

import jax
import jax.numpy as jnp
from jax import lax
from jax.experimental import pallas as pl
from jax.experimental.pallas import tpu as pltpu
from jax.sharding import PartitionSpec as P


DAMPING = 2.0 / 3.0
LANES = 128
WIDE = 256
HALO = 7
HALO_RHS = 6
FAR = 3
F32 = jnp.float32
VMEM_LIMIT = 24 * 1024 * 1024


class Plan:
    def __init__(self, sizes, shape):
        self.gx, self.gy, self.gz = sizes
        self.px, self.ny, self.nz = shape
        self.nx = self.px * self.gx
        self.by = self.ny // self.gx
        self.blocks = self.gx * self.gy
        self.rows = self.by + 2 * HALO
        self.paired = self.gz == 2
        self.ring = [0, 1, 3, 2] if self.gx == 4 else list(range(self.gx))
        self.place = [self.ring.index(i) for i in range(self.gx)]
        self.back = [0, 2, 3, 1] if self.gx == 4 else list(range(self.gx))

    def device(self, block):
        j, q = divmod(block, self.gx)
        return self.ring[(q - j) % self.gx] * self.gy + j

    def look_up(self, table, i):
        return sum(jnp.where(i == k, v, 0) for k, v in enumerate(table))

    def start_of(self, i):
        q = lax.rem(self.look_up(self.place, i) + lax.axis_index("gy"), self.gx)
        return pl.multiple_of(q * self.by, self.by)

    def distances(self, core):
        if self.gx != 4:
            return list(range(self.gx))
        return [0, 3, 2, 1] if core else [0, 3, 1, 2]

    def by_core(self, even, odd):
        return even if even == odd else jnp.where(lax.rem(lax.axis_index("gz"), 2) == 0, even, odd)

    def distance(self, slot):
        return self.by_core(self.distances(0)[slot], self.distances(1)[slot])

    def slot(self, distance):
        found = [self.by_core(self.distances(0).index(k), self.distances(1).index(k)) for k in range(self.gx)]
        return self.look_up(found, distance)

    def block_here(self):
        j = lax.axis_index("gy")
        return j * self.gx + lax.rem(self.look_up(self.place, lax.axis_index("gx")) + j, self.gx)

    def gx_of(self, block):
        block = jnp.clip(block, 0, self.blocks - 1)
        j, q = lax.div(block, self.gx), lax.rem(block, self.gx)
        return self.look_up(self.ring, lax.rem(q + self.gx * self.gy - j, self.gx))

    def is_up(self, block, k, one):
        return lax.rem(lax.div(block, k), 2) == one


def x_up(a, s=1):
    return pltpu.roll(a, a.shape[0] - s, 0)


def x_down(a, s=1):
    return pltpu.roll(a, s, 0)


def z_up(a, g):
    return pltpu.roll(a, a.shape[1] - g, 1)


def z_down(a, g):
    return pltpu.roll(a, g, 1)


def inverse(a):
    r = pl.reciprocal(a, approx=True)
    return r * (2.0 - a * r)


def each(first, last, step, body):
    count = last + 1 - first
    if count <= 2 * step:
        for i in range(first, last + 1):
            body(i)
        return

    def go(c, _):
        for k in range(step):
            body(first + c * step + k)
        return 0

    lax.fori_loop(0, count // step, go, 0)
    for i in range(first + count // step * step, last + 1):
        body(i)


def wave(*stages):
    start = min(first + delay for _, first, _, delay in stages)
    end = max(last + delay for _, _, last, delay in stages)
    full = max(first + delay for _, first, _, delay in stages)
    full_end = min(last + delay for _, _, last, delay in stages)

    def step(t):
        for body, first, last, delay in stages:
            if first <= t - delay <= last:
                body(t - delay)

    def all_of_them(t, _):
        for body, _, _, delay in stages:
            body(t - delay)
        return 0

    if full_end - full < 3:
        full = full_end = end + 1
    for t in range(start, min(full, end + 1)):
        step(t)
    if full <= end:
        lax.fori_loop(full, full_end + 1, all_of_them, 0)
        for t in range(full_end + 1, end + 1):
            step(t)


class Wide:
    def __init__(self, ref):
        self.ref = ref

    def __getitem__(self, key):
        r, xs = key if isinstance(key, tuple) else (key, slice(None))
        return jnp.concatenate([self.ref[r, 0, xs, :], self.ref[r, 1, xs, :]], axis=1)

    def __setitem__(self, key, value):
        r, xs = key if isinstance(key, tuple) else (key, slice(None))
        self.ref[r, 0, xs, :] = value[:, :LANES]
        self.ref[r, 1, xs, :] = value[:, LANES:]


class Level:
    def __init__(self, s, g, kx, ky, kz, d, w, f, step=2):
        self.s, self.g, self.step = s, g, step
        self.kx, self.ky, self.kz, self.d, self.w, self.f = kx, ky, kz, d, w, f

    def beside(self, u, r):
        here = u[r]
        kx, kz = self.kx[r], self.kz[r]
        a = kx * x_up(here, self.s) + x_down(kx * here, self.s)
        b = kz * z_up(here, self.g) + z_down(kz * here, self.g)
        return a + b + (self.ky[r + 1] * u[r + 1] + self.ky[r] * u[r - 1])

    def weigh(self, first, last):
        def body(r):
            self.w[r] = DAMPING * inverse(self.d[r])

        each(first, last, self.step, body)

    def first(self, u, first, last):
        def body(r):
            u[r] = self.w[r] * self.f[r]

        each(first, last, self.step, body)

    def swept(self, u, r):
        return (1.0 / 3.0) * u[r] + self.w[r] * (self.f[r] + self.beside(u, r))

    def sweep(self, u, v, first, last):
        def body(r):
            v[r] = self.swept(u, r)

        each(first, last, self.step, body)

    def residual(self, u, r):
        return self.f[r] + self.beside(u, r) - self.d[r] * u[r]

    def residual_pairs(self, u, out, first, count):
        def body(j):
            out[j] = self.residual(u, first + 2 * j) + self.residual(u, first + 2 * j + 1)

        each(0, count - 1, self.step // 2, body)


def z_pairs(low, g):
    return lambda a: a + jnp.where(low, z_up(a, g), z_down(a, g))


def coarse_coefficients(level, r, x_count):
    even, odd = pl.ds(0, x_count, stride=2), pl.ds(1, x_count, stride=2)
    g = level.g
    low = (lax.broadcasted_iota(jnp.int32, (x_count, WIDE), 1) & g) == 0
    z_pair = z_pairs(low, g)

    def all_x(ref, row):
        return ref[row, even] + ref[row, odd]

    kx = level.kx[r, odd] + level.kx[r + 1, odd]
    inner = level.kx[r, even] + level.kx[r + 1, even] + all_x(level.ky, r + 1)
    kz = all_x(level.kz, r) + all_x(level.kz, r + 1)
    d = all_x(level.d, r) + all_x(level.d, r + 1)
    d = d - 2.0 * (inner + jnp.where(low, kz, 0.0))
    return z_pair(kx), coarse_sum(level.ky, r + 2, x_count, g), jnp.where(low, z_up(kz, g), kz), z_pair(d)


def coarse_sum(ref, r, x_count, g):
    even, odd = pl.ds(0, x_count, stride=2), pl.ds(1, x_count, stride=2)
    low = (lax.broadcasted_iota(jnp.int32, (x_count, WIDE), 1) & g) == 0
    return z_pairs(low, g)(ref[r, even] + ref[r, odd])


def correct(u, v, e, t, x_count, first, last, to):
    def body(j):
        part = e[j]
        t[j, pl.ds(0, x_count, stride=2)] = part
        t[j, pl.ds(1, x_count, stride=2)] = part
        wide = t[j]
        r = to + 2 * (j - first)
        v[r] = u[r] + wide
        v[r + 1] = u[r + 1] + wide

    each(first, last, 2, body)


def pick_lanes(a, lanes):
    return jnp.take_along_axis(a, lanes, axis=1, mode="promise_in_bounds")


def prepare_kernel(plan, phase_in, density_in, rhs_in, *refs):
    outs, (phase, density, rhs, sems) = refs[: plan.gx], refs[plan.gx :]
    pairs = ((phase_in, phase), (density_in, density), (rhs_in, rhs))
    copies = [pltpu.make_async_copy(a, b, sems.at[k]) for k, (a, b) in enumerate(pairs)]
    for copy in copies:
        copy.start()
    here = lax.axis_index("gx")
    by, px = plan.by, plan.px
    places = [pl.ds(plan.start_of(here ^ plan.distance(slot)), by) for slot in range(plan.gx)]
    copies[0].wait()
    copies[1].wait()
    for out, rows in zip(outs, places):
        for p in range(px):
            half = jnp.where(phase[p, rows, :] == 1, 500.0, 0.5).astype(F32)
            out[pl.ds(p, by, stride=2 * px), :] = half * density[p, rows, :]
    copies[2].wait()
    for out, rows in zip(outs, places):
        for p in range(px):
            out[pl.ds(px + p, by, stride=2 * px), :] = rhs[0, p, rows, :]


def gather_kernel(plan, *refs):
    parts, (c, *sets) = refs[: plan.gx], refs[plan.gx :]
    block = plan.block_here()
    for slot, part in enumerate(parts):
        k = plan.distance(slot)
        c[k] = part[...]
        for one, out in enumerate(sets):
            up = plan.is_up(block, 1, one)
            for field, count, at in ((0, HALO, 0), (1, HALO_RHS, HALO)):
                first = jnp.where(up, plan.by - count, 0)
                for r in range(count):
                    out[k, at + r] = part[first + r, field]


def compress(stage, g):
    halves, _, rows, _ = stage.shape
    width = LANES // g
    cell = lax.broadcasted_iota(jnp.int32, (rows, LANES), 1)
    lanes, place = lax.rem(g * cell, LANES), lax.div(cell, width)
    total = pick_lanes(stage[0, 0], lanes)
    for k in range(1, 2 * halves):
        total = jnp.where(place == k, pick_lanes(stage[k // 2, k % 2], lanes), total)
    return total


class Finest:
    COUNT = 16

    @staticmethod
    def shapes(plan):
        level0 = in_vmem(plan.rows, 2, plan.nx, LANES)
        pairs = in_vmem(plan.by // 2 + 8, 2, plan.nx, LANES)
        level1 = in_vmem(plan.by // 2 + 8, 2, plan.nx // 2, LANES)
        return [level0] * 10 + [pairs] + [level1] * 5

    def __init__(self, plan, refs):
        self.plan = plan
        fields = [Wide(r) for r in refs]
        self.kx, self.ky, self.kz, self.d, self.w, self.f, self.ub = fields[:7]
        self.h, self.ua, self.face, self.r = fields[7:11]
        self.kx1, self.ky1, self.kz1, self.d1, self.f1 = fields[11:]
        self.level = Level(1, 1, self.kx, self.ky, self.kz, self.d, self.w, self.f)
        nx = plan.nx
        shape = (nx, WIDE)
        self.half_x = nx // 2
        self.base = plan.block_here() * plan.by - HALO
        self.y_count, z_count = plan.by * plan.blocks, plan.nz * plan.gz
        x = lax.broadcasted_iota(jnp.int32, shape, 0)
        lane = lax.broadcasted_iota(jnp.int32, shape, 1)
        core = lax.axis_index("gz")
        if plan.paired:
            z = lax.rem(core * LANES + lane, WIDE)
        else:
            z = core * LANES + jnp.where(lane < LANES + LANES // 2, lane, lane - WIDE)
        self.x_top, self.x_bottom = x == nx - 1, x == 0
        self.z_top, self.z_bottom = z == z_count - 1, z == 0
        self.z_shut = (z < 0) | (z >= z_count - 1)
        self.z_out = (z < 0) | (z >= z_count)

    def put_h(self, to, s, xs, tile):
        y = self.base + to
        tile = jnp.where((y >= 0) & (y < self.y_count), tile, 0.5)
        if not self.plan.paired:
            tile = jnp.where(self.z_out[: self.plan.px, s * LANES : (s + 1) * LANES], 0.5, tile)
        self.h.ref[to, s, xs, :] = tile

    def tiles(self, other):
        px = self.plan.px
        return [(k, pl.ds(pl.multiple_of((other ^ k) * px, px), px)) for k in range(self.plan.gx)]

    def is_open(self, r):
        y = self.base + r
        return (y >= 0) & (y < self.y_count - 1)

    def start(self, r):
        first = inverse(self.h[r] + self.h[r + 1])
        self.face[r + 1] = first
        self.ky[r + 1] = jnp.where(self.is_open(r), first, 0.0)

    def faces(self, j):
        yd = self.face[2 * j - 1]
        for r in (2 * j - 1, 2 * j):
            h = self.h[r]
            alone = 0.5 * inverse(h)
            xu = inverse(h + jnp.where(self.x_top, h, x_up(h)))
            xd = jnp.where(self.x_bottom, alone, x_down(xu))
            yu = inverse(h + self.h[r + 1])
            zu = inverse(h + jnp.where(self.z_top, h, z_up(h, 1)))
            zd = jnp.where(self.z_bottom, alone, z_down(zu, 1))
            d = xu + xd + yu + yd + zu + zd
            w = DAMPING * inverse(d)
            self.kx[r] = jnp.where(self.x_top, 0.0, xu)
            self.ky[r + 1] = jnp.where(self.is_open(r), yu, 0.0)
            self.kz[r] = jnp.where(self.z_shut, 0.0, zu)
            self.d[r], self.w[r] = d, w
            self.ua[r] = w * self.f[r]
            yd = yu
        self.face[2 * j + 1] = yd

    def coarsen(self, j):
        coarse = coarse_coefficients(self.level, 2 * j - 1, self.half_x)
        self.kx1[j], self.ky1[j + 1], self.kz1[j], self.d1[j] = coarse

    def sweep(self, j):
        self.ub[2 * j] = self.level.swept(self.ua, 2 * j)
        self.ub[2 * j + 1] = self.level.swept(self.ua, 2 * j + 1)

    def residual(self, j):
        self.r[j] = self.level.residual(self.ub, 2 * j - 1) + self.level.residual(self.ub, 2 * j)

    def restrict(self, j):
        self.f1[j] = coarse_sum(self.r, j, self.half_x, 1)


def inner_pairs(plan):
    return (HALO + 3) // 2, (HALO + plan.by - 2) // 2


def inner_kernel(plan, c, zc, *refs):
    fine = Finest(plan, refs)

    def take(r):
        for k, xs in fine.tiles(lax.axis_index("gx")):
            for s, ref in enumerate((c, zc)):
                fine.put_h(r + HALO, s, xs, ref[k, r, 0])
                fine.f.ref[r + HALO, s, xs, :] = ref[k, r, 1]

    each(0, plan.by - 1, 4, take)
    first, last = inner_pairs(plan)
    fine.start(2 * first - 2)
    wave(
        (fine.restrict, first + 1, last - 1, 4),
        (fine.residual, first + 1, last - 1, 3),
        (fine.sweep, first, last - 1, 2),
        (fine.coarsen, first, last, 1),
        (fine.faces, first, last, 0),
    )


def down_kernel(plan, sides, zsides, *refs):
    count = Finest.COUNT
    near_count = 1 if plan.paired else 2
    refs = refs[count:]
    fine = Finest(plan, refs[:count])
    kx1, ky1, kz1, d1, f1 = fine.kx1, fine.ky1, fine.kz1, fine.d1, fine.f1
    pack, nears, refs = refs[count], refs[count + 1 : count + 1 + near_count], refs[count + 1 + near_count :]
    w1, u1, uc, r1 = [Wide(r) for r in refs[:4]]
    stage, near_stage = refs[4:6]
    nx, by, gx = plan.nx, plan.by, plan.gx
    block, core = plan.block_here(), lax.axis_index("gz")

    def take_side(at, other, to, count, field):
        def one(r):
            for k, xs in fine.tiles(other):
                for s, ref in enumerate((sides, zsides)):
                    if field == 0:
                        fine.put_h(r + to, s, xs, ref[at + k, r])
                    else:
                        fine.f.ref[r + to, s, xs, :] = ref[at + k, HALO + r]

        each(0, count - 1, 4, one)

    up_first = plan.is_up(block, 1, 0)
    below, above = jnp.where(up_first, gx, 0), jnp.where(up_first, 0, gx)
    gx_below, gx_above = plan.gx_of(block - 1), plan.gx_of(block + 1)
    take_side(below, gx_below, 0, HALO, 0)
    take_side(above, gx_above, HALO + by, HALO, 0)
    take_side(below, gx_below, HALO - HALO_RHS, HALO_RHS, 1)
    take_side(above, gx_above, HALO + by, HALO_RHS, 1)

    @pl.when(block == 0)
    def _():
        fine.h[HALO - 1] = fine.h[HALO]

    @pl.when(block == plan.blocks - 1)
    def _():
        fine.h[HALO + by] = fine.h[HALO + by - 1]

    fine.start(0)
    first, last = inner_pairs(plan)
    end = by // 2 + 6
    late = -last
    wave(
        (fine.restrict, 2, first, 4),
        (fine.restrict, last, end - 1, late + 4),
        (fine.residual, 2, first, 3),
        (fine.residual, last, end - 1, late + 3),
        (fine.sweep, 1, first - 1, 2),
        (fine.sweep, last, end - 1, late + 2),
        (fine.coarsen, 1, first - 1, 1),
        (fine.coarsen, last + 1, end, late + 1),
        (fine.faces, 1, first - 1, 0),
        (fine.faces, last + 1, end, late),
    )
    ky1[1] = coarse_sum(fine.ky, 1, nx // 2, 1)

    own = by // 2
    half_x = nx // 2
    middle = Level(1, 2, kx1, ky1, kz1, d1, w1, f1, 8)
    middle.weigh(1, own + 6)
    middle.first(uc, 2, own + 5)
    middle.sweep(uc, u1, 3, own + 4)
    middle.residual_pairs(u1, r1, 4, own // 2)

    quarter_x = nx // 4
    own2 = own // 2
    part = own2 // 2
    for j in range(own2):
        fields = (coarse_sum(r1, j, quarter_x, 2),) + coarse_coefficients(middle, 4 + 2 * j, quarter_x)
        for t, a in enumerate(fields):
            xs = pl.ds((t * part + j % part) * quarter_x, quarter_x)
            stage[j // part, 0, xs, :] = a[:, :LANES]
            stage[j // part, 1, xs, :] = a[:, LANES:]
    total = compress(stage, 4)
    pack[...] = total

    size = pack.shape[0]
    for one, out in enumerate(nears):
        row = jnp.where(plan.is_up(block, 1, core if plan.paired else one), own, 5)
        for k, (ref, r) in enumerate(((u1, row), (u1, row + 1), (u1, row + 2), (f1, row + 1))):
            for s in range(2):
                near_stage[0, s, pl.ds(k * half_x, half_x), :] = ref.ref[r, s]
        out[pl.ds(0, size), :] = total
        out[pl.ds(size, 4 * half_x), :] = compress(near_stage, 2)


class Coarse:
    COUNT = 9

    @staticmethod
    def shapes(plan):
        rows = (2 * FAR + 1) * (plan.by // 4) + 1
        level2 = in_vmem(rows, 2, plan.nx // 4, LANES)
        level1 = in_vmem(plan.by // 2 + 8, 2, plan.nx // 2, LANES)
        return [level2] * 7 + [level1] * 2

    def __init__(self, plan, refs):
        self.plan = plan
        self.fields = [Wide(r) for r in refs[:5]]
        self.f, self.kx, self.ky, self.kz, self.d = self.fields
        self.w, self.u, self.f1, self.u1 = [Wide(r) for r in refs[5:]]
        self.block = plan.block_here()

    def spread(self, packed, at, turned):
        plan = self.plan
        own2, quarter_x = plan.by // 4, plan.nx // 4
        part = own2 // 2
        there = self.block + at - FAR
        exists = (there >= 0) & (there < plan.blocks)
        lane = lax.broadcasted_iota(jnp.int32, packed.shape, 1)
        for quarter in range(4):
            part_of, half = divmod(quarter, 2)
            s = half ^ turned
            a = pick_lanes(packed, lax.div(lane, 4) + quarter * (LANES // 4))
            for j in range(part):
                r = at * own2 + part_of * part + j
                tiles = [a[(t * part + j) * quarter_x : (t * part + j + 1) * quarter_x] for t in range(5)]
                for t, ref in enumerate(self.fields):
                    if t == 2:
                        ref.ref[r + 1, s] = jnp.where(exists, tiles[t], 0.0)
                    else:
                        ref.ref[r, s] = tiles[t]
                w = DAMPING * inverse(tiles[4])
                self.w.ref[r, s] = w
                self.u.ref[r, s] = w * tiles[0]

    def side(self, ref, ups, turned):
        plan = self.plan
        own, half_x = plan.by // 2, plan.nx // 2
        size = 5 * (plan.by // 8) * (plan.nx // 4)
        nearest = size + 4 * half_x
        for k, up in ups.items():
            first = 0 if k == 1 else nearest + (FAR - k) * size
            self.spread(ref[pl.ds(first, size), :], jnp.where(up, FAR + k, FAR - k), turned)
        row = jnp.where(ups[1], own + 5, 0)
        for k, (to, r) in enumerate(((self.u1, row), (self.u1, row + 1), (self.u1, row + 2), (self.f1, row + 1))):
            row_in = ref[pl.ds(size + k * half_x, half_x), :]
            lane = lax.broadcasted_iota(jnp.int32, row_in.shape, 1)
            for s in range(2):
                to.ref[r, s ^ turned] = pick_lanes(row_in, lax.div(lane, 2) + s * (LANES // 2))

    def ups(self, opposite):
        one = lax.axis_index("gz") if self.plan.paired else 0
        one = 1 - one if opposite else one
        return {k: self.plan.is_up(self.block, k, one) for k in range(1, FAR + 1)}


def spread_kernel(plan, pack, mine, f1, u1, *refs):
    coarse = Coarse(plan, refs)
    own = plan.by // 2
    for r in range(2, own + 6):
        coarse.f1.ref[r] = f1[r]
    for r in range(3, own + 5):
        coarse.u1.ref[r] = u1[r]
    coarse.spread(pack[...], FAR, 0)
    coarse.side(mine, coarse.ups(False), 0)


def up_kernel(plan, theirs, *refs):
    count = Coarse.COUNT
    refs = refs[count:]
    kx0, ky0, kz0, d0, w0, f0, u0, kx1, ky1, kz1, w1 = [Wide(r) for r in refs[:11]]
    out, coarse, scratch = refs[11], Coarse(plan, refs[12 : 12 + count]), refs[12 + count :]
    f2, kx2, ky2, kz2, d2, w2, ua2 = *coarse.fields, coarse.w, coarse.u
    f1, ua1 = coarse.f1, coarse.u1
    wide = [Wide(r) for r in scratch]
    ub2, r2, f3, kx3, ky3, kz3, d3, w3, ua3, ub3 = wide[:10]
    t1, t0, ub1, ua0, ub0, uc0 = wide[10:]
    nx, by = plan.nx, plan.by
    own, own2 = by // 2, by // 4
    half_x, quarter_x = nx // 2, nx // 4
    here = lax.axis_index("gx")
    coarse.side(theirs, coarse.ups(True), 1 if plan.paired else 0)

    rows2 = (2 * FAR + 1) * own2
    two = Level(1, 4, kx2, ky2, kz2, d2, w2, f2, 14)
    two.sweep(ua2, ub2, 1, rows2 - 2)
    two.residual_pairs(ub2, r2, 2, rows2 // 2 - 2)

    x = lax.broadcasted_iota(jnp.int32, (quarter_x, WIDE), 0)
    even_x = (x & 1) == 0
    low = (lax.broadcasted_iota(jnp.int32, (quarter_x, WIDE), 1) & 4) == 0
    z_pair = z_pairs(low, 4)

    def x_pair(a):
        return a + jnp.where(even_x, x_up(a), x_down(a))

    last3 = rows2 // 2 - 2

    def coarsen(j):
        r = 2 * j
        kx = kx2[r] + kx2[r + 1]
        kz = kz2[r] + kz2[r + 1]
        inner = ky2[r + 1] + jnp.where(even_x, kx, 0.0) + jnp.where(low, kz, 0.0)
        f3[j] = z_pair(x_pair(r2[j - 1]))
        kx3[j] = z_pair(jnp.where(even_x, x_up(kx), kx))
        ky3[j + 1] = z_pair(x_pair(ky2[r + 2]))
        kz = x_pair(kz)
        kz3[j] = jnp.where(low, z_up(kz, 4), kz)
        d3[j] = z_pair(x_pair(d2[r] + d2[r + 1] - 2.0 * inner))

    each(1, last3, 6, coarsen)
    three = Level(2, 8, kx3, ky3, kz3, d3, w3, f3, 16)
    three.weigh(1, last3)
    three.first(ua3, 1, last3)
    three.sweep(ua3, ub3, 2, last3 - 1)
    three.sweep(ub3, ua3, 3, last3 - 2)
    three.sweep(ua3, ub3, 4, last3 - 3)

    first2 = FAR * own2
    for j in range(4, last3 - 2):
        e = ub3[j]
        ua2[2 * j] = ub2[2 * j] + e
        ua2[2 * j + 1] = ub2[2 * j + 1] + e
    two.sweep(ua2, ub2, first2 - 3, first2 + own2 + 2)
    two.sweep(ub2, ua2, first2 - 2, first2 + own2 + 1)

    one = Level(1, 2, kx1, ky1, kz1, None, w1, f1, 8)
    correct(ua1, ub1, ua2, t1, quarter_x, first2 - 2, first2 + own2 + 1, 0)
    one.sweep(ub1, ua1, 1, own + 6)
    one.sweep(ua1, ub1, 2, own + 5)

    finest = Level(1, 1, kx0, ky0, kz0, d0, w0, f0)

    def corrected(j):
        part = ub1[j]
        t0[j, pl.ds(0, half_x, stride=2)] = part
        t0[j, pl.ds(1, half_x, stride=2)] = part
        both = t0[j]
        ua0[2 * j - 1] = u0[2 * j - 1] + both
        ua0[2 * j] = u0[2 * j] + both

    def sweep(j):
        ub0[2 * j - 1] = finest.swept(ua0, 2 * j - 1)
        ub0[2 * j] = finest.swept(ua0, 2 * j)

    def sweep_again(j):
        uc0[2 * j] = finest.swept(ub0, 2 * j)
        uc0[2 * j + 1] = finest.swept(ub0, 2 * j + 1)

    slots = [plan.slot(s ^ here) for s in range(plan.gx)]

    def finish(j):
        for r in (2 * j - 1, 2 * j):
            scaled = d0[r] * uc0[r]
            rest = f0[r] + finest.beside(uc0, r) - scaled
            for s in range(plan.gx):
                part = slice(s * plan.px, (s + 1) * plan.px)
                out[slots[s], r - HALO, 0] = scaled[part, :LANES]
                out[slots[s], r - HALO, 1] = rest[part, :LANES]

    wave(
        (finish, 4, own + 3, 5),
        (sweep_again, 3, own + 3, 4),
        (sweep, 3, own + 4, 2),
        (corrected, 2, own + 5, 0),
    )


def place_kernel(plan, *refs):
    parts, outs, (fields, sems) = refs[: plan.gx], refs[plan.gx : plan.gx + 2], refs[plan.gx + 2 :]
    here = lax.axis_index("gx")
    by, px = plan.by, plan.px
    copies = []
    for slot, part in zip(plan.back, parts):
        rows = pl.ds(plan.start_of(here ^ plan.distance(slot)), by)
        for t, out in enumerate(outs):
            for p in range(px):
                fields[t, p, rows, :] = part[pl.ds(t * px + p, by, stride=2 * px), :]
            copy = pltpu.make_async_copy(fields.at[t, :, rows, :], out.at[0, :, rows, :], sems.at[t, slot])
            copy.start()
            copies.append(copy)
    for copy in copies:
        copy.wait()


def in_vmem(*shape):
    return pltpu.VMEM(shape, F32)


def call(kernel, out_shape, scratch=(), work=0, **more):
    if work:
        more["cost_estimate"] = pl.CostEstimate(flops=0, bytes_accessed=work, transcendentals=0)
    return pl.pallas_call(
        kernel,
        out_shape=out_shape,
        scratch_shapes=list(scratch),
        compiler_params=pltpu.CompilerParams(vmem_limit_bytes=VMEM_LIMIT),
        **more,
    )


def pinned(*arrays, where=pltpu.VMEM):
    return [pltpu.with_memory_space_constraint(a, where) for a in arrays]


def beside_in_z(plan, a):
    count = plan.gz
    if plan.paired:
        return lax.ppermute(a, "gz", [(0, 1), (1, 0)])
    cut = LANES // 2
    right = lax.ppermute(a[..., :cut], "gz", [(i + 1, i) for i in range(count - 1)])
    left = lax.ppermute(a[..., cut:], "gz", [(i, i + 1) for i in range(count - 1)])
    return jnp.concatenate([right, left], axis=-1)


def exchange(plan, parts):
    got = [parts[0]]
    for slot in range(1, plan.gx):
        pairs = []
        for i in range(plan.gx):
            for g in range(plan.gz):
                to = i ^ plan.distances(g % 2)[slot]
                pairs.append((i * plan.gz + g, to * plan.gz + g))
        got.append(lax.ppermute(parts[slot], ("gx", "gz"), pairs))
    return got


def partners(plan, k, one):
    partner = [None] * plan.blocks
    for b in range(plan.blocks - k):
        if b // k % 2 == one:
            partner[b], partner[b + k] = b + k, b
    return partner


def swap_blocks(plan, a, k, one):
    pairs = []
    for b, partner in enumerate(partners(plan, k, one)):
        for g in range(plan.gz):
            to = (b, g ^ 1) if partner is None else (partner, g)
            pairs.append((plan.device(b) * plan.gz + g, plan.device(to[0]) * plan.gz + to[1]))
    return lax.ppermute(a, ("gx", "gy", "gz"), pairs)


def swap_blocks_apart(plan, a, k):
    pairs = []
    for one in range(2):
        partner = partners(plan, k, one)
        alone = [b for b in range(plan.blocks) if partner[b] is None]
        low = [b for b in alone if 2 * b < plan.blocks]
        high = [b for b in alone if 2 * b >= plan.blocks]
        couples = [(low.pop(0), high.pop())] if len(low) % 2 else []
        for group in (low, high):
            couples += zip(group[::2], group[1::2])
        for x, y in couples:
            partner[x], partner[y] = y, x
        pairs += [(2 * plan.device(b) + one, 2 * plan.device(p) + one) for b, p in enumerate(partner)]
    return lax.ppermute(a, ("gx", "gy", "gz"), pairs)


def far_blocks(plan, pack, nears):
    def line(move, near):
        parts = [move(near, 1)] + [move(pack, k) for k in range(FAR, 1, -1)]
        return jnp.concatenate(parts, axis=0)

    if plan.paired:
        mine = line(functools.partial(swap_blocks_apart, plan), nears[0])
        return mine, beside_in_z(plan, mine)
    return [line(functools.partial(swap_blocks, plan, one=one), nears[one]) for one in range(2)]


def on_device(plan, phase, density, rhs):
    nx, by, rows, px, gx = plan.nx, plan.by, plan.rows, plan.px, plan.gx
    flat = by * 2 * px
    block = (px, plan.ny, LANES)
    outside = pl.BlockSpec(memory_space=pltpu.HBM)
    parts = call(
        functools.partial(prepare_kernel, plan),
        [in_vmem(flat, LANES)] * gx,
        [pltpu.VMEM(block, jnp.int32), in_vmem(*block), in_vmem(1, *block), pltpu.SemaphoreType.DMA((3,))],
        in_specs=[outside] * 3,
    )(*pinned(phase, density, rhs, where=pltpu.HBM))
    parts = [a.reshape(by, 2, px, LANES) for a in exchange(plan, parts)]
    c, *sets = call(
        functools.partial(gather_kernel, plan),
        [in_vmem(gx, by, 2, px, LANES)] + [in_vmem(gx, HALO + HALO_RHS, px, LANES)] * 2,
    )(*pinned(*parts))
    sides = jnp.concatenate([swap_blocks(plan, sets[one], 1, one) for one in (0, 1)], axis=0)
    zc = beside_in_z(plan, c)
    zsides = beside_in_z(plan, sides)

    own, own2 = by // 2, by // 4
    size = 5 * (own2 // 2) * (nx // 4)
    side = size + 4 * (nx // 2)

    def level0(n):
        return in_vmem(n, 2, nx, LANES)

    def level1(n):
        return in_vmem(n, 2, nx // 2, LANES)

    inner = call(functools.partial(inner_kernel, plan), Finest.shapes(plan), work=9_000_000)(*pinned(c, zc))
    near_count = 1 if plan.paired else 2
    outs = Finest.shapes(plan) + [in_vmem(size, LANES)] + [in_vmem(side, LANES)] * near_count + [level1(own + 8)] * 2
    scratch = [level1(own + 8), level1(own2), in_vmem(2, 2, size, LANES), in_vmem(1, 2, 4 * (nx // 2), LANES)]
    down = call(
        functools.partial(down_kernel, plan),
        outs,
        scratch,
        input_output_aliases={2 + k: k for k in range(Finest.COUNT)},
    )(*pinned(sides, zsides, *inner))
    fine, rest = down[: Finest.COUNT], down[Finest.COUNT :]
    pack, nears, (w1, u1) = rest[0], rest[1 : 1 + near_count], rest[1 + near_count :]
    kx1, ky1, kz1, _, f1 = fine[11:]
    mine, theirs = far_blocks(plan, pack, nears)
    coarse = call(functools.partial(spread_kernel, plan), Coarse.shapes(plan), work=3_000_000)(
        *pinned(pack, mine, f1, u1)
    )
    rows2 = (2 * FAR + 1) * own2
    level2, level3 = in_vmem(rows2 + 1, 2, nx // 4, LANES), in_vmem(rows2 // 2 + 1, 2, nx // 4, LANES)
    scratch = [level2] * 2 + [level3] * 8 + [level1(rows2), level0(own + 8), level1(own + 8)] + [level0(rows)] * 3
    result = call(
        functools.partial(up_kernel, plan),
        [in_vmem(gx, by, 2, px, LANES)] + Coarse.shapes(plan),
        scratch,
        input_output_aliases={1 + k: 1 + k for k in range(Coarse.COUNT)},
    )(*pinned(theirs, *coarse, *fine[:7], kx1, ky1, kz1, w1))[0]

    parts = exchange(plan, [result[k].reshape(flat, LANES) for k in range(gx)])
    return call(
        functools.partial(place_kernel, plan),
        [jax.ShapeDtypeStruct((1, px, plan.ny, LANES), F32)] * 2,
        [in_vmem(2, px, plan.ny, LANES), pltpu.SemaphoreType.DMA((2, gx))],
        out_specs=[outside] * 2,
    )(*pinned(*[parts[slot] for slot in plan.back]))


def solution(mesh):
    sizes = [mesh.shape[a] for a in ("gx", "gy", "gz")]

    def local(phase, density, rhs):
        return tuple(on_device(Plan(sizes, phase.shape), phase, density, rhs))

    in_specs = (P("gx", "gy", "gz"), P("gx", "gy", "gz"), P(None, "gx", "gy", "gz"))
    out_specs = (P(None, "gx", "gy", "gz"), P(None, "gx", "gy", "gz"))
    return jax.shard_map(local, mesh=mesh, in_specs=in_specs, out_specs=out_specs, check_vma=False)
```

```python
import functools

import jax
import jax.numpy as jnp
from jax import lax
from jax.experimental import pallas as pl
from jax.experimental.pallas import tpu as pltpu
from jax.sharding import PartitionSpec as P


DAMPING = 2.0 / 3.0
LANES = 128
WIDE = 256
HALO = 7
HALO_RHS = 6
FAR = 3
F32 = jnp.float32
VMEM_LIMIT = 24 * 1024 * 1024


class Plan:
    def __init__(self, sizes, shape):
        self.gx, self.gy, self.gz = sizes
        self.px, self.ny, self.nz = shape
        self.nx = self.px * self.gx
        self.by = self.ny // self.gx
        self.blocks = self.gx * self.gy
        self.rows = self.by + 2 * HALO
        self.paired = self.gz == 2
        self.ring = [0, 1, 3, 2] if self.gx == 4 else list(range(self.gx))
        self.place = [self.ring.index(i) for i in range(self.gx)]
        self.back = [0, 3, 1, 2] if self.gx == 4 else list(range(self.gx))

    def device(self, block):
        j, q = divmod(block, self.gx)
        return self.ring[(q - j) % self.gx] * self.gy + j

    def look_up(self, table, i):
        return sum(jnp.where(i == k, v, 0) for k, v in enumerate(table))

    def start_of(self, i):
        q = lax.rem(self.look_up(self.place, i) + lax.axis_index("gy"), self.gx)
        return pl.multiple_of(q * self.by, self.by)

    def distances(self, core):
        if self.gx != 4:
            return list(range(self.gx))
        return [0, 1, 3, 2] if core else [0, 2, 3, 1]

    def by_core(self, even, odd):
        return even if even == odd else jnp.where(lax.rem(lax.axis_index("gz"), 2) == 0, even, odd)

    def distance(self, slot):
        return self.by_core(self.distances(0)[slot], self.distances(1)[slot])

    def slot(self, distance):
        found = [self.by_core(self.distances(0).index(k), self.distances(1).index(k)) for k in range(self.gx)]
        return self.look_up(found, distance)

    def block_here(self):
        j = lax.axis_index("gy")
        return j * self.gx + lax.rem(self.look_up(self.place, lax.axis_index("gx")) + j, self.gx)

    def gx_of(self, block):
        block = jnp.clip(block, 0, self.blocks - 1)
        j, q = lax.div(block, self.gx), lax.rem(block, self.gx)
        return self.look_up(self.ring, lax.rem(q + self.gx * self.gy - j, self.gx))

    def is_up(self, block, k, one):
        return lax.rem(lax.div(block, k), 2) == one


def x_up(a, s=1):
    return pltpu.roll(a, a.shape[0] - s, 0)


def x_down(a, s=1):
    return pltpu.roll(a, s, 0)


def z_up(a, g):
    return pltpu.roll(a, a.shape[1] - g, 1)


def z_down(a, g):
    return pltpu.roll(a, g, 1)


def inverse(a):
    r = pl.reciprocal(a, approx=True)
    return r * (2.0 - a * r)


def each(first, last, step, body):
    count = last + 1 - first
    if count <= 2 * step:
        for i in range(first, last + 1):
            body(i)
        return

    def go(c, _):
        for k in range(step):
            body(first + c * step + k)
        return 0

    lax.fori_loop(0, count // step, go, 0)
    for i in range(first + count // step * step, last + 1):
        body(i)


def wave(*stages):
    start = min(first + delay for _, first, _, delay in stages)
    end = max(last + delay for _, _, last, delay in stages)
    full = max(first + delay for _, first, _, delay in stages)
    full_end = min(last + delay for _, _, last, delay in stages)

    def step(t):
        for body, first, last, delay in stages:
            if first <= t - delay <= last:
                body(t - delay)

    def all_of_them(t, _):
        for body, _, _, delay in stages:
            body(t - delay)
        return 0

    if full_end - full < 3:
        full = full_end = end + 1
    for t in range(start, min(full, end + 1)):
        step(t)
    if full <= end:
        lax.fori_loop(full, full_end + 1, all_of_them, 0)
        for t in range(full_end + 1, end + 1):
            step(t)


class Wide:
    def __init__(self, ref):
        self.ref = ref

    def __getitem__(self, key):
        r, xs = key if isinstance(key, tuple) else (key, slice(None))
        return jnp.concatenate([self.ref[r, 0, xs, :], self.ref[r, 1, xs, :]], axis=1)

    def __setitem__(self, key, value):
        r, xs = key if isinstance(key, tuple) else (key, slice(None))
        self.ref[r, 0, xs, :] = value[:, :LANES]
        self.ref[r, 1, xs, :] = value[:, LANES:]


class Level:
    def __init__(self, s, g, kx, ky, kz, d, w, f, step=2):
        self.s, self.g, self.step = s, g, step
        self.kx, self.ky, self.kz, self.d, self.w, self.f = kx, ky, kz, d, w, f

    def beside(self, u, r):
        here = u[r]
        kx, kz = self.kx[r], self.kz[r]
        a = kx * x_up(here, self.s) + x_down(kx * here, self.s)
        b = kz * z_up(here, self.g) + z_down(kz * here, self.g)
        return a + b + (self.ky[r + 1] * u[r + 1] + self.ky[r] * u[r - 1])

    def weigh(self, first, last):
        def body(r):
            self.w[r] = DAMPING * inverse(self.d[r])

        each(first, last, self.step, body)

    def first(self, u, first, last):
        def body(r):
            u[r] = self.w[r] * self.f[r]

        each(first, last, self.step, body)

    def swept(self, u, r):
        return (1.0 / 3.0) * u[r] + self.w[r] * (self.f[r] + self.beside(u, r))

    def sweep(self, u, v, first, last):
        def body(r):
            v[r] = self.swept(u, r)

        each(first, last, self.step, body)

    def residual(self, u, r):
        return self.f[r] + self.beside(u, r) - self.d[r] * u[r]

    def residual_pairs(self, u, out, first, count):
        def body(j):
            out[j] = self.residual(u, first + 2 * j) + self.residual(u, first + 2 * j + 1)

        each(0, count - 1, self.step // 2, body)


def z_pairs(low, g):
    return lambda a: a + jnp.where(low, z_up(a, g), z_down(a, g))


def coarse_coefficients(level, r, x_count):
    even, odd = pl.ds(0, x_count, stride=2), pl.ds(1, x_count, stride=2)
    g = level.g
    low = (lax.broadcasted_iota(jnp.int32, (x_count, WIDE), 1) & g) == 0
    z_pair = z_pairs(low, g)

    def all_x(ref, row):
        return ref[row, even] + ref[row, odd]

    kx = level.kx[r, odd] + level.kx[r + 1, odd]
    inner = level.kx[r, even] + level.kx[r + 1, even] + all_x(level.ky, r + 1)
    kz = all_x(level.kz, r) + all_x(level.kz, r + 1)
    d = all_x(level.d, r) + all_x(level.d, r + 1)
    d = d - 2.0 * (inner + jnp.where(low, kz, 0.0))
    return z_pair(kx), coarse_sum(level.ky, r + 2, x_count, g), jnp.where(low, z_up(kz, g), kz), z_pair(d)


def coarse_sum(ref, r, x_count, g):
    even, odd = pl.ds(0, x_count, stride=2), pl.ds(1, x_count, stride=2)
    low = (lax.broadcasted_iota(jnp.int32, (x_count, WIDE), 1) & g) == 0
    return z_pairs(low, g)(ref[r, even] + ref[r, odd])


def correct(u, v, e, t, x_count, first, last, to):
    def body(j):
        part = e[j]
        t[j, pl.ds(0, x_count, stride=2)] = part
        t[j, pl.ds(1, x_count, stride=2)] = part
        wide = t[j]
        r = to + 2 * (j - first)
        v[r] = u[r] + wide
        v[r + 1] = u[r + 1] + wide

    each(first, last, 2, body)


def pick_lanes(a, lanes):
    return jnp.take_along_axis(a, lanes, axis=1, mode="promise_in_bounds")


def prepare_kernel(plan, phase_in, density_in, rhs_in, *refs):
    outs, (phase, density, rhs, sems) = refs[: plan.gx], refs[plan.gx :]
    pairs = ((phase_in, phase), (density_in, density), (rhs_in, rhs))
    copies = [pltpu.make_async_copy(a, b, sems.at[k]) for k, (a, b) in enumerate(pairs)]
    for copy in copies:
        copy.start()
    here = lax.axis_index("gx")
    by, px = plan.by, plan.px
    places = [pl.ds(plan.start_of(here ^ plan.distance(slot)), by) for slot in range(plan.gx)]
    copies[0].wait()
    copies[1].wait()
    for out, rows in zip(outs, places):
        for p in range(px):
            half = jnp.where(phase[p, rows, :] == 1, 500.0, 0.5).astype(F32)
            out[pl.ds(p, by, stride=2 * px), :] = half * density[p, rows, :]
    copies[2].wait()
    for out, rows in zip(outs, places):
        for p in range(px):
            out[pl.ds(px + p, by, stride=2 * px), :] = rhs[0, p, rows, :]


def gather_kernel(plan, *refs):
    parts, (c, *sets) = refs[: plan.gx], refs[plan.gx :]
    block = plan.block_here()
    for slot, part in enumerate(parts):
        k = plan.distance(slot)
        c[k] = part[...]
        for one, out in enumerate(sets):
            up = plan.is_up(block, 1, one)
            for field, count, at in ((0, HALO, 0), (1, HALO_RHS, HALO)):
                first = jnp.where(up, plan.by - count, 0)
                for r in range(count):
                    out[k, at + r] = part[first + r, field]


def compress(stage, g):
    halves, _, rows, _ = stage.shape
    width = LANES // g
    cell = lax.broadcasted_iota(jnp.int32, (rows, LANES), 1)
    lanes, place = lax.rem(g * cell, LANES), lax.div(cell, width)
    total = pick_lanes(stage[0, 0], lanes)
    for k in range(1, 2 * halves):
        total = jnp.where(place == k, pick_lanes(stage[k // 2, k % 2], lanes), total)
    return total


class Finest:
    COUNT = 16

    @staticmethod
    def shapes(plan):
        level0 = in_vmem(plan.rows, 2, plan.nx, LANES)
        pairs = in_vmem(plan.by // 2 + 8, 2, plan.nx, LANES)
        level1 = in_vmem(plan.by // 2 + 8, 2, plan.nx // 2, LANES)
        return [level0] * 10 + [pairs] + [level1] * 5

    def __init__(self, plan, refs):
        self.plan = plan
        fields = [Wide(r) for r in refs]
        self.kx, self.ky, self.kz, self.d, self.w, self.f, self.ub = fields[:7]
        self.h, self.ua, self.face, self.r = fields[7:11]
        self.kx1, self.ky1, self.kz1, self.d1, self.f1 = fields[11:]
        self.level = Level(1, 1, self.kx, self.ky, self.kz, self.d, self.w, self.f)
        nx = plan.nx
        shape = (nx, WIDE)
        self.half_x = nx // 2
        self.base = plan.block_here() * plan.by - HALO
        self.y_count, z_count = plan.by * plan.blocks, plan.nz * plan.gz
        x = lax.broadcasted_iota(jnp.int32, shape, 0)
        lane = lax.broadcasted_iota(jnp.int32, shape, 1)
        core = lax.axis_index("gz")
        if plan.paired:
            z = lax.rem(core * LANES + lane, WIDE)
        else:
            z = core * LANES + jnp.where(lane < LANES + LANES // 2, lane, lane - WIDE)
        self.x_top, self.x_bottom = x == nx - 1, x == 0
        self.z_top, self.z_bottom = z == z_count - 1, z == 0
        self.z_shut = (z < 0) | (z >= z_count - 1)
        self.z_out = (z < 0) | (z >= z_count)

    def put_h(self, to, s, xs, tile):
        y = self.base + to
        tile = jnp.where((y >= 0) & (y < self.y_count), tile, 0.5)
        if not self.plan.paired:
            tile = jnp.where(self.z_out[: self.plan.px, s * LANES : (s + 1) * LANES], 0.5, tile)
        self.h.ref[to, s, xs, :] = tile

    def tiles(self, other):
        px = self.plan.px
        return [(k, pl.ds(pl.multiple_of((other ^ k) * px, px), px)) for k in range(self.plan.gx)]

    def is_open(self, r):
        y = self.base + r
        return (y >= 0) & (y < self.y_count - 1)

    def start(self, r):
        first = inverse(self.h[r] + self.h[r + 1])
        self.face[r + 1] = first
        self.ky[r + 1] = jnp.where(self.is_open(r), first, 0.0)

    def faces(self, j):
        yd = self.face[2 * j - 1]
        for r in (2 * j - 1, 2 * j):
            h = self.h[r]
            alone = 0.5 * inverse(h)
            xu = inverse(h + jnp.where(self.x_top, h, x_up(h)))
            xd = jnp.where(self.x_bottom, alone, x_down(xu))
            yu = inverse(h + self.h[r + 1])
            zu = inverse(h + jnp.where(self.z_top, h, z_up(h, 1)))
            zd = jnp.where(self.z_bottom, alone, z_down(zu, 1))
            d = xu + xd + yu + yd + zu + zd
            w = DAMPING * inverse(d)
            self.kx[r] = jnp.where(self.x_top, 0.0, xu)
            self.ky[r + 1] = jnp.where(self.is_open(r), yu, 0.0)
            self.kz[r] = jnp.where(self.z_shut, 0.0, zu)
            self.d[r], self.w[r] = d, w
            self.ua[r] = w * self.f[r]
            yd = yu
        self.face[2 * j + 1] = yd

    def coarsen(self, j):
        coarse = coarse_coefficients(self.level, 2 * j - 1, self.half_x)
        self.kx1[j], self.ky1[j + 1], self.kz1[j], self.d1[j] = coarse

    def sweep(self, j):
        self.ub[2 * j] = self.level.swept(self.ua, 2 * j)
        self.ub[2 * j + 1] = self.level.swept(self.ua, 2 * j + 1)

    def residual(self, j):
        self.r[j] = self.level.residual(self.ub, 2 * j - 1) + self.level.residual(self.ub, 2 * j)

    def restrict(self, j):
        self.f1[j] = coarse_sum(self.r, j, self.half_x, 1)


def inner_pairs(plan):
    return (HALO + 3) // 2, (HALO + plan.by - 2) // 2


def inner_kernel(plan, c, zc, *refs):
    fine = Finest(plan, refs)

    def take(r):
        for k, xs in fine.tiles(lax.axis_index("gx")):
            for s, ref in enumerate((c, zc)):
                fine.put_h(r + HALO, s, xs, ref[k, r, 0])
                fine.f.ref[r + HALO, s, xs, :] = ref[k, r, 1]

    each(0, plan.by - 1, 4, take)
    first, last = inner_pairs(plan)
    fine.start(2 * first - 2)
    wave(
        (fine.restrict, first + 1, last - 1, 4),
        (fine.residual, first + 1, last - 1, 3),
        (fine.sweep, first, last - 1, 2),
        (fine.coarsen, first, last, 1),
        (fine.faces, first, last, 0),
    )


def down_kernel(plan, sides, zsides, *refs):
    count = Finest.COUNT
    near_count = 1 if plan.paired else 2
    refs = refs[count:]
    fine = Finest(plan, refs[:count])
    kx1, ky1, kz1, d1, f1 = fine.kx1, fine.ky1, fine.kz1, fine.d1, fine.f1
    pack, nears, refs = refs[count], refs[count + 1 : count + 1 + near_count], refs[count + 1 + near_count :]
    w1, u1, uc, r1 = [Wide(r) for r in refs[:4]]
    stage, near_stage = refs[4:6]
    nx, by, gx = plan.nx, plan.by, plan.gx
    block, core = plan.block_here(), lax.axis_index("gz")

    def take_side(at, other, to, count, field):
        def one(r):
            for k, xs in fine.tiles(other):
                for s, ref in enumerate((sides, zsides)):
                    if field == 0:
                        fine.put_h(r + to, s, xs, ref[at + k, r])
                    else:
                        fine.f.ref[r + to, s, xs, :] = ref[at + k, HALO + r]

        each(0, count - 1, 4, one)

    up_first = plan.is_up(block, 1, 0)
    below, above = jnp.where(up_first, gx, 0), jnp.where(up_first, 0, gx)
    gx_below, gx_above = plan.gx_of(block - 1), plan.gx_of(block + 1)
    take_side(below, gx_below, 0, HALO, 0)
    take_side(above, gx_above, HALO + by, HALO, 0)
    take_side(below, gx_below, HALO - HALO_RHS, HALO_RHS, 1)
    take_side(above, gx_above, HALO + by, HALO_RHS, 1)

    @pl.when(block == 0)
    def _():
        fine.h[HALO - 1] = fine.h[HALO]

    @pl.when(block == plan.blocks - 1)
    def _():
        fine.h[HALO + by] = fine.h[HALO + by - 1]

    fine.start(0)
    first, last = inner_pairs(plan)
    end = by // 2 + 6
    late = -last
    wave(
        (fine.restrict, 2, first, 4),
        (fine.restrict, last, end - 1, late + 4),
        (fine.residual, 2, first, 3),
        (fine.residual, last, end - 1, late + 3),
        (fine.sweep, 1, first - 1, 2),
        (fine.sweep, last, end - 1, late + 2),
        (fine.coarsen, 1, first - 1, 1),
        (fine.coarsen, last + 1, end, late + 1),
        (fine.faces, 1, first - 1, 0),
        (fine.faces, last + 1, end, late),
    )
    ky1[1] = coarse_sum(fine.ky, 1, nx // 2, 1)

    own = by // 2
    half_x = nx // 2
    middle = Level(1, 2, kx1, ky1, kz1, d1, w1, f1, 8)
    middle.weigh(1, own + 6)
    middle.first(uc, 2, own + 5)
    middle.sweep(uc, u1, 3, own + 4)
    middle.residual_pairs(u1, r1, 4, own // 2)

    quarter_x = nx // 4
    own2 = own // 2
    part = own2 // 2
    for j in range(own2):
        fields = (coarse_sum(r1, j, quarter_x, 2),) + coarse_coefficients(middle, 4 + 2 * j, quarter_x)
        for t, a in enumerate(fields):
            xs = pl.ds((t * part + j % part) * quarter_x, quarter_x)
            stage[j // part, 0, xs, :] = a[:, :LANES]
            stage[j // part, 1, xs, :] = a[:, LANES:]
    total = compress(stage, 4)
    pack[...] = total

    size = pack.shape[0]
    for one, out in enumerate(nears):
        row = jnp.where(plan.is_up(block, 1, core if plan.paired else one), own, 5)
        for k, (ref, r) in enumerate(((u1, row), (u1, row + 1), (u1, row + 2), (f1, row + 1))):
            for s in range(2):
                near_stage[0, s, pl.ds(k * half_x, half_x), :] = ref.ref[r, s]
        out[pl.ds(0, size), :] = total
        out[pl.ds(size, 4 * half_x), :] = compress(near_stage, 2)


class Coarse:
    COUNT = 9

    @staticmethod
    def shapes(plan):
        rows = (2 * FAR + 1) * (plan.by // 4) + 1
        level2 = in_vmem(rows, 2, plan.nx // 4, LANES)
        level1 = in_vmem(plan.by // 2 + 8, 2, plan.nx // 2, LANES)
        return [level2] * 7 + [level1] * 2

    def __init__(self, plan, refs):
        self.plan = plan
        self.fields = [Wide(r) for r in refs[:5]]
        self.f, self.kx, self.ky, self.kz, self.d = self.fields
        self.w, self.u, self.f1, self.u1 = [Wide(r) for r in refs[5:]]
        self.block = plan.block_here()

    def spread(self, packed, at, turned):
        plan = self.plan
        own2, quarter_x = plan.by // 4, plan.nx // 4
        part = own2 // 2
        there = self.block + at - FAR
        exists = (there >= 0) & (there < plan.blocks)
        lane = lax.broadcasted_iota(jnp.int32, packed.shape, 1)
        for quarter in range(4):
            part_of, half = divmod(quarter, 2)
            s = half ^ turned
            a = pick_lanes(packed, lax.div(lane, 4) + quarter * (LANES // 4))
            for j in range(part):
                r = at * own2 + part_of * part + j
                tiles = [a[(t * part + j) * quarter_x : (t * part + j + 1) * quarter_x] for t in range(5)]
                for t, ref in enumerate(self.fields):
                    if t == 2:
                        ref.ref[r + 1, s] = jnp.where(exists, tiles[t], 0.0)
                    else:
                        ref.ref[r, s] = tiles[t]
                w = DAMPING * inverse(tiles[4])
                self.w.ref[r, s] = w
                self.u.ref[r, s] = w * tiles[0]

    def side(self, ref, ups, turned):
        plan = self.plan
        own, half_x = plan.by // 2, plan.nx // 2
        size = 5 * (plan.by // 8) * (plan.nx // 4)
        nearest = size + 4 * half_x
        for k, up in ups.items():
            first = 0 if k == 1 else nearest + (k - 2) * size
            self.spread(ref[pl.ds(first, size), :], jnp.where(up, FAR + k, FAR - k), turned)
        row = jnp.where(ups[1], own + 5, 0)
        for k, (to, r) in enumerate(((self.u1, row), (self.u1, row + 1), (self.u1, row + 2), (self.f1, row + 1))):
            row_in = ref[pl.ds(size + k * half_x, half_x), :]
            lane = lax.broadcasted_iota(jnp.int32, row_in.shape, 1)
            for s in range(2):
                to.ref[r, s ^ turned] = pick_lanes(row_in, lax.div(lane, 2) + s * (LANES // 2))

    def ups(self, opposite):
        one = lax.axis_index("gz") if self.plan.paired else 0
        one = 1 - one if opposite else one
        return {k: self.plan.is_up(self.block, k, one) for k in range(1, FAR + 1)}


def spread_kernel(plan, pack, mine, f1, u1, *refs):
    coarse = Coarse(plan, refs)
    own = plan.by // 2
    for r in range(2, own + 6):
        coarse.f1.ref[r] = f1[r]
    for r in range(3, own + 5):
        coarse.u1.ref[r] = u1[r]
    coarse.spread(pack[...], FAR, 0)
    coarse.side(mine, coarse.ups(False), 0)


def up_kernel(plan, theirs, *refs):
    count = Coarse.COUNT
    refs = refs[count:]
    kx0, ky0, kz0, d0, w0, f0, u0, kx1, ky1, kz1, w1 = [Wide(r) for r in refs[:11]]
    out, coarse, scratch = refs[11], Coarse(plan, refs[12 : 12 + count]), refs[12 + count :]
    f2, kx2, ky2, kz2, d2, w2, ua2 = *coarse.fields, coarse.w, coarse.u
    f1, ua1 = coarse.f1, coarse.u1
    wide = [Wide(r) for r in scratch]
    ub2, r2, f3, kx3, ky3, kz3, d3, w3, ua3, ub3 = wide[:10]
    t1, t0, ub1, ua0, ub0, uc0 = wide[10:]
    nx, by = plan.nx, plan.by
    own, own2 = by // 2, by // 4
    half_x, quarter_x = nx // 2, nx // 4
    here = lax.axis_index("gx")
    coarse.side(theirs, coarse.ups(True), 1 if plan.paired else 0)

    rows2 = (2 * FAR + 1) * own2
    two = Level(1, 4, kx2, ky2, kz2, d2, w2, f2, 14)
    two.sweep(ua2, ub2, 1, rows2 - 2)
    two.residual_pairs(ub2, r2, 2, rows2 // 2 - 2)

    x = lax.broadcasted_iota(jnp.int32, (quarter_x, WIDE), 0)
    even_x = (x & 1) == 0
    low = (lax.broadcasted_iota(jnp.int32, (quarter_x, WIDE), 1) & 4) == 0
    z_pair = z_pairs(low, 4)

    def x_pair(a):
        return a + jnp.where(even_x, x_up(a), x_down(a))

    last3 = rows2 // 2 - 2

    def coarsen(j):
        r = 2 * j
        kx = kx2[r] + kx2[r + 1]
        kz = kz2[r] + kz2[r + 1]
        inner = ky2[r + 1] + jnp.where(even_x, kx, 0.0) + jnp.where(low, kz, 0.0)
        f3[j] = z_pair(x_pair(r2[j - 1]))
        kx3[j] = z_pair(jnp.where(even_x, x_up(kx), kx))
        ky3[j + 1] = z_pair(x_pair(ky2[r + 2]))
        kz = x_pair(kz)
        kz3[j] = jnp.where(low, z_up(kz, 4), kz)
        d3[j] = z_pair(x_pair(d2[r] + d2[r + 1] - 2.0 * inner))

    each(1, last3, 6, coarsen)
    three = Level(2, 8, kx3, ky3, kz3, d3, w3, f3, 16)
    three.weigh(1, last3)
    three.first(ua3, 1, last3)
    three.sweep(ua3, ub3, 2, last3 - 1)
    three.sweep(ub3, ua3, 3, last3 - 2)
    three.sweep(ua3, ub3, 4, last3 - 3)

    first2 = FAR * own2
    for j in range(4, last3 - 2):
        e = ub3[j]
        ua2[2 * j] = ub2[2 * j] + e
        ua2[2 * j + 1] = ub2[2 * j + 1] + e
    two.sweep(ua2, ub2, first2 - 3, first2 + own2 + 2)
    two.sweep(ub2, ua2, first2 - 2, first2 + own2 + 1)

    one = Level(1, 2, kx1, ky1, kz1, None, w1, f1, 8)
    correct(ua1, ub1, ua2, t1, quarter_x, first2 - 2, first2 + own2 + 1, 0)
    one.sweep(ub1, ua1, 1, own + 6)
    one.sweep(ua1, ub1, 2, own + 5)

    finest = Level(1, 1, kx0, ky0, kz0, d0, w0, f0)

    def corrected(j):
        part = ub1[j]
        t0[j, pl.ds(0, half_x, stride=2)] = part
        t0[j, pl.ds(1, half_x, stride=2)] = part
        both = t0[j]
        ua0[2 * j - 1] = u0[2 * j - 1] + both
        ua0[2 * j] = u0[2 * j] + both

    def sweep(j):
        ub0[2 * j - 1] = finest.swept(ua0, 2 * j - 1)
        ub0[2 * j] = finest.swept(ua0, 2 * j)

    def sweep_again(j):
        uc0[2 * j] = finest.swept(ub0, 2 * j)
        uc0[2 * j + 1] = finest.swept(ub0, 2 * j + 1)

    slots = [plan.slot(s ^ here) for s in range(plan.gx)]

    def finish(j):
        for r in (2 * j - 1, 2 * j):
            scaled = d0[r] * uc0[r]
            rest = f0[r] + finest.beside(uc0, r) - scaled
            for s in range(plan.gx):
                part = slice(s * plan.px, (s + 1) * plan.px)
                out[slots[s], r - HALO, 0] = scaled[part, :LANES]
                out[slots[s], r - HALO, 1] = rest[part, :LANES]

    wave(
        (finish, 4, own + 3, 5),
        (sweep_again, 3, own + 3, 4),
        (sweep, 3, own + 4, 2),
        (corrected, 2, own + 5, 0),
    )


def place_kernel(plan, *refs):
    parts, outs, (fields, sems) = refs[: plan.gx], refs[plan.gx : plan.gx + 2], refs[plan.gx + 2 :]
    here = lax.axis_index("gx")
    by, px = plan.by, plan.px
    copies = []
    for slot, part in zip(plan.back, parts):
        rows = pl.ds(plan.start_of(here ^ plan.distance(slot)), by)
        for t, out in enumerate(outs):
            for p in range(px):
                fields[t, p, rows, :] = part[pl.ds(t * px + p, by, stride=2 * px), :]
            copy = pltpu.make_async_copy(fields.at[t, :, rows, :], out.at[0, :, rows, :], sems.at[t, slot])
            copy.start()
            copies.append(copy)
    for copy in copies:
        copy.wait()


def in_vmem(*shape):
    return pltpu.VMEM(shape, F32)


def call(kernel, out_shape, scratch=(), work=0, **more):
    if work:
        more["cost_estimate"] = pl.CostEstimate(flops=0, bytes_accessed=work, transcendentals=0)
    return pl.pallas_call(
        kernel,
        out_shape=out_shape,
        scratch_shapes=list(scratch),
        compiler_params=pltpu.CompilerParams(vmem_limit_bytes=VMEM_LIMIT),
        **more,
    )


def pinned(*arrays, where=pltpu.VMEM):
    return [pltpu.with_memory_space_constraint(a, where) for a in arrays]


def beside_in_z(plan, a):
    count = plan.gz
    if plan.paired:
        return lax.ppermute(a, "gz", [(0, 1), (1, 0)])
    cut = LANES // 2
    right = lax.ppermute(a[..., :cut], "gz", [(i + 1, i) for i in range(count - 1)])
    left = lax.ppermute(a[..., cut:], "gz", [(i, i + 1) for i in range(count - 1)])
    return jnp.concatenate([right, left], axis=-1)


def exchange(plan, parts):
    got = [parts[0]]
    for slot in range(1, plan.gx):
        pairs = []
        for i in range(plan.gx):
            for g in range(plan.gz):
                to = i ^ plan.distances(g % 2)[slot]
                pairs.append((i * plan.gz + g, to * plan.gz + g))
        got.append(lax.ppermute(parts[slot], ("gx", "gz"), pairs))
    return got


def partners(plan, k, one):
    partner = [None] * plan.blocks
    for b in range(plan.blocks - k):
        if b // k % 2 == one:
            partner[b], partner[b + k] = b + k, b
    return partner


def swap_blocks(plan, a, k, one):
    pairs = []
    for b, partner in enumerate(partners(plan, k, one)):
        for g in range(plan.gz):
            to = (b, g ^ 1) if partner is None else (partner, g)
            pairs.append((plan.device(b) * plan.gz + g, plan.device(to[0]) * plan.gz + to[1]))
    return lax.ppermute(a, ("gx", "gy", "gz"), pairs)


def swap_blocks_apart(plan, a, k):
    pairs = []
    for one in range(2):
        partner = partners(plan, k, one)
        alone = [b for b in range(plan.blocks) if partner[b] is None]
        low = [b for b in alone if 2 * b < plan.blocks]
        high = [b for b in alone if 2 * b >= plan.blocks]
        couples = [(low.pop(0), high.pop())] if len(low) % 2 else []
        for group in (low, high):
            couples += zip(group[::2], group[1::2])
        for x, y in couples:
            partner[x], partner[y] = y, x
        pairs += [(2 * plan.device(b) + one, 2 * plan.device(p) + one) for b, p in enumerate(partner)]
    return lax.ppermute(a, ("gx", "gy", "gz"), pairs)


def far_blocks(plan, pack, nears):
    def line(move, near):
        parts = [move(pack, k) for k in range(FAR, 1, -1)] + [move(near, 1)]
        return jnp.concatenate(parts[::-1], axis=0)

    if plan.paired:
        mine = line(functools.partial(swap_blocks_apart, plan), nears[0])
        return mine, beside_in_z(plan, mine)
    return [line(functools.partial(swap_blocks, plan, one=one), nears[one]) for one in range(2)]


def on_device(plan, phase, density, rhs):
    nx, by, rows, px, gx = plan.nx, plan.by, plan.rows, plan.px, plan.gx
    flat = by * 2 * px
    block = (px, plan.ny, LANES)
    outside = pl.BlockSpec(memory_space=pltpu.HBM)
    parts = call(
        functools.partial(prepare_kernel, plan),
        [in_vmem(flat, LANES)] * gx,
        [pltpu.VMEM(block, jnp.int32), in_vmem(*block), in_vmem(1, *block), pltpu.SemaphoreType.DMA((3,))],
        in_specs=[outside] * 3,
    )(*pinned(phase, density, rhs, where=pltpu.HBM))
    parts = [a.reshape(by, 2, px, LANES) for a in exchange(plan, parts)]
    c, *sets = call(
        functools.partial(gather_kernel, plan),
        [in_vmem(gx, by, 2, px, LANES)] + [in_vmem(gx, HALO + HALO_RHS, px, LANES)] * 2,
    )(*pinned(*parts))
    sides = jnp.concatenate([swap_blocks(plan, sets[one], 1, one) for one in (0, 1)], axis=0)
    zc = beside_in_z(plan, c)
    zsides = beside_in_z(plan, sides)

    own, own2 = by // 2, by // 4
    size = 5 * (own2 // 2) * (nx // 4)
    side = size + 4 * (nx // 2)

    def level0(n):
        return in_vmem(n, 2, nx, LANES)

    def level1(n):
        return in_vmem(n, 2, nx // 2, LANES)

    inner = call(functools.partial(inner_kernel, plan), Finest.shapes(plan), work=9_000_000)(*pinned(c, zc))
    near_count = 1 if plan.paired else 2
    outs = Finest.shapes(plan) + [in_vmem(size, LANES)] + [in_vmem(side, LANES)] * near_count + [level1(own + 8)] * 2
    scratch = [level1(own + 8), level1(own2), in_vmem(2, 2, size, LANES), in_vmem(1, 2, 4 * (nx // 2), LANES)]
    down = call(
        functools.partial(down_kernel, plan),
        outs,
        scratch,
        input_output_aliases={2 + k: k for k in range(Finest.COUNT)},
    )(*pinned(sides, zsides, *inner))
    fine, rest = down[: Finest.COUNT], down[Finest.COUNT :]
    pack, nears, (w1, u1) = rest[0], rest[1 : 1 + near_count], rest[1 + near_count :]
    kx1, ky1, kz1, _, f1 = fine[11:]
    mine, theirs = far_blocks(plan, pack, nears)
    coarse = call(functools.partial(spread_kernel, plan), Coarse.shapes(plan), work=3_000_000)(
        *pinned(pack, mine, f1, u1)
    )
    rows2 = (2 * FAR + 1) * own2
    level2, level3 = in_vmem(rows2 + 1, 2, nx // 4, LANES), in_vmem(rows2 // 2 + 1, 2, nx // 4, LANES)
    scratch = [level2] * 2 + [level3] * 8 + [level1(rows2), level0(own + 8), level1(own + 8)] + [level0(rows)] * 3
    result = call(
        functools.partial(up_kernel, plan),
        [in_vmem(gx, by, 2, px, LANES)] + Coarse.shapes(plan),
        scratch,
        input_output_aliases={1 + k: 1 + k for k in range(Coarse.COUNT)},
    )(*pinned(theirs, *coarse, *fine[:7], kx1, ky1, kz1, w1))[0]

    parts = exchange(plan, [result[k].reshape(flat, LANES) for k in range(gx)])
    return call(
        functools.partial(place_kernel, plan),
        [jax.ShapeDtypeStruct((1, px, plan.ny, LANES), F32)] * 2,
        [in_vmem(2, px, plan.ny, LANES), pltpu.SemaphoreType.DMA((2, gx))],
        out_specs=[outside] * 2,
    )(*pinned(*[parts[slot] for slot in plan.back]))


def solution(mesh):
    sizes = [mesh.shape[a] for a in ("gx", "gy", "gz")]

    def local(phase, density, rhs):
        return tuple(on_device(Plan(sizes, phase.shape), phase, density, rhs))

    in_specs = (P("gx", "gy", "gz"), P("gx", "gy", "gz"), P(None, "gx", "gy", "gz"))
    out_specs = (P(None, "gx", "gy", "gz"), P(None, "gx", "gy", "gz"))
    return jax.shard_map(local, mesh=mesh, in_specs=in_specs, out_specs=out_specs, check_vma=False)
```

```python
import functools

import jax
import jax.numpy as jnp
from jax import lax
from jax.experimental import pallas as pl
from jax.experimental.pallas import tpu as pltpu
from jax.sharding import PartitionSpec as P


DAMPING = 2.0 / 3.0
LANES = 128
WIDE = 256
HALO = 7
HALO_RHS = 6
FAR = 3
F32 = jnp.float32
VMEM_LIMIT = 24 * 1024 * 1024


class Plan:
    def __init__(self, sizes, shape):
        self.gx, self.gy, self.gz = sizes
        self.px, self.ny, self.nz = shape
        self.nx = self.px * self.gx
        self.by = self.ny // self.gx
        self.blocks = self.gx * self.gy
        self.rows = self.by + 2 * HALO
        self.paired = self.gz == 2
        self.ring = [0, 1, 3, 2] if self.gx == 4 else list(range(self.gx))
        self.place = [self.ring.index(i) for i in range(self.gx)]
        self.back = [0, 2, 3, 1] if self.gx == 4 else list(range(self.gx))

    def device(self, block):
        j, q = divmod(block, self.gx)
        return self.ring[(q - j) % self.gx] * self.gy + j

    def look_up(self, table, i):
        return sum(jnp.where(i == k, v, 0) for k, v in enumerate(table))

    def start_of(self, i):
        q = lax.rem(self.look_up(self.place, i) + lax.axis_index("gy"), self.gx)
        return pl.multiple_of(q * self.by, self.by)

    def distances(self, core):
        if self.gx != 4:
            return list(range(self.gx))
        return [0, 3, 1, 2]

    def by_core(self, even, odd):
        return even if even == odd else jnp.where(lax.rem(lax.axis_index("gz"), 2) == 0, even, odd)

    def distance(self, slot):
        return self.by_core(self.distances(0)[slot], self.distances(1)[slot])

    def slot(self, distance):
        found = [self.by_core(self.distances(0).index(k), self.distances(1).index(k)) for k in range(self.gx)]
        return self.look_up(found, distance)

    def block_here(self):
        j = lax.axis_index("gy")
        return j * self.gx + lax.rem(self.look_up(self.place, lax.axis_index("gx")) + j, self.gx)

    def gx_of(self, block):
        block = jnp.clip(block, 0, self.blocks - 1)
        j, q = lax.div(block, self.gx), lax.rem(block, self.gx)
        return self.look_up(self.ring, lax.rem(q + self.gx * self.gy - j, self.gx))

    def is_up(self, block, k, one):
        return lax.rem(lax.div(block, k), 2) == one


def x_up(a, s=1):
    return pltpu.roll(a, a.shape[0] - s, 0)


def x_down(a, s=1):
    return pltpu.roll(a, s, 0)


def z_up(a, g):
    return pltpu.roll(a, a.shape[1] - g, 1)


def z_down(a, g):
    return pltpu.roll(a, g, 1)


def inverse(a):
    r = pl.reciprocal(a, approx=True)
    return r * (2.0 - a * r)


def each(first, last, step, body):
    count = last + 1 - first
    if count <= 2 * step:
        for i in range(first, last + 1):
            body(i)
        return

    def go(c, _):
        for k in range(step):
            body(first + c * step + k)
        return 0

    lax.fori_loop(0, count // step, go, 0)
    for i in range(first + count // step * step, last + 1):
        body(i)


def wave(*stages):
    start = min(first + delay for _, first, _, delay in stages)
    end = max(last + delay for _, _, last, delay in stages)
    full = max(first + delay for _, first, _, delay in stages)
    full_end = min(last + delay for _, _, last, delay in stages)

    def step(t):
        for body, first, last, delay in stages:
            if first <= t - delay <= last:
                body(t - delay)

    def all_of_them(t, _):
        for body, _, _, delay in stages:
            body(t - delay)
        return 0

    if full_end - full < 3:
        full = full_end = end + 1
    for t in range(start, min(full, end + 1)):
        step(t)
    if full <= end:
        lax.fori_loop(full, full_end + 1, all_of_them, 0)
        for t in range(full_end + 1, end + 1):
            step(t)


class Wide:
    def __init__(self, ref):
        self.ref = ref

    def __getitem__(self, key):
        r, xs = key if isinstance(key, tuple) else (key, slice(None))
        return jnp.concatenate([self.ref[r, 0, xs, :], self.ref[r, 1, xs, :]], axis=1)

    def __setitem__(self, key, value):
        r, xs = key if isinstance(key, tuple) else (key, slice(None))
        self.ref[r, 0, xs, :] = value[:, :LANES]
        self.ref[r, 1, xs, :] = value[:, LANES:]


class Level:
    def __init__(self, s, g, kx, ky, kz, d, w, f, step=2):
        self.s, self.g, self.step = s, g, step
        self.kx, self.ky, self.kz, self.d, self.w, self.f = kx, ky, kz, d, w, f

    def beside(self, u, r):
        here = u[r]
        kx, kz = self.kx[r], self.kz[r]
        a = kx * x_up(here, self.s) + x_down(kx * here, self.s)
        b = kz * z_up(here, self.g) + z_down(kz * here, self.g)
        return a + b + (self.ky[r + 1] * u[r + 1] + self.ky[r] * u[r - 1])

    def weigh(self, first, last):
        def body(r):
            self.w[r] = DAMPING * inverse(self.d[r])

        each(first, last, self.step, body)

    def first(self, u, first, last):
        def body(r):
            u[r] = self.w[r] * self.f[r]

        each(first, last, self.step, body)

    def swept(self, u, r):
        return (1.0 / 3.0) * u[r] + self.w[r] * (self.f[r] + self.beside(u, r))

    def sweep(self, u, v, first, last):
        def body(r):
            v[r] = self.swept(u, r)

        each(first, last, self.step, body)

    def residual(self, u, r):
        return self.f[r] + self.beside(u, r) - self.d[r] * u[r]

    def residual_pairs(self, u, out, first, count):
        def body(j):
            out[j] = self.residual(u, first + 2 * j) + self.residual(u, first + 2 * j + 1)

        each(0, count - 1, self.step // 2, body)


def z_pairs(low, g):
    return lambda a: a + jnp.where(low, z_up(a, g), z_down(a, g))


def coarse_coefficients(level, r, x_count):
    even, odd = pl.ds(0, x_count, stride=2), pl.ds(1, x_count, stride=2)
    g = level.g
    low = (lax.broadcasted_iota(jnp.int32, (x_count, WIDE), 1) & g) == 0
    z_pair = z_pairs(low, g)

    def all_x(ref, row):
        return ref[row, even] + ref[row, odd]

    kx = level.kx[r, odd] + level.kx[r + 1, odd]
    inner = level.kx[r, even] + level.kx[r + 1, even] + all_x(level.ky, r + 1)
    kz = all_x(level.kz, r) + all_x(level.kz, r + 1)
    d = all_x(level.d, r) + all_x(level.d, r + 1)
    d = d - 2.0 * (inner + jnp.where(low, kz, 0.0))
    return z_pair(kx), coarse_sum(level.ky, r + 2, x_count, g), jnp.where(low, z_up(kz, g), kz), z_pair(d)


def coarse_sum(ref, r, x_count, g):
    even, odd = pl.ds(0, x_count, stride=2), pl.ds(1, x_count, stride=2)
    low = (lax.broadcasted_iota(jnp.int32, (x_count, WIDE), 1) & g) == 0
    return z_pairs(low, g)(ref[r, even] + ref[r, odd])


def correct(u, v, e, t, x_count, first, last, to):
    def body(j):
        part = e[j]
        t[j, pl.ds(0, x_count, stride=2)] = part
        t[j, pl.ds(1, x_count, stride=2)] = part
        wide = t[j]
        r = to + 2 * (j - first)
        v[r] = u[r] + wide
        v[r + 1] = u[r + 1] + wide

    each(first, last, 2, body)


def pick_lanes(a, lanes):
    return jnp.take_along_axis(a, lanes, axis=1, mode="promise_in_bounds")


def prepare_kernel(plan, phase_in, density_in, rhs_in, *refs):
    outs, (phase, density, rhs, sems) = refs[: plan.gx], refs[plan.gx :]
    pairs = ((phase_in, phase), (density_in, density), (rhs_in, rhs))
    copies = [pltpu.make_async_copy(a, b, sems.at[k]) for k, (a, b) in enumerate(pairs)]
    for copy in copies:
        copy.start()
    here = lax.axis_index("gx")
    by, px = plan.by, plan.px
    places = [pl.ds(plan.start_of(here ^ plan.distance(slot)), by) for slot in range(plan.gx)]
    copies[0].wait()
    copies[1].wait()
    for out, rows in zip(outs, places):
        for p in range(px):
            half = jnp.where(phase[p, rows, :] == 1, 500.0, 0.5).astype(F32)
            out[pl.ds(p, by, stride=2 * px), :] = half * density[p, rows, :]
    copies[2].wait()
    for out, rows in zip(outs, places):
        for p in range(px):
            out[pl.ds(px + p, by, stride=2 * px), :] = rhs[0, p, rows, :]


def gather_kernel(plan, *refs):
    parts, (c, *sets) = refs[: plan.gx], refs[plan.gx :]
    block = plan.block_here()
    for slot, part in enumerate(parts):
        k = plan.distance(slot)
        c[k] = part[...]
        for one, out in enumerate(sets):
            up = plan.is_up(block, 1, one)
            for field, count, at in ((0, HALO, 0), (1, HALO_RHS, HALO)):
                first = jnp.where(up, plan.by - count, 0)
                for r in range(count):
                    out[k, at + r] = part[first + r, field]


def compress(stage, g):
    halves, _, rows, _ = stage.shape
    width = LANES // g
    cell = lax.broadcasted_iota(jnp.int32, (rows, LANES), 1)
    lanes, place = lax.rem(g * cell, LANES), lax.div(cell, width)
    total = pick_lanes(stage[0, 0], lanes)
    for k in range(1, 2 * halves):
        total = jnp.where(place == k, pick_lanes(stage[k // 2, k % 2], lanes), total)
    return total


class Finest:
    COUNT = 16

    @staticmethod
    def shapes(plan):
        level0 = in_vmem(plan.rows, 2, plan.nx, LANES)
        pairs = in_vmem(plan.by // 2 + 8, 2, plan.nx, LANES)
        level1 = in_vmem(plan.by // 2 + 8, 2, plan.nx // 2, LANES)
        return [level0] * 10 + [pairs] + [level1] * 5

    def __init__(self, plan, refs):
        self.plan = plan
        fields = [Wide(r) for r in refs]
        self.kx, self.ky, self.kz, self.d, self.w, self.f, self.ub = fields[:7]
        self.h, self.ua, self.face, self.r = fields[7:11]
        self.kx1, self.ky1, self.kz1, self.d1, self.f1 = fields[11:]
        self.level = Level(1, 1, self.kx, self.ky, self.kz, self.d, self.w, self.f)
        nx = plan.nx
        shape = (nx, WIDE)
        self.half_x = nx // 2
        self.base = plan.block_here() * plan.by - HALO
        self.y_count, z_count = plan.by * plan.blocks, plan.nz * plan.gz
        x = lax.broadcasted_iota(jnp.int32, shape, 0)
        lane = lax.broadcasted_iota(jnp.int32, shape, 1)
        core = lax.axis_index("gz")
        if plan.paired:
            z = lax.rem(core * LANES + lane, WIDE)
        else:
            z = core * LANES + jnp.where(lane < LANES + LANES // 2, lane, lane - WIDE)
        self.x_top, self.x_bottom = x == nx - 1, x == 0
        self.z_top, self.z_bottom = z == z_count - 1, z == 0
        self.z_shut = (z < 0) | (z >= z_count - 1)
        self.z_out = (z < 0) | (z >= z_count)

    def put_h(self, to, s, xs, tile):
        y = self.base + to
        tile = jnp.where((y >= 0) & (y < self.y_count), tile, 0.5)
        if not self.plan.paired:
            tile = jnp.where(self.z_out[: self.plan.px, s * LANES : (s + 1) * LANES], 0.5, tile)
        self.h.ref[to, s, xs, :] = tile

    def tiles(self, other):
        px = self.plan.px
        return [(k, pl.ds(pl.multiple_of((other ^ k) * px, px), px)) for k in range(self.plan.gx)]

    def is_open(self, r):
        y = self.base + r
        return (y >= 0) & (y < self.y_count - 1)

    def start(self, r):
        first = inverse(self.h[r] + self.h[r + 1])
        self.face[r + 1] = first
        self.ky[r + 1] = jnp.where(self.is_open(r), first, 0.0)

    def faces(self, j):
        yd = self.face[2 * j - 1]
        for r in (2 * j - 1, 2 * j):
            h = self.h[r]
            alone = 0.5 * inverse(h)
            xu = inverse(h + jnp.where(self.x_top, h, x_up(h)))
            xd = jnp.where(self.x_bottom, alone, x_down(xu))
            yu = inverse(h + self.h[r + 1])
            zu = inverse(h + jnp.where(self.z_top, h, z_up(h, 1)))
            zd = jnp.where(self.z_bottom, alone, z_down(zu, 1))
            d = xu + xd + yu + yd + zu + zd
            w = DAMPING * inverse(d)
            self.kx[r] = jnp.where(self.x_top, 0.0, xu)
            self.ky[r + 1] = jnp.where(self.is_open(r), yu, 0.0)
            self.kz[r] = jnp.where(self.z_shut, 0.0, zu)
            self.d[r], self.w[r] = d, w
            self.ua[r] = w * self.f[r]
            yd = yu
        self.face[2 * j + 1] = yd

    def coarsen(self, j):
        coarse = coarse_coefficients(self.level, 2 * j - 1, self.half_x)
        self.kx1[j], self.ky1[j + 1], self.kz1[j], self.d1[j] = coarse

    def sweep(self, j):
        self.ub[2 * j] = self.level.swept(self.ua, 2 * j)
        self.ub[2 * j + 1] = self.level.swept(self.ua, 2 * j + 1)

    def residual(self, j):
        self.r[j] = self.level.residual(self.ub, 2 * j - 1) + self.level.residual(self.ub, 2 * j)

    def restrict(self, j):
        self.f1[j] = coarse_sum(self.r, j, self.half_x, 1)


def inner_pairs(plan):
    return (HALO + 3) // 2, (HALO + plan.by - 2) // 2


def inner_kernel(plan, c, zc, *refs):
    fine = Finest(plan, refs)

    def take(r):
        for k, xs in fine.tiles(lax.axis_index("gx")):
            for s, ref in enumerate((c, zc)):
                fine.put_h(r + HALO, s, xs, ref[k, r, 0])
                fine.f.ref[r + HALO, s, xs, :] = ref[k, r, 1]

    each(0, plan.by - 1, 4, take)
    first, last = inner_pairs(plan)
    fine.start(2 * first - 2)
    wave(
        (fine.restrict, first + 1, last - 1, 4),
        (fine.residual, first + 1, last - 1, 3),
        (fine.sweep, first, last - 1, 2),
        (fine.coarsen, first, last, 1),
        (fine.faces, first, last, 0),
    )


def down_kernel(plan, sides, zsides, *refs):
    count = Finest.COUNT
    near_count = 1 if plan.paired else 2
    refs = refs[count:]
    fine = Finest(plan, refs[:count])
    kx1, ky1, kz1, d1, f1 = fine.kx1, fine.ky1, fine.kz1, fine.d1, fine.f1
    pack, nears, refs = refs[count], refs[count + 1 : count + 1 + near_count], refs[count + 1 + near_count :]
    w1, u1, uc, r1 = [Wide(r) for r in refs[:4]]
    stage, near_stage = refs[4:6]
    nx, by, gx = plan.nx, plan.by, plan.gx
    block, core = plan.block_here(), lax.axis_index("gz")

    def take_side(at, other, to, count, field):
        def one(r):
            for k, xs in fine.tiles(other):
                for s, ref in enumerate((sides, zsides)):
                    if field == 0:
                        fine.put_h(r + to, s, xs, ref[at + k, r])
                    else:
                        fine.f.ref[r + to, s, xs, :] = ref[at + k, HALO + r]

        each(0, count - 1, 4, one)

    up_first = plan.is_up(block, 1, 0)
    below, above = jnp.where(up_first, gx, 0), jnp.where(up_first, 0, gx)
    gx_below, gx_above = plan.gx_of(block - 1), plan.gx_of(block + 1)
    take_side(below, gx_below, 0, HALO, 0)
    take_side(above, gx_above, HALO + by, HALO, 0)
    take_side(below, gx_below, HALO - HALO_RHS, HALO_RHS, 1)
    take_side(above, gx_above, HALO + by, HALO_RHS, 1)

    @pl.when(block == 0)
    def _():
        fine.h[HALO - 1] = fine.h[HALO]

    @pl.when(block == plan.blocks - 1)
    def _():
        fine.h[HALO + by] = fine.h[HALO + by - 1]

    fine.start(0)
    first, last = inner_pairs(plan)
    end = by // 2 + 6
    late = -last
    wave(
        (fine.restrict, 2, first, 4),
        (fine.restrict, last, end - 1, late + 4),
        (fine.residual, 2, first, 3),
        (fine.residual, last, end - 1, late + 3),
        (fine.sweep, 1, first - 1, 2),
        (fine.sweep, last, end - 1, late + 2),
        (fine.coarsen, 1, first - 1, 1),
        (fine.coarsen, last + 1, end, late + 1),
        (fine.faces, 1, first - 1, 0),
        (fine.faces, last + 1, end, late),
    )
    ky1[1] = coarse_sum(fine.ky, 1, nx // 2, 1)

    own = by // 2
    half_x = nx // 2
    middle = Level(1, 2, kx1, ky1, kz1, d1, w1, f1, 8)
    middle.weigh(1, own + 6)
    middle.first(uc, 2, own + 5)
    middle.sweep(uc, u1, 3, own + 4)
    middle.residual_pairs(u1, r1, 4, own // 2)

    quarter_x = nx // 4
    own2 = own // 2
    part = own2 // 2
    for j in range(own2):
        fields = (coarse_sum(r1, j, quarter_x, 2),) + coarse_coefficients(middle, 4 + 2 * j, quarter_x)
        for t, a in enumerate(fields):
            xs = pl.ds((t * part + j % part) * quarter_x, quarter_x)
            stage[j // part, 0, xs, :] = a[:, :LANES]
            stage[j // part, 1, xs, :] = a[:, LANES:]
    total = compress(stage, 4)
    pack[...] = total

    size = pack.shape[0]
    for one, out in enumerate(nears):
        row = jnp.where(plan.is_up(block, 1, core if plan.paired else one), own, 5)
        for k, (ref, r) in enumerate(((u1, row), (u1, row + 1), (u1, row + 2), (f1, row + 1))):
            for s in range(2):
                near_stage[0, s, pl.ds(k * half_x, half_x), :] = ref.ref[r, s]
        out[pl.ds(0, size), :] = total
        out[pl.ds(size, 4 * half_x), :] = compress(near_stage, 2)


class Coarse:
    COUNT = 9

    @staticmethod
    def shapes(plan):
        rows = (2 * FAR + 1) * (plan.by // 4) + 1
        level2 = in_vmem(rows, 2, plan.nx // 4, LANES)
        level1 = in_vmem(plan.by // 2 + 8, 2, plan.nx // 2, LANES)
        return [level2] * 7 + [level1] * 2

    def __init__(self, plan, refs):
        self.plan = plan
        self.fields = [Wide(r) for r in refs[:5]]
        self.f, self.kx, self.ky, self.kz, self.d = self.fields
        self.w, self.u, self.f1, self.u1 = [Wide(r) for r in refs[5:]]
        self.block = plan.block_here()

    def spread(self, packed, at, turned):
        plan = self.plan
        own2, quarter_x = plan.by // 4, plan.nx // 4
        part = own2 // 2
        there = self.block + at - FAR
        exists = (there >= 0) & (there < plan.blocks)
        lane = lax.broadcasted_iota(jnp.int32, packed.shape, 1)
        for quarter in range(4):
            part_of, half = divmod(quarter, 2)
            s = half ^ turned
            a = pick_lanes(packed, lax.div(lane, 4) + quarter * (LANES // 4))
            for j in range(part):
                r = at * own2 + part_of * part + j
                tiles = [a[(t * part + j) * quarter_x : (t * part + j + 1) * quarter_x] for t in range(5)]
                for t, ref in enumerate(self.fields):
                    if t == 2:
                        ref.ref[r + 1, s] = jnp.where(exists, tiles[t], 0.0)
                    else:
                        ref.ref[r, s] = tiles[t]
                w = DAMPING * inverse(tiles[4])
                self.w.ref[r, s] = w
                self.u.ref[r, s] = w * tiles[0]

    def side(self, ref, ups, turned):
        plan = self.plan
        own, half_x = plan.by // 2, plan.nx // 2
        size = 5 * (plan.by // 8) * (plan.nx // 4)
        nearest = size + 4 * half_x
        for k, up in ups.items():
            first = 0 if k == 1 else nearest + (k - 2) * size
            self.spread(ref[pl.ds(first, size), :], jnp.where(up, FAR + k, FAR - k), turned)
        row = jnp.where(ups[1], own + 5, 0)
        for k, (to, r) in enumerate(((self.u1, row), (self.u1, row + 1), (self.u1, row + 2), (self.f1, row + 1))):
            row_in = ref[pl.ds(size + k * half_x, half_x), :]
            lane = lax.broadcasted_iota(jnp.int32, row_in.shape, 1)
            for s in range(2):
                to.ref[r, s ^ turned] = pick_lanes(row_in, lax.div(lane, 2) + s * (LANES // 2))

    def ups(self, opposite):
        one = lax.axis_index("gz") if self.plan.paired else 0
        one = 1 - one if opposite else one
        return {k: self.plan.is_up(self.block, k, one) for k in range(1, FAR + 1)}


def spread_kernel(plan, pack, mine, f1, u1, *refs):
    coarse = Coarse(plan, refs)
    own = plan.by // 2
    for r in range(2, own + 6):
        coarse.f1.ref[r] = f1[r]
    for r in range(3, own + 5):
        coarse.u1.ref[r] = u1[r]
    coarse.spread(pack[...], FAR, 0)
    coarse.side(mine, coarse.ups(False), 0)


def up_kernel(plan, theirs, *refs):
    count = Coarse.COUNT
    refs = refs[count:]
    kx0, ky0, kz0, d0, w0, f0, u0, kx1, ky1, kz1, w1 = [Wide(r) for r in refs[:11]]
    out, coarse, scratch = refs[11], Coarse(plan, refs[12 : 12 + count]), refs[12 + count :]
    f2, kx2, ky2, kz2, d2, w2, ua2 = *coarse.fields, coarse.w, coarse.u
    f1, ua1 = coarse.f1, coarse.u1
    wide = [Wide(r) for r in scratch]
    ub2, r2, f3, kx3, ky3, kz3, d3, w3, ua3, ub3 = wide[:10]
    t1, t0, ub1, ua0, ub0, uc0 = wide[10:]
    nx, by = plan.nx, plan.by
    own, own2 = by // 2, by // 4
    half_x, quarter_x = nx // 2, nx // 4
    here = lax.axis_index("gx")
    coarse.side(theirs, coarse.ups(True), 1 if plan.paired else 0)

    rows2 = (2 * FAR + 1) * own2
    two = Level(1, 4, kx2, ky2, kz2, d2, w2, f2, 14)
    two.sweep(ua2, ub2, 1, rows2 - 2)
    two.residual_pairs(ub2, r2, 2, rows2 // 2 - 2)

    x = lax.broadcasted_iota(jnp.int32, (quarter_x, WIDE), 0)
    even_x = (x & 1) == 0
    low = (lax.broadcasted_iota(jnp.int32, (quarter_x, WIDE), 1) & 4) == 0
    z_pair = z_pairs(low, 4)

    def x_pair(a):
        return a + jnp.where(even_x, x_up(a), x_down(a))

    last3 = rows2 // 2 - 2

    def coarsen(j):
        r = 2 * j
        kx = kx2[r] + kx2[r + 1]
        kz = kz2[r] + kz2[r + 1]
        inner = ky2[r + 1] + jnp.where(even_x, kx, 0.0) + jnp.where(low, kz, 0.0)
        f3[j] = z_pair(x_pair(r2[j - 1]))
        kx3[j] = z_pair(jnp.where(even_x, x_up(kx), kx))
        ky3[j + 1] = z_pair(x_pair(ky2[r + 2]))
        kz = x_pair(kz)
        kz3[j] = jnp.where(low, z_up(kz, 4), kz)
        d3[j] = z_pair(x_pair(d2[r] + d2[r + 1] - 2.0 * inner))

    each(1, last3, 6, coarsen)
    three = Level(2, 8, kx3, ky3, kz3, d3, w3, f3, 16)
    three.weigh(1, last3)
    three.first(ua3, 1, last3)
    three.sweep(ua3, ub3, 2, last3 - 1)
    three.sweep(ub3, ua3, 3, last3 - 2)
    three.sweep(ua3, ub3, 4, last3 - 3)

    first2 = FAR * own2
    for j in range(4, last3 - 2):
        e = ub3[j]
        ua2[2 * j] = ub2[2 * j] + e
        ua2[2 * j + 1] = ub2[2 * j + 1] + e
    two.sweep(ua2, ub2, first2 - 3, first2 + own2 + 2)
    two.sweep(ub2, ua2, first2 - 2, first2 + own2 + 1)

    one = Level(1, 2, kx1, ky1, kz1, None, w1, f1, 8)
    correct(ua1, ub1, ua2, t1, quarter_x, first2 - 2, first2 + own2 + 1, 0)
    one.sweep(ub1, ua1, 1, own + 6)
    one.sweep(ua1, ub1, 2, own + 5)

    finest = Level(1, 1, kx0, ky0, kz0, d0, w0, f0)

    def corrected(j):
        part = ub1[j]
        t0[j, pl.ds(0, half_x, stride=2)] = part
        t0[j, pl.ds(1, half_x, stride=2)] = part
        both = t0[j]
        ua0[2 * j - 1] = u0[2 * j - 1] + both
        ua0[2 * j] = u0[2 * j] + both

    def sweep(j):
        ub0[2 * j - 1] = finest.swept(ua0, 2 * j - 1)
        ub0[2 * j] = finest.swept(ua0, 2 * j)

    def sweep_again(j):
        uc0[2 * j] = finest.swept(ub0, 2 * j)
        uc0[2 * j + 1] = finest.swept(ub0, 2 * j + 1)

    slots = [plan.slot(s ^ here) for s in range(plan.gx)]

    def finish(j):
        for r in (2 * j - 1, 2 * j):
            scaled = d0[r] * uc0[r]
            rest = f0[r] + finest.beside(uc0, r) - scaled
            for s in range(plan.gx):
                part = slice(s * plan.px, (s + 1) * plan.px)
                out[slots[s], r - HALO, 0] = scaled[part, :LANES]
                out[slots[s], r - HALO, 1] = rest[part, :LANES]

    wave(
        (finish, 4, own + 3, 5),
        (sweep_again, 3, own + 3, 4),
        (sweep, 3, own + 4, 2),
        (corrected, 2, own + 5, 0),
    )


def place_kernel(plan, *refs):
    parts, outs, (fields, sems) = refs[: plan.gx], refs[plan.gx : plan.gx + 2], refs[plan.gx + 2 :]
    here = lax.axis_index("gx")
    by, px = plan.by, plan.px
    copies = []
    for slot, part in zip(plan.back, parts):
        rows = pl.ds(plan.start_of(here ^ plan.distance(slot)), by)
        for t, out in enumerate(outs):
            for p in range(px):
                fields[t, p, rows, :] = part[pl.ds(t * px + p, by, stride=2 * px), :]
            copy = pltpu.make_async_copy(fields.at[t, :, rows, :], out.at[0, :, rows, :], sems.at[t, slot])
            copy.start()
            copies.append(copy)
    for copy in copies:
        copy.wait()


def in_vmem(*shape):
    return pltpu.VMEM(shape, F32)


def call(kernel, out_shape, scratch=(), work=0, **more):
    if work:
        more["cost_estimate"] = pl.CostEstimate(flops=0, bytes_accessed=work, transcendentals=0)
    return pl.pallas_call(
        kernel,
        out_shape=out_shape,
        scratch_shapes=list(scratch),
        compiler_params=pltpu.CompilerParams(vmem_limit_bytes=VMEM_LIMIT),
        **more,
    )


def pinned(*arrays, where=pltpu.VMEM):
    return [pltpu.with_memory_space_constraint(a, where) for a in arrays]


def beside_in_z(plan, a):
    count = plan.gz
    if plan.paired:
        return lax.ppermute(a, "gz", [(0, 1), (1, 0)])
    cut = LANES // 2
    right = lax.ppermute(a[..., :cut], "gz", [(i + 1, i) for i in range(count - 1)])
    left = lax.ppermute(a[..., cut:], "gz", [(i, i + 1) for i in range(count - 1)])
    return jnp.concatenate([right, left], axis=-1)


def exchange(plan, parts):
    got = [parts[0]]
    for slot in range(1, plan.gx):
        pairs = []
        for i in range(plan.gx):
            for g in range(plan.gz):
                to = i ^ plan.distances(g % 2)[slot]
                pairs.append((i * plan.gz + g, to * plan.gz + g))
        got.append(lax.ppermute(parts[slot], ("gx", "gz"), pairs))
    return got


def partners(plan, k, one):
    partner = [None] * plan.blocks
    for b in range(plan.blocks - k):
        if b // k % 2 == one:
            partner[b], partner[b + k] = b + k, b
    return partner


def swap_blocks(plan, a, k, one):
    pairs = []
    for b, partner in enumerate(partners(plan, k, one)):
        for g in range(plan.gz):
            to = (b, g ^ 1) if partner is None else (partner, g)
            pairs.append((plan.device(b) * plan.gz + g, plan.device(to[0]) * plan.gz + to[1]))
    return lax.ppermute(a, ("gx", "gy", "gz"), pairs)


def swap_blocks_apart(plan, a, k):
    pairs = []
    for one in range(2):
        partner = partners(plan, k, one)
        alone = [b for b in range(plan.blocks) if partner[b] is None]
        low = [b for b in alone if 2 * b < plan.blocks]
        high = [b for b in alone if 2 * b >= plan.blocks]
        couples = [(low.pop(0), high.pop())] if len(low) % 2 else []
        for group in (low, high):
            couples += zip(group[::2], group[1::2])
        for x, y in couples:
            partner[x], partner[y] = y, x
        pairs += [(2 * plan.device(b) + one, 2 * plan.device(p) + one) for b, p in enumerate(partner)]
    return lax.ppermute(a, ("gx", "gy", "gz"), pairs)


def far_blocks(plan, pack, nears):
    def line(move, near):
        parts = [move(pack, k) for k in range(FAR, 1, -1)] + [move(near, 1)]
        return jnp.concatenate(parts[::-1], axis=0)

    if plan.paired:
        mine = line(functools.partial(swap_blocks_apart, plan), nears[0])
        return mine, beside_in_z(plan, mine)
    return [line(functools.partial(swap_blocks, plan, one=one), nears[one]) for one in range(2)]


def on_device(plan, phase, density, rhs):
    nx, by, rows, px, gx = plan.nx, plan.by, plan.rows, plan.px, plan.gx
    flat = by * 2 * px
    block = (px, plan.ny, LANES)
    outside = pl.BlockSpec(memory_space=pltpu.HBM)
    parts = call(
        functools.partial(prepare_kernel, plan),
        [in_vmem(flat, LANES)] * gx,
        [pltpu.VMEM(block, jnp.int32), in_vmem(*block), in_vmem(1, *block), pltpu.SemaphoreType.DMA((3,))],
        in_specs=[outside] * 3,
    )(*pinned(phase, density, rhs, where=pltpu.HBM))
    parts = [a.reshape(by, 2, px, LANES) for a in exchange(plan, parts)]
    c, *sets = call(
        functools.partial(gather_kernel, plan),
        [in_vmem(gx, by, 2, px, LANES)] + [in_vmem(gx, HALO + HALO_RHS, px, LANES)] * 2,
    )(*pinned(*parts))
    sides = jnp.concatenate([swap_blocks(plan, sets[one], 1, one) for one in (0, 1)], axis=0)
    zc = beside_in_z(plan, c)
    zsides = beside_in_z(plan, sides)

    own, own2 = by // 2, by // 4
    size = 5 * (own2 // 2) * (nx // 4)
    side = size + 4 * (nx // 2)

    def level0(n):
        return in_vmem(n, 2, nx, LANES)

    def level1(n):
        return in_vmem(n, 2, nx // 2, LANES)

    inner = call(functools.partial(inner_kernel, plan), Finest.shapes(plan), work=9_000_000)(*pinned(c, zc))
    near_count = 1 if plan.paired else 2
    outs = Finest.shapes(plan) + [in_vmem(size, LANES)] + [in_vmem(side, LANES)] * near_count + [level1(own + 8)] * 2
    scratch = [level1(own + 8), level1(own2), in_vmem(2, 2, size, LANES), in_vmem(1, 2, 4 * (nx // 2), LANES)]
    down = call(
        functools.partial(down_kernel, plan),
        outs,
        scratch,
        input_output_aliases={2 + k: k for k in range(Finest.COUNT)},
    )(*pinned(sides, zsides, *inner))
    fine, rest = down[: Finest.COUNT], down[Finest.COUNT :]
    pack, nears, (w1, u1) = rest[0], rest[1 : 1 + near_count], rest[1 + near_count :]
    kx1, ky1, kz1, _, f1 = fine[11:]
    mine, theirs = far_blocks(plan, pack, nears)
    coarse = call(functools.partial(spread_kernel, plan), Coarse.shapes(plan), work=3_000_000)(
        *pinned(pack, mine, f1, u1)
    )
    rows2 = (2 * FAR + 1) * own2
    level2, level3 = in_vmem(rows2 + 1, 2, nx // 4, LANES), in_vmem(rows2 // 2 + 1, 2, nx // 4, LANES)
    scratch = [level2] * 2 + [level3] * 8 + [level1(rows2), level0(own + 8), level1(own + 8)] + [level0(rows)] * 3
    result = call(
        functools.partial(up_kernel, plan),
        [in_vmem(gx, by, 2, px, LANES)] + Coarse.shapes(plan),
        scratch,
        input_output_aliases={1 + k: 1 + k for k in range(Coarse.COUNT)},
    )(*pinned(theirs, *coarse, *fine[:7], kx1, ky1, kz1, w1))[0]

    parts = exchange(plan, [result[k].reshape(flat, LANES) for k in range(gx)])
    return call(
        functools.partial(place_kernel, plan),
        [jax.ShapeDtypeStruct((1, px, plan.ny, LANES), F32)] * 2,
        [in_vmem(2, px, plan.ny, LANES), pltpu.SemaphoreType.DMA((2, gx))],
        out_specs=[outside] * 2,
    )(*pinned(*[parts[slot] for slot in plan.back]))


def solution(mesh):
    sizes = [mesh.shape[a] for a in ("gx", "gy", "gz")]

    def local(phase, density, rhs):
        return tuple(on_device(Plan(sizes, phase.shape), phase, density, rhs))

    in_specs = (P("gx", "gy", "gz"), P("gx", "gy", "gz"), P(None, "gx", "gy", "gz"))
    out_specs = (P(None, "gx", "gy", "gz"), P(None, "gx", "gy", "gz"))
    return jax.shard_map(local, mesh=mesh, in_specs=in_specs, out_specs=out_specs, check_vma=False)
```
